32 devices in a mesh: section: 2 (over x), group: 2 (over core), dp: 8 (over z, y).
Axes of the slice: x: 2, y: 2, z: 4, core: 2. Of those that a mesh axis runs over, the one named last changes fastest.
Arguments:
- ends: bfloat16 [2, 32, 128, 768], P('section', ('group', 'dp')), may hold values from -6 to 6
- w_qk: bfloat16 [2, 768, 1536], P('section', 'dp'), may hold values from -0.21875 to 0.21875
- w_value: bfloat16 [768, 1152], P('dp'), may hold values from -0.21875 to 0.21875
- w_out: bfloat16 [2, 768, 768], P('section', 'dp'), may hold values from -0.875 to 0.875
- w_fc: bfloat16 [2, 768, 3072], P('section', 'dp'), may hold values from -0.21875 to 0.21875
- w_proj: bfloat16 [2, 3072, 768], P('section', 'dp'), may hold values from -0.109375 to 0.109375
- gains: bfloat16 [2, 2, 768], P('section', None, 'dp'), may hold values from 0.5 to 1.5
- shifts: bfloat16 [2, 5, 768], P('section', None, 'dp'), may hold values from -1.796875 to 1.796875
- fc_shift: bfloat16 [2, 3072], P('section', 'dp'), may hold values from -1.796875 to 1.796875
- value_shift: bfloat16 [1152], P('dp'), may hold values from -1.796875 to 1.796875
Outputs:
- ends_out: bfloat16 [2, 32, 128, 768], P('section', ('group', 'dp'))
- grad_w_qk: float32 [2, 768, 1536], P('section', 'dp')
- grad_w_value: float32 [768, 1152], P('dp')
- grad_w_out: float32 [2, 768, 768], P('section', 'dp')
- grad_w_fc: float32 [2, 768, 3072], P('section', 'dp')
- grad_w_proj: float32 [2, 3072, 768], P('section', 'dp')
- grad_gains: float32 [2, 2, 768], P('section', None, 'dp')
- grad_shifts: float32 [2, 5, 768], P('section', None, 'dp')
- grad_fc_shift: float32 [2, 3072], P('section', 'dp')
- grad_value_shift: float32 [1152], P('dp')
The draws below stay inside these ranges and needn't reach their ends.
All inputs are finite; a program needn't handle non-finite values.
Results may differ from the reference program's by a relative error of at most 0.02.
Values may be sent and summed in bfloat16 or wider, within the bound.
No kernel may reach another device: no remote copies, remote signals or barrier semaphores. Data moves between devices by JAX's collectives and lax.ppermute only.
A program may use at most 128 MiB of HBM per device.

```python
import jax
import jax.numpy as jnp
from jax import lax

D = 768
HEADS = 12
FF = 3072
VW = 1152
SEQ = 128
SEQS = 32


def steps_of(stream_key, shape, pieces, least, top_value):
    level, own = 1.0, jax.random.fold_in(stream_key, 6)
    for axis_at, shards_of in pieces:
        steps = jnp.exp(jax.random.uniform(jax.random.fold_in(own, axis_at), (shards_of,), jnp.float32, least / len(pieces), top_value / len(pieces)))
        level = level * jnp.repeat(steps, shape[axis_at] // shards_of).reshape([-1 if axis == axis_at else 1 for axis in range(len(shape))])
    return level


def scatter_about(own_key, shape, spread, most, pieces=(), kind=jnp.bfloat16):
    drawn = jax.random.normal(own_key, shape, jnp.float32) * spread
    if len(pieces) > 0:
        drawn = steps_of(own_key, shape, pieces, -0.22, 0.18) * drawn
    return jnp.clip(drawn, min=-most, max=most).astype(kind)


def setup_inputs(seed: int = 0) -> dict:
    keys = jax.random.split(jax.random.key(seed), 11)
    ends = scatter_about(keys[0], (2, SEQS, SEQ, D), 1.0, 6.0, ((0, 2), (1, 16)))
    w_qk = scatter_about(keys[1], (2, D, 2 * D), D ** -0.5, 0.21875, ((0, 2), (1, 8)))
    w_value = scatter_about(keys[2], (D, VW), D ** -0.5, 0.21875, ((0, 8),))
    w_out = scatter_about(keys[3], (2, D, D), (D // 16) ** -0.5, 0.875, ((0, 2), (1, 8)))
    w_fc = scatter_about(keys[4], (2, D, FF), D ** -0.5, 0.21875, ((0, 2), (1, 8)))
    w_proj = scatter_about(keys[5], (2, FF, D), FF ** -0.5, 0.109375, ((0, 2), (1, 8)))
    gains = jnp.clip(1.0 + 0.1 * jax.random.normal(keys[6], (2, 2, D), jnp.float32), 0.5, 1.5).astype(jnp.bfloat16)
    shifts = scatter_about(keys[7], (2, 5, D), 0.3, 1.796875, ((0, 2), (2, 8)))
    fc_shift = scatter_about(keys[8], (2, FF), 0.3, 1.796875, ((0, 2), (1, 8)))
    value_shift = scatter_about(keys[9], (VW,), 0.3, 1.796875, ((0, 8),))
    return {"ends": ends, "w_qk": w_qk, "w_value": w_value, "w_out": w_out, "w_fc": w_fc, "w_proj": w_proj, "gains": gains, "shifts": shifts, "fc_shift": fc_shift, "value_shift": value_shift}


norm_eps = 1e-05
masked_score = -1e+30

@jax.custom_vjp
def low(v):
    return lax.optimization_barrier(v.astype(jnp.bfloat16)).astype(jnp.float32)

@jax.custom_vjp
def low_back(v):
    return v

def low_keep(v):
    return (low(v), None)

def low_pass(kept, grad):
    return (grad,)

def back_keep(v):
    return (v, None)

def back_low(kept, grad):
    return (low(grad),)
low.defvjp(low_keep, low_pass)
low_back.defvjp(back_keep, back_low)

def matmul(left_op, right_op):
    return jnp.einsum('...d,de->...e', left_op, right_op, precision=lax.Precision.HIGHEST)

def normalize(rows, gain_row, shift_row):
    centered = rows - lax.optimization_barrier(jnp.mean(rows, axis=-1, keepdims=True))
    inv_std = lax.rsqrt(lax.optimization_barrier(jnp.mean(centered * centered, axis=-1, keepdims=True)) + norm_eps)
    return centered * inv_std * gain_row + shift_row

def attention(queries, key_rows, values):
    batch_size, seq_len, model_width = queries.shape
    head_size = model_width // HEADS
    query_heads = queries.reshape(batch_size, seq_len, HEADS, head_size)
    key_heads = key_rows.reshape(batch_size, seq_len, HEADS, head_size)
    value_heads = values.reshape(batch_size, seq_len, HEADS, head_size)
    scores = jnp.einsum('bqhd,bkhd->bhqk', query_heads, key_heads, precision=lax.Precision.HIGHEST)
    scores = low_back(scores * head_size ** (-0.5))
    positions = jnp.arange(seq_len)
    causal_mask = positions[:, None] >= positions[None, :]
    attn_prob = jax.nn.softmax(jnp.where(causal_mask, scores, masked_score), axis=-1)
    mixed = jnp.einsum('bhqk,bkhd->bqhd', low(attn_prob), value_heads, precision=lax.Precision.HIGHEST)
    return mixed.reshape(batch_size, seq_len, model_width)

def layer(inputs, w_qk, w_own, b_own, w_other, b_other, reused, w_out, w_fc, w_proj, gain_rows, shift_rows, fc_bias):
    model_width = inputs.shape[-1]
    normed = low(normalize(inputs, gain_rows[0], shift_rows[0]))
    query_key = matmul(normed, w_qk)
    queries = low_back(low(query_key[..., :model_width] + shift_rows[2]))
    key_rows = low_back(low(query_key[..., model_width:]))
    own_vals = low_back(low(matmul(normed, w_own) + b_own))
    if reused is None:
        other_vals = low_back(low(matmul(normed, w_other) + b_other))
    else:
        other_vals = reused
    values = jnp.concatenate([own_vals, other_vals], axis=-1)
    mixed = low_back(low(attention(queries, key_rows, values)))
    residual = inputs + low_back(matmul(mixed, w_out) + shift_rows[3])
    normed_two = low(normalize(residual, gain_rows[1], shift_rows[1]))
    pre_act = low_back(matmul(normed_two, w_fc) + fc_bias)
    hidden = low(jax.nn.gelu(pre_act, approximate=True))
    return (residual + low_back(matmul(hidden, w_proj) + shift_rows[4]), values)

def network(params, inputs):
    w_qk, w_value, w_out, w_fc, w_proj, gains, shifts, fc_shift, value_shift = params
    half_width = D // 2
    first_out, first_values = layer(inputs, w_qk[0], w_value[:, :half_width], value_shift[:half_width], w_value[:, half_width:D], value_shift[half_width:D], None, w_out[0], w_fc[0], w_proj[0], gains[0], shifts[0], fc_shift[0])
    passed = low_back(low(first_out))
    reused = low_back(first_values[..., half_width:])
    second_out, unused_vals = layer(passed, w_qk[1], w_value[:, D:], value_shift[D:], None, None, reused, w_out[1], w_fc[1], w_proj[1], gains[1], shifts[1], fc_shift[1])
    return second_out

def reference(ends, w_qk, w_value, w_out, w_fc, w_proj, gains, shifts, fc_shift, value_shift):
    params = tuple((item.astype(jnp.float32) for item in (w_qk, w_value, w_out, w_fc, w_proj, gains, shifts, fc_shift, value_shift)))
    per_block = 4
    block_count = ends.shape[1] // per_block
    inputs = ends[0].astype(jnp.float32).reshape(block_count, per_block, SEQ, D)
    cotangents = ends[1].astype(jnp.float32).reshape(block_count, per_block, SEQ, D)

    def one_block(totals, pair):
        block_in, block_cot = pair
        block_out, pull_back = jax.vjp(network, params, block_in)
        grad_params, grad_in = pull_back(block_cot)
        totals = jax.tree.map(lambda left_op, right_op: left_op + right_op, totals, grad_params)
        return (totals, (block_out, grad_in))
    start_totals = jax.tree.map(jnp.zeros_like, params)
    totals, (outputs, grad_inputs) = lax.scan(one_block, start_totals, (inputs, cotangents))
    outputs = outputs.reshape(ends.shape[1:])
    grad_inputs = grad_inputs.reshape(ends.shape[1:])
    ends_out = jnp.stack([grad_inputs, outputs]).astype(jnp.bfloat16)
    return (ends_out, totals[0], totals[1], totals[2], totals[3], totals[4], totals[5], totals[6], totals[7], totals[8])
```

```python
import jax
import jax.numpy as jnp
from jax import lax
from jax.sharding import PartitionSpec as P

HEADS = 12
BF = jnp.bfloat16
F32 = jnp.float32
norm_eps = 1e-05
masked_score = -1e30
SMALL = 16


def ring_order(count):
    wide = 2 if count < 16 else 4
    tall = count // wide
    order = [i * wide for i in range(tall)]
    for n, row in enumerate(reversed(range(tall))):
        cols = range(1, wide)
        order += [row * wide + col for col in (cols if n % 2 == 0 else reversed(cols))]
    return order


def dot(a, b):
    return jnp.dot(a, b, preferred_element_type=F32)


def dot_tn(a, b):
    return lax.dot_general(a, b, (((0,), (0,)), ((), ())), preferred_element_type=F32)


def dot_nt(a, b):
    return lax.dot_general(a, b, (((1,), (1,)), ((), ())), preferred_element_type=F32)


def unit_rows(v):
    centered = v - jnp.mean(v, axis=-1, keepdims=True)
    inv = lax.rsqrt(jnp.mean(centered * centered, axis=-1, keepdims=True) + norm_eps)
    return centered * inv, inv


def norm_back(dn, x, inv, gain):
    scaled = dn * gain
    inner = jnp.mean(scaled * x, axis=-1, keepdims=True)
    return inv * (scaled - jnp.mean(scaled, axis=-1, keepdims=True) - x * inner)


def colsum(v):
    return jnp.sum(v.astype(F32), axis=0)


def heads_of(x, seqs, heads):
    return x.reshape(seqs, -1, heads, x.shape[1] // heads)


def f1(h, wq, wk, wv, wo, prm, v_in, seqs, heads):
    g0, b0, bq, bv = prm["g0"], prm["b0"], prm["bq"], prm["bv"]
    x, _ = unit_rows(h.astype(F32))
    a = (x * g0 + b0).astype(BF)
    q = (dot(a, wq) + bq).astype(BF)
    k = dot(a, wk).astype(BF)
    v = (dot(a, wv) + bv).astype(BF)
    if v_in is not None:
        reuse, old = v_in
        v = jnp.where(reuse, old, v)
    qh, kh, vh = (heads_of(i, seqs, heads) for i in (q, k, v))
    sc = jnp.einsum("nqhd,nkhd->nhqk", qh, kh, preferred_element_type=F32) * qh.shape[-1] ** -0.5
    size = sc.shape[-1]
    mask = lax.broadcasted_iota(jnp.int32, (size, size), 0) >= lax.broadcasted_iota(jnp.int32, (size, size), 1)
    p = jax.nn.softmax(jnp.where(mask, sc, masked_score), axis=-1).astype(BF)
    o = jnp.einsum("nhqk,nkhd->nqhd", p, vh, preferred_element_type=F32).reshape(q.shape).astype(BF)
    return dot(o, wo).astype(BF), (q, k, v, p, o)


def f2(r, wfc, wproj, prm):
    x, _ = unit_rows(r)
    cn = (x * prm["g1"] + prm["b1"]).astype(BF)
    z = dot(cn, wfc) + prm["bf"]
    th = jnp.tanh(0.7978845608 * (z + 0.044715 * z * z * z))
    u = (0.5 * z * (1 + th)).astype(BF)
    gp = 0.5 * (1 + th) + 0.5 * z * (1 - th * th) * 0.7978845608 * (1 + 3 * 0.044715 * z * z)
    return dot(u, wproj).astype(BF), (u, gp.astype(BF))


def b2(e, u, gp, r, wfc, wproj, prm):
    g_proj = dot_tn(u, e)
    dz = (dot_nt(e, wproj) * gp.astype(F32)).astype(BF)
    x, _ = unit_rows(r)
    cn = (x * prm["g1"] + prm["b1"]).astype(BF)
    g_fc = dot_tn(cn, dz)
    return dot_nt(dz, wfc).astype(BF), g_proj, g_fc, colsum(e), colsum(dz)


def b1(e, dc, r, h, q, k, v, p, o, wq, wk, wv, wo, prm, seqs, heads, extra, fresh):
    x, inv = unit_rows(r)
    dr = e.astype(F32) + norm_back(dc, x, inv, prm["g1"])
    sg1, sb1 = colsum(dc * x), colsum(dc)
    dy = dr.astype(BF)
    g_o = dot_tn(o, dy)
    do = dot_nt(dy, wo).astype(BF)
    qh, kh, vh, dh = (heads_of(i, seqs, heads) for i in (q, k, v, do))
    scale = qh.shape[-1] ** -0.5
    dp = jnp.einsum("nqhd,nkhd->nhqk", dh, vh, preferred_element_type=F32)
    dv = jnp.einsum("nhqk,nqhd->nkhd", p, dh, preferred_element_type=F32).reshape(q.shape)
    pf = p.astype(F32)
    ds = (pf * (dp - jnp.sum(pf * dp, axis=-1, keepdims=True))).astype(BF)
    dq = (jnp.einsum("nhqk,nkhd->nqhd", ds, kh, preferred_element_type=F32) * scale).reshape(q.shape).astype(BF)
    dk = (jnp.einsum("nhqk,nqhd->nkhd", ds, qh, preferred_element_type=F32) * scale).reshape(q.shape).astype(BF)
    if extra is not None:
        dv = dv + extra.astype(F32)
    dv = dv.astype(BF)
    xa, _ = unit_rows(h.astype(F32))
    a = (xa * prm["g0"] + prm["b0"]).astype(BF)
    da = dot_nt(dq, wq) + dot_nt(dk, wk) + dot_nt(dv, wv) * fresh
    return da.astype(BF), dr, g_o, dot_tn(a, dq), dot_tn(a, dk), dot_tn(a, dv), dv, (sg1, sb1, colsum(dq), colsum(dy), colsum(dv))


def b0(dr, da, h, prm):
    x, inv = unit_rows(h.astype(F32))
    dh = dr + norm_back(da, x, inv, prm["g0"])
    return dh.astype(BF), colsum(da * x), colsum(da)


def per_device(ends, w_qk, w_value, w_out, w_fc, w_proj, gains, shifts, fc_shift, value_shift):
    s, grp, d = lax.axis_index("section"), lax.axis_index("group"), lax.axis_index("dp")
    c = grp % 2
    count, groups = lax.axis_size("dp"), lax.axis_size("group")
    rows, width = w_qk.shape[1], ends.shape[3]
    half = width // 2
    ff = w_fc.shape[2]
    unit = ff // count // 2
    fh = ff // 2
    seqs, seq = ends.shape[1], ends.shape[2]
    heads = HEADS // 2
    tokens = seqs * seq
    order = ring_order(count)
    place = [0] * count
    for i, dev in enumerate(order):
        place[dev] = i
    pos = jnp.array(place, jnp.int32)[d]
    order_arr = jnp.array(order, jnp.int32)
    routes = [
        [(order[i], order[(i + 1) % count]) for i in range(count)],
        [(order[(i + 1) % count], order[i]) for i in range(count)],
    ]
    way = (1, -1)

    def swap_x(x):
        return lax.ppermute(x, "section", [(0, 1), (1, 0)])

    def swap_c(x):
        return lax.ppermute(x, "group", [(i, i ^ 1) for i in range(groups)])

    first = s == 0
    even = d % 2 == 0
    hc = count // 2
    spread = [
        [(l * count + i, (i // hc) * count + 2 * (i % hc) + (l if w == 0 else 1 - l)) for l in range(2) for i in range(count)]
        for w in range(2)
    ]
    o_lo, o_hi = w_out[0][:, :half], w_out[0][:, half:]
    o_a = lax.ppermute(jnp.where(first, o_lo, o_hi), ("section", "dp"), spread[0])
    o_b = lax.ppermute(jnp.where(first, o_hi, o_lo), ("section", "dp"), spread[1])
    o_blocks = (jnp.where(even, o_a, o_b), jnp.where(even, o_b, o_a))

    qk = w_qk[0].reshape(rows, 2, 2, half)
    fc = w_fc[0].reshape(rows, count, 2, unit).transpose(2, 0, 1, 3).reshape(2, rows, 4, half).transpose(0, 2, 1, 3)
    proj = w_proj[0].reshape(2, 2, rows, 2, half).transpose(0, 1, 3, 2, 4).reshape(2, 4, rows, half)

    def pick(blocks, side):
        return lax.dynamic_slice_in_dim(lax.dynamic_index_in_dim(blocks, side, 0, False), 2 * c, 2, 0)

    small_own = jnp.concatenate([gains[0].reshape(-1), shifts[0].reshape(-1), fc_shift[0]])

    def side_pack(side):
        q = lax.dynamic_index_in_dim(qk[:, 0], side, 1, False)
        k = lax.dynamic_index_in_dim(qk[:, 1], side, 1, False)
        return q, k, pick(fc, side), pick(proj, side)

    mine = side_pack(s)
    theirs = jax.tree.map(swap_x, side_pack(1 - s))
    small_other = swap_x(small_own)
    lay = [
        jax.tree.map(lambda m, t: jnp.where(first, m, t), mine, theirs),
        jax.tree.map(lambda m, t: jnp.where(first, t, m), mine, theirs),
    ]
    v_side = (
        lax.dynamic_slice_in_dim(w_value, s * half, half, 1),
        w_value[:, width:],
    )
    small = jnp.concatenate(
        [jnp.where(first, small_own, small_other), jnp.where(first, small_other, small_own), value_shift]
    )
    small_n = small.shape[0]
    small_rows = jnp.pad(small, (0, SMALL * half - small_n)).reshape(SMALL, half)

    def gather(l):
        q, k, f, p = lay[l]
        a0 = jnp.where(c == 0, q, v_side[l])
        a1 = jnp.where(c == 0, k, o_blocks[l])
        x0 = [a0, f[0], p[0]] + ([small_rows] if l == 0 else [])
        x1 = [a1, f[1], p[1]]
        got = []
        for t, x in enumerate((x0, x1)):
            x = jnp.concatenate(x, axis=0)
            steps = [x]
            for _ in range(count - 1):
                x = lax.ppermute(x, "dp", routes[t])
                steps.append(x)
            got.append((steps, [swap_c(x) for x in steps]))
        return got

    def assemble(got):
        wq = jnp.zeros((width, half), BF)
        wk, wv = wq, wq
        wo = jnp.zeros((half, width), BF)
        wfc = jnp.zeros((width, fh), BF)
        wproj = jnp.zeros((fh, width), BF)
        put = lax.dynamic_update_slice
        for t in range(2):
            for n in range(count):
                sh = order_arr[(pos - way[t] * n) % count]
                for same in range(2):
                    blk = got[t][same][n]
                    core = c ^ same
                    at, fcb, prb = blk[:rows], blk[rows : 2 * rows], blk[2 * rows : 3 * rows]
                    if t == 0:
                        wq = jnp.where(core == 0, put(wq, at, (sh * rows, 0)), wq)
                        wv = jnp.where(core == 1, put(wv, at, (sh * rows, 0)), wv)
                    else:
                        wk = jnp.where(core == 0, put(wk, at, (sh * rows, 0)), wk)
                        wo = jnp.where(core == 1, put(wo, at, (sh // 2 * rows, sh % 2 * half)), wo)
                    wfc = put(wfc, fcb, (sh * rows, (2 * core + t) * half))
                    wproj = put(wproj, prb, (sh * 2 * rows + core * rows, t * half))
        return wq, wk, wv, wo, wfc, wproj

    got0, got1 = gather(0), gather(1)
    smalls = jnp.zeros((count, small_n), BF)
    for n in range(count):
        sh = order_arr[(pos - n) % count]
        smalls = lax.dynamic_update_slice(smalls, got0[0][0][n][3 * rows :].reshape(1, -1)[:, :small_n], (sh, 0))
    smalls = smalls.astype(F32)
    W = [assemble(got0), assemble(got1)]
    per_layer = 11 * rows
    vals = smalls[:, 2 * per_layer :].reshape(-1)

    def params(l):
        m = smalls[:, l * per_layer : (l + 1) * per_layer]
        rws = m[:, : 7 * rows].reshape(count, 7, rows).transpose(1, 0, 2).reshape(7, width)
        bf = lax.dynamic_index_in_dim(m[:, 7 * rows :].reshape(count, 2, unit), s, 1, False).reshape(-1)
        bv = lax.dynamic_slice_in_dim(vals, s * half, half, 0) if l == 0 else vals[width:]
        bq = lax.dynamic_slice_in_dim(rws[4], s * half, half, 0)
        return dict(g0=rws[0], g1=rws[1], b0=rws[2], b1=rws[3], bq=bq, b3=rws[5], b4=rws[6], bf=bf, bv=bv)

    prm = [params(0), params(1)]

    ends_own = ends[0].reshape(tokens, width)
    ends_other = swap_x(ends_own)
    h = jnp.where(first, ends_own, ends_other)
    cot = jnp.where(first, ends_other, ends_own)
    kept = []
    v_in = None
    hs = []
    rs = []
    for l in range(2):
        wq, wk, wv, wo, wfc, wproj = W[l]
        hs.append(h)
        part, att = f1(h, wq, wk, wv, wo, prm[l], v_in, seqs, heads)
        r = h.astype(F32) + (part.astype(F32) + swap_x(part).astype(F32)) + prm[l]["b3"]
        rs.append(r)
        part, mlp = f2(r, wfc, wproj, prm[l])
        kept.append((att, mlp))
        h = (r + (part.astype(F32) + swap_x(part).astype(F32)) + prm[l]["b4"]).astype(BF)
        v_in = (s == 1, att[2])
    y_out = h

    e = cot
    extra = None
    grads = [None, None]
    for l in (1, 0):
        wq, wk, wv, wo, wfc, wproj = W[l]
        (q, k, v, p, o), (u, gp) = kept[l]
        part, g_proj, g_fc, sb4, sbf = b2(e, u, gp, rs[l], wfc, wproj, prm[l])
        dc = part.astype(F32) + swap_x(part).astype(F32)
        fresh = jnp.where(first, 1.0, 0.0) if l == 1 else 1.0
        part, dr, g_o, g_q, g_k, g_v, dv, (sg1, sb1, sbq, sb3, sbv) = b1(
            e, dc, rs[l], hs[l], q, k, v, p, o, wq, wk, wv, wo, prm[l], seqs, heads, extra, fresh
        )
        da = part.astype(F32) + swap_x(part).astype(F32)
        e, sg0, sb0 = b0(dr, da, hs[l], prm[l])
        extra = jnp.where(s == 1, dv, jnp.zeros_like(dv))
        grads[l] = (g_q, g_k, g_v, g_o, g_fc, g_proj, (sg0, sg1, sb0, sb1, sbq, sb3, sb4, sbf, sbv))
    x_out = e

    def small_grads():
        zero = jnp.zeros((half,), F32)
        out = []
        for l in range(2):
            sg0, sg1, sb0, sb1, sbq, sb3, sb4, sbf, sbv = grads[l][6]
            bq = jnp.where(first, jnp.concatenate([sbq, zero]), jnp.concatenate([zero, sbq]))
            rws = jnp.stack([sg0, sg1, sb0, sb1, bq, sb3, sb4]).reshape(7, count, rows).transpose(1, 0, 2).reshape(count, 7 * rows)
            bf = sbf.reshape(count, 1, unit)
            bf = jnp.where(first, jnp.concatenate([bf, 0 * bf], 1), jnp.concatenate([0 * bf, bf], 1)).reshape(count, 2 * unit)
            out += [rws, bf]
        v1, v2 = grads[0][6][8], grads[1][6][8]
        vs = jnp.where(first, jnp.concatenate([v1, zero, v2]), jnp.concatenate([zero, v1, zero]))
        out.append(vs.reshape(count, -1))
        flat = jnp.concatenate(out, axis=1)
        return jnp.pad(flat, ((0, 0), (0, SMALL * half - small_n))).reshape(count, SMALL, half).astype(BF)

    def chunks(l):
        g_q, g_k, g_v, g_o, g_fc, g_proj, _ = grads[l]
        att = [i.reshape(count, rows, half) for i in (g_q, g_k, g_v)]
        att.append(g_o.reshape(hc, rows, 2, half).transpose(0, 2, 1, 3).reshape(count, rows, half))
        att = jnp.stack(att).astype(BF)
        fcb = g_fc.reshape(count, rows, 4, half).transpose(2, 0, 1, 3).astype(BF)
        prb = g_proj.reshape(count, 2, rows, 2, half).transpose(1, 3, 0, 2, 4).reshape(4, count, rows, half).astype(BF)
        allq = jnp.concatenate([att[jnp.array([0, 1, 2, 3])], fcb, prb], axis=2).reshape(2, 2, count, 3 * rows, half)
        return allq

    def reduce_ring(x, t):
        def own(n):
            return lax.dynamic_index_in_dim(x, order_arr[(pos - way[t] * (n + 1)) % count], 0, False).astype(F32)

        run = own(0).astype(BF)
        for n in range(1, count):
            run = lax.ppermute(run, "dp", routes[t])
            run = run.astype(F32) + own(n)
            if n < count - 1:
                run = run.astype(BF)
        total = run
        for n in range(1, groups // 2):
            total = total + lax.ppermute(run.astype(BF), "group", [(i, (i + 2 * n) % groups) for i in range(groups)]).astype(F32)
        return total

    red = []
    sm = small_grads()
    for l in range(2):
        allq = chunks(l)
        own = lax.dynamic_index_in_dim(allq, c, 0, False)
        sib = swap_c(lax.dynamic_index_in_dim(allq, 1 - c, 0, False))
        tot = own.astype(F32) + sib.astype(F32)
        xs = [tot[0], tot[1]]
        if l == 0:
            sm_tot = sm.astype(F32) + swap_c(sm).astype(F32)
            xs[0] = jnp.concatenate([xs[0], sm_tot], axis=1)
        res = [reduce_ring(xs[t], t) for t in range(2)]
        red.append(res)

    small_tot = red[0][0][3 * rows :].reshape(-1)[:small_n]
    red[0][0] = red[0][0][: 3 * rows]
    r2 = [jnp.stack(red[l]).astype(BF) for l in range(2)]
    send = jnp.where(first, r2[1], r2[0])
    keep = jnp.where(first, r2[0], r2[1])
    recv = swap_x(send)
    both = jnp.where(first, jnp.stack([keep, recv]), jnp.stack([recv, keep]))
    sibl = swap_c(both)
    full = jnp.where(c == 0, jnp.stack([both, sibl]), jnp.stack([sibl, both])).astype(F32)
    full = full.reshape(2, 2, 2, 3, rows, half)
    o_qk = jnp.concatenate([full[0, 0, 0, 0], full[0, 1, 0, 0], full[0, 0, 1, 0], full[0, 1, 1, 0]], axis=1)
    o_fc = full[:, :, :, 1].transpose(1, 3, 0, 2, 4).reshape(2, rows, count, unit).transpose(1, 2, 0, 3).reshape(rows, ff)
    o_proj = full[:, :, :, 2].transpose(1, 0, 3, 2, 4).reshape(4 * rows, width)
    my_o = [jnp.where(c == 1, r2[l][1, :rows], jnp.zeros((rows, half), BF)) for l in range(2)]
    my_o = [i + swap_c(i) for i in my_o]
    back = [[(b, a) for a, b in w] for w in spread]
    out_a = lax.ppermute(jnp.where(even, my_o[0], my_o[1]), ("section", "dp"), back[0])
    out_b = lax.ppermute(jnp.where(even, my_o[1], my_o[0]), ("section", "dp"), back[1])
    o_out = jnp.where(first, jnp.concatenate([out_a, out_b], 1), jnp.concatenate([out_b, out_a], 1)).astype(F32)
    my_v = [jnp.where(c == 1, r2[l][0, :rows], jnp.zeros((rows, half), BF)) for l in range(2)]
    my_v = [i + swap_c(i) for i in my_v]
    their_v = [swap_x(i) for i in my_v]
    v10 = jnp.where(first, my_v[0], their_v[0])
    v11 = jnp.where(first, their_v[0], my_v[0])
    v20 = jnp.where(first, my_v[1], their_v[1])
    o_val = jnp.concatenate([v10, v11, v20], axis=1).astype(F32)
    other = swap_x(small_tot.astype(BF)).astype(F32)
    n7 = 7 * rows

    def layer_small(l):
        lo = l * per_layer
        mine_, oth = small_tot[lo : lo + per_layer], other[lo : lo + per_layer]
        rw = mine_[:n7].reshape(7, rows)
        bq = (mine_ + oth)[:n7].reshape(7, rows)[4]
        return rw[:2], jnp.concatenate([rw[2:4], bq[None], rw[5:]], 0), (mine_ + oth)[n7:]

    sm0, sm1 = layer_small(0), layer_small(1)
    o_gain, o_shift, o_bf = (jnp.where(first, a, b) for a, b in zip(sm0, sm1))
    o_vs = (small_tot + other)[2 * per_layer :]
    res = jnp.where(first, x_out, y_out).reshape(1, seqs, seq, width)
    return (res, o_qk[None], o_val, o_out[None], o_fc[None], o_proj[None], o_gain[None], o_shift[None], o_bf[None], o_vs)


def solution(mesh):
    placed = (
        P("section", ("group", "dp"), None, None),
        P("section", "dp", None),
        P("dp", None),
        P("section", "dp", None),
        P("section", "dp", None),
        P("section", "dp", None),
        P("section", None, "dp"),
        P("section", None, "dp"),
        P("section", "dp"),
        P("dp"),
    )
    return jax.shard_map(per_device, mesh=mesh, in_specs=placed, out_specs=placed, check_vma=False)
```

```python
import functools

import jax
import jax.numpy as jnp
import numpy as np
from jax import lax
from jax.experimental import pallas as pl
from jax.experimental.pallas import tpu as pltpu
from jax.sharding import PartitionSpec as P

HEADS = 12
BF = jnp.bfloat16
F32 = jnp.float32
norm_eps = 1e-05
masked_score = -1e30
SMALL = 16


def ring_order(count):
    wide = 2 if count < 16 else 4
    tall = count // wide
    order = [i * wide for i in range(tall)]
    for n, row in enumerate(reversed(range(tall))):
        cols = range(1, wide)
        order += [row * wide + col for col in (cols if n % 2 == 0 else reversed(cols))]
    return order


def dot(a, b):
    return jnp.dot(a, b, preferred_element_type=F32)


def dot_tn(a, b):
    return lax.dot_general(a, b, (((0,), (0,)), ((), ())), preferred_element_type=F32)


def dot_nt(a, b):
    return lax.dot_general(a, b, (((1,), (1,)), ((), ())), preferred_element_type=F32)


def unit_rows(v):
    centered = v - jnp.mean(v, axis=-1, keepdims=True)
    inv = lax.rsqrt(jnp.mean(centered * centered, axis=-1, keepdims=True) + norm_eps)
    return centered * inv, inv


def norm_back(dn, x, inv, gain):
    scaled = dn * gain
    inner = jnp.mean(scaled * x, axis=-1, keepdims=True)
    return inv * (scaled - jnp.mean(scaled, axis=-1, keepdims=True) - x * inner)


def colsum(v):
    return jnp.sum(v.astype(F32), axis=0)


VMEM_BYTES = 56 * 1024 * 1024


class Plan:
    def __init__(self, count, rows, width, fh, tokens, seq, heads):
        self.count, self.rows, self.width, self.half = count, rows, width, width // 2
        self.fh, self.tokens, self.seq = fh, tokens, seq
        self.seqs = tokens // seq
        self.pairs = heads // 2


def dma(src, dst, sem):
    return pltpu.make_async_copy(src, dst, sem)


def start_att(pl_, idx, chunks, wqk, wv, wo, sems):
    n_, r_, h_ = pl_.count, pl_.rows, pl_.half
    c = idx[2 * n_]
    for t in range(2):
        for same in range(2):
            core = c if same == 0 else 1 - c
            for n in range(n_):
                sh = idx[t * n_ + n]
                src = chunks[(t * 2 + same) * n_ + n].at[pl.ds(0, r_), :]
                row = pl.multiple_of(sh * r_, 16)

                @pl.when(core == 0)
                def _():
                    dma(src, wqk.at[pl.ds(row, r_), pl.ds(t * h_, h_)], sems.at[0]).start()

                @pl.when(core == 1)
                def _():
                    if t == 0:
                        dma(src, wv.at[pl.ds(row, r_), :], sems.at[1]).start()
                    else:
                        orow = pl.multiple_of((sh // 2) * r_, 16)
                        ocol = pl.multiple_of((sh % 2) * h_, 128)
                        dma(src, wo.at[pl.ds(orow, r_), pl.ds(ocol, h_)], sems.at[2]).start()


def start_mlp(pl_, idx, chunks, wfc, wproj, sems):
    n_, r_, h_ = pl_.count, pl_.rows, pl_.half
    c = idx[2 * n_]
    for kind in range(2):
        for t in range(2):
            for same in range(2):
                core = c if same == 0 else 1 - c
                for n in range(n_):
                    sh = idx[t * n_ + n]
                    src = chunks[(t * 2 + same) * n_ + n].at[pl.ds((1 + kind) * r_, r_), :]
                    if kind == 0:
                        row = pl.multiple_of(sh * r_, 16)
                        col = pl.multiple_of((2 * core + t) * h_, 128)
                        dst = wfc.at[pl.ds(row, r_), pl.ds(col, h_)]
                    else:
                        row = pl.multiple_of(sh * 2 * r_ + core * r_, 16)
                        dst = wproj.at[pl.ds(row, r_), pl.ds(t * h_, h_)]
                    dma(src, dst, sems.at[kind]).start()


def wait_all(ref, sem):
    dma(ref, ref, sem).wait()


STEP = 32


def normed(src, gain, bias, dst, tokens):
    for i in range(0, tokens, STEP):
        x, _ = unit_rows(src(i))
        dst[i : i + STEP, :] = (x * gain + bias).astype(BF)


def pair_masks(seq, lanes):
    low = lax.broadcasted_iota(jnp.int32, (seq, lanes), 1) < lanes // 2
    return low


def stack_pair(x, low):
    zero = jnp.zeros_like(x)
    return jnp.concatenate([jnp.where(low, x, zero), jnp.where(low, zero, x)], axis=0)


def f1_kernel(pl_, layer, *refs):
    n_, h_, d_, t_, sq = pl_.count, pl_.half, pl_.width, pl_.tokens, pl_.seq
    idx, h, prm = refs[:3]
    refs = refs[3:]
    if layer == 1:
        v_old, refs = refs[0], refs[1:]
    chunks, refs = refs[: 4 * n_], refs[4 * n_ :]
    part, q, k, v, p, o, wqk, wv, wo, a, sems = refs
    start_att(pl_, idx, chunks, wqk, wv, wo, sems)
    normed(lambda i: h[i : i + STEP, :].astype(F32), prm[0:1, :], prm[2:3, :], a, t_)
    wait_all(wqk, sems.at[0])
    qk = dot(a[...], wqk[...])
    q[...] = (qk[:, :h_] + prm[4:5, :h_]).astype(BF)
    k[...] = qk[:, h_:].astype(BF)
    wait_all(wv, sems.at[1])
    val = (dot(a[...], wv[...]) + prm[7:8, :h_]).astype(BF)
    if layer == 1:
        val = jnp.where(idx[2 * n_ + 1] == 1, v_old[...], val)
    v[...] = val
    lanes = h_ // pl_.pairs
    low = pair_masks(sq, lanes)
    causal = lax.broadcasted_iota(jnp.int32, (2 * sq, sq), 0) % sq >= lax.broadcasted_iota(jnp.int32, (2 * sq, sq), 1)
    scale = (lanes // 2) ** -0.5
    for s_ in range(pl_.seqs):
        for j in range(pl_.pairs):
            rws, cls = slice(s_ * sq, (s_ + 1) * sq), slice(j * lanes, (j + 1) * lanes)
            q2 = stack_pair(q[rws, cls], low)
            sc = jnp.where(causal, dot_nt(q2, k[rws, cls]) * scale, masked_score)
            ex = jnp.exp(sc - jnp.max(sc, axis=-1, keepdims=True))
            pr = (ex / jnp.sum(ex, axis=-1, keepdims=True)).astype(BF)
            p[s_ * pl_.pairs + j] = pr
            o2 = dot(pr, v[rws, cls])
            o[rws, cls] = jnp.where(low, o2[:sq], o2[sq:]).astype(BF)
    wait_all(wo, sems.at[2])
    part[...] = dot(o[...], wo[...]).astype(BF)


def f2_kernel(pl_, *refs):
    n_, h_, d_, t_ = pl_.count, pl_.half, pl_.width, pl_.tokens
    idx, h, pa, pb, prm, bf = refs[:6]
    refs = refs[6:]
    chunks, refs = refs[: 4 * n_], refs[4 * n_ :]
    part, r, u, gp, wfc, wproj, cn, z, sems = refs
    start_mlp(pl_, idx, chunks, wfc, wproj, sems)
    for i in range(0, t_, STEP):
        sl = slice(i, i + STEP)
        rr = h[sl, :].astype(F32) + (pa[sl, :].astype(F32) + pb[sl, :].astype(F32)) + prm[5:6, :]
        r[sl, :] = rr
        x, _ = unit_rows(rr)
        cn[sl, :] = (x * prm[1:2, :] + prm[3:4, :]).astype(BF)
    wait_all(wfc, sems.at[0])
    cols = pl_.fh // 3
    for j in range(3):
        cs = slice(j * cols, (j + 1) * cols)
        z[...] = dot(cn[...], wfc[:, cs])

        def body(i, carry):
            sl = pl.ds(pl.multiple_of(i * STEP, STEP), STEP)
            zz = z[sl, :] + bf[:, cs]
            sq_ = zz * zz
            th = jnp.tanh(0.7978845608 * zz * (1.0 + 0.044715 * sq_))
            hp = 0.5 * (1.0 + th)
            u[sl, cs] = (zz * hp).astype(BF)
            slope = 0.7978845608 * (1.0 + 3 * 0.044715 * sq_)
            gp[sl, cs] = (hp + 0.5 * zz * (1.0 - th * th) * slope).astype(BF)
            return carry

        lax.fori_loop(0, t_ // STEP, body, 0)
    wait_all(wproj, sems.at[1])
    part[...] = dot(u[...], wproj[...]).astype(BF)


def put_blocks(pl_, idx, own, sib_a, sib_b, sem, pick, row0, rows_out):
    n_, h_ = pl_.count, pl_.half
    c = idx[2 * n_]
    for other in (1, 0):
        core = 1 - c if other else c
        for n in range(n_):
            for t in range(2):
                sh = idx[t * n_ + (n + 1) % n_]
                if other:
                    dst = sib_a.at[t, n] if n < 2 else sib_b.at[t, n - 2]
                else:
                    dst = own.at[t, n]
                slot = 0 if not other else (1 if n < 2 else 2)
                pick(core, t, sh, dst.at[pl.ds(row0, rows_out), :], sem.at[slot])


def b2_kernel(pl_, layer, *refs):
    n_, r_, h_, d_, t_ = pl_.count, pl_.rows, pl_.half, pl_.width, pl_.tokens
    idx, u, gp, r, prm = refs[:5]
    refs = refs[5:]
    if layer == 1:
        e, refs = refs[0], refs[1:]
    else:
        dr, da_a, da_b, h_up, prm_up = refs[:5]
        refs = refs[5:]
    chunks, refs = refs[: 4 * n_], refs[4 * n_ :]
    part, sums, sbf, own, sib_a, sib_b = refs[:6]
    refs = refs[6:]
    if layer == 0:
        e, refs = refs[0], refs[1:]
    wfc, wproj, cn, dz, gfc, gproj, acc, sems, osem = refs
    start_mlp(pl_, idx, chunks, wfc, wproj, sems)
    zero = jnp.zeros((1, d_), F32)
    sg0, sb0, sb4 = zero, zero, zero
    for i in range(0, t_, STEP):
        sl = slice(i, i + STEP)
        if layer == 0:
            x, inv = unit_rows(h_up[sl, :].astype(F32))
            dn = da_a[sl, :].astype(F32) + da_b[sl, :].astype(F32)
            sg0 = sg0 + jnp.sum(dn * x, axis=0, keepdims=True)
            sb0 = sb0 + jnp.sum(dn, axis=0, keepdims=True)
            ee = (dr[sl, :] + norm_back(dn, x, inv, prm_up[0:1, :])).astype(BF)
            e[sl, :] = ee
        else:
            ee = e[sl, :]
        sb4 = sb4 + jnp.sum(ee.astype(F32), axis=0, keepdims=True)
        x, _ = unit_rows(r[sl, :])
        cn[sl, :] = (x * prm[1:2, :] + prm[3:4, :]).astype(BF)
    sums[0:1, :], sums[1:2, :], sums[2:3, :] = sg0, sb0, sb4
    gproj[...] = dot_tn(u[...], e[...]).astype(BF)

    def pick_proj(core, t, sh, dst, sem):
        row = pl.multiple_of(sh * 2 * r_ + core * r_, 16)
        dma(gproj.at[pl.ds(row, r_), pl.ds(t * h_, h_)], dst, sem).start()

    put_blocks(pl_, idx, own, sib_a, sib_b, osem, pick_proj, r_, r_)
    wait_all(wproj, sems.at[1])
    wait_all(wfc, sems.at[0])
    cols = pl_.fh // 3
    for j in range(3):
        cs = slice(j * cols, (j + 1) * cols)
        dzj = (dot_nt(e[...], wproj[cs, :]) * gp[:, cs].astype(F32)).astype(BF)
        dz[:, cs] = dzj
        sbf[:, cs] = jnp.sum(dzj.astype(F32), axis=0, keepdims=True)
        gfc[:, cs] = dot_tn(cn[...], dz[:, cs]).astype(BF)
    part[...] = dot_nt(dz[...], wfc[...]).astype(BF)

    def pick_fc(core, t, sh, dst, sem):
        row = pl.multiple_of(sh * r_, 16)
        col = pl.multiple_of((2 * core + t) * h_, 128)
        dma(gfc.at[pl.ds(row, r_), pl.ds(col, h_)], dst, sem).start()

    put_blocks(pl_, idx, own, sib_a, sib_b, osem, pick_fc, 0, r_)
    wait_all(own, osem.at[0])
    wait_all(sib_a, osem.at[1])
    wait_all(sib_b, osem.at[2])


def b1_kernel(pl_, layer, *refs):
    n_, r_, h_, d_, t_, sq = pl_.count, pl_.rows, pl_.half, pl_.width, pl_.tokens, pl_.seq
    idx, e, dc_a, dc_b, r, h, q, k, v, p, o, prm = refs[:12]
    refs = refs[12:]
    if layer == 0:
        extra, refs = refs[0], refs[1:]
    chunks, refs = refs[: 4 * n_], refs[4 * n_ :]
    part, dr, dv_out, sums, own, sib_a, sib_b, wqk, wv, wo, a, dy, do, dqk, gatt, go, sems, osem = refs
    start_att(pl_, idx, chunks, wqk, wv, wo, sems)
    zero = jnp.zeros((1, d_), F32)
    sg1, sb1, sb3 = zero, zero, zero
    for i in range(0, t_, STEP):
        sl = slice(i, i + STEP)
        x, inv = unit_rows(r[sl, :])
        dn = dc_a[sl, :].astype(F32) + dc_b[sl, :].astype(F32)
        sg1 = sg1 + jnp.sum(dn * x, axis=0, keepdims=True)
        sb1 = sb1 + jnp.sum(dn, axis=0, keepdims=True)
        dd = e[sl, :].astype(F32) + norm_back(dn, x, inv, prm[1:2, :])
        dr[sl, :] = dd
        dyb = dd.astype(BF)
        dy[sl, :] = dyb
        sb3 = sb3 + jnp.sum(dyb.astype(F32), axis=0, keepdims=True)
    normed(lambda i: h[i : i + STEP, :].astype(F32), prm[0:1, :], prm[2:3, :], a, t_)
    go[...] = dot_tn(o[...], dy[...]).astype(BF)
    wait_all(wo, sems.at[2])
    do[...] = dot_nt(dy[...], wo[...]).astype(BF)
    lanes = h_ // pl_.pairs
    low = pair_masks(sq, lanes)
    scale = (lanes // 2) ** -0.5
    for s_ in range(pl_.seqs):
        for j in range(pl_.pairs):
            rws, cls = slice(s_ * sq, (s_ + 1) * sq), slice(j * lanes, (j + 1) * lanes)
            kcls = slice(h_ + j * lanes, h_ + (j + 1) * lanes)
            q2 = stack_pair(q[rws, cls], low)
            do2 = stack_pair(do[rws, cls], low)
            pr = p[s_ * pl_.pairs + j]
            dp = dot_nt(do2, v[rws, cls])
            dv = dot_tn(pr, do2)
            if layer == 0:
                dv = dv + extra[rws, cls].astype(F32) * (idx[2 * n_ + 1] == 1).astype(F32)
            dv_out[rws, cls] = dv.astype(BF)
            pf = pr.astype(F32)
            ds = (pf * (dp - jnp.sum(pf * dp, axis=-1, keepdims=True))).astype(BF)
            dq2 = dot(ds, k[rws, cls])
            dqk[rws, cls] = (jnp.where(low, dq2[:sq], dq2[sq:]) * scale).astype(BF)
            dqk[rws, kcls] = (dot_tn(ds, q2) * scale).astype(BF)
    gatt[:, :d_] = dot_tn(a[...], dqk[...]).astype(BF)
    gatt[:, d_:] = dot_tn(a[...], dv_out[...]).astype(BF)
    wait_all(wqk, sems.at[0])
    wait_all(wv, sems.at[1])
    da = dot_nt(dqk[...], wqk[...])
    dav = dot_nt(dv_out[...], wv[...])
    if layer == 1:
        dav = dav * (idx[2 * n_ + 1] == 0).astype(F32)
    part[...] = (da + dav).astype(BF)
    sums[0:1, :], sums[1:2, :], sums[2:3, :] = sg1, sb1, sb3
    sums[3:4, :] = jnp.sum(dqk[...].astype(F32), axis=0, keepdims=True)
    sums[4:5, :h_] = jnp.sum(dv_out[...].astype(F32), axis=0, keepdims=True)
    sums[4:5, h_:] = jnp.zeros((1, h_), F32)

    def pick_att(core, t, sh, dst, sem):
        row = pl.multiple_of(sh * r_, 16)

        @pl.when(core == 0)
        def _():
            dma(gatt.at[pl.ds(row, r_), pl.ds(t * h_, h_)], dst, sem).start()

        @pl.when(core == 1)
        def _():
            if t == 0:
                dma(gatt.at[pl.ds(row, r_), pl.ds(2 * h_, h_)], dst, sem).start()
            else:
                orow = pl.multiple_of((sh // 2) * r_, 16)
                ocol = pl.multiple_of((sh % 2) * h_, 128)
                dma(go.at[pl.ds(orow, r_), pl.ds(ocol, h_)], dst, sem).start()

    put_blocks(pl_, idx, own, sib_a, sib_b, osem, pick_att, 0, r_)
    wait_all(own, osem.at[0])
    wait_all(sib_a, osem.at[1])
    wait_all(sib_b, osem.at[2])


VM = pl.BlockSpec(memory_space=pltpu.VMEM)
SM = pl.BlockSpec(memory_space=pltpu.SMEM)
ANY = pl.BlockSpec(memory_space=pl.ANY)


def call(kernel, ins, outs, scratch, flops, nbytes):
    return pl.pallas_call(
        kernel,
        out_shape=[jax.ShapeDtypeStruct(sh, dt) for sh, dt, _ in outs],
        in_specs=[sp for _, sp in ins],
        out_specs=[sp for _, _, sp in outs],
        scratch_shapes=scratch,
        compiler_params=pltpu.CompilerParams(vmem_limit_bytes=VMEM_BYTES),
        cost_estimate=pl.CostEstimate(flops=flops, bytes_accessed=nbytes, transcendentals=0),
    )(*[x for x, _ in ins])


def att_scratch(pl_):
    return [
        pltpu.VMEM((pl_.width, pl_.width), BF),
        pltpu.VMEM((pl_.width, pl_.half), BF),
        pltpu.VMEM((pl_.half, pl_.width), BF),
    ]


def mlp_scratch(pl_):
    return [pltpu.VMEM((pl_.width, pl_.fh), BF), pltpu.VMEM((pl_.fh, pl_.width), BF)]


def run_f1(pl_, layer, idx, h, prm, v_old, chunks):
    t_, h_, d_ = pl_.tokens, pl_.half, pl_.width
    ins = [(idx, SM), (h, VM), (prm, VM)] + ([(v_old, VM)] if layer else []) + [(x, ANY) for x in chunks]
    narrow = ((t_, h_), BF, VM)
    outs = [((t_, d_), BF, VM), narrow, narrow, narrow, ((pl_.seqs * pl_.pairs, 2 * pl_.seq, pl_.seq), BF, VM), narrow]
    scratch = att_scratch(pl_) + [pltpu.VMEM((t_, d_), BF), pltpu.SemaphoreType.DMA((3,))]
    return call(functools.partial(f1_kernel, pl_, layer), ins, outs, scratch, 2 * t_ * d_ * h_ * 5, 6_000_000)


def run_f2(pl_, idx, h, pa, pb, prm, bf, chunks):
    t_, d_, f_ = pl_.tokens, pl_.width, pl_.fh
    ins = [(idx, SM)] + [(x, VM) for x in (h, pa, pb, prm, bf)] + [(x, ANY) for x in chunks]
    outs = [((t_, d_), BF, VM), ((t_, d_), F32, VM), ((t_, f_), BF, VM), ((t_, f_), BF, VM)]
    scratch = mlp_scratch(pl_) + [pltpu.VMEM((t_, d_), BF), pltpu.VMEM((t_, f_ // 3), F32), pltpu.SemaphoreType.DMA((2,))]
    return call(functools.partial(f2_kernel, pl_), ins, outs, scratch, 4 * t_ * d_ * f_, 9_000_000)


def run_b2(pl_, layer, idx, u, gp, r, prm, more, chunks):
    t_, d_, f_, n_, r_, h_ = pl_.tokens, pl_.width, pl_.fh, pl_.count, pl_.rows, pl_.half
    ins = [(idx, SM)] + [(x, VM) for x in (u, gp, r, prm) + more] + [(x, ANY) for x in chunks]
    outs = [((t_, d_), BF, VM), ((3, d_), F32, VM), ((1, f_), F32, VM)]
    outs += [((2, m, 2 * r_, h_), BF, ANY) for m in (n_, 2, n_ - 2)]
    if layer == 0:
        outs.append(((t_, d_), BF, VM))
    scratch = mlp_scratch(pl_) + [
        pltpu.VMEM((t_, d_), BF),
        pltpu.VMEM((t_, f_), BF),
        pltpu.VMEM((d_, f_), BF),
        pltpu.VMEM((f_, d_), BF),
        pltpu.VMEM((8, 128), F32),
        pltpu.SemaphoreType.DMA((2,)),
        pltpu.SemaphoreType.DMA((3,)),
    ]
    return call(functools.partial(b2_kernel, pl_, layer), ins, outs, scratch, 8 * t_ * d_ * f_, 18_000_000)


def run_b1(pl_, layer, idx, e, dca, dcb, r, h, att, prm, extra, chunks):
    t_, d_, n_, r_, h_ = pl_.tokens, pl_.width, pl_.count, pl_.rows, pl_.half
    q, k, v, p, o = att
    ins = [(idx, SM)] + [(x, VM) for x in (e, dca, dcb, r, h, q, k, v, p, o, prm)]
    ins += ([(extra, VM)] if layer == 0 else []) + [(x, ANY) for x in chunks]
    outs = [((t_, d_), BF, VM), ((t_, d_), F32, VM), ((t_, h_), BF, VM), ((5, d_), F32, VM)]
    outs += [((2, m, r_, h_), BF, ANY) for m in (n_, 2, n_ - 2)]
    scratch = att_scratch(pl_) + [
        pltpu.VMEM((t_, d_), BF),
        pltpu.VMEM((t_, d_), BF),
        pltpu.VMEM((t_, h_), BF),
        pltpu.VMEM((t_, d_), BF),
        pltpu.VMEM((d_, d_ + h_), BF),
        pltpu.VMEM((h_, d_), BF),
        pltpu.SemaphoreType.DMA((3,)),
        pltpu.SemaphoreType.DMA((3,)),
    ]
    return call(functools.partial(b1_kernel, pl_, layer), ins, outs, scratch, 4 * t_ * d_ * h_ * 5, 14_000_000)


def per_device(ends, w_qk, w_value, w_out, w_fc, w_proj, gains, shifts, fc_shift, value_shift):
    s, grp, d = lax.axis_index("section"), lax.axis_index("group"), lax.axis_index("dp")
    c = grp % 2
    count, groups = lax.axis_size("dp"), lax.axis_size("group")
    rows, width = w_qk.shape[1], ends.shape[3]
    half = width // 2
    ff = w_fc.shape[2]
    unit = ff // count // 2
    fh = ff // 2
    seqs, seq = ends.shape[1], ends.shape[2]
    heads = HEADS // 2
    tokens = seqs * seq
    order = ring_order(count)
    place = [0] * count
    for i, dev in enumerate(order):
        place[dev] = i
    plan = Plan(count, rows, width, fh, tokens, seq, heads)
    table = np.zeros((2, groups, count, 2 * count + 2), np.int32)
    for i in range(count):
        table[:, :, i, :count] = [order[(place[i] - n) % count] for n in range(count)]
        table[:, :, i, count : 2 * count] = [order[(place[i] + n) % count] for n in range(count)]
    table[:, :, :, 2 * count] = (np.arange(groups) % 2)[None, :, None]
    table[:, :, :, 2 * count + 1] = np.arange(2)[:, None, None]
    idx = lax.dynamic_slice(jnp.asarray(table), (s, grp, d, 0), (1, 1, 1, 2 * count + 2)).reshape(-1)
    routes = [
        [(order[i], order[(i + 1) % count]) for i in range(count)],
        [(order[(i + 1) % count], order[i]) for i in range(count)],
    ]
    way = (1, -1)

    def swap_x(x):
        return lax.ppermute(x, "section", [(0, 1), (1, 0)])

    def swap_c(x):
        return lax.ppermute(x, "group", [(i, i ^ 1) for i in range(groups)])

    first = s == 0
    even = d % 2 == 0
    hc = count // 2
    spread = [
        [(l * count + i, (i // hc) * count + 2 * (i % hc) + (l if w == 0 else 1 - l)) for l in range(2) for i in range(count)]
        for w in range(2)
    ]
    o_lo, o_hi = w_out[0][:, :half], w_out[0][:, half:]
    o_a = lax.ppermute(jnp.where(first, o_lo, o_hi), ("section", "dp"), spread[0])
    o_b = lax.ppermute(jnp.where(first, o_hi, o_lo), ("section", "dp"), spread[1])
    o_blocks = (jnp.where(even, o_a, o_b), jnp.where(even, o_b, o_a))

    qk = w_qk[0].reshape(rows, 2, 2, half)
    fc = w_fc[0].reshape(rows, count, 2, unit).transpose(2, 0, 1, 3).reshape(2, rows, 4, half).transpose(0, 2, 1, 3)
    proj = w_proj[0].reshape(2, 2, rows, 2, half).transpose(0, 1, 3, 2, 4).reshape(2, 4, rows, half)

    def pick(blocks, side):
        return lax.dynamic_slice_in_dim(lax.dynamic_index_in_dim(blocks, side, 0, False), 2 * c, 2, 0)

    small_own = jnp.concatenate([gains[0].reshape(-1), shifts[0].reshape(-1), fc_shift[0]])

    def side_pack(side):
        q = lax.dynamic_index_in_dim(qk[:, 0], side, 1, False)
        k = lax.dynamic_index_in_dim(qk[:, 1], side, 1, False)
        return q, k, pick(fc, side), pick(proj, side)

    mine = side_pack(s)
    theirs = jax.tree.map(swap_x, side_pack(1 - s))
    small_other = swap_x(small_own)
    lay = [
        jax.tree.map(lambda m, t: jnp.where(first, m, t), mine, theirs),
        jax.tree.map(lambda m, t: jnp.where(first, t, m), mine, theirs),
    ]
    v_side = (
        lax.dynamic_slice_in_dim(w_value, s * half, half, 1),
        w_value[:, width:],
    )
    small = jnp.concatenate(
        [jnp.where(first, small_own, small_other), jnp.where(first, small_other, small_own), value_shift]
    )
    small_n = small.shape[0]
    small_rows = jnp.pad(small, (0, SMALL * half - small_n)).reshape(SMALL, half)

    def gather(l):
        q, k, f, p = lay[l]
        a0 = jnp.where(c == 0, q, v_side[l])
        a1 = jnp.where(c == 0, k, o_blocks[l])
        x0 = [a0, f[0], p[0]] + ([small_rows] if l == 0 else [])
        x1 = [a1, f[1], p[1]]
        got = []
        for t, x in enumerate((x0, x1)):
            x = jnp.concatenate(x, axis=0)
            steps = [x]
            for _ in range(count - 1):
                x = lax.ppermute(x, "dp", routes[t])
                steps.append(x)
            got.append((steps, [swap_c(x) for x in steps]))
        return got

    got0, got1 = gather(0), gather(1)
    smalls = jnp.zeros((count, small_n), BF)
    for n in range(count):
        sh = idx[n]
        smalls = lax.dynamic_update_slice(smalls, got0[0][0][n][3 * rows :].reshape(1, -1)[:, :small_n], (sh, 0))
    smalls = smalls.astype(F32)
    chunks = [[x for t in range(2) for same in range(2) for x in got[t][same]] for got in (got0, got1)]
    per_layer = 11 * rows
    vals = smalls[:, 2 * per_layer :].reshape(-1)

    def params(l):
        m = smalls[:, l * per_layer : (l + 1) * per_layer]
        rws = m[:, : 7 * rows].reshape(count, 7, rows).transpose(1, 0, 2).reshape(7, width)
        bf = lax.dynamic_index_in_dim(m[:, 7 * rows :].reshape(count, 2, unit), s, 1, False).reshape(-1)
        bv = lax.dynamic_slice_in_dim(vals, s * half, half, 0) if l == 0 else vals[width:]
        bq = lax.dynamic_slice_in_dim(rws[4], s * half, half, 0)
        zero = jnp.zeros((half,), F32)
        rws = rws.at[4].set(jnp.concatenate([bq, zero]))
        return jnp.concatenate([rws, jnp.concatenate([bv, zero])[None]], axis=0), bf[None]

    prm = [params(0), params(1)]

    ends_own = ends[0].reshape(tokens, width)
    ends_other = swap_x(ends_own)
    h = jnp.where(first, ends_own, ends_other)
    cot = jnp.where(first, ends_other, ends_own)
    kept, hs, rs = [], [], []
    v_old = None
    for l in range(2):
        hs.append(h)
        part, q, k, v, p, o = run_f1(plan, l, idx, h, prm[l][0], v_old, chunks[l])
        v_old = v
        part, r, u, gp = run_f2(plan, idx, h, part, swap_x(part), *prm[l], chunks[l])
        rs.append(r)
        kept.append(((q, k, v, p, o), u, gp))
        h = (r + (part.astype(F32) + swap_x(part).astype(F32)) + prm[l][0][6:7]).astype(BF)
    y_out = h

    grads = [None, None]
    att, u, gp = kept[1]
    part, sums_b2, sbf, *g_mlp1 = run_b2(plan, 1, idx, u, gp, rs[1], prm[1][0], (cot,), chunks[1])
    sb4_1, sbf_1 = sums_b2[2], sbf[0]
    part, dr, dv, sums1, *g_att1 = run_b1(plan, 1, idx, cot, part, swap_x(part), rs[1], hs[1], att, prm[1][0], None, chunks[1])
    att, u, gp = kept[0]
    part, sums_b2, sbf, *g_mlp0, e = run_b2(
        plan, 0, idx, u, gp, rs[0], prm[0][0], (dr, part, swap_x(part), hs[1], prm[1][0]), chunks[0]
    )
    part, dr, _, sums0, *g_att0 = run_b1(plan, 0, idx, e, part, swap_x(part), rs[0], hs[0], att, prm[0][0], dv, chunks[0])
    da = part.astype(F32) + swap_x(part).astype(F32)
    x, inv = unit_rows(hs[0].astype(F32))
    e = (dr + norm_back(da, x, inv, prm[0][0][0:1])).astype(BF)
    tiny = [
        (colsum(da * x), sums0[0], colsum(da), sums0[1], sums0[3, :half], sums0[2], sums_b2[2], sbf[0], sums0[4, :half]),
        (sums_b2[0], sums1[0], sums_b2[1], sums1[1], sums1[3, :half], sums1[2], sb4_1, sbf_1, sums1[4, :half]),
    ]
    x_out = e

    def small_grads():
        zero = jnp.zeros((half,), F32)
        out = []
        for l in range(2):
            sg0, sg1, sb0, sb1, sbq, sb3, sb4, sbf, sbv = tiny[l]
            bq = jnp.where(first, jnp.concatenate([sbq, zero]), jnp.concatenate([zero, sbq]))
            rws = jnp.stack([sg0, sg1, sb0, sb1, bq, sb3, sb4]).reshape(7, count, rows).transpose(1, 0, 2).reshape(count, 7 * rows)
            bf = sbf.reshape(count, 1, unit)
            bf = jnp.where(first, jnp.concatenate([bf, 0 * bf], 1), jnp.concatenate([0 * bf, bf], 1)).reshape(count, 2 * unit)
            out += [rws, bf]
        v1, v2 = tiny[0][8], tiny[1][8]
        vs = jnp.where(first, jnp.concatenate([v1, zero, v2]), jnp.concatenate([zero, v1, zero]))
        out.append(vs.reshape(count, -1))
        flat = jnp.concatenate(out, axis=1)
        return jnp.pad(flat, ((0, 0), (0, SMALL * half - small_n))).reshape(count, SMALL, half).astype(BF)

    def reduce_ring(own, sib, t):
        def mine_at(n):
            return own[n].astype(F32) + sib[n].astype(F32)

        run = mine_at(0).astype(BF)
        for n in range(1, count):
            run = lax.ppermute(run, "dp", routes[t])
            run = run.astype(F32) + mine_at(n)
            if n < count - 1:
                run = run.astype(BF)
        total = run
        for n in range(1, groups // 2):
            total = total + lax.ppermute(run.astype(BF), "group", [(i, (i + 2 * n) % groups) for i in range(groups)]).astype(F32)
        return total

    def reduce_all(g, tail=None):
        own, sib_a, sib_b = g
        sib_a, sib_b = swap_c(sib_a), swap_c(sib_b)
        res = []
        for t in range(2):
            o_, s_ = [own[t, n] for n in range(count)], [sib_a[t, 0], sib_a[t, 1]] + [sib_b[t, n] for n in range(count - 2)]
            if tail is not None and t == 0:
                sib_t = swap_c(tail)
                for n in range(count):
                    sh = idx[(n + 1) % count]
                    o_[n] = jnp.concatenate([o_[n], lax.dynamic_index_in_dim(tail, sh, 0, False)], 0)
                    s_[n] = jnp.concatenate([s_[n], lax.dynamic_index_in_dim(sib_t, sh, 0, False)], 0)
            res.append(reduce_ring(o_, s_, t))
        return res

    mlp1, att1 = reduce_all(g_mlp1), reduce_all(g_att1)
    mlp0, att0 = reduce_all(g_mlp0), reduce_all(g_att0, small_grads())
    small_tot = att0[0][rows:].reshape(-1)[:small_n]
    att0[0] = att0[0][:rows]
    red = [[jnp.concatenate([at_[t], ml_[t]], 0) for t in range(2)] for at_, ml_ in ((att0, mlp0), (att1, mlp1))]
    r2 = [jnp.stack(red[l]).astype(BF) for l in range(2)]
    send = jnp.where(first, r2[1], r2[0])
    keep = jnp.where(first, r2[0], r2[1])
    recv = swap_x(send)
    both = jnp.where(first, jnp.stack([keep, recv]), jnp.stack([recv, keep]))
    sibl = swap_c(both)
    full = jnp.where(c == 0, jnp.stack([both, sibl]), jnp.stack([sibl, both])).astype(F32)
    full = full.reshape(2, 2, 2, 3, rows, half)
    o_qk = jnp.concatenate([full[0, 0, 0, 0], full[0, 1, 0, 0], full[0, 0, 1, 0], full[0, 1, 1, 0]], axis=1)
    o_fc = full[:, :, :, 1].transpose(1, 3, 0, 2, 4).reshape(2, rows, count, unit).transpose(1, 2, 0, 3).reshape(rows, ff)
    o_proj = full[:, :, :, 2].transpose(1, 0, 3, 2, 4).reshape(4 * rows, width)
    my_o = [jnp.where(c == 1, r2[l][1, :rows], jnp.zeros((rows, half), BF)) for l in range(2)]
    my_o = [i + swap_c(i) for i in my_o]
    back = [[(b, a) for a, b in w] for w in spread]
    out_a = lax.ppermute(jnp.where(even, my_o[0], my_o[1]), ("section", "dp"), back[0])
    out_b = lax.ppermute(jnp.where(even, my_o[1], my_o[0]), ("section", "dp"), back[1])
    o_out = jnp.where(first, jnp.concatenate([out_a, out_b], 1), jnp.concatenate([out_b, out_a], 1)).astype(F32)
    my_v = [jnp.where(c == 1, r2[l][0, :rows], jnp.zeros((rows, half), BF)) for l in range(2)]
    my_v = [i + swap_c(i) for i in my_v]
    their_v = [swap_x(i) for i in my_v]
    v10 = jnp.where(first, my_v[0], their_v[0])
    v11 = jnp.where(first, their_v[0], my_v[0])
    v20 = jnp.where(first, my_v[1], their_v[1])
    o_val = jnp.concatenate([v10, v11, v20], axis=1).astype(F32)
    other = swap_x(small_tot.astype(BF)).astype(F32)
    n7 = 7 * rows

    def layer_small(l):
        lo = l * per_layer
        mine_, oth = small_tot[lo : lo + per_layer], other[lo : lo + per_layer]
        rw = mine_[:n7].reshape(7, rows)
        bq = (mine_ + oth)[:n7].reshape(7, rows)[4]
        return rw[:2], jnp.concatenate([rw[2:4], bq[None], rw[5:]], 0), (mine_ + oth)[n7:]

    sm0, sm1 = layer_small(0), layer_small(1)
    o_gain, o_shift, o_bf = (jnp.where(first, a, b) for a, b in zip(sm0, sm1))
    o_vs = (small_tot + other)[2 * per_layer :]
    res = jnp.where(first, x_out, y_out).reshape(1, seqs, seq, width)
    return (res, o_qk[None], o_val, o_out[None], o_fc[None], o_proj[None], o_gain[None], o_shift[None], o_bf[None], o_vs)


def solution(mesh):
    placed = (
        P("section", ("group", "dp"), None, None),
        P("section", "dp", None),
        P("dp", None),
        P("section", "dp", None),
        P("section", "dp", None),
        P("section", "dp", None),
        P("section", None, "dp"),
        P("section", None, "dp"),
        P("section", "dp"),
        P("dp"),
    )
    return jax.shard_map(per_device, mesh=mesh, in_specs=placed, out_specs=placed, check_vma=False)
```

```python
import functools

import jax
import jax.numpy as jnp
import numpy as np
from jax import lax
from jax.experimental import pallas as pl
from jax.experimental.pallas import tpu as pltpu
from jax.sharding import PartitionSpec as P

HEADS = 12
BF = jnp.bfloat16
F32 = jnp.float32
norm_eps = 1e-05
masked_score = -1e30
TAIL = 32
STEP = 32
VMEM_BYTES = 56 * 1024 * 1024


def dot(a, b):
    return jnp.dot(a, b, preferred_element_type=F32)


def dot_tn(a, b):
    return lax.dot_general(a, b, (((0,), (0,)), ((), ())), preferred_element_type=F32)


def dot_nt(a, b):
    return lax.dot_general(a, b, (((1,), (1,)), ((), ())), preferred_element_type=F32)


def unit_rows(v):
    centered = v - jnp.mean(v, axis=-1, keepdims=True)
    inv = lax.rsqrt(jnp.mean(centered * centered, axis=-1, keepdims=True) + norm_eps)
    return centered * inv, inv


def norm_back(dn, x, inv, gain):
    scaled = dn * gain
    inner = jnp.mean(scaled * x, axis=-1, keepdims=True)
    return inv * (scaled - jnp.mean(scaled, axis=-1, keepdims=True) - x * inner)


def row_sum(v):
    return jnp.sum(v, axis=0, keepdims=True)


def ring_order(count):
    wide = 2 if count < 16 else 4
    tall = count // wide
    order = [i * wide for i in range(tall)]
    for n, row in enumerate(reversed(range(tall))):
        cols = range(1, wide)
        order += [row * wide + col for col in (cols if n % 2 == 0 else reversed(cols))]
    return order


class Plan:
    def __init__(self, count, rows, width, ff, values, tokens, seq, heads):
        self.count, self.rows, self.width, self.half = count, rows, width, width // 2
        self.ff, self.fh, self.unit, self.values = ff, ff // 2, ff // count // 2, values
        self.tokens, self.seq, self.seqs = tokens, seq, tokens // seq
        self.pairs = heads // 2
        self.bits = count.bit_length() - 1
        down = [1 << i for i in reversed(range(self.bits))]
        other = down[:-2] + [down[-1], down[-2]]
        self.orders = (down, other)
        self.masks = []
        for order in self.orders:
            mask = [0] * count
            for j in range(count):
                for k, bit in enumerate(order):
                    if j >> k & 1:
                        mask[j] ^= bit
            self.masks.append(mask)

    def core_at(self):
        return 6 * self.count

    def side_at(self):
        return 6 * self.count + 1

    def table(self, groups):
        n = self.count
        out = np.zeros((2, groups, n, 6 * n + 2), np.int32)
        order = ring_order(n)
        for p, d in enumerate(order):
            for t in range(2):
                out[:, :, d, t * n : (t + 1) * n] = [d ^ m for m in self.masks[t]]
                out[:, :, d, (3 + t) * n : (4 + t) * n] = [order[(p - (1 - 2 * t) * j) % n] for j in range(n)]
            for j, m in enumerate(self.masks[0]):
                out[:, :, d, 2 * n + (d ^ m)] = j
            for j in range(n):
                out[:, :, d, 5 * n + order[(p - j) % n]] = j
        out[:, :, :, 6 * n] = (np.arange(groups) % 2)[None, :, None]
        out[:, :, :, 6 * n + 1] = np.arange(2)[:, None, None]
        return out


def aligned(x, size):
    return x if isinstance(x, int) else pl.multiple_of(x, size)


def dma(src, dst, sem):
    return pltpu.make_async_copy(src, dst, sem)


def wait_all(ref, sem):
    dma(ref, ref, sem).wait()


def chunk_refs(plan, idx, chunks, row):
    for j in range(plan.count):
        for t in range(2):
            for other in range(2):
                ref = chunks[(t * 2 + other) * plan.count + j]
                yield t, other, idx[(3 + t) * plan.count + j], ref.at[pl.ds(row, plan.rows), :]


def take_chunks(plan, refs):
    n = 4 * plan.count
    return refs[:n], refs[n:]


def start_att(plan, layer, idx, chunks, wqk, wv, wo, sems):
    r_, h_ = plan.rows, plan.half
    c = idx[plan.core_at()]
    for t, other, sh, src in chunk_refs(plan, idx, chunks, 3 * r_ * layer):
        core = 1 - c if other else c
        row = pl.multiple_of(sh * r_, 16)

        @pl.when(core == 0)
        def _():
            dma(src, wqk.at[pl.ds(row, r_), pl.ds(t * h_, h_)], sems.at[0]).start()

        @pl.when(core == 1)
        def _():
            if t == 0:
                dma(src, wv.at[pl.ds(row, r_), :], sems.at[1]).start()
            else:
                orow = pl.multiple_of((sh // 2) * r_, 16)
                ocol = pl.multiple_of((sh % 2) * h_, 128)
                dma(src, wo.at[pl.ds(orow, r_), pl.ds(ocol, h_)], sems.at[2]).start()


def start_mlp(plan, layer, idx, chunks, wfc, wproj, sems):
    r_, h_ = plan.rows, plan.half
    c = idx[plan.core_at()]
    for kind in range(2):
        for t, other, sh, src in chunk_refs(plan, idx, chunks, (kind if layer else 1 + kind) * r_):
            core = 1 - c if other else c
            if kind == 0:
                row = pl.multiple_of(sh * r_, 16)
                col = pl.multiple_of((2 * core + t) * h_, 128)
                dst = wfc.at[pl.ds(row, r_), pl.ds(col, h_)]
            else:
                row = pl.multiple_of(sh * 2 * r_ + t * r_, 16)
                col = pl.multiple_of(core * h_, 128)
                dst = wproj.at[pl.ds(row, r_), pl.ds(col, h_)]
            dma(src, dst, sems.at[kind]).start()


def put_blocks(plan, idx, outs, sem, pick, row0):
    n_, r_ = plan.count, plan.rows
    half = n_ // 2
    for j in reversed(range(n_)):
        for t in range(2):
            part = 0 if j >= half else 1
            dst = outs[2 * part + t].at[j % half, pl.ds(row0, r_), :]
            pick(t, idx[t * n_ + j], dst, sem.at[2 * part + t])


def wait_blocks(outs, sem):
    for i, ref in enumerate(outs):
        wait_all(ref, sem.at[i])


def pack_kernel(plan, idx, wqk, wfc, wproj, mine, send):
    r_, h_, d_, u_ = plan.rows, plan.half, plan.width, plan.unit
    per = h_ // u_
    s, c = idx[plan.side_at()], idx[plan.core_at()]
    for side in range(2):
        for core in range(2):
            for keep in range(2):
                out = mine if keep else send

                @pl.when(jnp.logical_and(c == core, s == (side if keep else 1 - side)))
                def _():
                    for t in range(2):
                        lo = t * d_ + side * h_
                        out[t, :r_] = wqk[:, lo : lo + h_]
                        q = 2 * core + t
                        cols = [(q * per + i) * 2 * u_ + side * u_ for i in range(per)]
                        out[t, r_ : 2 * r_] = jnp.concatenate([wfc[:, x : x + u_] for x in cols], axis=1)
                        row = side * 2 * r_ + t * r_
                        out[t, 2 * r_ :] = wproj[row : row + r_, core * h_ : (core + 1) * h_]


def param_kernel(plan, idx, *refs):
    n_, r_, h_, d_ = plan.count, plan.rows, plan.half, plan.width
    steps, (prm, bf, stack, sem) = refs[:n_], refs[n_:]
    s = idx[plan.side_at()]
    for j, ref in enumerate(steps):
        dma(ref.at[pl.ds(4 * r_, TAIL), :], stack.at[j], sem).start()
    wait_all(stack, sem)
    blocks = [stack[idx[5 * n_ + sh]][:, :r_].astype(F32) for sh in range(n_)]
    per = 11
    more = plan.values // n_ - r_
    vals = jnp.concatenate([x for b in blocks for x in (b[22:23, :], b[23:24, :more])], axis=1)
    full = jnp.concatenate(blocks, axis=1)
    for l in range(2):
        m = full[l * per : l * per + 7]
        prm[l, 0:7] = m
        bq = jnp.where(s == 0, m[4:5, :h_], m[4:5, h_:])
        prm[l, 4:5] = jnp.concatenate([bq, jnp.zeros((1, d_ - h_), F32)], axis=1)
        if l == 0:
            bv = jnp.where(s == 0, vals[:, :h_], vals[:, h_:d_])
        else:
            bv = vals[:, d_:]
        prm[l, 7:8] = jnp.concatenate([bv, jnp.zeros((1, d_ - h_), F32)], axis=1)
        sides = []
        for side in range(2):
            row = l * per + 7 + 2 * side
            sides.append(jnp.concatenate([b[row + i : row + i + 1] for b in blocks for i in range(2)], axis=1))
        bf[l] = jnp.where(s == 0, sides[0], sides[1])


def pair_mask(seq, lanes):
    return lax.broadcasted_iota(jnp.int32, (seq, lanes), 1) < lanes // 2


def stack_pair(x, low):
    zero = jnp.zeros_like(x)
    return jnp.concatenate([jnp.where(low, x, zero), jnp.where(low, zero, x)], axis=0)


def f1_kernel(plan, layer, *refs):
    h_, t_, sq = plan.half, plan.tokens, plan.seq
    idx, prm, refs = refs[0], refs[1], refs[2:]
    if layer == 1:
        r_up, pa, pb, v_old = refs[:4]
        refs = refs[4:]
    else:
        h, refs = refs[0], refs[1:]
    chunks, refs = take_chunks(plan, refs)
    part, q, k, v, p, o, a = refs[:7]
    refs = refs[7:]
    if layer == 1:
        h, refs = refs[0], refs[1:]
    wqk, wv, wo, sems = refs
    start_att(plan, layer, idx, chunks, wqk, wv, wo, sems)
    for i in range(0, t_, STEP):
        sl = slice(i, i + STEP)
        if layer == 1:
            hh = r_up[sl, :] + (pa[sl, :].astype(F32) + pb[sl, :].astype(F32)) + prm[0, 6:7, :]
            h[sl, :] = hh.astype(BF)
        x, _ = unit_rows(h[sl, :].astype(F32))
        a[sl, :] = (x * prm[layer, 0:1, :] + prm[layer, 2:3, :]).astype(BF)
    wait_all(wqk, sems.at[0])
    qk = dot(a[...], wqk[...])
    q[...] = (qk[:, :h_] + prm[layer, 4:5, :h_]).astype(BF)
    k[...] = qk[:, h_:].astype(BF)
    wait_all(wv, sems.at[1])
    val = (dot(a[...], wv[...]) + prm[layer, 7:8, :h_]).astype(BF)
    if layer == 1:
        val = jnp.where(idx[plan.side_at()] == 1, v_old[...], val)
    v[...] = val
    lanes = h_ // plan.pairs
    low = pair_mask(sq, lanes)
    causal = lax.broadcasted_iota(jnp.int32, (2 * sq, sq), 0) % sq >= lax.broadcasted_iota(jnp.int32, (2 * sq, sq), 1)
    scale = (lanes // 2) ** -0.5
    for s_ in range(plan.seqs):
        for j in range(plan.pairs):
            rws, cls = slice(s_ * sq, (s_ + 1) * sq), slice(j * lanes, (j + 1) * lanes)
            q2 = stack_pair(q[rws, cls], low)
            sc = jnp.where(causal, dot_nt(q2, k[rws, cls]) * scale, masked_score)
            ex = jnp.exp(sc - jnp.max(sc, axis=-1, keepdims=True))
            pr = (ex / jnp.sum(ex, axis=-1, keepdims=True)).astype(BF)
            p[s_ * plan.pairs + j] = pr
            o2 = dot(pr, v[rws, cls])
            o[rws, cls] = jnp.where(low, o2[:sq], o2[sq:]).astype(BF)
    wait_all(wo, sems.at[2])
    part[...] = dot(o[...], wo[...]).astype(BF)


def f2_kernel(plan, layer, *refs):
    t_ = plan.tokens
    idx, prm, bf, h, pa, pb = refs[:6]
    chunks, refs = take_chunks(plan, refs[6:])
    part, r, ucn, gp, wfc, wproj, z, sems = refs
    f_ = plan.fh
    start_mlp(plan, layer, idx, chunks, wfc, wproj, sems)
    for i in range(0, t_, STEP):
        sl = slice(i, i + STEP)
        rr = h[sl, :].astype(F32) + (pa[sl, :].astype(F32) + pb[sl, :].astype(F32)) + prm[layer, 5:6, :]
        r[sl, :] = rr
        x, _ = unit_rows(rr)
        ucn[sl, f_:] = (x * prm[layer, 1:2, :] + prm[layer, 3:4, :]).astype(BF)
    wait_all(wfc, sems.at[0])
    cols = plan.fh // 3
    for j in range(3):
        cs = slice(j * cols, (j + 1) * cols)
        z[...] = dot(ucn[:, f_:], wfc[:, cs])

        def body(i, carry):
            sl = pl.ds(pl.multiple_of(i * STEP, STEP), STEP)
            zz = z[sl, :] + bf[layer, :, cs]
            sq_ = zz * zz
            th = jnp.tanh(0.7978845608 * zz * (1.0 + 0.044715 * sq_))
            hp = 0.5 * (1.0 + th)
            ucn[sl, cs] = (zz * hp).astype(BF)
            slope = 0.7978845608 * (1.0 + 3 * 0.044715 * sq_)
            gp[sl, cs] = (hp + 0.5 * zz * (1.0 - th * th) * slope).astype(BF)
            return carry

        lax.fori_loop(0, t_ // STEP, body, 0)
    wait_all(wproj, sems.at[1])
    part[...] = dot(ucn[:, :f_], wproj[...]).astype(BF)


def b2_kernel(plan, layer, *refs):
    d_, t_, f_ = plan.width, plan.tokens, plan.fh
    idx, prm, gp, r = refs[:4]
    refs = refs[4:]
    if layer == 1:
        e, refs = refs[0], refs[1:]
    else:
        dr, da_a, da_b, h_up = refs[:4]
        refs = refs[4:]
    chunks, refs = take_chunks(plan, refs)
    part, dze, sums, sbf, wfc, wproj, acc, sems = refs
    start_mlp(plan, layer, idx, chunks, wfc, wproj, sems)
    zero = jnp.zeros((1, d_), F32)
    sb4 = zero
    for i in range(0, t_, STEP):
        sl = slice(i, i + STEP)
        if layer == 0:
            x, inv = unit_rows(h_up[sl, :].astype(F32))
            dn = da_a[sl, :].astype(F32) + da_b[sl, :].astype(F32)
            ee = (dr[sl, :] + norm_back(dn, x, inv, prm[1, 0:1, :])).astype(BF)
        else:
            ee = e[sl, :]
        dze[sl, f_:] = ee
        sb4 = sb4 + row_sum(ee.astype(F32))
    wait_all(wproj, sems.at[1])
    wait_all(wfc, sems.at[0])
    cols = f_ // 3
    for j in range(3):
        cs = slice(j * cols, (j + 1) * cols)
        dzj = (dot_nt(dze[:, f_:], wproj[cs, :]) * gp[:, cs].astype(F32)).astype(BF)
        dze[:, cs] = dzj
        sbf[:, cs] = row_sum(dzj.astype(F32))
    acc[...] = dot_nt(dze[:, :f_], wfc[...])
    sg1, sb1 = zero, zero
    for i in range(0, t_, STEP):
        sl = slice(i, i + STEP)
        dn = acc[sl, :]
        part[sl, :] = dn.astype(BF)
        x, _ = unit_rows(r[sl, :])
        sg1 = sg1 + row_sum(dn * x)
        sb1 = sb1 + row_sum(dn)
    sums[0:1, :], sums[1:2, :], sums[2:3, :] = sg1, sb1, 0.5 * sb4


def g2_kernel(plan, *refs):
    r_, h_, f_, d_ = plan.rows, plan.half, plan.fh, plan.width
    idx, ucn, ucn_sib, dze, dze_sib = refs[:5]
    outs, (gfc, gproj, osem) = refs[5:-3], refs[-3:]
    c = idx[plan.core_at()]
    ecols = pl.ds(pl.multiple_of(f_ + c * h_, 128), h_)
    gproj[...] = (dot_tn(ucn[:, :f_], dze[:, ecols]) + dot_tn(ucn_sib[:, :f_], dze_sib[:, ecols])).astype(BF)

    def pick_proj(t, sh, dst, sem):
        dma(gproj.at[pl.ds(pl.multiple_of(sh * 2 * r_ + t * r_, 16), r_), :], dst, sem).start()

    put_blocks(plan, idx, outs, osem, pick_proj, r_)
    zcols = pl.ds(pl.multiple_of(c * d_, 128), d_)
    gfc[...] = (dot_tn(ucn[:, f_:], dze[:, zcols]) + dot_tn(ucn_sib[:, f_:], dze_sib[:, zcols])).astype(BF)

    def pick_fc(t, sh, dst, sem):
        dma(gfc.at[pl.ds(pl.multiple_of(sh * r_, 16), r_), pl.ds(t * h_, h_)], dst, sem).start()

    put_blocks(plan, idx, outs, osem, pick_fc, 0)
    wait_blocks(outs, osem)


def b1_kernel(plan, layer, *refs):
    h_, d_, t_, sq = plan.half, plan.width, plan.tokens, plan.seq
    idx, prm, ucn, dc_a, dc_b, r, h, q, k, v, p = refs[:11]
    refs = refs[11:]
    if layer == 0:
        extra, refs = refs[0], refs[1:]
    chunks, refs = take_chunks(plan, refs)
    part, dr, keep, send, sums = refs[:5]
    refs = refs[5:]
    if layer == 1:
        dv_out, refs = refs[0], refs[1:]
    else:
        dv_out, refs = refs[-1], refs[:-1]
    wqk, wv, wo, dy, dqk, do, acc, sems = refs
    s, c = idx[plan.side_at()], idx[plan.core_at()]
    start_att(plan, layer, idx, chunks, wqk, wv, wo, sems)
    zero = jnp.zeros((1, d_), F32)
    sb3 = zero
    for i in range(0, t_, STEP):
        sl = slice(i, i + STEP)
        x, inv = unit_rows(r[sl, :])
        dn = dc_a[sl, :].astype(F32) + dc_b[sl, :].astype(F32)
        dd = ucn[sl, :].astype(F32) + norm_back(dn, x, inv, prm[layer, 1:2, :])
        dr[sl, :] = dd
        dyb = dd.astype(BF)
        dy[sl, :] = dyb
        sb3 = sb3 + row_sum(dyb.astype(F32))
    wait_all(wo, sems.at[2])
    do[...] = dot_nt(dy[...], wo[...]).astype(BF)
    lanes = h_ // plan.pairs
    low = pair_mask(sq, lanes)
    scale = (lanes // 2) ** -0.5
    for s_ in range(plan.seqs):
        for j in range(plan.pairs):
            rws, cls = slice(s_ * sq, (s_ + 1) * sq), slice(j * lanes, (j + 1) * lanes)
            kcls = slice(h_ + j * lanes, h_ + (j + 1) * lanes)
            q2 = stack_pair(q[rws, cls], low)
            do2 = stack_pair(do[rws, cls], low)
            pr = p[s_ * plan.pairs + j]
            dp = dot_nt(do2, v[rws, cls])
            dv = dot_tn(pr, do2)
            if layer == 0:
                dv = dv + extra[rws, cls].astype(F32) * (s == 1).astype(F32)
            dv_out[rws, cls] = dv.astype(BF)
            pf = pr.astype(F32)
            ds = (pf * (dp - jnp.sum(pf * dp, axis=-1, keepdims=True))).astype(BF)
            dq2 = dot(ds, k[rws, cls])
            dqk[rws, cls] = (jnp.where(low, dq2[:sq], dq2[sq:]) * scale).astype(BF)
            dqk[rws, kcls] = (dot_tn(ds, q2) * scale).astype(BF)
    wait_all(wqk, sems.at[0])
    wait_all(wv, sems.at[1])
    da = dot_nt(dqk[...], wqk[...])
    dav = dot_nt(dv_out[...], wv[...])
    if layer == 1:
        dav = dav * (s == 0).astype(F32)
    acc[...] = da + dav
    dys = pl.ds(pl.multiple_of(s * h_, 128), h_)
    for core in range(2):

        @pl.when(c == core)
        def _():
            one, two = (keep, send) if core == 0 else (send, keep)
            one[...] = dqk[...]
            two[:, :h_] = dv_out[...]
            two[:, h_:] = dy[:, dys]

    sg0, sb0 = zero, zero
    for i in range(0, t_, STEP):
        sl = slice(i, i + STEP)
        dn = acc[sl, :]
        part[sl, :] = dn.astype(BF)
        x, _ = unit_rows(h[sl, :].astype(F32))
        sg0 = sg0 + row_sum(dn * x)
        sb0 = sb0 + row_sum(dn)
    sums[0:1, :], sums[1:2, :], sums[2:3, :] = sg0, sb0, 0.5 * sb3
    sq_ = row_sum(dqk[...].astype(F32))[:, :h_]
    none = jnp.zeros((1, h_), F32)
    sums[3:4, :] = jnp.where(s == 0, jnp.concatenate([sq_, none], axis=1), jnp.concatenate([none, sq_], axis=1))
    sums[4:5, :] = jnp.concatenate([row_sum(dv_out[...].astype(F32)), none], axis=1)


def g1_kernel(plan, layer, *refs):
    r_, h_, d_, n_ = plan.rows, plan.half, plan.width, plan.count
    idx, a, a_sib, oo, oo_sib, keep, got = refs[:7]
    refs = refs[7:]
    if layer == 0:
        tiny, refs = refs[:6], refs[6:]
    outs, refs = refs[:4], refs[4:]
    if layer == 0:
        gatt, tail, osem, tsem = refs
    else:
        gatt, osem = refs
    c = idx[plan.core_at()]

    @pl.when(c == 0)
    def _():
        gatt[...] = (dot_tn(a[...], keep[...]) + dot_tn(a_sib[...], got[...])).astype(BF)

    @pl.when(c == 1)
    def _():
        gatt[:, :h_] = (dot_tn(a[...], keep[:, :h_]) + dot_tn(a_sib[...], got[:, :h_])).astype(BF)
        gatt[:, h_:] = (dot_tn(oo[...], keep[:, h_:]) + dot_tn(oo_sib[...], got[:, h_:])).astype(BF)

    def pick_att(t, sh, dst, sem):
        dma(gatt.at[pl.ds(pl.multiple_of(sh * r_, 16), r_), pl.ds(t * h_, h_)], dst, sem).start()

    put_blocks(plan, idx, outs, osem, pick_att, 0)
    if layer == 0:
        small_sums(plan, idx, tiny, tail)
        half = n_ // 2
        for part, rng in ((0, range(half, n_)), (1, range(half))):
            for j in rng:
                dma(tail.at[j], outs[2 * part].at[j % half, pl.ds(r_, TAIL), :], tsem.at[part]).start()
        for part in range(2):
            wait_all(tail.at[pl.ds(0, half)], tsem.at[part])
        for i in range(4):
            ref = outs[i] if i % 2 else outs[i].at[:, pl.ds(0, r_), :]
            wait_all(ref, osem.at[i])
    else:
        wait_blocks(outs, osem)


def small_sums(plan, idx, tiny, tail):
    n_, r_, h_, d_, u_ = plan.count, plan.rows, plan.half, plan.width, plan.unit
    s = idx[plan.side_at()]
    rows = []
    for l in range(2):
        s2, s1, sbf = tiny[3 * l : 3 * l + 3]
        rows += [s1[0:1], s2[0:1], s1[1:2], s2[1:2], s1[3:4], s1[2:3], s2[2:3]]
        bf = sbf[...]
        cut = [jnp.concatenate([bf[:, sh * u_ + i * r_ : sh * u_ + (i + 1) * r_] for sh in range(n_)], axis=1) for i in range(2)]
        for side in range(2):
            on = (s == side).astype(F32)
            rows += [cut[0] * on, cut[1] * on]
    v1, v2 = tiny[1][4:5, :h_], tiny[4][4:5, :h_]
    first = (s == 0).astype(F32)
    vals = jnp.concatenate([v1 * first, v1 * (1.0 - first), v2 * first], axis=1)
    each = plan.values // n_
    pad = jnp.zeros((1, 2 * r_ - each), F32)
    rows.append(jnp.concatenate([vals[:, sh * each : sh * each + r_] for sh in range(n_)], axis=1))
    rows.append(jnp.concatenate([x for sh in range(n_) for x in (vals[:, sh * each + r_ : (sh + 1) * each], pad)], axis=1))
    rows.append(jnp.zeros((TAIL - 24, d_), F32))
    full = jnp.concatenate(rows, axis=0).astype(BF)
    for sh in range(n_):
        block = jnp.concatenate([full[:, sh * r_ : (sh + 1) * r_], jnp.zeros((TAIL, h_ - r_), BF)], axis=1)
        tail[idx[2 * n_ + sh]] = block


def add_kernel(*refs):
    n = len(refs) // 2 - 1
    for t in range(2):
        x = refs[t][0].astype(F32)
        for i in range(1, n):
            x = x + refs[2 * i + t][0].astype(F32)
        refs[2 * n + t][0] = x.astype(BF)


def run_add(pairs, low, top):
    ins = [(x, pl.BlockSpec((1,) + x.shape[1:], lambda j: (low + j, 0, 0))) for pair in pairs for x in pair]
    return pl.pallas_call(
        add_kernel,
        grid=(top - low,),
        out_shape=[jax.ShapeDtypeStruct((top - low,) + x.shape[1:], BF) for x in pairs[0]],
        in_specs=[sp for _, sp in ins],
        out_specs=[pl.BlockSpec((1,) + x.shape[1:], lambda j: (j, 0, 0)) for x in pairs[0]],
        compiler_params=pltpu.CompilerParams(vmem_limit_bytes=VMEM_BYTES),
        cost_estimate=pl.CostEstimate(flops=int(2.0 * 4.2e8), bytes_accessed=1000, transcendentals=0),
    )(*[x for x, _ in ins])


def pick_kernel(plan, counts, idx, *refs):
    r_ = plan.rows
    ins, (own, send) = list(refs[:-2]), refs[-2:]
    first = idx[plan.side_at()] == 0
    sums = []
    for n in counts:
        pairs, ins = ins[: 2 * n], ins[2 * n :]
        sums.append([sum(pairs[2 * i + t][0].astype(F32) for i in range(n)).astype(BF) for t in range(2)])
    a0, a1, m0, m1 = sums
    for t in range(2):
        for at, size, x, y in ((3 * t * r_, r_, a0[t][:r_], a1[t]), ((3 * t + 1) * r_, 2 * r_, m0[t], m1[t])):
            own[at : at + size] = jnp.where(first, x, y)
            send[at : at + size] = jnp.where(first, y, x)
    for ref in (own, send):
        ref[6 * r_ :] = a0[0]


def run_pick(plan, idx, sums):
    ins = [x for pairs in sums for pair in pairs for x in pair]
    shape = (7 * plan.rows + TAIL, plan.half)
    return pl.pallas_call(
        functools.partial(pick_kernel, plan, [len(pairs) for pairs in sums]),
        grid=(1,),
        out_shape=[jax.ShapeDtypeStruct(shape, BF)] * 2,
        in_specs=[SM] + [pl.BlockSpec((1,) + x.shape[1:], lambda j: (0, 0, 0)) for x in ins],
        out_specs=[pl.BlockSpec(shape, lambda j: (0, 0))] * 2,
        compiler_params=pltpu.CompilerParams(vmem_limit_bytes=VMEM_BYTES),
        cost_estimate=pl.CostEstimate(flops=int(2.5 * 4.2e8), bytes_accessed=1000, transcendentals=0),
    )(idx, *ins)


def finish_kernel(plan, *refs):
    r_, h_, d_, u_ = plan.rows, plan.half, plan.width, plan.unit
    idx, own, own_sib, far, far_sib, val, val_sib = refs[:7]
    o_qk, o_val, o_out, o_fc, o_proj, o_gain, o_shift, o_bf, o_vs = refs[7:16]
    buf, vals, sems = refs[16:]
    s, c = idx[plan.side_at()], idx[plan.core_at()]
    for i, ref in enumerate((own, own_sib, far, far_sib)):
        side = s if i < 2 else 1 - s
        core = c if i % 2 == 0 else 1 - c
        dma(ref, buf.at[side, core], sems.at[0]).start()

    @pl.when(c == 1)
    def _():
        dma(val, vals, sems.at[1]).start()

    @pl.when(c == 0)
    def _():
        dma(val_sib, vals, sems.at[1]).start()

    wait_all(buf, sems.at[0])
    wait_all(vals, sems.at[1])
    sm = sum(buf[side, core, 7 * r_ :, :r_].astype(F32) for side in range(2) for core in range(2))
    mine = jnp.where(s == 0, sm[:11], sm[11:22])
    o_gain[...] = mine[0:2]
    o_shift[...] = mine[2:7]
    o_bf[...] = jnp.concatenate([mine[7 + i : 8 + i] for i in range(4)], axis=1)
    o_vs[...] = jnp.concatenate([sm[22:23], sm[23:24, : plan.values // plan.count - r_]], axis=1)
    low, high = buf[0, 1, :r_].astype(F32), buf[1, 1, :r_].astype(F32)
    other, rest = vals[...].astype(F32), buf[0, 1, 6 * r_ : 7 * r_].astype(F32)
    o_val[:, :h_] = jnp.where(s == 0, low, rest)
    o_val[:, h_:d_] = jnp.where(s == 0, high, other)
    o_val[:, d_:] = jnp.where(s == 0, other, low)
    per = h_ // u_
    for side in range(2):
        o_out[:, side * h_ : (side + 1) * h_] = buf[side, 1, 3 * r_ : 4 * r_].astype(F32)
        for t in range(2):
            o_qk[:, t * d_ + side * h_ : t * d_ + (side + 1) * h_] = buf[side, 0, 3 * t * r_ : (3 * t + 1) * r_].astype(F32)
            for core in range(2):
                lo = side * 2 * r_ + t * r_
                o_proj[lo : lo + r_, core * h_ : (core + 1) * h_] = buf[side, core, (3 * t + 2) * r_ : (3 * t + 3) * r_].astype(F32)
    for core in range(2):
        for t in range(2):
            q = 2 * core + t
            b0, b1 = (buf[side, core, (3 * t + 1) * r_ : (3 * t + 2) * r_].astype(F32) for side in range(2))
            pieces = [x[:, i * u_ : (i + 1) * u_] for i in range(per) for x in (b0, b1)]
            o_fc[:, 2 * q * h_ : 2 * (q + 1) * h_] = jnp.concatenate(pieces, axis=1)


VM = pl.BlockSpec(memory_space=pltpu.VMEM)
SM = pl.BlockSpec(memory_space=pltpu.SMEM)
ANY = pl.BlockSpec(memory_space=pl.ANY)


def call(kernel, ins, outs, scratch, us):
    return pl.pallas_call(
        kernel,
        out_shape=[jax.ShapeDtypeStruct(sh, dt) for sh, dt, _ in outs],
        in_specs=[sp for _, sp in ins],
        out_specs=[sp for _, _, sp in outs],
        scratch_shapes=scratch,
        compiler_params=pltpu.CompilerParams(vmem_limit_bytes=VMEM_BYTES),
        cost_estimate=pl.CostEstimate(flops=int(us * 4.2e8), bytes_accessed=1000, transcendentals=0),
    )(*[x for x, _ in ins])


def vm(*arrays):
    return [(x, VM) for x in arrays]


def hbm(arrays):
    return [(x, ANY) for x in arrays]


def att_scratch(plan):
    w, h = plan.width, plan.half
    return [pltpu.VMEM((w, w), BF), pltpu.VMEM((w, h), BF), pltpu.VMEM((h, w), BF)]


def mlp_scratch(plan):
    return [pltpu.VMEM((plan.width, plan.fh), BF), pltpu.VMEM((plan.fh, plan.width), BF)]


def dma_sems(n):
    return pltpu.SemaphoreType.DMA((n,))


def run_pack(plan, idx, wqk, wfc, wproj):
    r_, h_ = plan.rows, plan.half
    both = ((2, 3 * r_, h_), BF, VM)
    return call(functools.partial(pack_kernel, plan), [(idx, SM)] + vm(wqk, wfc, wproj), [both, both], [], 2.5)


def run_param(plan, idx, steps):
    outs = [((2, 8, plan.width), F32, VM), ((2, 1, plan.fh), F32, VM)]
    scratch = [pltpu.VMEM((plan.count, TAIL, plan.half), BF), pltpu.SemaphoreType.DMA]
    return call(functools.partial(param_kernel, plan), [(idx, SM)] + hbm(steps), outs, scratch, 2.3)


def run_f1(plan, layer, idx, prm, inputs, chunks):
    t_, h_, d_ = plan.tokens, plan.half, plan.width
    narrow, wide = ((t_, h_), BF, VM), ((t_, d_), BF, VM)
    outs = [wide, narrow, narrow, narrow, ((plan.seqs * plan.pairs, 2 * plan.seq, plan.seq), BF, VM), narrow, wide]
    outs += [wide] if layer else []
    scratch = att_scratch(plan) + [dma_sems(3)]
    ins = [(idx, SM)] + vm(prm, *inputs) + hbm(chunks)
    return call(functools.partial(f1_kernel, plan, layer), ins, outs, scratch, 5.5)


def run_f2(plan, layer, idx, prm, bf, h, pa, pb, chunks):
    t_, d_, f_ = plan.tokens, plan.width, plan.fh
    wide = ((t_, d_), BF, VM)
    outs = [wide, ((t_, d_), F32, VM), ((t_, f_ + d_), BF, VM), ((t_, f_), BF, VM)]
    scratch = mlp_scratch(plan) + [pltpu.VMEM((t_, f_ // 3), F32), dma_sems(2)]
    ins = [(idx, SM)] + vm(prm, bf, h, pa, pb) + hbm(chunks)
    return call(functools.partial(f2_kernel, plan, layer), ins, outs, scratch, 7.2)


def run_b2(plan, layer, idx, prm, gp, r, more, chunks):
    t_, d_, f_ = plan.tokens, plan.width, plan.fh
    outs = [((t_, d_), BF, VM), ((t_, f_ + d_), BF, VM), ((3, d_), F32, VM), ((1, f_), F32, VM)]
    scratch = mlp_scratch(plan) + [pltpu.VMEM((t_, d_), F32), dma_sems(2)]
    ins = [(idx, SM)] + vm(prm, gp, r, *more) + hbm(chunks)
    return call(functools.partial(b2_kernel, plan, layer), ins, outs, scratch, 6.7)


def grad_outs(plan, rows, tail=0):
    return [((plan.count // 2, r, plan.half), BF, ANY) for r in (rows + tail, rows) * 2]


def run_g2(plan, idx, ucn, ucn_sib, dze, dze_sib):
    d_, f_, h_ = plan.width, plan.fh, plan.half
    scratch = [pltpu.VMEM((d_, d_), BF), pltpu.VMEM((f_, h_), BF), dma_sems(4)]
    ins = [(idx, SM)] + vm(ucn, ucn_sib, dze, dze_sib)
    return call(functools.partial(g2_kernel, plan), ins, grad_outs(plan, 2 * plan.rows), scratch, 4.5)


def run_b1(plan, layer, idx, prm, more, chunks):
    t_, d_, h_ = plan.tokens, plan.width, plan.half
    wide, narrow = (t_, d_), (t_, h_)
    outs = [(wide, BF, VM), (wide, F32, VM), (wide, BF, VM), (wide, BF, VM), ((5, d_), F32, VM)]
    scratch = att_scratch(plan) + [pltpu.VMEM(wide, BF), pltpu.VMEM(wide, BF), pltpu.VMEM(narrow, BF), pltpu.VMEM(wide, F32), dma_sems(3)]
    if layer:
        outs.append((narrow, BF, VM))
    else:
        scratch.append(pltpu.VMEM(narrow, BF))
    ins = [(idx, SM)] + vm(prm, *more) + hbm(chunks)
    return call(functools.partial(b1_kernel, plan, layer), ins, outs, scratch, 7.5)


def run_g1(plan, layer, idx, a, a_sib, oo, oo_sib, keep, got, tiny):
    d_, h_ = plan.width, plan.half
    scratch = [pltpu.VMEM((d_, d_), BF)]
    if layer == 0:
        scratch += [pltpu.VMEM((plan.count, TAIL, h_), BF), dma_sems(4), dma_sems(2)]
    else:
        scratch += [dma_sems(4)]
    ins = [(idx, SM)] + vm(a, a_sib, oo, oo_sib, keep, got, *tiny)
    return call(functools.partial(g1_kernel, plan, layer), ins, grad_outs(plan, plan.rows, 0 if layer else TAIL), scratch, 3.5)


def run_finish(plan, idx, arrays):
    r_, h_, d_, n_ = plan.rows, plan.half, plan.width, plan.count
    outs = [(sh, F32, VM) for sh in ((r_, 2 * d_), (r_, plan.values), (r_, d_), (r_, plan.ff), (4 * r_, d_), (2, r_), (5, r_), (1, 4 * r_), (1, plan.values // n_))]
    scratch = [pltpu.VMEM((2, 2, 7 * r_ + TAIL, h_), BF), pltpu.VMEM((r_, h_), BF), dma_sems(2)]
    return call(functools.partial(finish_kernel, plan), [(idx, SM)] + hbm(arrays), outs, scratch, 4.5)


def after(x, *earlier):
    return lax.optimization_barrier((x,) + earlier)[0]


def per_device(ends, w_qk, w_value, w_out, w_fc, w_proj, gains, shifts, fc_shift, value_shift):
    s, grp, d = lax.axis_index("section"), lax.axis_index("group"), lax.axis_index("dp")
    c = grp % 2
    count, groups = lax.axis_size("dp"), lax.axis_size("group")
    rows, width = w_qk.shape[1], ends.shape[3]
    half = width // 2
    seqs, seq = ends.shape[1], ends.shape[2]
    tokens = seqs * seq
    plan = Plan(count, rows, width, w_fc.shape[2], w_value.shape[1], tokens, seq, HEADS // 2)
    table = plan.table(groups)
    idx = lax.dynamic_slice(jnp.asarray(table), (s, grp, d, 0), (1, 1, 1, table.shape[3])).reshape(-1)
    first, even = s == 0, d % 2 == 0

    def swap_x(x):
        return lax.ppermute(x, "section", [(0, 1), (1, 0)])

    def swap_c(x):
        return lax.ppermute(x, "group", [(i, i ^ 1) for i in range(groups)])

    def swap_d(x, bit):
        return lax.ppermute(x, "dp", [(i, i ^ bit) for i in range(count)])

    hc = count // 2
    spread = [
        [(l * count + i, (i // hc) * count + 2 * (i % hc) + (l if w == 0 else 1 - l)) for l in range(2) for i in range(count)]
        for w in range(2)
    ]
    mine, send = run_pack(plan, idx, w_qk[0], w_fc[0], w_proj[0])
    o_lo, o_hi = w_out[0][:, :half], w_out[0][:, half:]
    flat = jnp.concatenate([gains[0], shifts[0], fc_shift[0].reshape(4, rows)], axis=0)
    got = swap_x(send)
    flat_got = swap_x(after(flat, send))
    o_a = lax.ppermute(jnp.where(first, o_lo, o_hi), ("section", "dp"), spread[0])
    o_b = lax.ppermute(jnp.where(first, o_hi, o_lo), ("section", "dp"), spread[1])
    ends_own = ends[0].reshape(tokens, width)
    ends_got = swap_x(after(ends_own, got))
    more = value_shift.shape[0] - rows
    tail = jnp.concatenate(
        [
            jnp.where(first, flat, flat_got),
            jnp.where(first, flat_got, flat),
            value_shift[None, :rows],
            jnp.pad(value_shift[None, rows:], ((0, 0), (0, rows - more))),
        ],
        axis=0,
    )
    tail = jnp.pad(tail, ((0, TAIL - tail.shape[0]), (0, half - rows)))
    v_side = (lax.dynamic_slice_in_dim(w_value, s * half, half, 1), w_value[:, width:])
    o_side = (jnp.where(even, o_a, o_b), jnp.where(even, o_b, o_a))

    def head(t, l, other):
        x = jnp.where(first if l == 0 else ~first, mine[t, :rows], got[t, :rows])
        return jnp.where(c == 0, x, other)

    early, late = [], []
    for t, side in ((0, v_side), (1, o_side)):
        mlp = jnp.where(first, mine[t, rows:], got[t, rows:])
        early.append(jnp.concatenate([head(t, 0, side[0]), mlp, head(t, 1, side[1])] + ([tail] if t == 0 else []), axis=0))
        late.append(jnp.where(first, got[t, rows:], mine[t, rows:]))

    routes = [[(a, b) for a, b in zip(order, order[1:] + order[:1])] for order in (ring_order(count), ring_order(count)[::-1])]

    def ring(x):
        return lax.optimization_barrier([lax.ppermute(x[t], "dp", routes[t]) for t in range(2)])

    def with_sibling(steps):
        return [y for t in range(2) for y in [x[t] for x in steps] + [swap_c(x[t]) for x in steps]]

    steps = [early]
    for n in range(count - 1):
        steps.append(ring(steps[-1]))
        if n == 1:
            steps[-1] = [after(x, ends_got) for x in steps[-1]]
    chunks = with_sibling(steps)
    prm, bf = run_param(plan, idx, [x[0] for x in steps])

    h0 = jnp.where(first, ends_own, ends_got)
    cot = jnp.where(first, ends_got, ends_own)
    part, q0, k0, v0, p0, o0, a0 = run_f1(plan, 0, idx, prm, (h0,), chunks)
    steps = [late, ring([after(x, steps[-1][t]) for t, x in enumerate(late)])]
    for n in range(count - 2):
        steps.append(ring([after(x, part) for x in steps[-1]] if n == 0 else steps[-1]))
    wide = with_sibling(steps)
    got = swap_x(part)
    o0_far = swap_x(after(o0, got))
    part, r0, ucn0, gp0 = run_f2(plan, 0, idx, prm, bf, h0, part, got, chunks)
    got = after(swap_x(part), o0_far)
    part, q1, k1, v1, p1, o1, a1, h1 = run_f1(plan, 1, idx, prm, (r0, part, got, v0), chunks)
    got = swap_x(part)
    o1_far = swap_x(after(o1, got))
    y_part, r1, ucn1, gp1 = run_f2(plan, 1, idx, prm, bf, h1, part, got, wide)

    class Sum:
        def __init__(self, g):
            self.out, self.parts = list(g[:2]), [list(g[2:])]
            self.top = count // 2

        def load(self, *others):
            if others:
                self.parts[-1] = [after(x, *others) for x in self.parts[-1]]
            low = self.top // 2
            self.out = run_add(self.parts, low, self.top)
            self.top = low
            return self.out

        def send(self):
            k = plan.bits - len(self.parts)
            self.parts.append([swap_d(self.out[t], plan.orders[t][k]) for t in range(2)])
            return self.parts[-1]

    def over_pairs(x):
        total = x
        for n in range(1, groups // 2):
            total = total + lax.ppermute(x, "group", [(i, (i + 2 * n) % groups) for i in range(groups)])
        return total

    def by_side(o, far):
        return jnp.concatenate([jnp.where(first, o, far), jnp.where(first, far, o)], axis=1)

    oo0, oo1 = by_side(o0, o0_far), by_side(o1, o1_far)
    part, dze, s2_1, sbf_1 = run_b2(plan, 1, idx, prm, gp1, r1, (after(cot, o1_far),), wide)
    got = swap_x(part)
    g_mlp1 = run_g2(plan, idx, ucn1, swap_c(ucn1), dze, swap_c(dze))
    mlp1 = Sum(g_mlp1)
    got = after(got, *mlp1.out)
    mlp1.send()
    part, dr, keep, send, s1_1, dv1 = run_b1(plan, 1, idx, prm, (cot, part, got, r1, h1, q1, k1, v1, p1), chunks)
    got = swap_x(part)
    g_att1 = run_g1(plan, 1, idx, a1, swap_c(a1), oo1, swap_c(oo1), keep, swap_c(send), ())
    att1 = Sum(g_att1)
    got = after(got, *att1.out)
    part, dze, s2_0, sbf_0 = run_b2(plan, 0, idx, prm, gp0, r0, (dr, part, got, h1), chunks)
    mlp1.load(part)
    mlp1.send()
    att1.send()
    got = swap_x(part)
    g_mlp0 = run_g2(plan, idx, ucn0, swap_c(ucn0), dze, swap_c(dze))
    mlp0 = Sum(g_mlp0)
    got = after(got, *mlp0.out)
    e = dze[:, plan.fh :]
    part, dr, keep, send, s1_0 = run_b1(plan, 0, idx, prm, (e, part, got, r0, h0, q0, k0, v0, p0, dv1), chunks)
    att1.load(part)
    att1.send()
    mlp1.load(part)
    mlp1.send()
    mlp0.send()
    x_part = part
    g_att0 = run_g1(plan, 0, idx, a0, swap_c(a0), oo0, swap_c(oo0), keep, swap_c(send), (s2_0, s1_0, sbf_0, s2_1, s1_1, sbf_1))
    att0 = Sum(g_att0)
    att0.send()
    att1.load()
    att1.send()
    x_got, y_got = swap_x(after(x_part, mlp0.parts[1][0])), swap_x(after(y_part, mlp0.parts[1][0]))
    mlp0.load()
    mlp0.send()
    att0.load()
    att0.send()
    mlp0.load()
    mlp0.send()
    att0.load()
    att0.send()
    own, send = (over_pairs(x) for x in run_pick(plan, idx, [x.parts for x in (att0, att1, mlp0, mlp1)]))
    far = swap_x(send)
    val = send[:rows]
    o_qk, o_val, o_out, o_fc, o_proj, o_gain, o_shift, o_bf, o_vs = run_finish(
        plan, idx, [own, swap_c(own), far, swap_c(far), val, swap_c(val)]
    )

    y = (r1 + (y_part.astype(F32) + y_got.astype(F32)) + prm[1, 6:7]).astype(BF)
    x, inv = unit_rows(h0.astype(F32))
    x_out = (dr + norm_back(x_part.astype(F32) + x_got.astype(F32), x, inv, prm[0, 0:1])).astype(BF)
    res = jnp.where(first, x_out, y).reshape(1, seqs, seq, width)
    return (res, o_qk[None], o_val, o_out[None], o_fc[None], o_proj[None], o_gain[None], o_shift[None], o_bf, o_vs[0])


def solution(mesh):
    placed = (
        P("section", ("group", "dp"), None, None),
        P("section", "dp", None),
        P("dp", None),
        P("section", "dp", None),
        P("section", "dp", None),
        P("section", "dp", None),
        P("section", None, "dp"),
        P("section", None, "dp"),
        P("section", "dp"),
        P("dp"),
    )
    return jax.shard_map(per_device, mesh=mesh, in_specs=placed, out_specs=placed, check_vma=False)
```

```python
import functools

import jax
import jax.numpy as jnp
import numpy as np
from jax import lax
from jax.experimental import pallas as pl
from jax.experimental.pallas import tpu as pltpu
from jax.sharding import PartitionSpec as P

HEADS = 12
BF = jnp.bfloat16
F32 = jnp.float32
norm_eps = 1e-05
masked_score = -1e30
TAIL = 32
SMALL = 16
STEP = 32
VMEM_BYTES = 16 * 1024 * 1024


def dot(a, b):
    return jnp.dot(a, b, preferred_element_type=F32)


def dot_tn(a, b):
    return lax.dot_general(a, b, (((0,), (0,)), ((), ())), preferred_element_type=F32)


def dot_nt(a, b):
    return lax.dot_general(a, b, (((1,), (1,)), ((), ())), preferred_element_type=F32)


def unit_rows(v):
    centered = v - jnp.mean(v, axis=-1, keepdims=True)
    inv = lax.rsqrt(jnp.mean(centered * centered, axis=-1, keepdims=True) + norm_eps)
    return centered * inv, inv


def norm_back(dn, x, inv, gain):
    scaled = dn * gain
    inner = jnp.mean(scaled * x, axis=-1, keepdims=True)
    return inv * (scaled - jnp.mean(scaled, axis=-1, keepdims=True) - x * inner)


def row_sum(v):
    return jnp.sum(v, axis=0, keepdims=True)


def ring_order(count):
    wide = 2 if count < 16 else 4
    tall = count // wide
    order = [i * wide for i in range(tall)]
    for n, row in enumerate(reversed(range(tall))):
        cols = range(1, wide)
        order += [row * wide + col for col in (cols if n % 2 == 0 else reversed(cols))]
    return order


class Plan:
    def __init__(self, count, rows, width, ff, values, tokens, seq, heads):
        self.count, self.rows, self.width, self.half = count, rows, width, width // 2
        self.ff, self.fh, self.unit, self.values = ff, ff // 2, ff // count // 2, values
        self.tokens, self.seq, self.seqs = tokens, seq, tokens // seq
        self.pairs = heads // 2
        self.bits = count.bit_length() - 1
        down = [1 << i for i in reversed(range(self.bits))]
        other = down[:-2] + [down[-1], down[-2]]
        self.orders = (down, other)
        self.masks = []
        for order in self.orders:
            mask = [0] * count
            for j in range(count):
                for k, bit in enumerate(order):
                    if j >> k & 1:
                        mask[j] ^= bit
            self.masks.append(mask)

    def core_at(self):
        return 6 * self.count

    def side_at(self):
        return 6 * self.count + 1

    def table(self, groups):
        n = self.count
        out = np.zeros((2, groups, n, 6 * n + 2), np.int32)
        order = ring_order(n)
        for p, d in enumerate(order):
            for t in range(2):
                out[:, :, d, t * n : (t + 1) * n] = [d ^ m for m in self.masks[t]]
                out[:, :, d, (3 + t) * n : (4 + t) * n] = [order[(p - (1 - 2 * t) * j) % n] for j in range(n)]
            for j, m in enumerate(self.masks[0]):
                out[:, :, d, 2 * n + (d ^ m)] = j
            for j in range(n):
                out[:, :, d, 5 * n + order[(p - j) % n]] = j
        out[:, :, :, 6 * n] = (np.arange(groups) % 2)[None, :, None]
        out[:, :, :, 6 * n + 1] = np.arange(2)[:, None, None]
        return out


def aligned(x, size):
    return x if isinstance(x, int) else pl.multiple_of(x, size)


def dma(src, dst, sem):
    return pltpu.make_async_copy(src, dst, sem)


def wait_all(ref, sem):
    dma(ref, ref, sem).wait()


def chunk_refs(plan, idx, chunks, row):
    for j in range(plan.count):
        for t in range(2):
            for other in range(2):
                ref = chunks[(t * 2 + other) * plan.count + j]
                yield t, other, idx[(3 + t) * plan.count + j], ref.at[pl.ds(row, plan.rows), :]


def take_chunks(plan, refs):
    n = 4 * plan.count
    return refs[:n], refs[n:]


def start_att(plan, layer, idx, chunks, wqk, wv, wo, sems):
    r_, h_ = plan.rows, plan.half
    c = idx[plan.core_at()]
    for t, other, sh, src in chunk_refs(plan, idx, chunks, 3 * r_ * layer):
        core = 1 - c if other else c
        row = pl.multiple_of(sh * r_, 16)

        @pl.when(core == 0)
        def _():
            dma(src, wqk.at[pl.ds(row, r_), pl.ds(t * h_, h_)], sems.at[0]).start()

        @pl.when(core == 1)
        def _():
            if t == 0:
                dma(src, wv.at[pl.ds(row, r_), :], sems.at[1]).start()
            else:
                orow = pl.multiple_of((sh // 2) * r_, 16)
                ocol = pl.multiple_of((sh % 2) * h_, 128)
                dma(src, wo.at[pl.ds(orow, r_), pl.ds(ocol, h_)], sems.at[2]).start()


def start_mlp(plan, layer, idx, chunks, wfc, wproj, sems):
    r_, h_ = plan.rows, plan.half
    c = idx[plan.core_at()]
    for kind in range(2):
        for t, other, sh, src in chunk_refs(plan, idx, chunks, ((4 if layer else 1) + kind) * r_):
            core = 1 - c if other else c
            if kind == 0:
                row = pl.multiple_of(sh * r_, 16)
                col = pl.multiple_of((2 * core + t) * h_, 128)
                dst = wfc.at[pl.ds(row, r_), pl.ds(col, h_)]
            else:
                row = pl.multiple_of(sh * 2 * r_ + t * r_, 16)
                col = pl.multiple_of(core * h_, 128)
                dst = wproj.at[pl.ds(row, r_), pl.ds(col, h_)]
            dma(src, dst, sems.at[kind]).start()


def put_blocks(plan, idx, outs, sem, pick, row0):
    n_, r_ = plan.count, plan.rows
    half = n_ // 2
    for j in reversed(range(n_)):
        for t in range(2):
            part = 0 if j >= half else 1
            dst = outs[2 * part + t].at[j % half, pl.ds(row0, r_), :]
            pick(t, idx[t * n_ + j], dst, sem.at[2 * part + t])


def wait_blocks(outs, sem):
    for i, ref in enumerate(outs):
        wait_all(ref, sem.at[i])


def pack_kernel(plan, idx, wqk, wfc, wproj, wout, gains, shifts, fc_shift, v_shift, mine, send, o_a, o_b, small):
    r_, h_, d_, u_ = plan.rows, plan.half, plan.width, plan.unit
    per = h_ // u_
    s, c = idx[plan.side_at()], idx[plan.core_at()]
    lo, hi = wout[:, :h_], wout[:, h_:]
    o_a[...] = jnp.where(s == 0, lo, hi)
    o_b[...] = jnp.where(s == 0, hi, lo)
    rows = [gains[...], shifts[...]] + [fc_shift[:, i * r_ : (i + 1) * r_] for i in range(4)] + [v_shift[:, :r_]]
    more = v_shift.shape[1] - r_
    rows.append(jnp.concatenate([v_shift[:, r_:], jnp.zeros((1, r_ - more), BF)], axis=1))
    rows = jnp.concatenate([x.astype(F32) for x in rows] + [jnp.zeros((SMALL - 13, r_), F32)], axis=0)
    small[0] = jnp.concatenate([rows, jnp.zeros((SMALL, h_ - r_), F32)], axis=1).astype(BF)
    for side in range(2):
        for core in range(2):
            for keep in range(2):
                out = mine if keep else send

                @pl.when(jnp.logical_and(c == core, s == (side if keep else 1 - side)))
                def _():
                    for t in range(2):
                        lo = t * d_ + side * h_
                        out[t, :r_] = wqk[:, lo : lo + h_]
                        q = 2 * core + t
                        cols = [(q * per + i) * 2 * u_ + side * u_ for i in range(per)]
                        out[t, r_ : 2 * r_] = jnp.concatenate([wfc[:, x : x + u_] for x in cols], axis=1)
                        row = side * 2 * r_ + t * r_
                        out[t, 2 * r_ :] = wproj[row : row + r_, core * h_ : (core + 1) * h_]


def param_kernel(plan, idx, *refs):
    n_, r_, h_, d_ = plan.count, plan.rows, plan.half, plan.width
    s = idx[plan.side_at()]
    ins, (prm, bf, stack, sem) = refs[:4], refs[4:]
    for i, ref in enumerate(ins):
        dma(ref, stack.at[i // 2, pl.ds(i % 2 * (n_ // 2), n_ // 2)], sem.at[i]).start()
    for i, ref in enumerate(ins):
        wait_all(ref, sem.at[i])
    pairs = [[stack[i, idx[2 * n_ + sh]][:, :r_].astype(F32) for i in range(2)] for sh in range(n_)]
    more = plan.values // n_ - r_
    vals = jnp.concatenate([x for own, _ in pairs for x in (own[11:12, :], own[12:13, :more])], axis=1)
    for l in range(2):
        blocks = [jnp.where(s == l, own, far) for own, far in pairs]
        m = jnp.concatenate([b[:7] for b in blocks], axis=1)
        prm[l, 0:7] = m
        bq = jnp.where(s == 0, m[4:5, :h_], m[4:5, h_:])
        prm[l, 4:5] = jnp.concatenate([bq, jnp.zeros((1, d_ - h_), F32)], axis=1)
        if l == 0:
            bv = jnp.where(s == 0, vals[:, :h_], vals[:, h_:d_])
        else:
            bv = vals[:, d_:]
        prm[l, 7:8] = jnp.concatenate([bv, jnp.zeros((1, d_ - h_), F32)], axis=1)
        sides = []
        for side in range(2):
            row = 7 + 2 * side
            sides.append(jnp.concatenate([b[row + i : row + i + 1] for b in blocks for i in range(2)], axis=1))
        bf[l] = jnp.where(s == 0, sides[0], sides[1])


def pair_mask(seq, lanes):
    return lax.broadcasted_iota(jnp.int32, (seq, lanes), 1) < lanes // 2


def stack_pair(x, low):
    zero = jnp.zeros_like(x)
    return jnp.concatenate([jnp.where(low, x, zero), jnp.where(low, zero, x)], axis=0)


def f1_kernel(plan, layer, *refs):
    h_, t_, sq = plan.half, plan.tokens, plan.seq
    idx, prm, refs = refs[0], refs[1], refs[2:]
    if layer == 1:
        r_up, pa, pb, v_old = refs[:4]
        refs = refs[4:]
    else:
        here, there = refs[:2]
        refs = refs[2:]
    chunks, refs = take_chunks(plan, refs)
    part, q, k, v, p, o, a, h = refs[:8]
    if layer == 0:
        cot = refs[8]
    wqk, wv, wo, sems = refs[-4:]
    first = idx[plan.side_at()] == 0
    start_att(plan, layer, idx, chunks, wqk, wv, wo, sems)
    for i in range(0, t_, STEP):
        sl = slice(i, i + STEP)
        if layer == 1:
            hh = r_up[sl, :] + (pa[sl, :].astype(F32) + pb[sl, :].astype(F32)) + prm[0, 6:7, :]
            h[sl, :] = hh.astype(BF)
        else:
            mine, theirs = here[sl, :], there[sl, :]
            h[sl, :] = jnp.where(first, mine, theirs)
            cot[sl, :] = jnp.where(first, theirs, mine)
        x, _ = unit_rows(h[sl, :].astype(F32))
        a[sl, :] = (x * prm[layer, 0:1, :] + prm[layer, 2:3, :]).astype(BF)
    wait_all(wqk, sems.at[0])
    qk = dot(a[...], wqk[...])
    q[...] = (qk[:, :h_] + prm[layer, 4:5, :h_]).astype(BF)
    k[...] = qk[:, h_:].astype(BF)
    wait_all(wv, sems.at[1])
    val = (dot(a[...], wv[...]) + prm[layer, 7:8, :h_]).astype(BF)
    if layer == 1:
        val = jnp.where(idx[plan.side_at()] == 1, v_old[...], val)
    v[...] = val
    lanes = h_ // plan.pairs
    low = pair_mask(sq, lanes)
    causal = lax.broadcasted_iota(jnp.int32, (2 * sq, sq), 0) % sq >= lax.broadcasted_iota(jnp.int32, (2 * sq, sq), 1)
    scale = (lanes // 2) ** -0.5
    for s_ in range(plan.seqs):
        for j in range(plan.pairs):
            rws, cls = slice(s_ * sq, (s_ + 1) * sq), slice(j * lanes, (j + 1) * lanes)
            q2 = stack_pair(q[rws, cls], low)
            sc = jnp.where(causal, dot_nt(q2, k[rws, cls]) * scale, masked_score)
            ex = jnp.exp(sc - jnp.max(sc, axis=-1, keepdims=True))
            pr = (ex / jnp.sum(ex, axis=-1, keepdims=True)).astype(BF)
            p[s_ * plan.pairs + j] = pr
            o2 = dot(pr, v[rws, cls])
            o[rws, cls] = jnp.where(low, o2[:sq], o2[sq:]).astype(BF)
    wait_all(wo, sems.at[2])
    part[...] = dot(o[...], wo[...]).astype(BF)


def f2_kernel(plan, layer, *refs):
    t_ = plan.tokens
    idx, prm, bf, h, pa, pb = refs[:6]
    chunks, refs = take_chunks(plan, refs[6:])
    part, r, ucn, gp, wfc, wproj, z, sems = refs
    f_ = plan.fh
    start_mlp(plan, layer, idx, chunks, wfc, wproj, sems)
    for i in range(0, t_, STEP):
        sl = slice(i, i + STEP)
        rr = h[sl, :].astype(F32) + (pa[sl, :].astype(F32) + pb[sl, :].astype(F32)) + prm[layer, 5:6, :]
        r[sl, :] = rr
        x, _ = unit_rows(rr)
        ucn[sl, f_:] = (x * prm[layer, 1:2, :] + prm[layer, 3:4, :]).astype(BF)
    wait_all(wfc, sems.at[0])
    cols = plan.fh // 3
    for j in range(3):
        cs = slice(j * cols, (j + 1) * cols)
        z[...] = dot(ucn[:, f_:], wfc[:, cs])

        def body(i, carry):
            sl = pl.ds(pl.multiple_of(i * STEP, STEP), STEP)
            zz = z[sl, :] + bf[layer, :, cs]
            sq_ = zz * zz
            th = jnp.tanh(0.7978845608 * zz * (1.0 + 0.044715 * sq_))
            hp = 0.5 * (1.0 + th)
            ucn[sl, cs] = (zz * hp).astype(BF)
            slope = 0.7978845608 * (1.0 + 3 * 0.044715 * sq_)
            gp[sl, cs] = (hp + 0.5 * zz * (1.0 - th * th) * slope).astype(BF)
            return carry

        lax.fori_loop(0, t_ // STEP, body, 0)
    wait_all(wproj, sems.at[1])
    part[...] = dot(ucn[:, :f_], wproj[...]).astype(BF)


def b2_kernel(plan, layer, *refs):
    d_, t_, f_ = plan.width, plan.tokens, plan.fh
    idx, prm, gp, r = refs[:4]
    refs = refs[4:]
    if layer == 1:
        e, refs = refs[0], refs[1:]
    else:
        dr, da_a, da_b, h_up = refs[:4]
        refs = refs[4:]
    chunks, refs = take_chunks(plan, refs)
    part, e_out, z_keep, z_send, e_send, sums, sbf = refs[:7]
    h_, c = plan.half, idx[plan.core_at()]
    wfc, wproj, acc, dz, sems = refs[-5:]
    start_mlp(plan, layer, idx, chunks, wfc, wproj, sems)
    zero = jnp.zeros((1, d_), F32)
    sb4 = zero
    for i in range(0, t_, STEP):
        sl = slice(i, i + STEP)
        if layer == 0:
            x, inv = unit_rows(h_up[sl, :].astype(F32))
            dn = da_a[sl, :].astype(F32) + da_b[sl, :].astype(F32)
            ee = (dr[sl, :] + norm_back(dn, x, inv, prm[1, 0:1, :])).astype(BF)
        else:
            ee = e[sl, :]
        e_out[sl, :] = ee
        sb4 = sb4 + row_sum(ee.astype(F32))
    wait_all(wproj, sems.at[1])
    wait_all(wfc, sems.at[0])
    cols = f_ // 3
    for j in range(3):
        cs = slice(j * cols, (j + 1) * cols)
        dzj = (dot_nt(e_out[...], wproj[cs, :]) * gp[:, cs].astype(F32)).astype(BF)
        dz[:, cs] = dzj
        sbf[:, cs] = row_sum(dzj.astype(F32))
    z_keep[...] = dz[:, pl.ds(pl.multiple_of(c * d_, 128), d_)]
    z_send[...] = dz[:, pl.ds(pl.multiple_of((1 - c) * d_, 128), d_)]
    e_send[...] = e_out[:, pl.ds(pl.multiple_of((1 - c) * h_, 128), h_)]
    acc[...] = dot_nt(dz[...], wfc[...])
    sg1, sb1 = zero, zero
    for i in range(0, t_, STEP):
        sl = slice(i, i + STEP)
        dn = acc[sl, :]
        part[sl, :] = dn.astype(BF)
        x, _ = unit_rows(r[sl, :])
        sg1 = sg1 + row_sum(dn * x)
        sb1 = sb1 + row_sum(dn)
    sums[0:1, :], sums[1:2, :], sums[2:3, :] = sg1, sb1, 0.5 * sb4


def g2_kernel(plan, *refs):
    r_, h_, f_, d_ = plan.rows, plan.half, plan.fh, plan.width
    idx, ucn, ucn_sib, e, e_sib, dz, dz_sib = refs[:7]
    outs, (gfc, gproj, osem) = refs[7:-3], refs[-3:]
    c = idx[plan.core_at()]
    ecols = pl.ds(pl.multiple_of(c * h_, 128), h_)
    gproj[...] = (dot_tn(ucn[:, :f_], e[:, ecols]) + dot_tn(ucn_sib[:, :f_], e_sib[...])).astype(BF)

    def pick_proj(t, sh, dst, sem):
        dma(gproj.at[pl.ds(pl.multiple_of(sh * 2 * r_ + t * r_, 16), r_), :], dst, sem).start()

    put_blocks(plan, idx, outs, osem, pick_proj, r_)
    gfc[...] = (dot_tn(ucn[:, f_:], dz[...]) + dot_tn(ucn_sib[:, f_:], dz_sib[...])).astype(BF)

    def pick_fc(t, sh, dst, sem):
        dma(gfc.at[pl.ds(pl.multiple_of(sh * r_, 16), r_), pl.ds(t * h_, h_)], dst, sem).start()

    put_blocks(plan, idx, outs, osem, pick_fc, 0)
    wait_blocks(outs, osem)


def b1_kernel(plan, layer, *refs):
    h_, d_, t_, sq = plan.half, plan.width, plan.tokens, plan.seq
    idx, prm, e, dc_a, dc_b, r, h, q, k, v, p = refs[:11]
    refs = refs[11:]
    if layer == 0:
        extra, refs = refs[0], refs[1:]
    else:
        os, refs = refs[:4], refs[4:]
    chunks, refs = take_chunks(plan, refs)
    part, dr, keep, send, sums = refs[:5]
    refs = refs[5:]
    if layer == 1:
        dv_out, oos, refs = refs[0], refs[1:3], refs[3:]
        first = idx[plan.side_at()] == 0
        for i, oo in enumerate(oos):
            own, far = os[2 * i][...], os[2 * i + 1][...]
            oo[:, :h_] = jnp.where(first, own, far)
            oo[:, h_:] = jnp.where(first, far, own)
    else:
        dv_out, refs = refs[-1], refs[:-1]
    wqk, wv, wo, dy, dqk, do, acc, sems = refs
    s, c = idx[plan.side_at()], idx[plan.core_at()]
    start_att(plan, layer, idx, chunks, wqk, wv, wo, sems)
    zero = jnp.zeros((1, d_), F32)
    sb3 = zero
    for i in range(0, t_, STEP):
        sl = slice(i, i + STEP)
        x, inv = unit_rows(r[sl, :])
        dn = dc_a[sl, :].astype(F32) + dc_b[sl, :].astype(F32)
        dd = e[sl, :].astype(F32) + norm_back(dn, x, inv, prm[layer, 1:2, :])
        dr[sl, :] = dd
        dyb = dd.astype(BF)
        dy[sl, :] = dyb
        sb3 = sb3 + row_sum(dyb.astype(F32))
    wait_all(wo, sems.at[2])
    do[...] = dot_nt(dy[...], wo[...]).astype(BF)
    lanes = h_ // plan.pairs
    low = pair_mask(sq, lanes)
    scale = (lanes // 2) ** -0.5
    for s_ in range(plan.seqs):
        for j in range(plan.pairs):
            rws, cls = slice(s_ * sq, (s_ + 1) * sq), slice(j * lanes, (j + 1) * lanes)
            kcls = slice(h_ + j * lanes, h_ + (j + 1) * lanes)
            q2 = stack_pair(q[rws, cls], low)
            do2 = stack_pair(do[rws, cls], low)
            pr = p[s_ * plan.pairs + j]
            dp = dot_nt(do2, v[rws, cls])
            dv = dot_tn(pr, do2)
            if layer == 0:
                dv = dv + extra[rws, cls].astype(F32) * (s == 1).astype(F32)
            dv_out[rws, cls] = dv.astype(BF)
            pf = pr.astype(F32)
            ds = (pf * (dp - jnp.sum(pf * dp, axis=-1, keepdims=True))).astype(BF)
            dq2 = dot(ds, k[rws, cls])
            dqk[rws, cls] = (jnp.where(low, dq2[:sq], dq2[sq:]) * scale).astype(BF)
            dqk[rws, kcls] = (dot_tn(ds, q2) * scale).astype(BF)
    wait_all(wqk, sems.at[0])
    wait_all(wv, sems.at[1])
    da = dot_nt(dqk[...], wqk[...])
    dav = dot_nt(dv_out[...], wv[...])
    if layer == 1:
        dav = dav * (s == 0).astype(F32)
    acc[...] = da + dav
    dys = pl.ds(pl.multiple_of(s * h_, 128), h_)
    for core in range(2):

        @pl.when(c == core)
        def _():
            one, two = (keep, send) if core == 0 else (send, keep)
            one[...] = dqk[...]
            two[:, :h_] = dv_out[...]
            two[:, h_:] = dy[:, dys]

    sg0, sb0 = zero, zero
    for i in range(0, t_, STEP):
        sl = slice(i, i + STEP)
        dn = acc[sl, :]
        part[sl, :] = dn.astype(BF)
        x, _ = unit_rows(h[sl, :].astype(F32))
        sg0 = sg0 + row_sum(dn * x)
        sb0 = sb0 + row_sum(dn)
    sums[0:1, :], sums[1:2, :], sums[2:3, :] = sg0, sb0, 0.5 * sb3
    sq_ = row_sum(dqk[...].astype(F32))[:, :h_]
    none = jnp.zeros((1, h_), F32)
    sums[3:4, :] = jnp.where(s == 0, jnp.concatenate([sq_, none], axis=1), jnp.concatenate([none, sq_], axis=1))
    sums[4:5, :] = jnp.concatenate([row_sum(dv_out[...].astype(F32)), none], axis=1)


def g1_kernel(plan, layer, *refs):
    r_, h_, d_, n_ = plan.rows, plan.half, plan.width, plan.count
    idx, a, a_sib, oo, oo_sib, keep, got = refs[:7]
    refs = refs[7:]
    if layer == 0:
        tiny, refs = refs[:6], refs[6:]
    outs, refs = refs[:4], refs[4:]
    if layer == 0:
        gatt, tail, osem, tsem = refs
    else:
        gatt, osem = refs
    c = idx[plan.core_at()]

    @pl.when(c == 0)
    def _():
        gatt[...] = (dot_tn(a[...], keep[...]) + dot_tn(a_sib[...], got[...])).astype(BF)

    @pl.when(c == 1)
    def _():
        gatt[:, :h_] = (dot_tn(a[...], keep[:, :h_]) + dot_tn(a_sib[...], got[:, :h_])).astype(BF)
        gatt[:, h_:] = (dot_tn(oo[...], keep[:, h_:]) + dot_tn(oo_sib[...], got[:, h_:])).astype(BF)

    def pick_att(t, sh, dst, sem):
        dma(gatt.at[pl.ds(pl.multiple_of(sh * r_, 16), r_), pl.ds(t * h_, h_)], dst, sem).start()

    put_blocks(plan, idx, outs, osem, pick_att, 0)
    if layer == 0:
        small_sums(plan, idx, tiny, tail)
        half = n_ // 2
        for part, rng in ((0, range(half, n_)), (1, range(half))):
            for j in rng:
                dma(tail.at[j], outs[2 * part].at[j % half, pl.ds(r_, TAIL), :], tsem.at[part]).start()
        for part in range(2):
            wait_all(tail.at[pl.ds(0, half)], tsem.at[part])
        for i in range(4):
            ref = outs[i] if i % 2 else outs[i].at[:, pl.ds(0, r_), :]
            wait_all(ref, osem.at[i])
    else:
        wait_blocks(outs, osem)


def small_sums(plan, idx, tiny, tail):
    n_, r_, h_, d_, u_ = plan.count, plan.rows, plan.half, plan.width, plan.unit
    s = idx[plan.side_at()]
    rows = []
    for l in range(2):
        s2, s1, sbf = tiny[3 * l : 3 * l + 3]
        rows += [s1[0:1], s2[0:1], s1[1:2], s2[1:2], s1[3:4], s1[2:3], s2[2:3]]
        bf = sbf[...]
        cut = [jnp.concatenate([bf[:, sh * u_ + i * r_ : sh * u_ + (i + 1) * r_] for sh in range(n_)], axis=1) for i in range(2)]
        for side in range(2):
            on = (s == side).astype(F32)
            rows += [cut[0] * on, cut[1] * on]
    v1, v2 = tiny[1][4:5, :h_], tiny[4][4:5, :h_]
    first = (s == 0).astype(F32)
    vals = jnp.concatenate([v1 * first, v1 * (1.0 - first), v2 * first], axis=1)
    each = plan.values // n_
    pad = jnp.zeros((1, 2 * r_ - each), F32)
    rows.append(jnp.concatenate([vals[:, sh * each : sh * each + r_] for sh in range(n_)], axis=1))
    rows.append(jnp.concatenate([x for sh in range(n_) for x in (vals[:, sh * each + r_ : (sh + 1) * each], pad)], axis=1))
    rows.append(jnp.zeros((TAIL - 24, d_), F32))
    full = jnp.concatenate(rows, axis=0).astype(BF)
    for sh in range(n_):
        block = jnp.concatenate([full[:, sh * r_ : (sh + 1) * r_], jnp.zeros((TAIL, h_ - r_), BF)], axis=1)
        tail[idx[2 * n_ + sh]] = block


def add_kernel(*refs):
    n = len(refs) // 2 - 1
    for t in range(2):
        x = refs[t][0].astype(F32)
        for i in range(1, n):
            x = x + refs[2 * i + t][0].astype(F32)
        refs[2 * n + t][0] = x.astype(BF)


def run_add(pairs, low, top):
    ins = [(x, pl.BlockSpec((1,) + x.shape[1:], lambda j: (low + j, 0, 0))) for pair in pairs for x in pair]
    return pl.pallas_call(
        add_kernel,
        grid=(top - low,),
        out_shape=[jax.ShapeDtypeStruct((top - low,) + x.shape[1:], BF) for x in pairs[0]],
        in_specs=[sp for _, sp in ins],
        out_specs=[pl.BlockSpec((1,) + x.shape[1:], lambda j: (j, 0, 0)) for x in pairs[0]],
        compiler_params=pltpu.CompilerParams(vmem_limit_bytes=VMEM_BYTES),
        cost_estimate=pl.CostEstimate(flops=int(2.0 * 4.2e8), bytes_accessed=1000, transcendentals=0),
    )(*[x for x, _ in ins])


def pick_kernel(plan, counts, idx, *refs):
    ins, (own, send) = list(refs[:-2]), refs[-2:]
    first = idx[plan.side_at()] == 0
    sums = []
    for n in counts:
        pairs, ins = ins[: 2 * n], ins[2 * n :]
        sums.append([sum(pairs[2 * i + t][0].astype(F32) for i in range(n)).astype(BF) for t in range(2)])
    one, two = sums
    size = two[0].shape[0]
    for t in range(2):
        x, y = one[t][:size], two[t]
        own[t * size : (t + 1) * size] = jnp.where(first, x, y)
        send[t * size : (t + 1) * size] = jnp.where(first, y, x)
    if one[0].shape[0] > size:
        for ref in (own, send):
            ref[2 * size :] = one[0]


def run_pick(plan, idx, sums):
    ins = [x for pairs in sums for pair in pairs for x in pair]
    one, two = sums[0][0][0].shape[1], sums[0][0][1].shape[1]
    shape = (2 * two + (one if one > two else 0), plan.half)
    return pl.pallas_call(
        functools.partial(pick_kernel, plan, [len(pairs) for pairs in sums]),
        grid=(1,),
        out_shape=[jax.ShapeDtypeStruct(shape, BF)] * 2,
        in_specs=[SM] + [pl.BlockSpec((1,) + x.shape[1:], lambda j: (0, 0, 0)) for x in ins],
        out_specs=[pl.BlockSpec(shape, lambda j: (0, 0))] * 2,
        compiler_params=pltpu.CompilerParams(vmem_limit_bytes=VMEM_BYTES),
        cost_estimate=pl.CostEstimate(flops=int(2.0 * 4.2e8), bytes_accessed=1000, transcendentals=0),
    )(idx, *ins)


def finish_kernel(plan, *refs):
    r_, h_, d_, u_ = plan.rows, plan.half, plan.width, plan.unit
    idx, att, mlp, val = refs[0], refs[1:5], refs[5:9], refs[9:11]
    o_qk, o_val, o_out, o_fc, o_proj, o_gain, o_shift, o_bf, o_vs = refs[11:20]
    b_att, b_mlp, vals, sems = refs[20:]
    s, c = idx[plan.side_at()], idx[plan.core_at()]
    for i in range(4):
        side = s if i < 2 else 1 - s
        core = c if i % 2 == 0 else 1 - c
        dma(mlp[i], b_mlp.at[side, core], sems.at[1]).start()
        dma(att[i], b_att.at[side, core], sems.at[0]).start()
    for core in range(2):

        @pl.when(c == core)
        def _():
            dma(val[1 - core].at[pl.ds(0, r_), :], vals, sems.at[2]).start()

    wait_all(b_mlp, sems.at[1])
    per = h_ // u_
    for side in range(2):
        for t in range(2):
            for core in range(2):
                lo = side * 2 * r_ + t * r_
                o_proj[lo : lo + r_, core * h_ : (core + 1) * h_] = b_mlp[side, core, (2 * t + 1) * r_ : (2 * t + 2) * r_].astype(F32)
    for core in range(2):
        for t in range(2):
            q = 2 * core + t
            b0, b1 = (b_mlp[side, core, 2 * t * r_ : (2 * t + 1) * r_].astype(F32) for side in range(2))
            pieces = [x[:, i * u_ : (i + 1) * u_] for i in range(per) for x in (b0, b1)]
            o_fc[:, 2 * q * h_ : 2 * (q + 1) * h_] = jnp.concatenate(pieces, axis=1)
    wait_all(b_att, sems.at[0])
    wait_all(vals, sems.at[2])
    sm = sum(b_att[side, core, 3 * r_ :, :r_].astype(F32) for side in range(2) for core in range(2))
    mine = jnp.where(s == 0, sm[:11], sm[11:22])
    o_gain[...] = mine[0:2]
    o_shift[...] = mine[2:7]
    o_bf[...] = jnp.concatenate([mine[7 + i : 8 + i] for i in range(4)], axis=1)
    o_vs[...] = jnp.concatenate([sm[22:23], sm[23:24, : plan.values // plan.count - r_]], axis=1)
    low, high = b_att[0, 1, :r_].astype(F32), b_att[1, 1, :r_].astype(F32)
    other, rest = vals[...].astype(F32), b_att[0, 1, 2 * r_ : 3 * r_].astype(F32)
    o_val[:, :h_] = jnp.where(s == 0, low, rest)
    o_val[:, h_:d_] = jnp.where(s == 0, high, other)
    o_val[:, d_:] = jnp.where(s == 0, other, low)
    for side in range(2):
        o_out[:, side * h_ : (side + 1) * h_] = b_att[side, 1, r_ : 2 * r_].astype(F32)
        for t in range(2):
            o_qk[:, t * d_ + side * h_ : t * d_ + (side + 1) * h_] = b_att[side, 0, t * r_ : (t + 1) * r_].astype(F32)


def ends_kernel(plan, idx, prm, r, y_a, y_b, dr, da_a, da_b, h, out):
    s = idx[plan.side_at()]

    @pl.when(s == 1)
    def _():
        for i in range(0, plan.tokens, STEP):
            sl = slice(i, i + STEP)
            out[sl, :] = (r[sl, :] + (y_a[sl, :].astype(F32) + y_b[sl, :].astype(F32)) + prm[1, 6:7, :]).astype(BF)

    @pl.when(s == 0)
    def _():
        for i in range(0, plan.tokens, STEP):
            sl = slice(i, i + STEP)
            x, inv = unit_rows(h[sl, :].astype(F32))
            dn = da_a[sl, :].astype(F32) + da_b[sl, :].astype(F32)
            out[sl, :] = (dr[sl, :] + norm_back(dn, x, inv, prm[0, 0:1, :])).astype(BF)


VM = pl.BlockSpec(memory_space=pltpu.VMEM)
SM = pl.BlockSpec(memory_space=pltpu.SMEM)
ANY = pl.BlockSpec(memory_space=pl.ANY)


def call(kernel, ins, outs, scratch, us):
    return pl.pallas_call(
        kernel,
        out_shape=[jax.ShapeDtypeStruct(sh, dt) for sh, dt, _ in outs],
        in_specs=[sp for _, sp in ins],
        out_specs=[sp for _, _, sp in outs],
        scratch_shapes=scratch,
        compiler_params=pltpu.CompilerParams(vmem_limit_bytes=VMEM_BYTES),
        cost_estimate=pl.CostEstimate(flops=int(us * 4.2e8), bytes_accessed=1000, transcendentals=0),
    )(*[x for x, _ in ins])


def vm(*arrays):
    return [(x, VM) for x in arrays]


def hbm(arrays):
    return [(x, ANY) for x in arrays]


def att_scratch(plan):
    w, h = plan.width, plan.half
    return [pltpu.VMEM((w, w), BF), pltpu.VMEM((w, h), BF), pltpu.VMEM((h, w), BF)]


def mlp_scratch(plan):
    return [pltpu.VMEM((plan.width, plan.fh), BF), pltpu.VMEM((plan.fh, plan.width), BF)]


def dma_sems(n):
    return pltpu.SemaphoreType.DMA((n,))


def run_pack(plan, idx, arrays):
    r_, h_ = plan.rows, plan.half
    both, one = ((2, 3 * r_, h_), BF, VM), ((r_, h_), BF, VM)
    outs = [both, both, one, one, ((1, SMALL, h_), BF, VM)]
    return call(functools.partial(pack_kernel, plan), [(idx, SM)] + vm(*arrays), outs, [], 2.5)


def run_param(plan, idx, arrays):
    outs = [((2, 8, plan.width), F32, VM), ((2, 1, plan.fh), F32, VM)]
    scratch = [pltpu.VMEM((2, plan.count, SMALL, plan.half), BF), dma_sems(4)]
    return call(functools.partial(param_kernel, plan), [(idx, SM)] + hbm(arrays), outs, scratch, 2.3)


def run_f1(plan, layer, idx, prm, inputs, chunks):
    t_, h_, d_ = plan.tokens, plan.half, plan.width
    narrow, wide = ((t_, h_), BF, VM), ((t_, d_), BF, VM)
    outs = [wide, narrow, narrow, narrow, ((plan.seqs * plan.pairs, 2 * plan.seq, plan.seq), BF, VM), narrow, wide]
    outs += [wide] if layer else [wide, wide]
    scratch = att_scratch(plan) + [dma_sems(3)]
    ins = [(idx, SM)] + vm(prm, *inputs) + hbm(chunks)
    return call(functools.partial(f1_kernel, plan, layer), ins, outs, scratch, 5.5)


def run_f2(plan, layer, idx, prm, bf, h, pa, pb, chunks):
    t_, d_, f_ = plan.tokens, plan.width, plan.fh
    wide = ((t_, d_), BF, VM)
    outs = [wide, ((t_, d_), F32, VM), ((t_, f_ + d_), BF, VM), ((t_, f_), BF, VM)]
    scratch = mlp_scratch(plan) + [pltpu.VMEM((t_, f_ // 3), F32), dma_sems(2)]
    ins = [(idx, SM)] + vm(prm, bf, h, pa, pb) + hbm(chunks)
    return call(functools.partial(f2_kernel, plan, layer), ins, outs, scratch, 7.2)


def run_b2(plan, layer, idx, prm, gp, r, more, chunks):
    t_, d_, f_ = plan.tokens, plan.width, plan.fh
    outs = [((t_, d_), BF, VM)] * 4 + [((t_, plan.half), BF, VM), ((3, d_), F32, VM), ((1, f_), F32, VM)]
    scratch = mlp_scratch(plan) + [pltpu.VMEM((t_, d_), F32), pltpu.VMEM((t_, f_), BF), dma_sems(2)]
    ins = [(idx, SM)] + vm(prm, gp, r, *more) + hbm(chunks)
    return call(functools.partial(b2_kernel, plan, layer), ins, outs, scratch, 6.7)


def grad_outs(plan, rows, tail=0):
    return [((plan.count // 2, r, plan.half), BF, ANY) for r in (rows + tail, rows) * 2]


def run_g2(plan, idx, *arrays):
    d_, f_, h_ = plan.width, plan.fh, plan.half
    scratch = [pltpu.VMEM((d_, d_), BF), pltpu.VMEM((f_, h_), BF), dma_sems(4)]
    ins = [(idx, SM)] + vm(*arrays)
    return call(functools.partial(g2_kernel, plan), ins, grad_outs(plan, 2 * plan.rows), scratch, 4.5)


def run_b1(plan, layer, idx, prm, more, chunks):
    t_, d_, h_ = plan.tokens, plan.width, plan.half
    wide, narrow = (t_, d_), (t_, h_)
    outs = [(wide, BF, VM), (wide, F32, VM), (wide, BF, VM), (wide, BF, VM), ((5, d_), F32, VM)]
    scratch = att_scratch(plan) + [pltpu.VMEM(wide, BF), pltpu.VMEM(wide, BF), pltpu.VMEM(narrow, BF), pltpu.VMEM(wide, F32), dma_sems(3)]
    if layer:
        outs += [(narrow, BF, VM), (wide, BF, VM), (wide, BF, VM)]
    else:
        scratch.append(pltpu.VMEM(narrow, BF))
    ins = [(idx, SM)] + vm(prm, *more) + hbm(chunks)
    return call(functools.partial(b1_kernel, plan, layer), ins, outs, scratch, 7.5)


def run_g1(plan, layer, idx, a, a_sib, oo, oo_sib, keep, got, tiny):
    d_, h_ = plan.width, plan.half
    scratch = [pltpu.VMEM((d_, d_), BF)]
    if layer == 0:
        scratch += [pltpu.VMEM((plan.count, TAIL, h_), BF), dma_sems(4), dma_sems(2)]
    else:
        scratch += [dma_sems(4)]
    ins = [(idx, SM)] + vm(a, a_sib, oo, oo_sib, keep, got, *tiny)
    return call(functools.partial(g1_kernel, plan, layer), ins, grad_outs(plan, plan.rows, 0 if layer else TAIL), scratch, 3.5)


def run_finish(plan, idx, arrays):
    r_, h_, d_, n_ = plan.rows, plan.half, plan.width, plan.count
    outs = [(sh, F32, VM) for sh in ((r_, 2 * d_), (r_, plan.values), (r_, d_), (r_, plan.ff), (4 * r_, d_), (2, r_), (5, r_), (1, 4 * r_), (1, plan.values // n_))]
    scratch = [pltpu.VMEM((2, 2, 3 * r_ + TAIL, h_), BF), pltpu.VMEM((2, 2, 4 * r_, h_), BF), pltpu.VMEM((r_, h_), BF), dma_sems(3)]
    return call(functools.partial(finish_kernel, plan), [(idx, SM)] + hbm(arrays), outs, scratch, 4.5)


def run_ends(plan, idx, arrays):
    return call(functools.partial(ends_kernel, plan), [(idx, SM)] + vm(*arrays), [((plan.tokens, plan.width), BF, VM)], [], 2.5)[0]


def after(x, *earlier):
    return lax.optimization_barrier((x,) + earlier)[0]


def per_device(ends, w_qk, w_value, w_out, w_fc, w_proj, gains, shifts, fc_shift, value_shift):
    s, grp, d = lax.axis_index("section"), lax.axis_index("group"), lax.axis_index("dp")
    c = grp % 2
    count, groups = lax.axis_size("dp"), lax.axis_size("group")
    rows, width = w_qk.shape[1], ends.shape[3]
    half = width // 2
    seqs, seq = ends.shape[1], ends.shape[2]
    tokens = seqs * seq
    plan = Plan(count, rows, width, w_fc.shape[2], w_value.shape[1], tokens, seq, HEADS // 2)
    table = plan.table(groups)
    idx = lax.dynamic_slice(jnp.asarray(table), (s, grp, d, 0), (1, 1, 1, table.shape[3])).reshape(-1)
    first, even = s == 0, d % 2 == 0

    def swap_x(x):
        return lax.ppermute(x, "section", [(0, 1), (1, 0)])

    def swap_c(x):
        return lax.ppermute(x, "group", [(i, i ^ 1) for i in range(groups)])

    def swap_d(x, bit):
        return lax.ppermute(x, "dp", [(i, i ^ bit) for i in range(count)])

    hc = count // 2
    spread = [
        [(l * count + i, (i // hc) * count + 2 * (i % hc) + (l if w == 0 else 1 - l)) for l in range(2) for i in range(count)]
        for w in range(2)
    ]
    mine, send, o_lo, o_hi, small = run_pack(
        plan, idx, (w_qk[0], w_fc[0], w_proj[0], w_out[0], gains[0], shifts[0], fc_shift, value_shift[None])
    )
    got = swap_x(send)
    o_a = lax.ppermute(o_lo, ("section", "dp"), spread[0])
    o_b = lax.ppermute(o_hi, ("section", "dp"), spread[1])
    ends_own = ends[0].reshape(tokens, width)
    ends_got = swap_x(after(ends_own, got))
    v_side = (lax.dynamic_slice_in_dim(w_value, s * half, half, 1), w_value[:, width:])
    o_side = (jnp.where(even, o_a, o_b), jnp.where(even, o_b, o_a))

    def head(t, l, other):
        x = jnp.where(first if l == 0 else ~first, mine[t, :rows], got[t, :rows])
        return jnp.where(c == 0, x, other)

    early = []
    for t, side in ((0, v_side), (1, o_side)):
        x, y = mine[t, rows:], got[t, rows:]
        blocks = [head(t, 0, side[0]), jnp.where(first, x, y), head(t, 1, side[1]), jnp.where(first, y, x)]
        early.append(jnp.concatenate(blocks, axis=0))

    routes = [[(a, b) for a, b in zip(order, order[1:] + order[:1])] for order in (ring_order(count), ring_order(count)[::-1])]

    def ring(x):
        return lax.optimization_barrier([lax.ppermute(x[t], "dp", routes[t]) for t in range(2)])

    def with_sibling(steps):
        return [y for t in range(2) for y in [x[t] for x in steps] + [swap_c(x[t]) for x in steps]]

    have = small
    for k in range(plan.bits):
        came = swap_d(have, plan.orders[0][k])
        if k < plan.bits - 1:
            have = jnp.concatenate([have, came], axis=0)
    prm, bf = run_param(plan, idx, [have, came, swap_x(have), swap_x(came)])

    steps = [[after(x, came) for x in early]]
    for n in range(count - 1):
        steps.append(ring(steps[-1]))
        if n == 1:
            steps[-1] = [after(x, ends_got) for x in steps[-1]]
        if n == 0:
            steps[-1] = [after(x, prm) for x in steps[-1]]
    chunks = with_sibling(steps)

    part, q0, k0, v0, p0, o0, a0, h0, cot = run_f1(plan, 0, idx, prm, (ends_own, ends_got), chunks)
    got = swap_x(part)
    o0_far = swap_x(after(o0, got))
    part, r0, ucn0, gp0 = run_f2(plan, 0, idx, prm, bf, h0, part, got, chunks)
    got = swap_x(after(part, o0_far))
    part, q1, k1, v1, p1, o1, a1, h1 = run_f1(plan, 1, idx, prm, (r0, part, got, v0), chunks)
    got = swap_x(part)
    o1_far = swap_x(after(o1, got))
    y_part, r1, ucn1, gp1 = run_f2(plan, 1, idx, prm, bf, h1, part, got, chunks)

    class Sum:
        def __init__(self, g):
            self.out, self.parts = list(g[:2]), [list(g[2:])]
            self.top = count // 2

        def load(self, *others):
            if others:
                self.parts[-1] = [after(x, *others) for x in self.parts[-1]]
            low = self.top // 2
            self.out = run_add(self.parts, low, self.top)
            self.top = low
            return self.out

        def send(self):
            k = plan.bits - len(self.parts)
            self.parts.append([swap_d(self.out[t], plan.orders[t][k]) for t in range(2)])
            return self.parts[-1]

    def over_pairs(x):
        total = x
        for n in range(1, groups // 2):
            total = total + lax.ppermute(x, "group", [(i, (i + 2 * n) % groups) for i in range(groups)])
        return total

    part, e, z_keep, z_send, e_send, s2_1, sbf_1 = run_b2(plan, 1, idx, prm, gp1, r1, (cot,), chunks)
    got = swap_x(after(part, o1_far))
    g_mlp1 = run_g2(plan, idx, ucn1, swap_c(ucn1), e, swap_c(e_send), z_keep, swap_c(z_send))
    mlp1 = Sum(g_mlp1)
    got = after(got, *mlp1.out)
    came = mlp1.send()
    part, dr, keep, send, s1_1, dv1, oo0, oo1 = run_b1(
        plan, 1, idx, prm, (cot, part, got, r1, h1, q1, k1, v1, p1, o0, o0_far, o1, o1_far), chunks
    )
    y_got = swap_x(after(y_part, got))
    got = swap_x(part)
    g_att1 = run_g1(plan, 1, idx, after(a1, y_got, *came), swap_c(a1), oo1, swap_c(oo1), keep, swap_c(send), ())
    att1 = Sum(g_att1)
    got = after(got, *att1.out, *mlp1.load())
    came = mlp1.send() + att1.send()
    part, e, z_keep, z_send, e_send, s2_0, sbf_0 = run_b2(plan, 0, idx, prm, gp0, r0, (dr, part, got, h1), chunks)
    got = swap_x(after(part, *came))
    g_mlp0 = run_g2(plan, idx, ucn0, swap_c(ucn0), e, swap_c(e_send), z_keep, swap_c(z_send))
    mlp0 = Sum(g_mlp0)
    got = after(got, *mlp0.out, *mlp1.load())
    mlp0.send()
    came = mlp1.send()
    part, dr, keep, send, s1_0 = run_b1(plan, 0, idx, prm, (e, part, got, r0, h0, q0, k0, v0, p0, dv1), chunks)
    x_got = swap_x(part)
    g_att0 = run_g1(plan, 0, idx, a0, swap_c(a0), oo0, swap_c(oo0), keep, swap_c(send), (s2_0, s1_0, sbf_0, s2_1, s1_1, sbf_1))
    att1.load(part)
    att1.send()
    att0 = Sum(g_att0)
    att0.send()
    mlp0.load(g_att0[0], *came)
    mlp0.send()
    mlp0.load(x_got)
    mlp0.send()
    att1.load()
    att1.send()
    att0.load()
    att0.send()
    att0.load()
    att0.send()

    def ending(*sums):
        own, send = (over_pairs(x) for x in run_pick(plan, idx, [x.parts for x in sums]))
        far = swap_x(send)
        return [own, swap_c(own), far, swap_c(far)], send

    e_mlp, _ = ending(mlp0, mlp1)
    e_att, sent = ending(att0, att1)
    o_qk, o_val, o_out, o_fc, o_proj, o_gain, o_shift, o_bf, o_vs = run_finish(plan, idx, e_att + e_mlp + [sent, swap_c(sent)])

    res = run_ends(plan, idx, (prm, r1, y_part, y_got, dr, part, x_got, h0)).reshape(1, seqs, seq, width)
    return (res, o_qk[None], o_val, o_out[None], o_fc[None], o_proj[None], o_gain[None], o_shift[None], o_bf, o_vs[0])


def solution(mesh):
    placed = (
        P("section", ("group", "dp"), None, None),
        P("section", "dp", None),
        P("dp", None),
        P("section", "dp", None),
        P("section", "dp", None),
        P("section", "dp", None),
        P("section", None, "dp"),
        P("section", None, "dp"),
        P("section", "dp"),
        P("dp"),
    )
    return jax.shard_map(per_device, mesh=mesh, in_specs=placed, out_specs=placed, check_vma=False)
```

```python
import functools

import jax
import jax.numpy as jnp
import numpy as np
from jax import lax
from jax.experimental import pallas as pl
from jax.experimental.pallas import tpu as pltpu
from jax.sharding import PartitionSpec as P

HEADS = 12
BF = jnp.bfloat16
F32 = jnp.float32
norm_eps = 1e-05
masked_score = -1e30
TAIL = 32
SMALL = 16
STEP = 32
VMEM_BYTES = 16 * 1024 * 1024


def dot(a, b):
    return jnp.dot(a, b, preferred_element_type=F32)


def dot_tn(a, b):
    return lax.dot_general(a, b, (((0,), (0,)), ((), ())), preferred_element_type=F32)


def dot_nt(a, b):
    return lax.dot_general(a, b, (((1,), (1,)), ((), ())), preferred_element_type=F32)


def unit_rows(v):
    centered = v - jnp.mean(v, axis=-1, keepdims=True)
    inv = lax.rsqrt(jnp.mean(centered * centered, axis=-1, keepdims=True) + norm_eps)
    return centered * inv, inv


def norm_back(dn, x, inv, gain):
    scaled = dn * gain
    inner = jnp.mean(scaled * x, axis=-1, keepdims=True)
    return inv * (scaled - jnp.mean(scaled, axis=-1, keepdims=True) - x * inner)


def row_sum(v):
    return jnp.sum(v, axis=0, keepdims=True)


def ring_order(count):
    wide = 2 if count < 16 else 4
    tall = count // wide
    order = [i * wide for i in range(tall)]
    for n, row in enumerate(reversed(range(tall))):
        cols = range(1, wide)
        order += [row * wide + col for col in (cols if n % 2 == 0 else reversed(cols))]
    return order


class Plan:
    def __init__(self, count, rows, width, ff, values, tokens, seq, heads):
        self.count, self.rows, self.width, self.half = count, rows, width, width // 2
        self.ff, self.fh, self.unit, self.values = ff, ff // 2, ff // count // 2, values
        self.tokens, self.seq, self.seqs = tokens, seq, tokens // seq
        self.pairs = heads // 2
        self.bits = count.bit_length() - 1
        down = [1 << i for i in reversed(range(self.bits))]
        other = down[:-2] + [down[-1], down[-2]]
        self.orders = (down, other)
        self.masks = []
        for order in self.orders:
            mask = [0] * count
            for j in range(count):
                for k, bit in enumerate(order):
                    if j >> k & 1:
                        mask[j] ^= bit
            self.masks.append(mask)

    def core_at(self):
        return 7 * self.count

    def side_at(self):
        return 7 * self.count + 1

    def table(self, groups):
        n = self.count
        out = np.zeros((2, groups, n, 7 * n + 2), np.int32)
        order = ring_order(n)
        for p, d in enumerate(order):
            for t in range(2):
                out[:, :, d, t * n : (t + 1) * n] = [d ^ m for m in self.masks[t]]
                out[:, :, d, (3 + t) * n : (4 + t) * n] = [order[(p - (1 - 2 * t) * j) % n] for j in range(n)]
            for j, m in enumerate(self.masks[0]):
                out[:, :, d, 2 * n + (d ^ m)] = j
            for j in range(n):
                for t in range(2):
                    out[:, :, d, (5 + t) * n + order[(p - (1 - 2 * t) * j) % n]] = j
        out[:, :, :, 7 * n] = (np.arange(groups) % 2)[None, :, None]
        out[:, :, :, 7 * n + 1] = np.arange(2)[:, None, None]
        return out


def aligned(x, size):
    return x if isinstance(x, int) else pl.multiple_of(x, size)


def dma(src, dst, sem):
    return pltpu.make_async_copy(src, dst, sem)


def wait_all(ref, sem):
    dma(ref, ref, sem).wait()


def chunk_refs(plan, idx, chunks, row):
    for j in range(plan.count):
        for t in range(2):
            for other in range(2):
                ref = chunks[(t * 2 + other) * plan.count + j]
                yield t, other, idx[(3 + t) * plan.count + j], ref.at[pl.ds(row, plan.rows), :]


def place_att(plan, layer, idx, chunks, wqk, wv, wo):
    r_, h_ = plan.rows, plan.half
    c = idx[plan.core_at()]
    for t, other, sh, src in chunk_refs(plan, idx, chunks, 3 * r_ * layer):
        core = 1 - c if other else c
        row = pl.multiple_of(sh * r_, 16)

        @pl.when(core == 0)
        def _():
            wqk[pl.ds(row, r_), t * h_ : (t + 1) * h_] = src[...]

        @pl.when(core == 1)
        def _():
            if t == 0:
                wv[pl.ds(row, r_), :] = src[...]
            else:
                orow = pl.multiple_of((sh // 2) * r_, 16)
                ocol = pl.multiple_of((sh % 2) * h_, 128)
                wo[pl.ds(orow, r_), pl.ds(ocol, h_)] = src[...]


def place_mlp(plan, layer, idx, chunks, wfc, wproj):
    r_, h_ = plan.rows, plan.half
    c = idx[plan.core_at()]
    for kind in range(1 if layer else 2):
        for t, other, sh, src in chunk_refs(plan, idx, chunks, ((4 if layer else 1) + kind) * r_):
            core = 1 - c if other else c
            if kind == 0:
                row = pl.multiple_of(sh * r_, 16)
                col = pl.multiple_of((2 * core + t) * h_, 128)
                wfc[pl.ds(row, r_), pl.ds(col, h_)] = src[...]
            else:
                row = pl.multiple_of(sh * 2 * r_ + t * r_, 16)
                col = pl.multiple_of(core * h_, 128)
                wproj[pl.ds(row, r_), pl.ds(col, h_)] = src[...]


def put_blocks(plan, idx, outs, pick, row0):
    n_, r_ = plan.count, plan.rows
    half = n_ // 2
    for j in reversed(range(n_)):
        for t in range(2):
            out = outs[2 * (0 if j >= half else 1) + t]
            at = j % half * (out.shape[0] // half) + row0
            out[at : at + r_, :] = pick(t, idx[t * n_ + j])


def pack_kernel(plan, idx, *refs):
    from_hbm, (mine, send, o_a, o_b, small), here, sems = refs[:8], refs[8:13], refs[13:21], refs[21]
    for i, ref in enumerate(here):
        dma(from_hbm[i], ref, sems.at[i]).start()
    for i, ref in enumerate(here):
        wait_all(ref, sems.at[i])
    wqk, wfc, wproj, wout, gains, shifts, fc_shift, v_shift = here
    r_, h_, d_, u_ = plan.rows, plan.half, plan.width, plan.unit
    per = h_ // u_
    s, c = idx[plan.side_at()], idx[plan.core_at()]
    lo, hi = wout[:, :h_], wout[:, h_:]
    o_a[...] = jnp.where(s == 0, lo, hi)
    o_b[...] = jnp.where(s == 0, hi, lo)
    rows = [gains[...], shifts[...]] + [fc_shift[:, i * r_ : (i + 1) * r_] for i in range(4)] + [v_shift[:, :r_]]
    more = v_shift.shape[1] - r_
    rows.append(jnp.concatenate([v_shift[:, r_:], jnp.zeros((1, r_ - more), BF)], axis=1))
    rows = jnp.concatenate([x.astype(F32) for x in rows] + [jnp.zeros((SMALL - 13, r_), F32)], axis=0)
    small[...] = jnp.concatenate([rows, jnp.zeros((SMALL, h_ - r_), F32)], axis=1).astype(BF)
    for side in range(2):
        for core in range(2):
            for keep in range(2):
                out = mine if keep else send

                @pl.when(jnp.logical_and(c == core, s == (side if keep else 1 - side)))
                def _():
                    for t in range(2):
                        lo = t * d_ + side * h_
                        out[t, :r_] = wqk[:, lo : lo + h_]
                        q = 2 * core + t
                        cols = [(q * per + i) * 2 * u_ + side * u_ for i in range(per)]
                        out[t, r_ : 2 * r_] = jnp.concatenate([wfc[:, x : x + u_] for x in cols], axis=1)
                        row = side * 2 * r_ + t * r_
                        out[t, 2 * r_ :] = wproj[row : row + r_, core * h_ : (core + 1) * h_]


def param_kernel(plan, idx, *refs):
    n_, r_, h_, d_ = plan.count, plan.rows, plan.half, plan.width
    s = idx[plan.side_at()]
    steps, (prm, bf, stack) = refs[: 2 * n_], refs[2 * n_ :]
    for j, ref in enumerate(steps):
        stack[j // n_, j % n_] = ref[5 * r_ :, :]
    pairs = [[stack[t, idx[(5 + t) * n_ + sh]][:, :r_].astype(F32) for t in range(2)] for sh in range(n_)]
    more = plan.values // n_ - r_
    vals = jnp.concatenate([x for b, _ in pairs for x in (b[11:12, :], b[12:13, :more])], axis=1)
    for l in range(2):
        blocks = [b[l] for b in pairs]
        m = jnp.concatenate([b[:7] for b in blocks], axis=1)
        prm[l, 0:7] = m
        bq = jnp.where(s == 0, m[4:5, :h_], m[4:5, h_:])
        prm[l, 4:5] = jnp.concatenate([bq, jnp.zeros((1, d_ - h_), F32)], axis=1)
        if l == 0:
            bv = jnp.where(s == 0, vals[:, :h_], vals[:, h_:d_])
        else:
            bv = vals[:, d_:]
        prm[l, 7:8] = jnp.concatenate([bv, jnp.zeros((1, d_ - h_), F32)], axis=1)
        sides = []
        for side in range(2):
            row = 7 + 2 * side
            sides.append(jnp.concatenate([b[row + i : row + i + 1] for b in blocks for i in range(2)], axis=1))
        bf[l] = jnp.where(s == 0, sides[0], sides[1])


def att_weights_kernel(plan, layer, *refs):
    place_att(plan, layer, refs[0], refs[1:-3], *refs[-3:])


def mlp_weights_kernel(plan, layer, *refs):
    outs = refs[1 + 4 * plan.count :]
    place_mlp(plan, layer, refs[0], refs[1 : 1 + 4 * plan.count], outs[0], outs[-1])


def proj_weights_kernel(plan, *refs):
    n_, r_, h_ = plan.count, plan.rows, plan.half
    idx, parts, wproj = refs[0], refs[1:9], refs[9]
    c = idx[plan.core_at()]
    for t in range(2):
        for other in range(2):
            core = 1 - c if other else c
            for j in range(n_):
                at = j % (n_ // 2) * r_
                row = pl.multiple_of(idx[t * n_ + j] * 2 * r_ + t * r_, 16)
                src = parts[(2 * t + other) * 2 + j // (n_ // 2)]
                wproj[pl.ds(row, r_), pl.ds(pl.multiple_of(core * h_, 128), h_)] = src[at : at + r_, :]


def pair_mask(seq, lanes):
    return lax.broadcasted_iota(jnp.int32, (seq, lanes), 1) < lanes // 2


def stack_pair(x, low):
    zero = jnp.zeros_like(x)
    return jnp.concatenate([jnp.where(low, x, zero), jnp.where(low, zero, x)], axis=0)


def f1_kernel(plan, layer, *refs):
    h_, t_, sq = plan.half, plan.tokens, plan.seq
    idx, prm, refs = refs[0], refs[1], refs[2:]
    if layer == 1:
        r_up, pa, pb, v_old = refs[:4]
        refs = refs[4:]
    else:
        here, there = refs[:2]
        refs = refs[2:]
    weights, refs = refs[:3], refs[3:]
    part, q, k, v, p, o, a, h = refs[:8]
    if layer == 0:
        cot = refs[8]
    wqk, wv, wo = weights
    first = idx[plan.side_at()] == 0
    for i in range(0, t_, STEP):
        sl = slice(i, i + STEP)
        if layer == 1:
            hh = r_up[sl, :] + (pa[sl, :].astype(F32) + pb[sl, :].astype(F32)) + prm[0, 6:7, :]
            h[sl, :] = hh.astype(BF)
        else:
            mine, theirs = here[sl, :], there[sl, :]
            h[sl, :] = jnp.where(first, mine, theirs)
            cot[sl, :] = jnp.where(first, theirs, mine)
        x, _ = unit_rows(h[sl, :].astype(F32))
        a[sl, :] = (x * prm[layer, 0:1, :] + prm[layer, 2:3, :]).astype(BF)
    qk = dot(a[...], wqk[...])
    q[...] = (qk[:, :h_] + prm[layer, 4:5, :h_]).astype(BF)
    k[...] = qk[:, h_:].astype(BF)
    val = (dot(a[...], wv[...]) + prm[layer, 7:8, :h_]).astype(BF)
    if layer == 1:
        val = jnp.where(idx[plan.side_at()] == 1, v_old[...], val)
    v[...] = val
    lanes = h_ // plan.pairs
    low = pair_mask(sq, lanes)
    causal = lax.broadcasted_iota(jnp.int32, (2 * sq, sq), 0) % sq >= lax.broadcasted_iota(jnp.int32, (2 * sq, sq), 1)
    scale = (lanes // 2) ** -0.5
    for s_ in range(plan.seqs):
        for j in range(plan.pairs):
            rws, cls = slice(s_ * sq, (s_ + 1) * sq), slice(j * lanes, (j + 1) * lanes)
            q2 = stack_pair(q[rws, cls], low)
            sc = jnp.where(causal, dot_nt(q2, k[rws, cls]) * scale, masked_score)
            ex = jnp.exp(sc - jnp.max(sc, axis=-1, keepdims=True))
            pr = (ex / jnp.sum(ex, axis=-1, keepdims=True)).astype(BF)
            p[s_ * plan.pairs + j] = pr
            o2 = dot(pr, v[rws, cls])
            o[rws, cls] = jnp.where(low, o2[:sq], o2[sq:]).astype(BF)
    part[...] = dot(o[...], wo[...]).astype(BF)


def f2_kernel(plan, layer, *refs):
    t_ = plan.tokens
    idx, prm, bf, h, pa, pb = refs[:6]
    weights, refs = refs[6:8], refs[8:]
    part, r, ucn, gp, z = refs
    wfc, wproj = weights
    f_ = plan.fh
    for i in range(0, t_, STEP):
        sl = slice(i, i + STEP)
        rr = h[sl, :].astype(F32) + (pa[sl, :].astype(F32) + pb[sl, :].astype(F32)) + prm[layer, 5:6, :]
        r[sl, :] = rr
        x, _ = unit_rows(rr)
        ucn[sl, f_:] = (x * prm[layer, 1:2, :] + prm[layer, 3:4, :]).astype(BF)
    cols = plan.fh // 3
    for j in range(3):
        cs = slice(j * cols, (j + 1) * cols)
        z[...] = dot(ucn[:, f_:], wfc[:, cs])

        def body(i, carry):
            sl = pl.ds(pl.multiple_of(i * STEP, STEP), STEP)
            zz = z[sl, :] + bf[layer, :, cs]
            sq_ = zz * zz
            th = jnp.tanh(0.7978845608 * zz * (1.0 + 0.044715 * sq_))
            hp = 0.5 * (1.0 + th)
            ucn[sl, cs] = (zz * hp).astype(BF)
            slope = 0.7978845608 * (1.0 + 3 * 0.044715 * sq_)
            gp[sl, cs] = (hp + 0.5 * zz * (1.0 - th * th) * slope).astype(BF)
            return carry

        lax.fori_loop(0, t_ // STEP, body, 0)
    part[...] = dot(ucn[:, :f_], wproj[...]).astype(BF)


def b2_kernel(plan, layer, *refs):
    d_, t_, f_ = plan.width, plan.tokens, plan.fh
    idx, prm, gp, r = refs[:4]
    refs = refs[4:]
    if layer == 1:
        e, refs = refs[0], refs[1:]
    else:
        dr, da_a, da_b, h_up = refs[:4]
        refs = refs[4:]
    weights, refs = refs[:2], refs[2:]
    part, e_out, z_keep, z_send, e_send, sums, sbf = refs[:7]
    h_, c = plan.half, idx[plan.core_at()]
    wfc, wproj = weights
    acc, dz = refs[-2:]
    zero = jnp.zeros((1, d_), F32)
    sb4 = zero
    for i in range(0, t_, STEP):
        sl = slice(i, i + STEP)
        if layer == 0:
            x, inv = unit_rows(h_up[sl, :].astype(F32))
            dn = da_a[sl, :].astype(F32) + da_b[sl, :].astype(F32)
            ee = (dr[sl, :] + norm_back(dn, x, inv, prm[1, 0:1, :])).astype(BF)
        else:
            ee = e[sl, :]
        e_out[sl, :] = ee
        sb4 = sb4 + row_sum(ee.astype(F32))
    cols = f_ // 3
    for j in range(3):
        cs = slice(j * cols, (j + 1) * cols)
        dzj = (dot_nt(e_out[...], wproj[cs, :]) * gp[:, cs].astype(F32)).astype(BF)
        dz[:, cs] = dzj
        sbf[:, cs] = row_sum(dzj.astype(F32))
    z_keep[...] = dz[:, pl.ds(pl.multiple_of(c * d_, 128), d_)]
    z_send[...] = dz[:, pl.ds(pl.multiple_of((1 - c) * d_, 128), d_)]
    e_send[...] = e_out[:, pl.ds(pl.multiple_of((1 - c) * h_, 128), h_)]
    acc[...] = dot_nt(dz[...], wfc[...])
    sg1, sb1 = zero, zero
    for i in range(0, t_, STEP):
        sl = slice(i, i + STEP)
        dn = acc[sl, :]
        part[sl, :] = dn.astype(BF)
        x, _ = unit_rows(r[sl, :])
        sg1 = sg1 + row_sum(dn * x)
        sb1 = sb1 + row_sum(dn)
    sums[0:1, :], sums[1:2, :], sums[2:3, :] = sg1, sb1, 0.5 * sb4


def g2_kernel(plan, *refs):
    r_, h_, f_ = plan.rows, plan.half, plan.fh
    idx, ucn, ucn_sib, e, e_sib, dz, dz_sib = refs[:7]
    outs, (gfc, gproj) = refs[7:-2], refs[-2:]
    c = idx[plan.core_at()]
    ecols = pl.ds(pl.multiple_of(c * h_, 128), h_)
    gproj[...] = (dot_tn(ucn[:, :f_], e[:, ecols]) + dot_tn(ucn_sib[:, :f_], e_sib[...])).astype(BF)
    put_blocks(plan, idx, outs, lambda t, sh: gproj[pl.ds(pl.multiple_of(sh * 2 * r_ + t * r_, 16), r_), :], r_)
    gfc[...] = (dot_tn(ucn[:, f_:], dz[...]) + dot_tn(ucn_sib[:, f_:], dz_sib[...])).astype(BF)
    put_blocks(plan, idx, outs, lambda t, sh: gfc[pl.ds(pl.multiple_of(sh * r_, 16), r_), t * h_ : (t + 1) * h_], 0)


def b1_kernel(plan, layer, *refs):
    h_, d_, t_, sq = plan.half, plan.width, plan.tokens, plan.seq
    idx, prm, e, dc_a, dc_b, r, h, q, k, v, p = refs[:11]
    refs = refs[11:]
    if layer == 0:
        extra, refs = refs[0], refs[1:]
    weights, refs = refs[:3], refs[3:]
    part, dr, keep, send, sums = refs[:5]
    refs = refs[5:]
    if layer == 1:
        dv_out, refs = refs[0], refs[1:]
    else:
        dv_out, refs = refs[-1], refs[:-1]
    wqk, wv, wo = weights
    dy, dqk, do, acc = refs
    s, c = idx[plan.side_at()], idx[plan.core_at()]
    zero = jnp.zeros((1, d_), F32)
    sb3 = zero
    for i in range(0, t_, STEP):
        sl = slice(i, i + STEP)
        x, inv = unit_rows(r[sl, :])
        dn = dc_a[sl, :].astype(F32) + dc_b[sl, :].astype(F32)
        dd = e[sl, :].astype(F32) + norm_back(dn, x, inv, prm[layer, 1:2, :])
        dr[sl, :] = dd
        dyb = dd.astype(BF)
        dy[sl, :] = dyb
        sb3 = sb3 + row_sum(dyb.astype(F32))
    do[...] = dot_nt(dy[...], wo[...]).astype(BF)
    lanes = h_ // plan.pairs
    low = pair_mask(sq, lanes)
    scale = (lanes // 2) ** -0.5
    for s_ in range(plan.seqs):
        for j in range(plan.pairs):
            rws, cls = slice(s_ * sq, (s_ + 1) * sq), slice(j * lanes, (j + 1) * lanes)
            kcls = slice(h_ + j * lanes, h_ + (j + 1) * lanes)
            q2 = stack_pair(q[rws, cls], low)
            do2 = stack_pair(do[rws, cls], low)
            pr = p[s_ * plan.pairs + j]
            dp = dot_nt(do2, v[rws, cls])
            dv = dot_tn(pr, do2)
            if layer == 0:
                dv = dv + extra[rws, cls].astype(F32) * (s == 1).astype(F32)
            dv_out[rws, cls] = dv.astype(BF)
            pf = pr.astype(F32)
            ds = (pf * (dp - jnp.sum(pf * dp, axis=-1, keepdims=True))).astype(BF)
            dq2 = dot(ds, k[rws, cls])
            dqk[rws, cls] = (jnp.where(low, dq2[:sq], dq2[sq:]) * scale).astype(BF)
            dqk[rws, kcls] = (dot_tn(ds, q2) * scale).astype(BF)
    da = dot_nt(dqk[...], wqk[...])
    dav = dot_nt(dv_out[...], wv[...])
    if layer == 1:
        dav = dav * (s == 0).astype(F32)
    acc[...] = da + dav
    dys = pl.ds(pl.multiple_of(s * h_, 128), h_)
    for core in range(2):

        @pl.when(c == core)
        def _():
            one, two = (keep, send) if core == 0 else (send, keep)
            one[...] = dqk[...]
            two[:, :h_] = dv_out[...]
            two[:, h_:] = dy[:, dys]

    sg0, sb0 = zero, zero
    for i in range(0, t_, STEP):
        sl = slice(i, i + STEP)
        dn = acc[sl, :]
        part[sl, :] = dn.astype(BF)
        x, _ = unit_rows(h[sl, :].astype(F32))
        sg0 = sg0 + row_sum(dn * x)
        sb0 = sb0 + row_sum(dn)
    sums[0:1, :], sums[1:2, :], sums[2:3, :] = sg0, sb0, 0.5 * sb3
    sq_ = row_sum(dqk[...].astype(F32))[:, :h_]
    none = jnp.zeros((1, h_), F32)
    sums[3:4, :] = jnp.where(s == 0, jnp.concatenate([sq_, none], axis=1), jnp.concatenate([none, sq_], axis=1))
    sums[4:5, :] = jnp.concatenate([row_sum(dv_out[...].astype(F32)), none], axis=1)


def g1_kernel(plan, layer, *refs):
    r_, h_, d_, n_ = plan.rows, plan.half, plan.width, plan.count
    idx, a, a_sib, o, o_sib, far, far_sib, keep, got = refs[:9]
    refs = refs[9:]
    if layer == 0:
        tiny, refs = refs[:6], refs[6:]
    outs, refs = refs[:4], refs[4:]
    gatt = refs[0]
    c = idx[plan.core_at()]

    @pl.when(c == 0)
    def _():
        gatt[...] = (dot_tn(a[...], keep[...]) + dot_tn(a_sib[...], got[...])).astype(BF)

    @pl.when(c == 1)
    def _():
        gatt[:, :h_] = (dot_tn(a[...], keep[:, :h_]) + dot_tn(a_sib[...], got[:, :h_])).astype(BF)
        s = idx[plan.side_at()]
        for side, x, y in ((s, o, o_sib), (1 - s, far, far_sib)):
            rows = pl.ds(pl.multiple_of(side * h_, 16), h_)
            gatt[rows, h_:] = (dot_tn(x[...], keep[:, h_:]) + dot_tn(y[...], got[:, h_:])).astype(BF)

    put_blocks(plan, idx, outs, lambda t, sh: gatt[pl.ds(pl.multiple_of(sh * r_, 16), r_), t * h_ : (t + 1) * h_], 0)
    if layer == 0:
        tail = refs[1]
        small_sums(plan, idx, tiny, tail)
        half = n_ // 2
        for j in range(n_):
            out, at = outs[0 if j >= half else 2], j % half * (r_ + TAIL) + r_
            out[at : at + TAIL, :] = tail[j]


def small_sums(plan, idx, tiny, tail):
    n_, r_, h_, d_, u_ = plan.count, plan.rows, plan.half, plan.width, plan.unit
    s = idx[plan.side_at()]
    rows = []
    for l in range(2):
        s2, s1, sbf = tiny[3 * l : 3 * l + 3]
        rows += [s1[0:1], s2[0:1], s1[1:2], s2[1:2], s1[3:4], s1[2:3], s2[2:3]]
        bf = sbf[...]
        cut = [jnp.concatenate([bf[:, sh * u_ + i * r_ : sh * u_ + (i + 1) * r_] for sh in range(n_)], axis=1) for i in range(2)]
        for side in range(2):
            on = (s == side).astype(F32)
            rows += [cut[0] * on, cut[1] * on]
    v1, v2 = tiny[1][4:5, :h_], tiny[4][4:5, :h_]
    first = (s == 0).astype(F32)
    vals = jnp.concatenate([v1 * first, v1 * (1.0 - first), v2 * first], axis=1)
    each = plan.values // n_
    pad = jnp.zeros((1, 2 * r_ - each), F32)
    rows.append(jnp.concatenate([vals[:, sh * each : sh * each + r_] for sh in range(n_)], axis=1))
    rows.append(jnp.concatenate([x for sh in range(n_) for x in (vals[:, sh * each + r_ : (sh + 1) * each], pad)], axis=1))
    rows.append(jnp.zeros((TAIL - 24, d_), F32))
    full = jnp.concatenate(rows, axis=0).astype(BF)
    for sh in range(n_):
        block = jnp.concatenate([full[:, sh * r_ : (sh + 1) * r_], jnp.zeros((TAIL, h_ - r_), BF)], axis=1)
        tail[idx[2 * n_ + sh]] = block


def total(refs, terms, rows):
    x = None
    for at, row in terms:
        y = refs[at][row : row + rows, :].astype(F32)
        x = y if x is None else x + y
    return x.astype(BF)


def round_kernel(plans, n, *refs):
    for out, segments in zip(refs[n:], plans):
        row = 0
        for terms, rows in segments:
            out[row : row + rows, :] = total(refs, terms, rows)
            row += rows


def listed(segments):
    arrays, plans = [], []
    for terms, rows in segments:
        named = []
        for x, row in terms:
            at = next((i for i, y in enumerate(arrays) if y is x), len(arrays))
            if at == len(arrays):
                arrays.append(x)
            named.append((at, row))
        plans.append((named, rows))
    return arrays, plans


def run_round(outs):
    arrays, plans = listed([seg for segments in outs for seg in segments])
    cut, at = [], 0
    for segments in outs:
        cut.append(plans[at : at + len(segments)])
        at += len(segments)
    width = arrays[0].shape[1]
    shapes = [((sum(rows for _, rows in segments), width), BF, VM) for segments in outs]
    return call(functools.partial(round_kernel, cut, len(arrays)), vm(*arrays), shapes, [], 1.2)


def pick_kernel(plans, n, side_at, idx, *refs):
    own, send = refs[n:]
    first = idx[side_at] == 0
    sums = [total(refs, terms, rows) for terms, rows in plans]
    size = sums[1].shape[0]
    for t in range(2):
        x, y = sums[2 * t][:size], sums[2 * t + 1]
        own[t * size : (t + 1) * size] = jnp.where(first, x, y)
        send[t * size : (t + 1) * size] = jnp.where(first, y, x)
    if sums[0].shape[0] > size:
        for ref in (own, send):
            ref[2 * size :] = sums[0]


def run_pick(plan, idx, segments):
    arrays, plans = listed(segments)
    one, two = segments[0][1], segments[1][1]
    shape = (2 * two + (one if one > two else 0), plan.half)
    kernel = functools.partial(pick_kernel, plans, len(arrays), plan.side_at())
    return call(kernel, [(idx, SM)] + vm(*arrays), [(shape, BF, VM)] * 2, [], 1.0)


def finish_mlp_kernel(plan, idx, *refs):
    r_, h_, u_ = plan.rows, plan.half, plan.unit
    mlp, (o_fc, o_proj) = refs[:4], refs[4:]
    s, c = idx[plan.side_at()], idx[plan.core_at()]
    per = h_ // u_
    for t in range(2):
        fc = [[None] * 2, [None] * 2]
        for i in range(2):
            a, b = mlp[2 * i], mlp[2 * i + 1]
            for core in range(2):
                x = jnp.where(c == core, a[2 * t * r_ : (2 * t + 2) * r_, :], b[2 * t * r_ : (2 * t + 2) * r_, :])
                fc[i][core] = x[:r_]
                for side in range(2):

                    @pl.when((s == side) if i == 0 else (s != side))
                    def _():
                        lo = side * 2 * r_ + t * r_
                        o_proj[lo : lo + r_, core * h_ : (core + 1) * h_] = x[r_:].astype(F32)

        for core in range(2):
            q = 2 * core + t
            b0 = jnp.where(s == 0, fc[0][core], fc[1][core]).astype(F32)
            b1 = jnp.where(s == 0, fc[1][core], fc[0][core]).astype(F32)
            pieces = [x[:, i * u_ : (i + 1) * u_] for i in range(per) for x in (b0, b1)]
            o_fc[:, 2 * q * h_ : 2 * (q + 1) * h_] = jnp.concatenate(pieces, axis=1)


def finish_att_kernel(plan, idx, *refs):
    r_, h_, d_ = plan.rows, plan.half, plan.width
    att, val = refs[:4], refs[4:6]
    o_qk, o_val, o_out, o_gain, o_shift, o_bf, o_vs = refs[6:]
    s, c = idx[plan.side_at()], idx[plan.core_at()]

    def block(side, core, lo, hi):
        pick = [jnp.where(c == core, att[2 * i][lo:hi, :], att[2 * i + 1][lo:hi, :]) for i in range(2)]
        return jnp.where(s == side, pick[0], pick[1]).astype(F32)

    sm = sum(x[3 * r_ :, :r_].astype(F32) for x in att)
    mine = jnp.where(s == 0, sm[:11], sm[11:22])
    o_gain[...] = mine[0:2]
    o_shift[...] = mine[2:7]
    o_bf[...] = jnp.concatenate([mine[7 + i : 8 + i] for i in range(4)], axis=1)
    o_vs[...] = jnp.concatenate([sm[22:23], sm[23:24, : plan.values // plan.count - r_]], axis=1)
    low, high = block(0, 1, 0, r_), block(1, 1, 0, r_)
    other, rest = jnp.where(c == 1, val[0][:r_, :], val[1][:r_, :]).astype(F32), block(0, 1, 2 * r_, 3 * r_)
    o_val[:, :h_] = jnp.where(s == 0, low, rest)
    o_val[:, h_:d_] = jnp.where(s == 0, high, other)
    o_val[:, d_:] = jnp.where(s == 0, other, low)
    for side in range(2):
        o_out[:, side * h_ : (side + 1) * h_] = block(side, 1, r_, 2 * r_)
        for t in range(2):
            o_qk[:, t * d_ + side * h_ : t * d_ + (side + 1) * h_] = block(side, 0, t * r_, (t + 1) * r_)


def ends_kernel(plan, idx, prm, r, y_a, y_b, dr, da_a, da_b, h, out):
    s = idx[plan.side_at()]

    @pl.when(s == 1)
    def _():
        for i in range(0, plan.tokens, STEP):
            sl = slice(i, i + STEP)
            out[sl, :] = (r[sl, :] + (y_a[sl, :].astype(F32) + y_b[sl, :].astype(F32)) + prm[1, 6:7, :]).astype(BF)

    @pl.when(s == 0)
    def _():
        for i in range(0, plan.tokens, STEP):
            sl = slice(i, i + STEP)
            x, inv = unit_rows(h[sl, :].astype(F32))
            dn = da_a[sl, :].astype(F32) + da_b[sl, :].astype(F32)
            out[sl, :] = (dr[sl, :] + norm_back(dn, x, inv, prm[0, 0:1, :])).astype(BF)


VM = pl.BlockSpec(memory_space=pltpu.VMEM)
SM = pl.BlockSpec(memory_space=pltpu.SMEM)
ANY = pl.BlockSpec(memory_space=pl.ANY)
HBM = pl.BlockSpec(memory_space=pltpu.HBM)


def call(kernel, ins, outs, scratch, us, vmem=VMEM_BYTES):
    return pl.pallas_call(
        kernel,
        out_shape=[jax.ShapeDtypeStruct(sh, dt) for sh, dt, _ in outs],
        in_specs=[sp for _, sp in ins],
        out_specs=[sp for _, _, sp in outs],
        scratch_shapes=scratch,
        compiler_params=pltpu.CompilerParams(vmem_limit_bytes=vmem),
        cost_estimate=pl.CostEstimate(flops=int(us * 4.2e8), bytes_accessed=1000, transcendentals=0),
    )(*[x for x, _ in ins])


def vm(*arrays):
    return [(x, VM) for x in arrays]


def hbm(arrays):
    return [(x, ANY) for x in arrays]


def run_weights(plan, layer, idx, chunks):
    w, h, f = plan.width, plan.half, plan.fh
    ins = [(idx, SM)] + vm(*chunks)
    att = call(functools.partial(att_weights_kernel, plan, layer), ins, [((w, w), BF, VM), ((w, h), BF, VM), ((h, w), BF, VM)], [], 1.2)
    outs = [((w, f), BF, VM)] + ([] if layer else [((f, w), BF, VM)])
    mlp = call(functools.partial(mlp_weights_kernel, plan, layer), ins, outs, [], 1.5)
    return att, mlp


def run_proj(plan, idx, parts):
    out = ((plan.fh, plan.width), BF, VM)
    return call(functools.partial(proj_weights_kernel, plan), [(idx, SM)] + vm(*parts), [out], [], 1.0)


def dma_sems(n):
    return pltpu.SemaphoreType.DMA((n,))


def run_pack(plan, idx, arrays):
    r_, h_ = plan.rows, plan.half
    both, one = ((2, 3 * r_, h_), BF, VM), ((r_, h_), BF, VM)
    outs = [both, both, one, one, ((SMALL, h_), BF, VM)]
    scratch = [pltpu.VMEM(x.shape, BF) for x in arrays] + [dma_sems(8)]
    ins = [(idx, SM)] + [(x, HBM) for x in arrays]
    return call(functools.partial(pack_kernel, plan), ins, outs, scratch, 1.5, 60 * 1024 * 1024)


def run_param(plan, idx, arrays):
    outs = [((2, 8, plan.width), F32, VM), ((2, 1, plan.fh), F32, VM)]
    scratch = [pltpu.VMEM((2, plan.count, SMALL, plan.half), BF)]
    return call(functools.partial(param_kernel, plan), [(idx, SM)] + vm(*arrays), outs, scratch, 1.0)


def run_f1(plan, layer, idx, prm, inputs, weights):
    t_, h_, d_ = plan.tokens, plan.half, plan.width
    narrow, wide = ((t_, h_), BF, VM), ((t_, d_), BF, VM)
    outs = [wide, narrow, narrow, narrow, ((plan.seqs * plan.pairs, 2 * plan.seq, plan.seq), BF, VM), narrow, wide]
    outs += [wide] if layer else [wide, wide]
    scratch = []
    ins = [(idx, SM)] + vm(prm, *inputs, *weights)
    return call(functools.partial(f1_kernel, plan, layer), ins, outs, scratch, 2.5)


def run_f2(plan, layer, idx, prm, bf, h, pa, pb, weights):
    t_, d_, f_ = plan.tokens, plan.width, plan.fh
    wide = ((t_, d_), BF, VM)
    outs = [wide, ((t_, d_), F32, VM), ((t_, f_ + d_), BF, VM), ((t_, f_), BF, VM)]
    scratch = [pltpu.VMEM((t_, f_ // 3), F32)]
    ins = [(idx, SM)] + vm(prm, bf, h, pa, pb, *weights)
    return call(functools.partial(f2_kernel, plan, layer), ins, outs, scratch, 4.4)


def run_b2(plan, layer, idx, prm, gp, r, more, weights):
    t_, d_, f_ = plan.tokens, plan.width, plan.fh
    outs = [((t_, d_), BF, VM)] * 4 + [((t_, plan.half), BF, VM), ((3, d_), F32, VM), ((1, f_), F32, VM)]
    scratch = [pltpu.VMEM((t_, d_), F32), pltpu.VMEM((t_, f_), BF)]
    ins = [(idx, SM)] + vm(prm, gp, r, *more, *weights)
    return call(functools.partial(b2_kernel, plan, layer), ins, outs, scratch, 2.6)


def grad_outs(plan, rows, tail=0):
    return [((plan.count // 2 * r, plan.half), BF, VM) for r in (rows + tail, rows) * 2]


def run_g2(plan, idx, *arrays):
    d_, f_, h_ = plan.width, plan.fh, plan.half
    scratch = [pltpu.VMEM((d_, d_), BF), pltpu.VMEM((f_, h_), BF)]
    ins = [(idx, SM)] + vm(*arrays)
    return call(functools.partial(g2_kernel, plan), ins, grad_outs(plan, 2 * plan.rows), scratch, 4.6)


def run_b1(plan, layer, idx, prm, more, weights):
    t_, d_, h_ = plan.tokens, plan.width, plan.half
    wide, narrow = (t_, d_), (t_, h_)
    outs = [(wide, BF, VM), (wide, F32, VM), (wide, BF, VM), (wide, BF, VM), ((5, d_), F32, VM)]
    scratch = [pltpu.VMEM(wide, BF), pltpu.VMEM(wide, BF), pltpu.VMEM(narrow, BF), pltpu.VMEM(wide, F32)]
    if layer:
        outs.append((narrow, BF, VM))
    else:
        scratch.append(pltpu.VMEM(narrow, BF))
    ins = [(idx, SM)] + vm(prm, *more, *weights)
    return call(functools.partial(b1_kernel, plan, layer), ins, outs, scratch, 4.5)


def run_g1(plan, layer, idx, acts, keep, got, tiny):
    d_, h_ = plan.width, plan.half
    scratch = [pltpu.VMEM((d_, d_), BF)]
    if layer == 0:
        scratch += [pltpu.VMEM((plan.count, TAIL, h_), BF)]
    ins = [(idx, SM)] + vm(*acts, keep, got, *tiny)
    return call(functools.partial(g1_kernel, plan, layer), ins, grad_outs(plan, plan.rows, 0 if layer else TAIL), scratch, 1.8)


def run_finish_mlp(plan, idx, arrays):
    outs = [(sh, F32, VM) for sh in ((plan.rows, plan.ff), (4 * plan.rows, plan.width))]
    return call(functools.partial(finish_mlp_kernel, plan), [(idx, SM)] + vm(*arrays), outs, [], 3.0)


def run_finish_att(plan, idx, arrays):
    r_, d_ = plan.rows, plan.width
    outs = [(sh, F32, VM) for sh in ((r_, 2 * d_), (r_, plan.values), (r_, d_), (2, r_), (5, r_), (1, 4 * r_), (1, plan.values // plan.count))]
    return call(functools.partial(finish_att_kernel, plan), [(idx, SM)] + vm(*arrays), outs, [], 2.5)


def run_ends(plan, idx, arrays):
    return call(functools.partial(ends_kernel, plan), [(idx, SM)] + vm(*arrays), [((plan.tokens, plan.width), BF, VM)], [], 1.9)[0]


def after(x, *earlier):
    return lax.optimization_barrier((x,) + earlier)[0]


def per_device(ends, w_qk, w_value, w_out, w_fc, w_proj, gains, shifts, fc_shift, value_shift):
    s, grp, d = lax.axis_index("section"), lax.axis_index("group"), lax.axis_index("dp")
    c = grp % 2
    count, groups = lax.axis_size("dp"), lax.axis_size("group")
    rows, width = w_qk.shape[1], ends.shape[3]
    half = width // 2
    seqs, seq = ends.shape[1], ends.shape[2]
    tokens = seqs * seq
    plan = Plan(count, rows, width, w_fc.shape[2], w_value.shape[1], tokens, seq, HEADS // 2)
    table = plan.table(groups)
    idx = lax.dynamic_slice(jnp.asarray(table), (s, grp, d, 0), (1, 1, 1, table.shape[3])).reshape(-1)
    first, even = s == 0, d % 2 == 0

    def swap_x(x):
        return lax.ppermute(x, "section", [(0, 1), (1, 0)])

    def swap_c(x):
        return lax.ppermute(x, "group", [(i, i ^ 1) for i in range(groups)])

    def swap_d(x, bit):
        return lax.ppermute(x, "dp", [(i, i ^ bit) for i in range(count)])

    hc = count // 2
    spread = [
        [(l * count + i, (i // hc) * count + 2 * (i % hc) + (l if w == 0 else 1 - l)) for l in range(2) for i in range(count)]
        for w in range(2)
    ]
    mine, send, o_lo, o_hi, small = run_pack(
        plan, idx, (w_qk[0], w_fc[0], w_proj[0], w_out[0], gains[0], shifts[0], fc_shift, value_shift[None])
    )
    got = swap_x(send)
    small_got = swap_x(small)
    o_a = lax.ppermute(o_lo, ("section", "dp"), spread[0])
    o_b = lax.ppermute(o_hi, ("section", "dp"), spread[1])
    ends_own = ends[0].reshape(tokens, width)
    ends_got = swap_x(after(ends_own, got))
    v_side = (lax.dynamic_slice_in_dim(w_value, s * half, half, 1), w_value[:, width:])
    o_side = (jnp.where(even, o_a, o_b), jnp.where(even, o_b, o_a))

    def head(t, l, other):
        x = jnp.where(first if l == 0 else ~first, mine[t, :rows], got[t, :rows])
        return jnp.where(c == 0, x, other)

    params = [jnp.where(first, small, small_got), jnp.where(first, small_got, small)]
    early, late = [], []
    for t, side in ((0, v_side), (1, o_side)):
        x, y = mine[t, rows:], got[t, rows:]
        second = jnp.where(first, y, x)
        early.append(jnp.concatenate([head(t, 0, side[0]), jnp.where(first, x, y), head(t, 1, side[1]), second[:rows], params[t]], axis=0))
        late.append(second[rows:])

    routes = [[(a, b) for a, b in zip(order, order[1:] + order[:1])] for order in (ring_order(count), ring_order(count)[::-1])]

    def ring(x):
        return lax.optimization_barrier([lax.ppermute(x[t], "dp", routes[t]) for t in range(2)])

    steps = [early]
    sibs = []
    for n in range(count - 1):
        sibs.append([swap_c(x) for x in steps[-1]])
        steps.append(ring(steps[-1]))
        if n == 2:
            steps[-1] = [after(x, ends_got) for x in steps[-1]]
        if n >= 2:
            steps[-1] = [after(x, *sibs[n - 1]) for x in steps[-1]]
    sibs.append([swap_c(x) for x in steps[-1]])
    chunks = [y for t in range(2) for y in [x[t] for x in steps] + [x[t] for x in sibs]]
    prm, bf = run_param(plan, idx, [x[t] for t in range(2) for x in steps])
    (att_w0, mlp_w0), (att_w1, fc_w1) = (run_weights(plan, l, idx, chunks) for l in range(2))

    def doubled(x, *others):
        k = (x[0].shape[0] // rows).bit_length() - 1
        bits = [plan.orders[t][k] for t in range(2)]
        if bits[0] == bits[1]:
            size = x[0].shape[0]
            both = swap_d(after(jnp.concatenate(x, axis=0), *others), bits[0])
            got = [both[:size], both[size:]]
        else:
            got = [swap_d(after(x[t], *others), bits[t]) for t in range(2)]
        return got

    have = late
    got = doubled(have, *steps[-2])
    part, q0, k0, v0, p0, o0, a0, h0, cot = run_f1(plan, 0, idx, prm, (ends_own, ends_got), att_w0)
    sib0 = [swap_c(a0), swap_c(o0)]
    for _ in range(plan.bits - 2):
        have = [jnp.concatenate(x, axis=0) for x in zip(have, got)]
        got = doubled(have, part)
    sib0 += got + list(att_w1)
    have = [jnp.concatenate(x, axis=0) for x in zip(have, got)]
    got = after(swap_x(part), *sib0)
    part, r0, ucn0, gp0 = run_f2(plan, 0, idx, prm, bf, h0, part, got, mlp_w0)
    more = doubled(have, got)
    have_sib = [swap_c(after(x, part)) for x in have]
    ucn0_sib = swap_c(ucn0)
    got = after(swap_x(part), ucn0_sib, *have_sib, *more)
    part, q1, k1, v1, p1, o1, a1, h1 = run_f1(plan, 1, idx, prm, (r0, part, got, v0), att_w1)
    sib1 = [swap_c(a1), swap_c(o1)]
    got = after(swap_x(part), *sib1)
    parts = [x for t in range(2) for x in (have[t], more[t], have_sib[t], swap_c(after(more[t], part)))]
    mlp_w1 = fc_w1 + run_proj(plan, idx, parts)
    y_part, r1, ucn1, gp1 = run_f2(plan, 1, idx, prm, bf, h1, part, got, mlp_w1)

    class Sum:
        def __init__(self, g):
            self.first, self.keep = g[:2], g[2:]
            self.rows = [x.shape[0] // hc for x in self.keep]
            self.came = [[], []]

        def terms(self, t, low):
            return [(self.keep[t], low * self.rows[t])] + [(x, at + low * self.rows[t]) for x, at in self.came[t]]

        def bit(self, t):
            return plan.orders[t][plan.bits - 1 - len(self.came[t])]

        def segment(self, t):
            steps = len(self.came[t])
            if steps == 0:
                return [(self.first[t], 0)], self.first[t].shape[0]
            low = count >> (steps + 1)
            return self.terms(t, low), low * self.rows[t]

    def one_round(sums, *others):
        sums = [x for x in sums if len(x.came[0]) < plan.bits]
        if not sums:
            return []
        by_bit = {}
        for x in sums:
            for t in range(2):
                by_bit.setdefault(x.bit(t), []).append((x, t, x.segment(t)))
        bits = sorted(by_bit)
        if all(len(by_bit[b]) == 1 and not by_bit[b][0][0].came[0] for b in bits):
            outs = [by_bit[b][0][2][0][0][0] for b in bits]
        else:
            outs = run_round([[seg for _, _, seg in by_bit[b]] for b in bits])
        got = []
        for b, out in zip(bits, outs):
            here = swap_d(after(out, *others, *one_round.last), b)
            row = 0
            for x, t, (_, rows_) in by_bit[b]:
                x.came[t].append((here, row))
                row += rows_
            got.append(here)
        one_round.last = got
        return got

    one_round.last = []

    def over_pairs(x):
        total = x
        for n in range(1, groups // 2):
            total = total + lax.ppermute(x, "group", [(i, (i + 2 * n) % groups) for i in range(groups)])
        return total

    part, e, z_keep, z_send, e_send, s2_1, sbf_1 = run_b2(plan, 1, idx, prm, gp1, r1, (cot,), mlp_w1)
    got = swap_x(part)
    mlp1 = Sum(run_g2(plan, idx, ucn1, swap_c(ucn1), e, swap_c(e_send), z_keep, swap_c(z_send)))
    got = after(got, *mlp1.first)
    one_round([mlp1])
    part, dr, keep, send, s1_1, dv1 = run_b1(plan, 1, idx, prm, (cot, part, got, r1, h1, q1, k1, v1, p1), att_w1)
    o1_far = swap_x(after(o1, got))
    got = swap_x(part)
    acts = [a1, sib1[0], o1, sib1[1], o1_far, swap_c(o1_far)]
    att1 = Sum(run_g1(plan, 1, idx, acts, keep, swap_c(send), ()))
    got = after(got, *att1.first)
    came = one_round([mlp1, att1])
    part, e, z_keep, z_send, e_send, s2_0, sbf_0 = run_b2(plan, 0, idx, prm, gp0, r0, (dr, part, got, h1), mlp_w0)
    got = swap_x(part)
    mlp0 = Sum(run_g2(plan, idx, after(ucn0, *came), ucn0_sib, e, swap_c(e_send), z_keep, swap_c(z_send)))
    got = after(got, *mlp0.first)
    one_round([mlp1, att1, mlp0])
    o0_far = swap_x(after(o0, got))
    part, dr, keep, send, s1_0 = run_b1(plan, 0, idx, prm, (e, part, got, r0, h0, q0, k0, v0, p0, dv1), att_w0)
    acts = [a0, sib0[0], o0, sib0[1], o0_far, swap_c(o0_far)]
    att0 = Sum(run_g1(plan, 0, idx, acts, keep, swap_c(send), (s2_0, s1_0, sbf_0, s2_1, s1_1, sbf_1)))
    sums = [att0, att1, mlp0, mlp1]
    x_got, y_got = swap_x(after(part, *one_round.last)), swap_x(after(y_part, *one_round.last))
    res = run_ends(plan, idx, (prm, r1, y_part, y_got, dr, part, x_got, h0)).reshape(1, seqs, seq, width)
    one_round(sums)
    for _ in range(plan.bits - 2):
        one_round(sums, res)

    def ending(*sums):
        own, send = (over_pairs(x) for x in run_pick(plan, idx, [(x.terms(t, 0), x.rows[t]) for t in range(2) for x in sums]))
        far = swap_x(send)
        return [own, swap_c(own), far, swap_c(far)], send

    one_round(sums)
    e_mlp, _ = ending(mlp0, mlp1)
    o_fc, o_proj = run_finish_mlp(plan, idx, e_mlp)
    e_att, sent = ending(att0, att1)
    o_qk, o_val, o_out, o_gain, o_shift, o_bf, o_vs = run_finish_att(plan, idx, e_att + [after(sent, o_fc), swap_c(sent)])

    return (res, o_qk[None], o_val, o_out[None], o_fc[None], o_proj[None], o_gain[None], o_shift[None], o_bf, o_vs[0])


def solution(mesh):
    placed = (
        P("section", ("group", "dp"), None, None),
        P("section", "dp", None),
        P("dp", None),
        P("section", "dp", None),
        P("section", "dp", None),
        P("section", "dp", None),
        P("section", None, "dp"),
        P("section", None, "dp"),
        P("section", "dp"),
        P("dp"),
    )
    return jax.shard_map(per_device, mesh=mesh, in_specs=placed, out_specs=placed, check_vma=False)
```

```python
import functools

import jax
import jax.numpy as jnp
import numpy as np
from jax import lax
from jax.experimental import pallas as pl
from jax.experimental.pallas import tpu as pltpu
from jax.sharding import PartitionSpec as P

HEADS = 12
BF = jnp.bfloat16
F32 = jnp.float32
norm_eps = 1e-05
masked_score = -1e30
TAIL = 32
SMALL = 16
STEP = 32
VMEM_BYTES = 16 * 1024 * 1024


def dot(a, b):
    return jnp.dot(a, b, preferred_element_type=F32)


def dot_tn(a, b):
    return lax.dot_general(a, b, (((0,), (0,)), ((), ())), preferred_element_type=F32)


def dot_nt(a, b):
    return lax.dot_general(a, b, (((1,), (1,)), ((), ())), preferred_element_type=F32)


def unit_rows(v):
    centered = v - jnp.mean(v, axis=-1, keepdims=True)
    inv = lax.rsqrt(jnp.mean(centered * centered, axis=-1, keepdims=True) + norm_eps)
    return centered * inv, inv


def norm_back(dn, x, inv, gain):
    scaled = dn * gain
    inner = jnp.mean(scaled * x, axis=-1, keepdims=True)
    return inv * (scaled - jnp.mean(scaled, axis=-1, keepdims=True) - x * inner)


def row_sum(v):
    return jnp.sum(v, axis=0, keepdims=True)


def ring_order(count):
    wide = 2 if count < 16 else 4
    tall = count // wide
    order = [i * wide for i in range(tall)]
    for n, row in enumerate(reversed(range(tall))):
        cols = range(1, wide)
        order += [row * wide + col for col in (cols if n % 2 == 0 else reversed(cols))]
    return order


class Plan:
    def __init__(self, count, rows, width, ff, values, tokens, seq, heads):
        self.count, self.rows, self.width, self.half = count, rows, width, width // 2
        self.ff, self.fh, self.unit, self.values = ff, ff // 2, ff // count // 2, values
        self.tokens, self.seq, self.seqs = tokens, seq, tokens // seq
        self.pairs = heads // 2
        self.bits = count.bit_length() - 1
        down = [1 << i for i in reversed(range(self.bits))]
        other = down[:-2] + [down[-1], down[-2]]
        self.orders = (down, other)
        self.masks = []
        for order in self.orders:
            mask = [0] * count
            for j in range(count):
                for k, bit in enumerate(order):
                    if j >> k & 1:
                        mask[j] ^= bit
            self.masks.append(mask)

    def core_at(self):
        return 7 * self.count

    def side_at(self):
        return 7 * self.count + 1

    def table(self, groups):
        n = self.count
        out = np.zeros((2, groups, n, 7 * n + 2), np.int32)
        order = ring_order(n)
        for p, d in enumerate(order):
            for t in range(2):
                out[:, :, d, t * n : (t + 1) * n] = [d ^ m for m in self.masks[t]]
                out[:, :, d, (3 + t) * n : (4 + t) * n] = [order[(p - (1 - 2 * t) * j) % n] for j in range(n)]
            for j, m in enumerate(self.masks[0]):
                out[:, :, d, 2 * n + (d ^ m)] = j
            for j in range(n):
                for t in range(2):
                    out[:, :, d, (5 + t) * n + order[(p - (1 - 2 * t) * j) % n]] = j
        out[:, :, :, 7 * n] = (np.arange(groups) % 2)[None, :, None]
        out[:, :, :, 7 * n + 1] = np.arange(2)[:, None, None]
        return out


def aligned(x, size):
    return x if isinstance(x, int) else pl.multiple_of(x, size)


def dma(src, dst, sem):
    return pltpu.make_async_copy(src, dst, sem)


def wait_all(ref, sem):
    dma(ref, ref, sem).wait()


def chunk_refs(plan, idx, chunks, row):
    for j in range(plan.count):
        for t in range(2):
            for other in range(2):
                ref = chunks[(t * 2 + other) * plan.count + j]
                yield t, other, idx[(3 + t) * plan.count + j], ref.at[pl.ds(row, plan.rows), :]


def place_att(plan, layer, idx, chunks, wqk, wv, wo):
    r_, h_ = plan.rows, plan.half
    c = idx[plan.core_at()]
    for t, other, sh, src in chunk_refs(plan, idx, chunks, 3 * r_ * layer):
        core = 1 - c if other else c
        row = pl.multiple_of(sh * r_, 16)

        @pl.when(core == 0)
        def _():
            wqk[pl.ds(row, r_), t * h_ : (t + 1) * h_] = src[...]

        @pl.when(core == 1)
        def _():
            if t == 0:
                wv[pl.ds(row, r_), :] = src[...]
            else:
                orow = pl.multiple_of((sh // 2) * r_, 16)
                ocol = pl.multiple_of((sh % 2) * h_, 128)
                wo[pl.ds(orow, r_), pl.ds(ocol, h_)] = src[...]


def place_mlp(plan, layer, idx, chunks, wfc, wproj):
    r_, h_ = plan.rows, plan.half
    c = idx[plan.core_at()]
    for kind in range(1 if layer else 2):
        for t, other, sh, src in chunk_refs(plan, idx, chunks, ((4 if layer else 1) + kind) * r_):
            core = 1 - c if other else c
            if kind == 0:
                row = pl.multiple_of(sh * r_, 16)
                col = pl.multiple_of((2 * core + t) * h_, 128)
                wfc[pl.ds(row, r_), pl.ds(col, h_)] = src[...]
            else:
                row = pl.multiple_of(sh * 2 * r_ + t * r_, 16)
                col = pl.multiple_of(core * h_, 128)
                wproj[pl.ds(row, r_), pl.ds(col, h_)] = src[...]


def put_blocks(plan, idx, outs, pick, row0):
    n_, r_ = plan.count, plan.rows
    half = n_ // 2
    for j in reversed(range(n_)):
        for t in range(2):
            out = outs[2 * (0 if j >= half else 1) + t]
            at = j % half * (out.shape[0] // half) + row0
            out[at : at + r_, :] = pick(t, idx[t * n_ + j])


def pack_kernel(plan, *refs):
    from_hbm, (mine, send, o_a, o_b, small), here, sems = refs[:7], refs[7:12], refs[12:19], refs[19]
    for i, ref in enumerate(here):
        dma(from_hbm[i], ref, sems.at[i]).start()
    for i, ref in enumerate(here):
        wait_all(ref, sems.at[i])
    wqk, wfc, wproj, wout, gains, shifts, fc_shift = here
    r_, h_, d_, u_ = plan.rows, plan.half, plan.width, plan.unit
    per = h_ // u_
    s, c = lax.axis_index("section"), lax.rem(lax.axis_index("group"), 2)
    lo, hi = wout[:, :h_], wout[:, h_:]
    o_a[...] = jnp.where(s == 0, lo, hi)
    o_b[...] = jnp.where(s == 0, hi, lo)
    rows = [gains[...], shifts[...]] + [fc_shift[:, i * r_ : (i + 1) * r_] for i in range(4)]
    rows = jnp.concatenate([x.astype(F32) for x in rows] + [jnp.zeros((SMALL - 11, r_), F32)], axis=0)
    small[...] = jnp.concatenate([rows, jnp.zeros((SMALL, h_ - r_), F32)], axis=1).astype(BF)
    for side in range(2):
        for core in range(2):
            for keep in range(2):
                out = mine if keep else send

                @pl.when(jnp.logical_and(c == core, s == (side if keep else 1 - side)))
                def _():
                    for t in range(2):
                        lo = t * d_ + side * h_
                        out[t, :r_] = wqk[:, lo : lo + h_]
                        q = 2 * core + t
                        cols = [(q * per + i) * 2 * u_ + side * u_ for i in range(per)]
                        out[t, r_ : 2 * r_] = jnp.concatenate([wfc[:, x : x + u_] for x in cols], axis=1)
                        row = side * 2 * r_ + t * r_
                        out[t, 2 * r_ :] = wproj[row : row + r_, core * h_ : (core + 1) * h_]


def param_kernel(plan, idx, *refs):
    n_, r_, h_, d_ = plan.count, plan.rows, plan.half, plan.width
    s = idx[plan.side_at()]
    steps, (prm, bf, stack) = refs[: 2 * n_], refs[2 * n_ :]
    for j, ref in enumerate(steps):
        stack[j // n_, j % n_] = ref[5 * r_ :, :]
    pairs = [[stack[t, idx[(5 + t) * n_ + sh]][:, :r_].astype(F32) for t in range(2)] for sh in range(n_)]
    more = plan.values // n_ - r_
    vals = jnp.concatenate([x for b, _ in pairs for x in (b[11:12, :], b[12:13, :more])], axis=1)
    for l in range(2):
        blocks = [b[l] for b in pairs]
        m = jnp.concatenate([b[:7] for b in blocks], axis=1)
        prm[l, 0:7] = m
        bq = jnp.where(s == 0, m[4:5, :h_], m[4:5, h_:])
        prm[l, 4:5] = jnp.concatenate([bq, jnp.zeros((1, d_ - h_), F32)], axis=1)
        if l == 0:
            bv = jnp.where(s == 0, vals[:, :h_], vals[:, h_:d_])
        else:
            bv = vals[:, d_:]
        prm[l, 7:8] = jnp.concatenate([bv, jnp.zeros((1, d_ - h_), F32)], axis=1)
        sides = []
        for side in range(2):
            row = 7 + 2 * side
            sides.append(jnp.concatenate([b[row + i : row + i + 1] for b in blocks for i in range(2)], axis=1))
        bf[l] = jnp.where(s == 0, sides[0], sides[1])


def att_weights_kernel(plan, layer, *refs):
    place_att(plan, layer, refs[0], refs[1:-3], *refs[-3:])


def mlp_weights_kernel(plan, layer, *refs):
    outs = refs[1 + 4 * plan.count :]
    place_mlp(plan, layer, refs[0], refs[1 : 1 + 4 * plan.count], outs[0], outs[-1])


def proj_weights_kernel(plan, *refs):
    n_, r_, h_ = plan.count, plan.rows, plan.half
    idx, parts, wproj = refs[0], refs[1:9], refs[9]
    c = idx[plan.core_at()]
    for t in range(2):
        for other in range(2):
            core = 1 - c if other else c
            for j in range(n_):
                at = j % (n_ // 2) * r_
                row = pl.multiple_of(idx[t * n_ + j] * 2 * r_ + t * r_, 16)
                src = parts[(2 * t + other) * 2 + j // (n_ // 2)]
                wproj[pl.ds(row, r_), pl.ds(pl.multiple_of(core * h_, 128), h_)] = src[at : at + r_, :]


def pair_mask(seq, lanes):
    return lax.broadcasted_iota(jnp.int32, (seq, lanes), 1) < lanes // 2


def stack_pair(x, low):
    zero = jnp.zeros_like(x)
    return jnp.concatenate([jnp.where(low, x, zero), jnp.where(low, zero, x)], axis=0)


def f1_kernel(plan, layer, *refs):
    h_, t_, sq = plan.half, plan.tokens, plan.seq
    idx, prm, refs = refs[0], refs[1], refs[2:]
    if layer == 1:
        r_up, pa, pb, v_old = refs[:4]
        refs = refs[4:]
    else:
        here, there = refs[:2]
        refs = refs[2:]
    weights, refs = refs[:3], refs[3:]
    part, q, k, v, p, o, a, h = refs[:8]
    if layer == 0:
        cot = refs[8]
    wqk, wv, wo = weights
    first = idx[plan.side_at()] == 0
    for i in range(0, t_, STEP):
        sl = slice(i, i + STEP)
        if layer == 1:
            hh = r_up[sl, :] + (pa[sl, :].astype(F32) + pb[sl, :].astype(F32)) + prm[0, 6:7, :]
            h[sl, :] = hh.astype(BF)
        else:
            mine, theirs = here[sl, :], there[sl, :]
            h[sl, :] = jnp.where(first, mine, theirs)
            cot[sl, :] = jnp.where(first, theirs, mine)
        x, _ = unit_rows(h[sl, :].astype(F32))
        a[sl, :] = (x * prm[layer, 0:1, :] + prm[layer, 2:3, :]).astype(BF)
    qk = dot(a[...], wqk[...])
    q[...] = (qk[:, :h_] + prm[layer, 4:5, :h_]).astype(BF)
    k[...] = qk[:, h_:].astype(BF)
    val = (dot(a[...], wv[...]) + prm[layer, 7:8, :h_]).astype(BF)
    if layer == 1:
        val = jnp.where(idx[plan.side_at()] == 1, v_old[...], val)
    v[...] = val
    lanes = h_ // plan.pairs
    low = pair_mask(sq, lanes)
    causal = lax.broadcasted_iota(jnp.int32, (2 * sq, sq), 0) % sq >= lax.broadcasted_iota(jnp.int32, (2 * sq, sq), 1)
    scale = (lanes // 2) ** -0.5
    for s_ in range(plan.seqs):
        for j in range(plan.pairs):
            rws, cls = slice(s_ * sq, (s_ + 1) * sq), slice(j * lanes, (j + 1) * lanes)
            q2 = stack_pair(q[rws, cls], low)
            sc = jnp.where(causal, dot_nt(q2, k[rws, cls]) * scale, masked_score)
            ex = jnp.exp(sc - jnp.max(sc, axis=-1, keepdims=True))
            pr = (ex / jnp.sum(ex, axis=-1, keepdims=True)).astype(BF)
            p[s_ * plan.pairs + j] = pr
            o2 = dot(pr, v[rws, cls])
            o[rws, cls] = jnp.where(low, o2[:sq], o2[sq:]).astype(BF)
    part[...] = dot(o[...], wo[...]).astype(BF)


def f2_kernel(plan, layer, *refs):
    t_ = plan.tokens
    idx, prm, bf, h, pa, pb = refs[:6]
    if layer == 1:
        o_up, refs = refs[8], refs[:8] + refs[9:]
    weights, refs = refs[6:8], refs[8:]
    part, r, ucn, gp, z = refs
    wfc, wproj = weights
    f_ = plan.fh
    for i in range(0, t_, STEP):
        sl = slice(i, i + STEP)
        rr = h[sl, :].astype(F32) + (pa[sl, :].astype(F32) + pb[sl, :].astype(F32)) + prm[layer, 5:6, :]
        r[sl, :] = rr
        x, _ = unit_rows(rr)
        ucn[sl, f_:] = (x * prm[layer, 1:2, :] + prm[layer, 3:4, :]).astype(BF)
    cols = plan.fh // 3
    for j in range(3):
        cs = slice(j * cols, (j + 1) * cols)
        z[...] = dot(ucn[:, f_:], wfc[:, cs])

        def body(i, carry):
            sl = pl.ds(pl.multiple_of(i * STEP, STEP), STEP)
            zz = z[sl, :] + bf[layer, :, cs]
            sq_ = zz * zz
            th = jnp.tanh(0.7978845608 * zz * (1.0 + 0.044715 * sq_))
            hp = 0.5 * (1.0 + th)
            ucn[sl, cs] = (zz * hp).astype(BF)
            slope = 0.7978845608 * (1.0 + 3 * 0.044715 * sq_)
            gp[sl, cs] = (hp + 0.5 * zz * (1.0 - th * th) * slope).astype(BF)
            return carry

        lax.fori_loop(0, t_ // STEP, body, 0)
    d_ = plan.width
    part[:, :d_] = dot(ucn[:, :f_], wproj[...]).astype(BF)
    if layer == 1:
        part[:, d_:] = o_up[...]


def b2_kernel(plan, layer, *refs):
    d_, t_, f_ = plan.width, plan.tokens, plan.fh
    idx, prm, gp, r = refs[:4]
    refs = refs[4:]
    if layer == 1:
        e, refs = refs[0], refs[1:]
    else:
        dr, da_a, da_b, h_up = refs[:4]
        refs = refs[4:]
    weights, refs = refs[:2], refs[2:]
    part, e_out, z_keep, z_send, e_send, sums, sbf = refs[:7]
    h_, c = plan.half, idx[plan.core_at()]
    wfc, wproj = weights
    acc, dz = refs[-2:]
    zero = jnp.zeros((1, d_), F32)
    sb4 = zero
    for i in range(0, t_, STEP):
        sl = slice(i, i + STEP)
        if layer == 0:
            x, inv = unit_rows(h_up[sl, :].astype(F32))
            dn = da_a[sl, :].astype(F32) + da_b[sl, :].astype(F32)
            ee = (dr[sl, :] + norm_back(dn, x, inv, prm[1, 0:1, :])).astype(BF)
        else:
            ee = e[sl, :]
        e_out[sl, :] = ee
        sb4 = sb4 + row_sum(ee.astype(F32))
    cols = f_ // 3
    for j in range(3):
        cs = slice(j * cols, (j + 1) * cols)
        dzj = (dot_nt(e_out[...], wproj[cs, :]) * gp[:, cs].astype(F32)).astype(BF)
        dz[:, cs] = dzj
        sbf[:, cs] = row_sum(dzj.astype(F32))
    z_keep[...] = dz[:, pl.ds(pl.multiple_of(c * d_, 128), d_)]
    z_send[...] = dz[:, pl.ds(pl.multiple_of((1 - c) * d_, 128), d_)]
    e_send[...] = e_out[:, pl.ds(pl.multiple_of((1 - c) * h_, 128), h_)]
    acc[...] = dot_nt(dz[...], wfc[...])
    sg1, sb1 = zero, zero
    for i in range(0, t_, STEP):
        sl = slice(i, i + STEP)
        dn = acc[sl, :]
        part[sl, :] = dn.astype(BF)
        x, _ = unit_rows(r[sl, :])
        sg1 = sg1 + row_sum(dn * x)
        sb1 = sb1 + row_sum(dn)
    sums[0:1, :], sums[1:2, :], sums[2:3, :] = sg1, sb1, 0.5 * sb4


def g2_kernel(plan, *refs):
    r_, h_, f_ = plan.rows, plan.half, plan.fh
    idx, ucn, ucn_sib, e, e_sib, dz, dz_sib = refs[:7]
    outs, (gfc, gproj) = refs[7:-2], refs[-2:]
    c = idx[plan.core_at()]
    ecols = pl.ds(pl.multiple_of(c * h_, 128), h_)
    gproj[...] = (dot_tn(ucn[:, :f_], e[:, ecols]) + dot_tn(ucn_sib[:, :f_], e_sib[...])).astype(BF)
    put_blocks(plan, idx, outs, lambda t, sh: gproj[pl.ds(pl.multiple_of(sh * 2 * r_ + t * r_, 16), r_), :], r_)
    gfc[...] = (dot_tn(ucn[:, f_:], dz[...]) + dot_tn(ucn_sib[:, f_:], dz_sib[...])).astype(BF)
    put_blocks(plan, idx, outs, lambda t, sh: gfc[pl.ds(pl.multiple_of(sh * r_, 16), r_), t * h_ : (t + 1) * h_], 0)


def b1_kernel(plan, layer, *refs):
    h_, d_, t_, sq = plan.half, plan.width, plan.tokens, plan.seq
    idx, prm, e, dc_a, dc_b, r, h, q, k, v, p = refs[:11]
    refs = refs[11:]
    if layer == 0:
        extra, refs = refs[0], refs[1:]
    weights, refs = refs[:3], refs[3:]
    part, dr, keep, send, sums = refs[:5]
    refs = refs[5:]
    if layer == 1:
        dv_out, refs = refs[0], refs[1:]
    else:
        dv_out, refs = refs[-1], refs[:-1]
    wqk, wv, wo = weights
    dy, dqk, do, acc = refs
    s, c = idx[plan.side_at()], idx[plan.core_at()]
    zero = jnp.zeros((1, d_), F32)
    sb3 = zero
    for i in range(0, t_, STEP):
        sl = slice(i, i + STEP)
        x, inv = unit_rows(r[sl, :])
        dn = dc_a[sl, :].astype(F32) + dc_b[sl, :].astype(F32)
        dd = e[sl, :].astype(F32) + norm_back(dn, x, inv, prm[layer, 1:2, :])
        dr[sl, :] = dd
        dyb = dd.astype(BF)
        dy[sl, :] = dyb
        sb3 = sb3 + row_sum(dyb.astype(F32))
    do[...] = dot_nt(dy[...], wo[...]).astype(BF)
    lanes = h_ // plan.pairs
    low = pair_mask(sq, lanes)
    scale = (lanes // 2) ** -0.5
    for s_ in range(plan.seqs):
        for j in range(plan.pairs):
            rws, cls = slice(s_ * sq, (s_ + 1) * sq), slice(j * lanes, (j + 1) * lanes)
            kcls = slice(h_ + j * lanes, h_ + (j + 1) * lanes)
            q2 = stack_pair(q[rws, cls], low)
            do2 = stack_pair(do[rws, cls], low)
            pr = p[s_ * plan.pairs + j]
            dp = dot_nt(do2, v[rws, cls])
            dv = dot_tn(pr, do2)
            if layer == 0:
                dv = dv + extra[rws, cls].astype(F32) * (s == 1).astype(F32)
            dv_out[rws, cls] = dv.astype(BF)
            pf = pr.astype(F32)
            ds = (pf * (dp - jnp.sum(pf * dp, axis=-1, keepdims=True))).astype(BF)
            dq2 = dot(ds, k[rws, cls])
            dqk[rws, cls] = (jnp.where(low, dq2[:sq], dq2[sq:]) * scale).astype(BF)
            dqk[rws, kcls] = (dot_tn(ds, q2) * scale).astype(BF)
    da = dot_nt(dqk[...], wqk[...])
    dav = dot_nt(dv_out[...], wv[...])
    if layer == 1:
        dav = dav * (s == 0).astype(F32)
    acc[...] = da + dav
    dys = pl.ds(pl.multiple_of(s * h_, 128), h_)
    for core in range(2):

        @pl.when(c == core)
        def _():
            one, two = (keep, send) if core == 0 else (send, keep)
            one[...] = dqk[...]
            two[:, :h_] = dv_out[...]
            two[:, h_:] = dy[:, dys]

    sg0, sb0 = zero, zero
    for i in range(0, t_, STEP):
        sl = slice(i, i + STEP)
        dn = acc[sl, :]
        part[sl, :] = dn.astype(BF)
        x, _ = unit_rows(h[sl, :].astype(F32))
        sg0 = sg0 + row_sum(dn * x)
        sb0 = sb0 + row_sum(dn)
    sums[0:1, :], sums[1:2, :], sums[2:3, :] = sg0, sb0, 0.5 * sb3
    sq_ = row_sum(dqk[...].astype(F32))[:, :h_]
    none = jnp.zeros((1, h_), F32)
    sums[3:4, :] = jnp.where(s == 0, jnp.concatenate([sq_, none], axis=1), jnp.concatenate([none, sq_], axis=1))
    sums[4:5, :] = jnp.concatenate([row_sum(dv_out[...].astype(F32)), none], axis=1)


def g1_kernel(plan, layer, *refs):
    r_, h_, d_, n_ = plan.rows, plan.half, plan.width, plan.count
    idx, a, a_sib, o, o_sib, far, far_sib, keep, got = refs[:9]
    refs = refs[9:]
    if layer == 0:
        tiny, refs = refs[:6], refs[6:]
    outs, refs = refs[:4], refs[4:]
    gatt = refs[0]
    c = idx[plan.core_at()]

    @pl.when(c == 0)
    def _():
        gatt[...] = (dot_tn(a[...], keep[...]) + dot_tn(a_sib[...], got[...])).astype(BF)

    @pl.when(c == 1)
    def _():
        gatt[:, :h_] = (dot_tn(a[...], keep[:, :h_]) + dot_tn(a_sib[...], got[:, :h_])).astype(BF)
        s = idx[plan.side_at()]
        for side, x, y in ((s, o, o_sib), (1 - s, far, far_sib)):
            rows = pl.ds(pl.multiple_of(side * h_, 16), h_)
            at = x.shape[1] - h_
            gatt[rows, h_:] = (dot_tn(x[:, at:], keep[:, h_:]) + dot_tn(y[:, at:], got[:, h_:])).astype(BF)

    put_blocks(plan, idx, outs, lambda t, sh: gatt[pl.ds(pl.multiple_of(sh * r_, 16), r_), t * h_ : (t + 1) * h_], 0)
    if layer == 0:
        tail = refs[1]
        small_sums(plan, idx, tiny, tail)
        half = n_ // 2
        for j in range(n_):
            out, at = outs[0 if j >= half else 2], j % half * (r_ + TAIL) + r_
            out[at : at + TAIL, :] = tail[j]


def small_sums(plan, idx, tiny, tail):
    n_, r_, h_, d_, u_ = plan.count, plan.rows, plan.half, plan.width, plan.unit
    s = idx[plan.side_at()]
    rows = []
    for l in range(2):
        s2, s1, sbf = tiny[3 * l : 3 * l + 3]
        rows += [s1[0:1], s2[0:1], s1[1:2], s2[1:2], s1[3:4], s1[2:3], s2[2:3]]
        bf = sbf[...]
        cut = [jnp.concatenate([bf[:, sh * u_ + i * r_ : sh * u_ + (i + 1) * r_] for sh in range(n_)], axis=1) for i in range(2)]
        for side in range(2):
            on = (s == side).astype(F32)
            rows += [cut[0] * on, cut[1] * on]
    v1, v2 = tiny[1][4:5, :h_], tiny[4][4:5, :h_]
    first = (s == 0).astype(F32)
    vals = jnp.concatenate([v1 * first, v1 * (1.0 - first), v2 * first], axis=1)
    each = plan.values // n_
    pad = jnp.zeros((1, 2 * r_ - each), F32)
    rows.append(jnp.concatenate([vals[:, sh * each : sh * each + r_] for sh in range(n_)], axis=1))
    rows.append(jnp.concatenate([x for sh in range(n_) for x in (vals[:, sh * each + r_ : (sh + 1) * each], pad)], axis=1))
    rows.append(jnp.zeros((TAIL - 24, d_), F32))
    full = jnp.concatenate(rows, axis=0).astype(BF)
    for sh in range(n_):
        block = jnp.concatenate([full[:, sh * r_ : (sh + 1) * r_], jnp.zeros((TAIL, h_ - r_), BF)], axis=1)
        tail[idx[2 * n_ + sh]] = block


def total(refs, terms, rows):
    x = None
    for at, row in terms:
        y = refs[at][row : row + rows, :].astype(F32)
        x = y if x is None else x + y
    return x.astype(BF)


def round_kernel(plans, n, *refs):
    for out, segments in zip(refs[n:], plans):
        row = 0
        for terms, rows in segments:
            out[row : row + rows, :] = total(refs, terms, rows)
            row += rows


def listed(segments):
    arrays, plans = [], []
    for terms, rows in segments:
        named = []
        for x, row in terms:
            at = next((i for i, y in enumerate(arrays) if y is x), len(arrays))
            if at == len(arrays):
                arrays.append(x)
            named.append((at, row))
        plans.append((named, rows))
    return arrays, plans


def run_round(outs):
    arrays, plans = listed([seg for segments in outs for seg in segments])
    cut, at = [], 0
    for segments in outs:
        cut.append(plans[at : at + len(segments)])
        at += len(segments)
    width = arrays[0].shape[1]
    shapes = [((sum(rows for _, rows in segments), width), BF, VM) for segments in outs]
    return call(functools.partial(round_kernel, cut, len(arrays)), vm(*arrays), shapes, [], 1.2)


def pick_kernel(plans, n, side_at, idx, *refs):
    own, send = refs[n:]
    first = idx[side_at] == 0
    sums = [total(refs, terms, rows) for terms, rows in plans]
    size = sums[1].shape[0]
    for t in range(2):
        x, y = sums[2 * t][:size], sums[2 * t + 1]
        own[t * size : (t + 1) * size] = jnp.where(first, x, y)
        send[t * size : (t + 1) * size] = jnp.where(first, y, x)
    if sums[0].shape[0] > size:
        for ref in (own, send):
            ref[2 * size :] = sums[0]


def run_pick(plan, idx, segments):
    arrays, plans = listed(segments)
    one, two = segments[0][1], segments[1][1]
    shape = (2 * two + (one if one > two else 0), plan.half)
    kernel = functools.partial(pick_kernel, plans, len(arrays), plan.side_at())
    return call(kernel, [(idx, SM)] + vm(*arrays), [(shape, BF, VM)] * 2, [], 1.0)


def finish_mlp_kernel(plan, idx, *refs):
    r_, h_, u_ = plan.rows, plan.half, plan.unit
    mlp, (o_fc, o_proj) = refs[:4], refs[4:]
    s, c = idx[plan.side_at()], idx[plan.core_at()]
    per = h_ // u_
    for t in range(2):
        fc = [[None] * 2, [None] * 2]
        for i in range(2):
            a, b = mlp[2 * i], mlp[2 * i + 1]
            for core in range(2):
                x = jnp.where(c == core, a[2 * t * r_ : (2 * t + 2) * r_, :], b[2 * t * r_ : (2 * t + 2) * r_, :])
                fc[i][core] = x[:r_]
                for side in range(2):

                    @pl.when((s == side) if i == 0 else (s != side))
                    def _():
                        lo = side * 2 * r_ + t * r_
                        o_proj[lo : lo + r_, core * h_ : (core + 1) * h_] = x[r_:].astype(F32)

        for core in range(2):
            q = 2 * core + t
            b0 = jnp.where(s == 0, fc[0][core], fc[1][core]).astype(F32)
            b1 = jnp.where(s == 0, fc[1][core], fc[0][core]).astype(F32)
            pieces = [x[:, i * u_ : (i + 1) * u_] for i in range(per) for x in (b0, b1)]
            o_fc[:, 2 * q * h_ : 2 * (q + 1) * h_] = jnp.concatenate(pieces, axis=1)


def finish_att_kernel(plan, idx, *refs):
    r_, h_, d_ = plan.rows, plan.half, plan.width
    att, val = refs[:4], refs[4:6]
    o_qk, o_val, o_out, o_gain, o_shift, o_bf, o_vs = refs[6:]
    s, c = idx[plan.side_at()], idx[plan.core_at()]

    def block(side, core, lo, hi):
        pick = [jnp.where(c == core, att[2 * i][lo:hi, :], att[2 * i + 1][lo:hi, :]) for i in range(2)]
        return jnp.where(s == side, pick[0], pick[1]).astype(F32)

    sm = sum(x[3 * r_ :, :r_].astype(F32) for x in att)
    mine = jnp.where(s == 0, sm[:11], sm[11:22])
    o_gain[...] = mine[0:2]
    o_shift[...] = mine[2:7]
    o_bf[...] = jnp.concatenate([mine[7 + i : 8 + i] for i in range(4)], axis=1)
    o_vs[...] = jnp.concatenate([sm[22:23], sm[23:24, : plan.values // plan.count - r_]], axis=1)
    low, high = block(0, 1, 0, r_), block(1, 1, 0, r_)
    other, rest = jnp.where(c == 1, val[0][:r_, :], val[1][:r_, :]).astype(F32), block(0, 1, 2 * r_, 3 * r_)
    o_val[:, :h_] = jnp.where(s == 0, low, rest)
    o_val[:, h_:d_] = jnp.where(s == 0, high, other)
    o_val[:, d_:] = jnp.where(s == 0, other, low)
    for side in range(2):
        o_out[:, side * h_ : (side + 1) * h_] = block(side, 1, r_, 2 * r_)
        for t in range(2):
            o_qk[:, t * d_ + side * h_ : t * d_ + (side + 1) * h_] = block(side, 0, t * r_, (t + 1) * r_)


def ends_kernel(plan, idx, prm, r, y_a, y_b, dr, da_a, da_b, h, out):
    s = idx[plan.side_at()]

    @pl.when(s == 1)
    def _():
        for i in range(0, plan.tokens, STEP):
            sl = slice(i, i + STEP)
            out[sl, :] = (r[sl, :] + (y_a[sl, : plan.width].astype(F32) + y_b[sl, : plan.width].astype(F32)) + prm[1, 6:7, :]).astype(BF)

    @pl.when(s == 0)
    def _():
        for i in range(0, plan.tokens, STEP):
            sl = slice(i, i + STEP)
            x, inv = unit_rows(h[sl, :].astype(F32))
            dn = da_a[sl, :].astype(F32) + da_b[sl, :].astype(F32)
            out[sl, :] = (dr[sl, :] + norm_back(dn, x, inv, prm[0, 0:1, :])).astype(BF)


VM = pl.BlockSpec(memory_space=pltpu.VMEM)
SM = pl.BlockSpec(memory_space=pltpu.SMEM)
ANY = pl.BlockSpec(memory_space=pl.ANY)
HBM = pl.BlockSpec(memory_space=pltpu.HBM)


def call(kernel, ins, outs, scratch, us, vmem=VMEM_BYTES):
    return pl.pallas_call(
        kernel,
        out_shape=[jax.ShapeDtypeStruct(sh, dt) for sh, dt, _ in outs],
        in_specs=[sp for _, sp in ins],
        out_specs=[sp for _, _, sp in outs],
        scratch_shapes=scratch,
        compiler_params=pltpu.CompilerParams(vmem_limit_bytes=vmem),
        cost_estimate=pl.CostEstimate(flops=int(us * 4.2e8), bytes_accessed=1000, transcendentals=0),
    )(*[x for x, _ in ins])


def vm(*arrays):
    return [(x, VM) for x in arrays]


def hbm(arrays):
    return [(x, ANY) for x in arrays]


def run_weights(plan, layer, idx, chunks):
    w, h, f = plan.width, plan.half, plan.fh
    ins = [(idx, SM)] + vm(*chunks)
    att = call(functools.partial(att_weights_kernel, plan, layer), ins, [((w, w), BF, VM), ((w, h), BF, VM), ((h, w), BF, VM)], [], 1.2)
    outs = [((w, f), BF, VM)] + ([] if layer else [((f, w), BF, VM)])
    mlp = call(functools.partial(mlp_weights_kernel, plan, layer), ins, outs, [], 1.5)
    return att, mlp


def run_proj(plan, idx, parts):
    out = ((plan.fh, plan.width), BF, VM)
    return call(functools.partial(proj_weights_kernel, plan), [(idx, SM)] + vm(*parts), [out], [], 1.0)


def dma_sems(n):
    return pltpu.SemaphoreType.DMA((n,))


def run_pack(plan, arrays):
    r_, h_ = plan.rows, plan.half
    both, one = ((2, 3 * r_, h_), BF, VM), ((r_, h_), BF, VM)
    outs = [both, both, one, one, ((SMALL, h_), BF, VM)]
    scratch = [pltpu.VMEM(x.shape, BF) for x in arrays] + [dma_sems(7)]
    ins = [(x, HBM) for x in arrays]
    return call(functools.partial(pack_kernel, plan), ins, outs, scratch, 1.5, 60 * 1024 * 1024)


def run_param(plan, idx, arrays):
    outs = [((2, 8, plan.width), F32, VM), ((2, 1, plan.fh), F32, VM)]
    scratch = [pltpu.VMEM((2, plan.count, SMALL, plan.half), BF)]
    return call(functools.partial(param_kernel, plan), [(idx, SM)] + vm(*arrays), outs, scratch, 1.0)


def run_f1(plan, layer, idx, prm, inputs, weights):
    t_, h_, d_ = plan.tokens, plan.half, plan.width
    narrow, wide = ((t_, h_), BF, VM), ((t_, d_), BF, VM)
    outs = [wide, narrow, narrow, narrow, ((plan.seqs * plan.pairs, 2 * plan.seq, plan.seq), BF, VM), narrow, wide]
    outs += [wide] if layer else [wide, wide]
    scratch = []
    ins = [(idx, SM)] + vm(prm, *inputs, *weights)
    return call(functools.partial(f1_kernel, plan, layer), ins, outs, scratch, 2.5)


def run_f2(plan, layer, idx, prm, bf, h, pa, pb, weights, *more):
    t_, d_, f_ = plan.tokens, plan.width, plan.fh
    wide = ((t_, d_), BF, VM)
    first = ((t_, d_ + plan.half), BF, VM) if layer else wide
    outs = [first, ((t_, d_), F32, VM), ((t_, f_ + d_), BF, VM), ((t_, f_), BF, VM)]
    scratch = [pltpu.VMEM((t_, f_ // 3), F32)]
    ins = [(idx, SM)] + vm(prm, bf, h, pa, pb, *weights, *more)
    return call(functools.partial(f2_kernel, plan, layer), ins, outs, scratch, 4.4)


def run_b2(plan, layer, idx, prm, gp, r, more, weights):
    t_, d_, f_ = plan.tokens, plan.width, plan.fh
    outs = [((t_, d_), BF, VM)] * 4 + [((t_, plan.half), BF, VM), ((3, d_), F32, VM), ((1, f_), F32, VM)]
    scratch = [pltpu.VMEM((t_, d_), F32), pltpu.VMEM((t_, f_), BF)]
    ins = [(idx, SM)] + vm(prm, gp, r, *more, *weights)
    return call(functools.partial(b2_kernel, plan, layer), ins, outs, scratch, 2.6)


def grad_outs(plan, rows, tail=0):
    return [((plan.count // 2 * r, plan.half), BF, VM) for r in (rows + tail, rows) * 2]


def run_g2(plan, idx, *arrays):
    d_, f_, h_ = plan.width, plan.fh, plan.half
    scratch = [pltpu.VMEM((d_, d_), BF), pltpu.VMEM((f_, h_), BF)]
    ins = [(idx, SM)] + vm(*arrays)
    return call(functools.partial(g2_kernel, plan), ins, grad_outs(plan, 2 * plan.rows), scratch, 4.6)


def run_b1(plan, layer, idx, prm, more, weights):
    t_, d_, h_ = plan.tokens, plan.width, plan.half
    wide, narrow = (t_, d_), (t_, h_)
    outs = [(wide, BF, VM), (wide, F32, VM), (wide, BF, VM), (wide, BF, VM), ((5, d_), F32, VM)]
    scratch = [pltpu.VMEM(wide, BF), pltpu.VMEM(wide, BF), pltpu.VMEM(narrow, BF), pltpu.VMEM(wide, F32)]
    if layer:
        outs.append((narrow, BF, VM))
    else:
        scratch.append(pltpu.VMEM(narrow, BF))
    ins = [(idx, SM)] + vm(prm, *more, *weights)
    return call(functools.partial(b1_kernel, plan, layer), ins, outs, scratch, 0.5 if layer else 4.5)


def run_g1(plan, layer, idx, acts, keep, got, tiny):
    d_, h_ = plan.width, plan.half
    scratch = [pltpu.VMEM((d_, d_), BF)]
    if layer == 0:
        scratch += [pltpu.VMEM((plan.count, TAIL, h_), BF)]
    ins = [(idx, SM)] + vm(*acts, keep, got, *tiny)
    return call(functools.partial(g1_kernel, plan, layer), ins, grad_outs(plan, plan.rows, 0 if layer else TAIL), scratch, 0.3 if layer else 1.8)


def run_finish_mlp(plan, idx, arrays):
    outs = [(sh, F32, VM) for sh in ((plan.rows, plan.ff), (4 * plan.rows, plan.width))]
    return call(functools.partial(finish_mlp_kernel, plan), [(idx, SM)] + vm(*arrays), outs, [], 3.0)


def run_finish_att(plan, idx, arrays):
    r_, d_ = plan.rows, plan.width
    outs = [(sh, F32, VM) for sh in ((r_, 2 * d_), (r_, plan.values), (r_, d_), (2, r_), (5, r_), (1, 4 * r_), (1, plan.values // plan.count))]
    return call(functools.partial(finish_att_kernel, plan), [(idx, SM)] + vm(*arrays), outs, [], 2.5)


def run_ends(plan, idx, arrays):
    return call(functools.partial(ends_kernel, plan), [(idx, SM)] + vm(*arrays), [((plan.tokens, plan.width), BF, VM)], [], 1.9)[0]


def after(x, *earlier):
    return lax.optimization_barrier((x,) + earlier)[0]


def per_device(ends, w_qk, w_value, w_out, w_fc, w_proj, gains, shifts, fc_shift, value_shift):
    s, grp, d = lax.axis_index("section"), lax.axis_index("group"), lax.axis_index("dp")
    c = grp % 2
    count, groups = lax.axis_size("dp"), lax.axis_size("group")
    rows, width = w_qk.shape[1], ends.shape[3]
    half = width // 2
    seqs, seq = ends.shape[1], ends.shape[2]
    tokens = seqs * seq
    plan = Plan(count, rows, width, w_fc.shape[2], w_value.shape[1], tokens, seq, HEADS // 2)
    table = plan.table(groups)
    idx = lax.dynamic_slice(jnp.asarray(table), (s, grp, d, 0), (1, 1, 1, table.shape[3])).reshape(-1)
    first, even = s == 0, d % 2 == 0

    def swap_x(x):
        return lax.ppermute(x, "section", [(0, 1), (1, 0)])

    def swap_c(x):
        return lax.ppermute(x, "group", [(i, i ^ 1) for i in range(groups)])

    def swap_d(x, bit):
        return lax.ppermute(x, "dp", [(i, i ^ bit) for i in range(count)])

    hc = count // 2
    spread = [
        [(l * count + i, (i // hc) * count + 2 * (i % hc) + (l if w == 0 else 1 - l)) for l in range(2) for i in range(count)]
        for w in range(2)
    ]
    mine, send, o_lo, o_hi, small = run_pack(
        plan, (w_qk[0], w_fc[0], w_proj[0], w_out[0], gains[0], shifts[0], fc_shift)
    )
    got = swap_x(send)
    small_got = swap_x(small)
    o_a = lax.ppermute(o_lo, ("section", "dp"), spread[0])
    o_b = lax.ppermute(o_hi, ("section", "dp"), spread[1])
    ends_own = ends[0].reshape(tokens, width)
    ends_got = swap_x(after(ends_own, got))
    v_side = (lax.dynamic_slice_in_dim(w_value, s * half, half, 1), w_value[:, width:])
    o_side = (jnp.where(even, o_a, o_b), jnp.where(even, o_b, o_a))

    def head(t, l, other):
        x = jnp.where(first if l == 0 else ~first, mine[t, :rows], got[t, :rows])
        return jnp.where(c == 0, x, other)

    vs_rows = [jnp.pad(x, (0, half - x.shape[0]))[None] for x in (value_shift[:rows], value_shift[rows:])]
    vs_rows = jnp.pad(jnp.concatenate(vs_rows, axis=0), ((11, SMALL - 13), (0, 0)))
    params = [jnp.where(first, x, y) + vs_rows for x, y in ((small, small_got), (small_got, small))]
    early, late = [], []
    for t, side in ((0, v_side), (1, o_side)):
        x, y = mine[t, rows:], got[t, rows:]
        second = jnp.where(first, y, x)
        early.append(jnp.concatenate([head(t, 0, side[0]), jnp.where(first, x, y), head(t, 1, side[1]), second[:rows], params[t]], axis=0))
        late.append(second[rows:])

    routes = [[(a, b) for a, b in zip(order, order[1:] + order[:1])] for order in (ring_order(count), ring_order(count)[::-1])]

    def ring(x):
        return lax.optimization_barrier([lax.ppermute(x[t], "dp", routes[t]) for t in range(2)])

    steps = [[after(x, idx) for x in early]]
    sibs = []
    for n in range(count - 1):
        sibs.append([swap_c(x) for x in steps[-1]])
        steps.append(ring(steps[-1]))
        if n == 2:
            steps[-1] = [after(x, ends_got) for x in steps[-1]]
        if n >= 2:
            steps[-1] = [after(x, *sibs[n - 1]) for x in steps[-1]]
    sibs.append([swap_c(x) for x in steps[-1]])
    chunks = [y for t in range(2) for y in [x[t] for x in steps] + [x[t] for x in sibs]]
    prm, bf = run_param(plan, idx, [x[t] for t in range(2) for x in steps])
    (att_w0, mlp_w0), (att_w1, fc_w1) = (run_weights(plan, l, idx, chunks) for l in range(2))

    def doubled(x, *others):
        k = (x[0].shape[0] // rows).bit_length() - 1
        bits = [plan.orders[t][k] for t in range(2)]
        if bits[0] == bits[1]:
            size = x[0].shape[0]
            both = swap_d(after(jnp.concatenate(x, axis=0), *others), bits[0])
            got = [both[:size], both[size:]]
        else:
            got = [swap_d(after(x[t], *others), bits[t]) for t in range(2)]
        return got

    have = late
    got = doubled(have, *steps[-2])
    part, q0, k0, v0, p0, o0, a0, h0, cot = run_f1(plan, 0, idx, prm, (ends_own, ends_got), att_w0)
    sib0 = [swap_c(a0), swap_c(o0)]
    for _ in range(plan.bits - 2):
        have = [jnp.concatenate(x, axis=0) for x in zip(have, got)]
        got = doubled(have, part)
    sib0 += got + list(att_w1)
    have = [jnp.concatenate(x, axis=0) for x in zip(have, got)]
    got = after(swap_x(part), *sib0)
    part, r0, ucn0, gp0 = run_f2(plan, 0, idx, prm, bf, h0, part, got, mlp_w0)
    more = doubled(have, got)
    have_sib = [swap_c(after(x, part)) for x in have]
    ucn0_sib = swap_c(ucn0)
    got = after(swap_x(part), ucn0_sib, *have_sib, *more)
    part, q1, k1, v1, p1, o1, a1, h1 = run_f1(plan, 1, idx, prm, (r0, part, got, v0), att_w1)
    sib1 = [swap_c(a1), swap_c(o1)]
    got = after(swap_x(part), *sib1)
    parts = [x for t in range(2) for x in (have[t], more[t], have_sib[t], swap_c(after(more[t], part)))]
    mlp_w1 = fc_w1 + run_proj(plan, idx, parts)
    y_part, r1, ucn1, gp1 = run_f2(plan, 1, idx, prm, bf, h1, part, got, mlp_w1, o0)

    class Sum:
        def __init__(self, g):
            self.first, self.keep = g[:2], g[2:]
            self.rows = [x.shape[0] // hc for x in self.keep]
            self.came = [[], []]

        def terms(self, t, low):
            return [(self.keep[t], low * self.rows[t])] + [(x, at + low * self.rows[t]) for x, at in self.came[t]]

        def bit(self, t):
            return plan.orders[t][plan.bits - 1 - len(self.came[t])]

        def segment(self, t):
            steps = len(self.came[t])
            if steps == 0:
                return [(self.first[t], 0)], self.first[t].shape[0]
            low = count >> (steps + 1)
            return self.terms(t, low), low * self.rows[t]

    def one_round(sums, *others):
        sums = [x for x in sums if len(x.came[0]) < plan.bits]
        if not sums:
            return []
        by_bit = {}
        for x in sums:
            for t in range(2):
                by_bit.setdefault(x.bit(t), []).append((x, t, x.segment(t)))
        bits = sorted(by_bit)
        if all(len(by_bit[b]) == 1 and not by_bit[b][0][0].came[0] for b in bits):
            outs = [by_bit[b][0][2][0][0][0] for b in bits]
        else:
            outs = run_round([[seg for _, _, seg in by_bit[b]] for b in bits])
        got = []
        for b, out in zip(bits, outs):
            here = swap_d(after(out, *others, *one_round.last), b)
            row = 0
            for x, t, (_, rows_) in by_bit[b]:
                x.came[t].append((here, row))
                row += rows_
            got.append(here)
        one_round.last = got
        return got

    one_round.last = []

    def over_pairs(x):
        total = x
        for n in range(1, groups // 2):
            total = total + lax.ppermute(x, "group", [(i, (i + 2 * n) % groups) for i in range(groups)])
        return total

    part, e, z_keep, z_send, e_send, s2_1, sbf_1 = run_b2(plan, 1, idx, prm, gp1, r1, (cot,), mlp_w1)
    got = swap_x(part)
    mlp1 = Sum(run_g2(plan, idx, ucn1, swap_c(ucn1), e, swap_c(e_send), z_keep, swap_c(z_send)))
    got = after(got, *mlp1.first)
    one_round([mlp1])
    part, dr, keep, send, s1_1, dv1 = run_b1(plan, 1, idx, prm, (cot, part, got, r1, h1, q1, k1, v1, p1), att_w1)
    o1_far = swap_x(after(o1, got))
    got = swap_x(part)
    acts = [a1, sib1[0], o1, sib1[1], o1_far, swap_c(o1_far)]
    att1 = Sum(run_g1(plan, 1, idx, acts, keep, swap_c(send), ()))
    got = after(got, *att1.first)
    came = one_round([mlp1, att1])
    part, e, z_keep, z_send, e_send, s2_0, sbf_0 = run_b2(plan, 0, idx, prm, gp0, r0, (dr, part, got, h1), mlp_w0)
    got = swap_x(part)
    mlp0 = Sum(run_g2(plan, idx, after(ucn0, *came), ucn0_sib, e, swap_c(e_send), z_keep, swap_c(z_send)))
    got = after(got, *mlp0.first)
    came = one_round([mlp1, att1, mlp0])
    y_got = swap_x(after(y_part, got))
    part, dr, keep, send, s1_0 = run_b1(plan, 0, idx, prm, (e, part, got, r0, h0, q0, k0, v0, p0, dv1), att_w0)
    acts = [a0, sib0[0], o0, sib0[1], y_got, swap_c(y_got)]
    att0 = Sum(run_g1(plan, 0, idx, acts, keep, swap_c(after(send, came[-1])), (s2_0, s1_0, sbf_0, s2_1, s1_1, sbf_1)))
    sums = [att0, att1, mlp0, mlp1]
    x_got = swap_x(after(part, y_got))
    res = run_ends(plan, idx, (prm, r1, y_part, y_got, dr, part, x_got, h0)).reshape(1, seqs, seq, width)
    one_round(sums)
    for _ in range(plan.bits - 2):
        one_round(sums, x_got)

    def ending(sums, first, *others):
        own, send = (over_pairs(x) for x in run_pick(plan, after(idx, *first), [(x.terms(t, 0), x.rows[t]) for t in range(2) for x in sums]))
        far = after(swap_x(send), *others)
        return [own, swap_c(own), far, swap_c(far)], send

    arrived = one_round.last
    one_round(sums)
    e_mlp, _ = ending((mlp0, mlp1), arrived)
    o_fc, o_proj = run_finish_mlp(plan, idx, e_mlp)
    e_att, sent = ending((att0, att1), (), o_fc, res)
    o_qk, o_val, o_out, o_gain, o_shift, o_bf, o_vs = run_finish_att(plan, idx, e_att + [sent, swap_c(sent)])

    return (res, o_qk[None], o_val, o_out[None], o_fc[None], o_proj[None], o_gain[None], o_shift[None], o_bf, o_vs[0])


def solution(mesh):
    placed = (
        P("section", ("group", "dp"), None, None),
        P("section", "dp", None),
        P("dp", None),
        P("section", "dp", None),
        P("section", "dp", None),
        P("section", "dp", None),
        P("section", None, "dp"),
        P("section", None, "dp"),
        P("section", "dp"),
        P("dp"),
    )
    return jax.shard_map(per_device, mesh=mesh, in_specs=placed, out_specs=placed, check_vma=False)
```

```python
import functools

import jax
import jax.numpy as jnp
import numpy as np
from jax import lax
from jax.experimental import pallas as pl
from jax.experimental.pallas import tpu as pltpu
from jax.sharding import PartitionSpec as P

HEADS = 12
BF = jnp.bfloat16
F32 = jnp.float32
norm_eps = 1e-05
masked_score = -1e30
TAIL = 32
SMALL = 16
STEP = 32
VMEM_BYTES = 16 * 1024 * 1024


def dot(a, b):
    return jnp.dot(a, b, preferred_element_type=F32)


def dot_tn(a, b):
    return lax.dot_general(a, b, (((0,), (0,)), ((), ())), preferred_element_type=F32)


def dot_nt(a, b):
    return lax.dot_general(a, b, (((1,), (1,)), ((), ())), preferred_element_type=F32)


def unit_rows(v):
    centered = v - jnp.mean(v, axis=-1, keepdims=True)
    inv = lax.rsqrt(jnp.mean(centered * centered, axis=-1, keepdims=True) + norm_eps)
    return centered * inv, inv


def norm_back(dn, x, inv, gain):
    scaled = dn * gain
    inner = jnp.mean(scaled * x, axis=-1, keepdims=True)
    return inv * (scaled - jnp.mean(scaled, axis=-1, keepdims=True) - x * inner)


def row_sum(v):
    return jnp.sum(v, axis=0, keepdims=True)


def ring_order(count):
    wide = 2 if count < 16 else 4
    tall = count // wide
    order = [i * wide for i in range(tall)]
    for n, row in enumerate(reversed(range(tall))):
        cols = range(1, wide)
        order += [row * wide + col for col in (cols if n % 2 == 0 else reversed(cols))]
    return order


class Plan:
    def __init__(self, count, rows, width, ff, values, tokens, seq, heads):
        self.count, self.rows, self.width, self.half = count, rows, width, width // 2
        self.ff, self.fh, self.unit, self.values = ff, ff // 2, ff // count // 2, values
        self.tokens, self.seq, self.seqs = tokens, seq, tokens // seq
        self.pairs = heads // 2
        self.bits = count.bit_length() - 1
        down = [1 << i for i in reversed(range(self.bits))]
        other = down[:-2] + [down[-1], down[-2]]
        self.orders = (down, other)
        self.masks = []
        for order in self.orders:
            mask = [0] * count
            for j in range(count):
                for k, bit in enumerate(order):
                    if j >> k & 1:
                        mask[j] ^= bit
            self.masks.append(mask)

    def core_at(self):
        return 7 * self.count

    def side_at(self):
        return 7 * self.count + 1

    def table(self, groups):
        n = self.count
        out = np.zeros((2, groups, n, 7 * n + 2), np.int32)
        order = ring_order(n)
        for p, d in enumerate(order):
            for t in range(2):
                out[:, :, d, t * n : (t + 1) * n] = [d ^ m for m in self.masks[t]]
                out[:, :, d, (3 + t) * n : (4 + t) * n] = [order[(p - (1 - 2 * t) * j) % n] for j in range(n)]
            for j, m in enumerate(self.masks[0]):
                out[:, :, d, 2 * n + (d ^ m)] = j
            for j in range(n):
                for t in range(2):
                    out[:, :, d, (5 + t) * n + order[(p - (1 - 2 * t) * j) % n]] = j
        out[:, :, :, 7 * n] = (np.arange(groups) % 2)[None, :, None]
        out[:, :, :, 7 * n + 1] = np.arange(2)[:, None, None]
        return out


def aligned(x, size):
    return x if isinstance(x, int) else pl.multiple_of(x, size)


def dma(src, dst, sem):
    return pltpu.make_async_copy(src, dst, sem)


def wait_all(ref, sem):
    dma(ref, ref, sem).wait()


def chunk_refs(plan, idx, chunks, row):
    for j in range(plan.count):
        for t in range(2):
            for other in range(2):
                ref = chunks[(t * 2 + other) * plan.count + j]
                yield t, other, idx[(3 + t) * plan.count + j], ref.at[pl.ds(row, plan.rows), :]


def place_att(plan, layer, idx, chunks, wqk, wv, wo):
    r_, h_ = plan.rows, plan.half
    c = idx[plan.core_at()]
    for t, other, sh, src in chunk_refs(plan, idx, chunks, 3 * r_ * layer):
        core = 1 - c if other else c
        row = pl.multiple_of(sh * r_, 16)

        @pl.when(core == 0)
        def _():
            wqk[pl.ds(row, r_), t * h_ : (t + 1) * h_] = src[...]

        @pl.when(core == 1)
        def _():
            if t == 0:
                wv[pl.ds(row, r_), :] = src[...]
            else:
                orow = pl.multiple_of((sh // 2) * r_, 16)
                ocol = pl.multiple_of((sh % 2) * h_, 128)
                wo[pl.ds(orow, r_), pl.ds(ocol, h_)] = src[...]


def place_mlp(plan, layer, idx, chunks, wfc, wproj):
    r_, h_ = plan.rows, plan.half
    c = idx[plan.core_at()]
    for kind in range(1 if layer else 2):
        for t, other, sh, src in chunk_refs(plan, idx, chunks, ((4 if layer else 1) + kind) * r_):
            core = 1 - c if other else c
            if kind == 0:
                row = pl.multiple_of(sh * r_, 16)
                col = pl.multiple_of((2 * core + t) * h_, 128)
                wfc[pl.ds(row, r_), pl.ds(col, h_)] = src[...]
            else:
                row = pl.multiple_of(sh * 2 * r_ + t * r_, 16)
                col = pl.multiple_of(core * h_, 128)
                wproj[pl.ds(row, r_), pl.ds(col, h_)] = src[...]


def put_blocks(plan, idx, outs, pick, row0):
    n_, r_ = plan.count, plan.rows
    half = n_ // 2
    for j in reversed(range(n_)):
        for t in range(2):
            out = outs[2 * (0 if j >= half else 1) + t]
            at = j % half * (out.shape[0] // half) + row0
            out[at : at + r_, :] = pick(t, idx[t * n_ + j])


def pack_kernel(plan, *refs):
    from_hbm, (mine, send, o_a, o_b, small), here, sems = refs[:7], refs[7:12], refs[12:19], refs[19]
    for i, ref in enumerate(here):
        dma(from_hbm[i], ref, sems.at[i]).start()
    for i, ref in enumerate(here):
        wait_all(ref, sems.at[i])
    wqk, wfc, wproj, wout, gains, shifts, fc_shift = here
    r_, h_, d_, u_ = plan.rows, plan.half, plan.width, plan.unit
    per = h_ // u_
    s, c = lax.axis_index("section"), lax.rem(lax.axis_index("group"), 2)
    lo, hi = wout[:, :h_], wout[:, h_:]
    o_a[...] = jnp.where(s == 0, lo, hi)
    o_b[...] = jnp.where(s == 0, hi, lo)
    rows = [gains[...], shifts[...]] + [fc_shift[:, i * r_ : (i + 1) * r_] for i in range(4)]
    rows = jnp.concatenate([x.astype(F32) for x in rows] + [jnp.zeros((SMALL - 11, r_), F32)], axis=0)
    small[...] = jnp.concatenate([rows, jnp.zeros((SMALL, h_ - r_), F32)], axis=1).astype(BF)
    for side in range(2):
        for core in range(2):
            for keep in range(2):
                out = mine if keep else send

                @pl.when(jnp.logical_and(c == core, s == (side if keep else 1 - side)))
                def _():
                    for t in range(2):
                        lo = t * d_ + side * h_
                        out[t, :r_] = wqk[:, lo : lo + h_]
                        q = 2 * core + t
                        cols = [(q * per + i) * 2 * u_ + side * u_ for i in range(per)]
                        out[t, r_ : 2 * r_] = jnp.concatenate([wfc[:, x : x + u_] for x in cols], axis=1)
                        row = side * 2 * r_ + t * r_
                        out[t, 2 * r_ :] = wproj[row : row + r_, core * h_ : (core + 1) * h_]


def param_kernel(plan, idx, *refs):
    n_, r_, h_, d_ = plan.count, plan.rows, plan.half, plan.width
    s = idx[plan.side_at()]
    steps, (prm, bf, stack) = refs[: 2 * n_], refs[2 * n_ :]
    for j, ref in enumerate(steps):
        stack[j // n_, j % n_] = ref[5 * r_ :, :]
    pairs = [[stack[t, idx[(5 + t) * n_ + sh]][:, :r_].astype(F32) for t in range(2)] for sh in range(n_)]
    more = plan.values // n_ - r_
    vals = jnp.concatenate([x for b, _ in pairs for x in (b[11:12, :], b[12:13, :more])], axis=1)
    for l in range(2):
        blocks = [b[l] for b in pairs]
        m = jnp.concatenate([b[:7] for b in blocks], axis=1)
        prm[l, 0:7] = m
        bq = jnp.where(s == 0, m[4:5, :h_], m[4:5, h_:])
        prm[l, 4:5] = jnp.concatenate([bq, jnp.zeros((1, d_ - h_), F32)], axis=1)
        if l == 0:
            bv = jnp.where(s == 0, vals[:, :h_], vals[:, h_:d_])
        else:
            bv = vals[:, d_:]
        prm[l, 7:8] = jnp.concatenate([bv, jnp.zeros((1, d_ - h_), F32)], axis=1)
        sides = []
        for side in range(2):
            row = 7 + 2 * side
            sides.append(jnp.concatenate([b[row + i : row + i + 1] for b in blocks for i in range(2)], axis=1))
        bf[l] = jnp.where(s == 0, sides[0], sides[1])


def att_weights_kernel(plan, layer, *refs):
    place_att(plan, layer, refs[0], refs[1:-3], *refs[-3:])


def mlp_weights_kernel(plan, layer, *refs):
    outs = refs[1 + 4 * plan.count :]
    place_mlp(plan, layer, refs[0], refs[1 : 1 + 4 * plan.count], outs[0], outs[-1])


def proj_weights_kernel(plan, *refs):
    n_, r_, h_ = plan.count, plan.rows, plan.half
    idx, parts, wproj = refs[0], refs[1:9], refs[9]
    c = idx[plan.core_at()]
    for t in range(2):
        for other in range(2):
            core = 1 - c if other else c
            for j in range(n_):
                at = j % (n_ // 2) * r_
                row = pl.multiple_of(idx[t * n_ + j] * 2 * r_ + t * r_, 16)
                src = parts[(2 * t + other) * 2 + j // (n_ // 2)]
                wproj[pl.ds(row, r_), pl.ds(pl.multiple_of(core * h_, 128), h_)] = src[at : at + r_, :]


def pair_mask(seq, lanes):
    return lax.broadcasted_iota(jnp.int32, (seq, lanes), 1) < lanes // 2


def stack_pair(x, low):
    zero = jnp.zeros_like(x)
    return jnp.concatenate([jnp.where(low, x, zero), jnp.where(low, zero, x)], axis=0)


def f1_kernel(plan, layer, *refs):
    h_, t_, sq = plan.half, plan.tokens, plan.seq
    idx, prm, refs = refs[0], refs[1], refs[2:]
    if layer == 1:
        r_up, pa, pb, v_old = refs[:4]
        refs = refs[4:]
    else:
        here, there = refs[:2]
        refs = refs[2:]
    weights, refs = refs[:3], refs[3:]
    part, q, k, v, p, o, a, h = refs[:8]
    if layer == 0:
        cot = refs[8]
    wqk, wv, wo = weights
    first = idx[plan.side_at()] == 0
    for i in range(0, t_, STEP):
        sl = slice(i, i + STEP)
        if layer == 1:
            hh = r_up[sl, :] + (pa[sl, :].astype(F32) + pb[sl, :].astype(F32)) + prm[0, 6:7, :]
            h[sl, :] = hh.astype(BF)
        else:
            mine, theirs = here[sl, :], there[sl, :]
            h[sl, :] = jnp.where(first, mine, theirs)
            cot[sl, :] = jnp.where(first, theirs, mine)
        x, _ = unit_rows(h[sl, :].astype(F32))
        a[sl, :] = (x * prm[layer, 0:1, :] + prm[layer, 2:3, :]).astype(BF)
    qk = dot(a[...], wqk[...])
    q[...] = (qk[:, :h_] + prm[layer, 4:5, :h_]).astype(BF)
    k[...] = qk[:, h_:].astype(BF)
    val = (dot(a[...], wv[...]) + prm[layer, 7:8, :h_]).astype(BF)
    if layer == 1:
        val = jnp.where(idx[plan.side_at()] == 1, v_old[...], val)
    v[...] = val
    lanes = h_ // plan.pairs
    low = pair_mask(sq, lanes)
    causal = lax.broadcasted_iota(jnp.int32, (2 * sq, sq), 0) % sq >= lax.broadcasted_iota(jnp.int32, (2 * sq, sq), 1)
    scale = (lanes // 2) ** -0.5
    for s_ in range(plan.seqs):
        for j in range(plan.pairs):
            rws, cls = slice(s_ * sq, (s_ + 1) * sq), slice(j * lanes, (j + 1) * lanes)
            q2 = stack_pair(q[rws, cls], low)
            sc = jnp.where(causal, dot_nt(q2, k[rws, cls]) * scale, masked_score)
            ex = jnp.exp(sc - jnp.max(sc, axis=-1, keepdims=True))
            pr = (ex / jnp.sum(ex, axis=-1, keepdims=True)).astype(BF)
            p[s_ * plan.pairs + j] = pr
            o2 = dot(pr, v[rws, cls])
            o[rws, cls] = jnp.where(low, o2[:sq], o2[sq:]).astype(BF)
    part[...] = dot(o[...], wo[...]).astype(BF)


def f2_kernel(plan, layer, *refs):
    t_ = plan.tokens
    idx, prm, bf, h, pa, pb = refs[:6]
    if layer == 1:
        o_up, refs = refs[8:10], refs[:8] + refs[10:]
    weights, refs = refs[6:8], refs[8:]
    part, r, ucn, gp, *oo, z = refs
    wfc, wproj = weights
    f_ = plan.fh
    for i in range(0, t_, STEP):
        sl = slice(i, i + STEP)
        rr = h[sl, :].astype(F32) + (pa[sl, :].astype(F32) + pb[sl, :].astype(F32)) + prm[layer, 5:6, :]
        r[sl, :] = rr
        x, _ = unit_rows(rr)
        ucn[sl, f_:] = (x * prm[layer, 1:2, :] + prm[layer, 3:4, :]).astype(BF)
    cols = plan.fh // 3
    for j in range(3):
        cs = slice(j * cols, (j + 1) * cols)
        z[...] = dot(ucn[:, f_:], wfc[:, cs])

        def body(i, carry):
            sl = pl.ds(pl.multiple_of(i * STEP, STEP), STEP)
            zz = z[sl, :] + bf[layer, :, cs]
            sq_ = zz * zz
            th = jnp.tanh(0.7978845608 * zz * (1.0 + 0.044715 * sq_))
            hp = 0.5 * (1.0 + th)
            ucn[sl, cs] = (zz * hp).astype(BF)
            slope = 0.7978845608 * (1.0 + 3 * 0.044715 * sq_)
            gp[sl, cs] = (hp + 0.5 * zz * (1.0 - th * th) * slope).astype(BF)
            return carry

        lax.fori_loop(0, t_ // STEP, body, 0)
    part[...] = dot(ucn[:, :f_], wproj[...]).astype(BF)
    if layer == 1:
        oo[0][:, : plan.half] = o_up[0][...]
        oo[0][:, plan.half :] = o_up[1][...]


def b2_kernel(plan, layer, *refs):
    d_, t_, f_ = plan.width, plan.tokens, plan.fh
    idx, prm, gp, r = refs[:4]
    refs = refs[4:]
    if layer == 1:
        e, refs = refs[0], refs[1:]
    else:
        dr, da_a, da_b, h_up = refs[:4]
        refs = refs[4:]
    weights, refs = refs[:2], refs[2:]
    part, e_out, z_keep, z_send, e_send, sums, sbf = refs[:7]
    h_, c = plan.half, idx[plan.core_at()]
    wfc, wproj = weights
    acc, dz = refs[-2:]
    zero = jnp.zeros((1, d_), F32)
    sb4 = zero
    for i in range(0, t_, STEP):
        sl = slice(i, i + STEP)
        if layer == 0:
            x, inv = unit_rows(h_up[sl, :].astype(F32))
            dn = da_a[sl, :].astype(F32) + da_b[sl, :].astype(F32)
            ee = (dr[sl, :] + norm_back(dn, x, inv, prm[1, 0:1, :])).astype(BF)
        else:
            ee = e[sl, :]
        e_out[sl, :] = ee
        sb4 = sb4 + row_sum(ee.astype(F32))
    cols = f_ // 3
    for j in range(3):
        cs = slice(j * cols, (j + 1) * cols)
        dzj = (dot_nt(e_out[...], wproj[cs, :]) * gp[:, cs].astype(F32)).astype(BF)
        dz[:, cs] = dzj
        sbf[:, cs] = row_sum(dzj.astype(F32))
    z_keep[...] = dz[:, pl.ds(pl.multiple_of(c * d_, 128), d_)]
    z_send[...] = dz[:, pl.ds(pl.multiple_of((1 - c) * d_, 128), d_)]
    e_send[...] = e_out[:, pl.ds(pl.multiple_of((1 - c) * h_, 128), h_)]
    acc[...] = dot_nt(dz[...], wfc[...])
    sg1, sb1 = zero, zero
    for i in range(0, t_, STEP):
        sl = slice(i, i + STEP)
        dn = acc[sl, :]
        part[sl, :] = dn.astype(BF)
        x, _ = unit_rows(r[sl, :])
        sg1 = sg1 + row_sum(dn * x)
        sb1 = sb1 + row_sum(dn)
    sums[0:1, :], sums[1:2, :], sums[2:3, :] = sg1, sb1, 0.5 * sb4


def g2_kernel(plan, *refs):
    r_, h_, f_ = plan.rows, plan.half, plan.fh
    idx, ucn, ucn_sib, e, e_sib, dz, dz_sib = refs[:7]
    outs, (gfc, gproj) = refs[7:-2], refs[-2:]
    c = idx[plan.core_at()]
    ecols = pl.ds(pl.multiple_of(c * h_, 128), h_)
    gproj[...] = (dot_tn(ucn[:, :f_], e[:, ecols]) + dot_tn(ucn_sib[:, :f_], e_sib[...])).astype(BF)
    put_blocks(plan, idx, outs, lambda t, sh: gproj[pl.ds(pl.multiple_of(sh * 2 * r_ + t * r_, 16), r_), :], r_)
    gfc[...] = (dot_tn(ucn[:, f_:], dz[...]) + dot_tn(ucn_sib[:, f_:], dz_sib[...])).astype(BF)
    put_blocks(plan, idx, outs, lambda t, sh: gfc[pl.ds(pl.multiple_of(sh * r_, 16), r_), t * h_ : (t + 1) * h_], 0)


def b1_kernel(plan, layer, *refs):
    h_, d_, t_, sq = plan.half, plan.width, plan.tokens, plan.seq
    idx, prm, e, dc_a, dc_b, r, h, q, k, v, p = refs[:11]
    refs = refs[11:]
    if layer == 0:
        extra, refs = refs[0], refs[1:]
    weights, refs = refs[:3], refs[3:]
    part, dr, keep, send, sums = refs[:5]
    refs = refs[5:]
    if layer == 1:
        dv_out, refs = refs[0], refs[1:]
    else:
        dv_out, refs = refs[-1], refs[:-1]
    wqk, wv, wo = weights
    dy, dqk, do, acc = refs
    s, c = idx[plan.side_at()], idx[plan.core_at()]
    zero = jnp.zeros((1, d_), F32)
    sb3 = zero
    for i in range(0, t_, STEP):
        sl = slice(i, i + STEP)
        x, inv = unit_rows(r[sl, :])
        dn = dc_a[sl, :].astype(F32) + dc_b[sl, :].astype(F32)
        dd = e[sl, :].astype(F32) + norm_back(dn, x, inv, prm[layer, 1:2, :])
        dr[sl, :] = dd
        dyb = dd.astype(BF)
        dy[sl, :] = dyb
        sb3 = sb3 + row_sum(dyb.astype(F32))
    do[...] = dot_nt(dy[...], wo[...]).astype(BF)
    lanes = h_ // plan.pairs
    low = pair_mask(sq, lanes)
    scale = (lanes // 2) ** -0.5
    for s_ in range(plan.seqs):
        for j in range(plan.pairs):
            rws, cls = slice(s_ * sq, (s_ + 1) * sq), slice(j * lanes, (j + 1) * lanes)
            kcls = slice(h_ + j * lanes, h_ + (j + 1) * lanes)
            q2 = stack_pair(q[rws, cls], low)
            do2 = stack_pair(do[rws, cls], low)
            pr = p[s_ * plan.pairs + j]
            dp = dot_nt(do2, v[rws, cls])
            dv = dot_tn(pr, do2)
            if layer == 0:
                dv = dv + extra[rws, cls].astype(F32) * (s == 1).astype(F32)
            dv_out[rws, cls] = dv.astype(BF)
            pf = pr.astype(F32)
            ds = (pf * (dp - jnp.sum(pf * dp, axis=-1, keepdims=True))).astype(BF)
            dq2 = dot(ds, k[rws, cls])
            dqk[rws, cls] = (jnp.where(low, dq2[:sq], dq2[sq:]) * scale).astype(BF)
            dqk[rws, kcls] = (dot_tn(ds, q2) * scale).astype(BF)
    da = dot_nt(dqk[...], wqk[...])
    dav = dot_nt(dv_out[...], wv[...])
    if layer == 1:
        dav = dav * (s == 0).astype(F32)
    acc[...] = da + dav
    dys = pl.ds(pl.multiple_of(s * h_, 128), h_)
    for core in range(2):

        @pl.when(c == core)
        def _():
            one, two = (keep, send) if core == 0 else (send, keep)
            one[...] = dqk[...]
            two[:, :h_] = dv_out[...]
            two[:, h_:] = dy[:, dys]

    sg0, sb0 = zero, zero
    for i in range(0, t_, STEP):
        sl = slice(i, i + STEP)
        dn = acc[sl, :]
        part[sl, :] = dn.astype(BF)
        x, _ = unit_rows(h[sl, :].astype(F32))
        sg0 = sg0 + row_sum(dn * x)
        sb0 = sb0 + row_sum(dn)
    sums[0:1, :], sums[1:2, :], sums[2:3, :] = sg0, sb0, 0.5 * sb3
    sq_ = row_sum(dqk[...].astype(F32))[:, :h_]
    none = jnp.zeros((1, h_), F32)
    sums[3:4, :] = jnp.where(s == 0, jnp.concatenate([sq_, none], axis=1), jnp.concatenate([none, sq_], axis=1))
    sums[4:5, :] = jnp.concatenate([row_sum(dv_out[...].astype(F32)), none], axis=1)


def g1_kernel(plan, layer, *refs):
    r_, h_, d_, n_ = plan.rows, plan.half, plan.width, plan.count
    idx, a, a_sib, o, o_sib, far, far_sib, keep, got = refs[:9]
    refs = refs[9:]
    if layer == 0:
        tiny, refs = refs[:6], refs[6:]
    outs, refs = refs[:4], refs[4:]
    gatt = refs[0]
    c = idx[plan.core_at()]

    @pl.when(c == 0)
    def _():
        gatt[...] = (dot_tn(a[...], keep[...]) + dot_tn(a_sib[...], got[...])).astype(BF)

    @pl.when(c == 1)
    def _():
        gatt[:, :h_] = (dot_tn(a[...], keep[:, :h_]) + dot_tn(a_sib[...], got[:, :h_])).astype(BF)
        s = idx[plan.side_at()]
        apart = far.shape[1] - h_
        for side, x, y, at in ((s, o, o_sib, 0), (1 - s, far, far_sib, apart)):
            rows = pl.ds(pl.multiple_of(side * h_, 16), h_)
            gatt[rows, h_:] = (dot_tn(x[:, :h_], keep[:, h_:]) + dot_tn(y[:, at:], got[:, h_:])).astype(BF)

    put_blocks(plan, idx, outs, lambda t, sh: gatt[pl.ds(pl.multiple_of(sh * r_, 16), r_), t * h_ : (t + 1) * h_], 0)
    if layer == 0:
        tail = refs[1]
        small_sums(plan, idx, tiny, tail)
        half = n_ // 2
        for j in range(n_):
            out, at = outs[0 if j >= half else 2], j % half * (r_ + TAIL) + r_
            out[at : at + TAIL, :] = tail[j]


def small_sums(plan, idx, tiny, tail):
    n_, r_, h_, d_, u_ = plan.count, plan.rows, plan.half, plan.width, plan.unit
    s = idx[plan.side_at()]
    rows = []
    for l in range(2):
        s2, s1, sbf = tiny[3 * l : 3 * l + 3]
        rows += [s1[0:1], s2[0:1], s1[1:2], s2[1:2], s1[3:4], s1[2:3], s2[2:3]]
        bf = sbf[...]
        cut = [jnp.concatenate([bf[:, sh * u_ + i * r_ : sh * u_ + (i + 1) * r_] for sh in range(n_)], axis=1) for i in range(2)]
        for side in range(2):
            on = (s == side).astype(F32)
            rows += [cut[0] * on, cut[1] * on]
    v1, v2 = tiny[1][4:5, :h_], tiny[4][4:5, :h_]
    first = (s == 0).astype(F32)
    vals = jnp.concatenate([v1 * first, v1 * (1.0 - first), v2 * first], axis=1)
    each = plan.values // n_
    pad = jnp.zeros((1, 2 * r_ - each), F32)
    rows.append(jnp.concatenate([vals[:, sh * each : sh * each + r_] for sh in range(n_)], axis=1))
    rows.append(jnp.concatenate([x for sh in range(n_) for x in (vals[:, sh * each + r_ : (sh + 1) * each], pad)], axis=1))
    rows.append(jnp.zeros((TAIL - 24, d_), F32))
    full = jnp.concatenate(rows, axis=0).astype(BF)
    for sh in range(n_):
        block = jnp.concatenate([full[:, sh * r_ : (sh + 1) * r_], jnp.zeros((TAIL, h_ - r_), BF)], axis=1)
        tail[idx[2 * n_ + sh]] = block


def total(refs, terms, rows):
    x = None
    for at, row in terms:
        y = refs[at][row : row + rows, :].astype(F32)
        x = y if x is None else x + y
    return x.astype(BF)


def round_kernel(plans, n, *refs):
    for out, segments in zip(refs[n:], plans):
        row = 0
        for terms, rows in segments:
            out[row : row + rows, :] = total(refs, terms, rows)
            row += rows


def listed(segments):
    arrays, plans = [], []
    for terms, rows in segments:
        named = []
        for x, row in terms:
            at = next((i for i, y in enumerate(arrays) if y is x), len(arrays))
            if at == len(arrays):
                arrays.append(x)
            named.append((at, row))
        plans.append((named, rows))
    return arrays, plans


def run_round(outs):
    arrays, plans = listed([seg for segments in outs for seg in segments])
    cut, at = [], 0
    for segments in outs:
        cut.append(plans[at : at + len(segments)])
        at += len(segments)
    width = arrays[0].shape[1]
    shapes = [((sum(rows for _, rows in segments), width), BF, VM) for segments in outs]
    return call(functools.partial(round_kernel, cut, len(arrays)), vm(*arrays), shapes, [], 1.2)


def pick_kernel(plans, n, side_at, idx, *refs):
    own, send = refs[n:]
    first = idx[side_at] == 0
    sums = [total(refs, terms, rows) for terms, rows in plans]
    size = sums[1].shape[0]
    for t in range(2):
        x, y = sums[2 * t][:size], sums[2 * t + 1]
        own[t * size : (t + 1) * size] = jnp.where(first, x, y)
        send[t * size : (t + 1) * size] = jnp.where(first, y, x)
    if sums[0].shape[0] > size:
        for ref in (own, send):
            ref[2 * size :] = sums[0]


def run_pick(plan, idx, segments):
    arrays, plans = listed(segments)
    one, two = segments[0][1], segments[1][1]
    shape = (2 * two + (one if one > two else 0), plan.half)
    kernel = functools.partial(pick_kernel, plans, len(arrays), plan.side_at())
    return call(kernel, [(idx, SM)] + vm(*arrays), [(shape, BF, VM)] * 2, [], 1.0)


def finish_mlp_kernel(plan, idx, *refs):
    r_, h_, u_ = plan.rows, plan.half, plan.unit
    mlp, (o_fc, o_proj) = refs[:4], refs[4:]
    s, c = idx[plan.side_at()], idx[plan.core_at()]
    per = h_ // u_
    for t in range(2):
        fc = [[None] * 2, [None] * 2]
        for i in range(2):
            a, b = mlp[2 * i], mlp[2 * i + 1]
            for core in range(2):
                x = jnp.where(c == core, a[2 * t * r_ : (2 * t + 2) * r_, :], b[2 * t * r_ : (2 * t + 2) * r_, :])
                fc[i][core] = x[:r_]
                for side in range(2):

                    @pl.when((s == side) if i == 0 else (s != side))
                    def _():
                        lo = side * 2 * r_ + t * r_
                        o_proj[lo : lo + r_, core * h_ : (core + 1) * h_] = x[r_:].astype(F32)

        for core in range(2):
            q = 2 * core + t
            b0 = jnp.where(s == 0, fc[0][core], fc[1][core]).astype(F32)
            b1 = jnp.where(s == 0, fc[1][core], fc[0][core]).astype(F32)
            pieces = [x[:, i * u_ : (i + 1) * u_] for i in range(per) for x in (b0, b1)]
            o_fc[:, 2 * q * h_ : 2 * (q + 1) * h_] = jnp.concatenate(pieces, axis=1)


def finish_att_kernel(plan, idx, *refs):
    r_, h_, d_ = plan.rows, plan.half, plan.width
    att, val = refs[:4], refs[4:6]
    o_qk, o_val, o_out, o_gain, o_shift, o_bf, o_vs = refs[6:]
    s, c = idx[plan.side_at()], idx[plan.core_at()]

    def block(side, core, lo, hi):
        pick = [jnp.where(c == core, att[2 * i][lo:hi, :], att[2 * i + 1][lo:hi, :]) for i in range(2)]
        return jnp.where(s == side, pick[0], pick[1]).astype(F32)

    sm = sum(x[3 * r_ :, :r_].astype(F32) for x in att)
    mine = jnp.where(s == 0, sm[:11], sm[11:22])
    o_gain[...] = mine[0:2]
    o_shift[...] = mine[2:7]
    o_bf[...] = jnp.concatenate([mine[7 + i : 8 + i] for i in range(4)], axis=1)
    o_vs[...] = jnp.concatenate([sm[22:23], sm[23:24, : plan.values // plan.count - r_]], axis=1)
    low, high = block(0, 1, 0, r_), block(1, 1, 0, r_)
    other, rest = jnp.where(c == 1, val[0][:r_, :], val[1][:r_, :]).astype(F32), block(0, 1, 2 * r_, 3 * r_)
    o_val[:, :h_] = jnp.where(s == 0, low, rest)
    o_val[:, h_:d_] = jnp.where(s == 0, high, other)
    o_val[:, d_:] = jnp.where(s == 0, other, low)
    for side in range(2):
        o_out[:, side * h_ : (side + 1) * h_] = block(side, 1, r_, 2 * r_)
        for t in range(2):
            o_qk[:, t * d_ + side * h_ : t * d_ + (side + 1) * h_] = block(side, 0, t * r_, (t + 1) * r_)


def ends_kernel(plan, idx, prm, r, y_a, y_b, dr, da_a, da_b, h, out):
    s = idx[plan.side_at()]

    @pl.when(s == 1)
    def _():
        for i in range(0, plan.tokens, STEP):
            sl = slice(i, i + STEP)
            out[sl, :] = (r[sl, :] + (y_a[sl, : plan.width].astype(F32) + y_b[sl, : plan.width].astype(F32)) + prm[1, 6:7, :]).astype(BF)

    @pl.when(s == 0)
    def _():
        for i in range(0, plan.tokens, STEP):
            sl = slice(i, i + STEP)
            x, inv = unit_rows(h[sl, :].astype(F32))
            dn = da_a[sl, :].astype(F32) + da_b[sl, :].astype(F32)
            out[sl, :] = (dr[sl, :] + norm_back(dn, x, inv, prm[0, 0:1, :])).astype(BF)


VM = pl.BlockSpec(memory_space=pltpu.VMEM)
SM = pl.BlockSpec(memory_space=pltpu.SMEM)
ANY = pl.BlockSpec(memory_space=pl.ANY)
HBM = pl.BlockSpec(memory_space=pltpu.HBM)


def call(kernel, ins, outs, scratch, us, vmem=VMEM_BYTES):
    return pl.pallas_call(
        kernel,
        out_shape=[jax.ShapeDtypeStruct(sh, dt) for sh, dt, _ in outs],
        in_specs=[sp for _, sp in ins],
        out_specs=[sp for _, _, sp in outs],
        scratch_shapes=scratch,
        compiler_params=pltpu.CompilerParams(vmem_limit_bytes=vmem),
        cost_estimate=pl.CostEstimate(flops=int(us * 4.2e8), bytes_accessed=1000, transcendentals=0),
    )(*[x for x, _ in ins])


def vm(*arrays):
    return [(x, VM) for x in arrays]


def hbm(arrays):
    return [(x, ANY) for x in arrays]


def run_weights(plan, layer, idx, chunks):
    w, h, f = plan.width, plan.half, plan.fh
    ins = [(idx, SM)] + vm(*chunks)
    att = call(functools.partial(att_weights_kernel, plan, layer), ins, [((w, w), BF, VM), ((w, h), BF, VM), ((h, w), BF, VM)], [], 1.2)
    outs = [((w, f), BF, VM)] + ([] if layer else [((f, w), BF, VM)])
    mlp = call(functools.partial(mlp_weights_kernel, plan, layer), ins, outs, [], 1.5)
    return att, mlp


def run_proj(plan, idx, parts):
    out = ((plan.fh, plan.width), BF, VM)
    return call(functools.partial(proj_weights_kernel, plan), [(idx, SM)] + vm(*parts), [out], [], 1.0)


def dma_sems(n):
    return pltpu.SemaphoreType.DMA((n,))


def run_pack(plan, arrays):
    r_, h_ = plan.rows, plan.half
    both, one = ((2, 3 * r_, h_), BF, VM), ((r_, h_), BF, VM)
    outs = [both, both, one, one, ((SMALL, h_), BF, VM)]
    scratch = [pltpu.VMEM(x.shape, BF) for x in arrays] + [dma_sems(7)]
    ins = [(x, HBM) for x in arrays]
    return call(functools.partial(pack_kernel, plan), ins, outs, scratch, 1.5, 60 * 1024 * 1024)


def run_param(plan, idx, arrays):
    outs = [((2, 8, plan.width), F32, VM), ((2, 1, plan.fh), F32, VM)]
    scratch = [pltpu.VMEM((2, plan.count, SMALL, plan.half), BF)]
    return call(functools.partial(param_kernel, plan), [(idx, SM)] + vm(*arrays), outs, scratch, 1.0)


def run_f1(plan, layer, idx, prm, inputs, weights):
    t_, h_, d_ = plan.tokens, plan.half, plan.width
    narrow, wide = ((t_, h_), BF, VM), ((t_, d_), BF, VM)
    outs = [wide, narrow, narrow, narrow, ((plan.seqs * plan.pairs, 2 * plan.seq, plan.seq), BF, VM), narrow, wide]
    outs += [wide] if layer else [wide, wide]
    scratch = []
    ins = [(idx, SM)] + vm(prm, *inputs, *weights)
    return call(functools.partial(f1_kernel, plan, layer), ins, outs, scratch, 2.5)


def run_f2(plan, layer, idx, prm, bf, h, pa, pb, weights, *more):
    t_, d_, f_ = plan.tokens, plan.width, plan.fh
    wide = ((t_, d_), BF, VM)
    outs = [wide, ((t_, d_), F32, VM), ((t_, f_ + d_), BF, VM), ((t_, f_), BF, VM)] + ([wide] if layer else [])
    scratch = [pltpu.VMEM((t_, f_ // 3), F32)]
    ins = [(idx, SM)] + vm(prm, bf, h, pa, pb, *weights, *more)
    return call(functools.partial(f2_kernel, plan, layer), ins, outs, scratch, 4.4)


def run_b2(plan, layer, idx, prm, gp, r, more, weights):
    t_, d_, f_ = plan.tokens, plan.width, plan.fh
    outs = [((t_, d_), BF, VM)] * 4 + [((t_, plan.half), BF, VM), ((3, d_), F32, VM), ((1, f_), F32, VM)]
    scratch = [pltpu.VMEM((t_, d_), F32), pltpu.VMEM((t_, f_), BF)]
    ins = [(idx, SM)] + vm(prm, gp, r, *more, *weights)
    return call(functools.partial(b2_kernel, plan, layer), ins, outs, scratch, 2.6 if layer else 0.3)


def grad_outs(plan, rows, tail=0):
    return [((plan.count // 2 * r, plan.half), BF, VM) for r in (rows + tail, rows) * 2]


def run_g2(plan, idx, *arrays):
    d_, f_, h_ = plan.width, plan.fh, plan.half
    scratch = [pltpu.VMEM((d_, d_), BF), pltpu.VMEM((f_, h_), BF)]
    ins = [(idx, SM)] + vm(*arrays)
    return call(functools.partial(g2_kernel, plan), ins, grad_outs(plan, 2 * plan.rows), scratch, 4.6)


def run_b1(plan, layer, idx, prm, more, weights):
    t_, d_, h_ = plan.tokens, plan.width, plan.half
    wide, narrow = (t_, d_), (t_, h_)
    outs = [(wide, BF, VM), (wide, F32, VM), (wide, BF, VM), (wide, BF, VM), ((5, d_), F32, VM)]
    scratch = [pltpu.VMEM(wide, BF), pltpu.VMEM(wide, BF), pltpu.VMEM(narrow, BF), pltpu.VMEM(wide, F32)]
    if layer:
        outs.append((narrow, BF, VM))
    else:
        scratch.append(pltpu.VMEM(narrow, BF))
    ins = [(idx, SM)] + vm(prm, *more, *weights)
    return call(functools.partial(b1_kernel, plan, layer), ins, outs, scratch, 0.5 if layer else 4.5)


def run_g1(plan, layer, idx, acts, keep, got, tiny):
    d_, h_ = plan.width, plan.half
    scratch = [pltpu.VMEM((d_, d_), BF)]
    if layer == 0:
        scratch += [pltpu.VMEM((plan.count, TAIL, h_), BF)]
    ins = [(idx, SM)] + vm(*acts, keep, got, *tiny)
    return call(functools.partial(g1_kernel, plan, layer), ins, grad_outs(plan, plan.rows, 0 if layer else TAIL), scratch, 0.3 if layer else 1.8)


def run_finish_mlp(plan, idx, arrays):
    outs = [(sh, F32, VM) for sh in ((plan.rows, plan.ff), (4 * plan.rows, plan.width))]
    return call(functools.partial(finish_mlp_kernel, plan), [(idx, SM)] + vm(*arrays), outs, [], 3.0)


def run_finish_att(plan, idx, arrays):
    r_, d_ = plan.rows, plan.width
    outs = [(sh, F32, VM) for sh in ((r_, 2 * d_), (r_, plan.values), (r_, d_), (2, r_), (5, r_), (1, 4 * r_), (1, plan.values // plan.count))]
    return call(functools.partial(finish_att_kernel, plan), [(idx, SM)] + vm(*arrays), outs, [], 2.5)


def run_ends(plan, idx, arrays):
    return call(functools.partial(ends_kernel, plan), [(idx, SM)] + vm(*arrays), [((plan.tokens, plan.width), BF, VM)], [], 1.9)[0]


def after(x, *earlier):
    return lax.optimization_barrier((x,) + earlier)[0]


def per_device(ends, w_qk, w_value, w_out, w_fc, w_proj, gains, shifts, fc_shift, value_shift):
    s, grp, d = lax.axis_index("section"), lax.axis_index("group"), lax.axis_index("dp")
    c = grp % 2
    count, groups = lax.axis_size("dp"), lax.axis_size("group")
    rows, width = w_qk.shape[1], ends.shape[3]
    half = width // 2
    seqs, seq = ends.shape[1], ends.shape[2]
    tokens = seqs * seq
    plan = Plan(count, rows, width, w_fc.shape[2], w_value.shape[1], tokens, seq, HEADS // 2)
    table = plan.table(groups)
    idx = lax.dynamic_slice(jnp.asarray(table), (s, grp, d, 0), (1, 1, 1, table.shape[3])).reshape(-1)
    first, even = s == 0, d % 2 == 0

    def swap_x(x):
        return lax.ppermute(x, "section", [(0, 1), (1, 0)])

    def swap_c(x):
        return lax.ppermute(x, "group", [(i, i ^ 1) for i in range(groups)])

    def swap_d(x, bit):
        return lax.ppermute(x, "dp", [(i, i ^ bit) for i in range(count)])

    hc = count // 2
    spread = [
        [(l * count + i, (i // hc) * count + 2 * (i % hc) + (l if w == 0 else 1 - l)) for l in range(2) for i in range(count)]
        for w in range(2)
    ]
    mine, send, o_lo, o_hi, small = run_pack(
        plan, (w_qk[0], w_fc[0], w_proj[0], w_out[0], gains[0], shifts[0], fc_shift)
    )
    got = swap_x(send)
    small_got = swap_x(small)
    o_a = lax.ppermute(o_lo, ("section", "dp"), spread[0])
    o_b = lax.ppermute(o_hi, ("section", "dp"), spread[1])
    ends_own = ends[0].reshape(tokens, width)
    ends_got = swap_x(after(ends_own, got))
    v_side = (lax.dynamic_slice_in_dim(w_value, s * half, half, 1), w_value[:, width:])
    o_side = (jnp.where(even, o_a, o_b), jnp.where(even, o_b, o_a))

    def head(t, l, other):
        x = jnp.where(first if l == 0 else ~first, mine[t, :rows], got[t, :rows])
        return jnp.where(c == 0, x, other)

    vs_rows = [jnp.pad(x, (0, half - x.shape[0]))[None] for x in (value_shift[:rows], value_shift[rows:])]
    vs_rows = jnp.pad(jnp.concatenate(vs_rows, axis=0), ((11, SMALL - 13), (0, 0)))
    params = [jnp.where(first, x, y) + vs_rows for x, y in ((small, small_got), (small_got, small))]
    early, late = [], []
    for t, side in ((0, v_side), (1, o_side)):
        x, y = mine[t, rows:], got[t, rows:]
        second = jnp.where(first, y, x)
        early.append(jnp.concatenate([head(t, 0, side[0]), jnp.where(first, x, y), head(t, 1, side[1]), second[:rows], params[t]], axis=0))
        late.append(second[rows:])

    routes = [[(a, b) for a, b in zip(order, order[1:] + order[:1])] for order in (ring_order(count), ring_order(count)[::-1])]

    def ring(x):
        return lax.optimization_barrier([lax.ppermute(x[t], "dp", routes[t]) for t in range(2)])

    steps = [[after(x, idx) for x in early]]
    sibs = []
    for n in range(count - 1):
        sibs.append([swap_c(x) for x in steps[-1]])
        steps.append(ring(steps[-1]))
        if n == 2:
            steps[-1] = [after(x, ends_got) for x in steps[-1]]
        if n >= 2:
            steps[-1] = [after(x, *sibs[n - 1]) for x in steps[-1]]
    sibs.append([swap_c(x) for x in steps[-1]])
    chunks = [y for t in range(2) for y in [x[t] for x in steps] + [x[t] for x in sibs]]
    prm, bf = run_param(plan, idx, [x[t] for t in range(2) for x in steps])
    (att_w0, mlp_w0), (att_w1, fc_w1) = (run_weights(plan, l, idx, chunks) for l in range(2))

    def doubled(x, *others):
        k = (x[0].shape[0] // rows).bit_length() - 1
        bits = [plan.orders[t][k] for t in range(2)]
        if bits[0] == bits[1]:
            size = x[0].shape[0]
            both = swap_d(after(jnp.concatenate(x, axis=0), *others), bits[0])
            got = [both[:size], both[size:]]
        else:
            got = [swap_d(after(x[t], *others), bits[t]) for t in range(2)]
        return got

    have = late
    got = doubled(have, *steps[-2])
    part, q0, k0, v0, p0, o0, a0, h0, cot = run_f1(plan, 0, idx, prm, (ends_own, ends_got), att_w0)
    sib0 = [swap_c(a0), swap_c(o0)]
    for _ in range(plan.bits - 2):
        have = [jnp.concatenate(x, axis=0) for x in zip(have, got)]
        got = doubled(have, part)
    sib0 += got + list(att_w1)
    have = [jnp.concatenate(x, axis=0) for x in zip(have, got)]
    got = after(swap_x(part), *sib0)
    part, r0, ucn0, gp0 = run_f2(plan, 0, idx, prm, bf, h0, part, got, mlp_w0)
    more = doubled(have, got)
    have_sib = [swap_c(after(x, part)) for x in have]
    ucn0_sib = swap_c(ucn0)
    got = after(swap_x(part), ucn0_sib, *have_sib, *more)
    part, q1, k1, v1, p1, o1, a1, h1 = run_f1(plan, 1, idx, prm, (r0, part, got, v0), att_w1)
    sib1 = [swap_c(a1), swap_c(o1)]
    got = after(swap_x(part), *sib1)
    parts = [x for t in range(2) for x in (have[t], more[t], have_sib[t], swap_c(after(more[t], part)))]
    mlp_w1 = fc_w1 + run_proj(plan, idx, parts)
    y_part, r1, ucn1, gp1, oo0 = run_f2(plan, 1, idx, prm, bf, h1, part, got, mlp_w1, o0, sib0[1])

    class Sum:
        def __init__(self, g):
            self.first, self.keep = g[:2], g[2:]
            self.rows = [x.shape[0] // hc for x in self.keep]
            self.came = [[], []]

        def terms(self, t, low):
            return [(self.keep[t], low * self.rows[t])] + [(x, at + low * self.rows[t]) for x, at in self.came[t]]

        def bit(self, t):
            return plan.orders[t][plan.bits - 1 - len(self.came[t])]

        def segment(self, t):
            steps = len(self.came[t])
            if steps == 0:
                return [(self.first[t], 0)], self.first[t].shape[0]
            low = count >> (steps + 1)
            return self.terms(t, low), low * self.rows[t]

    def one_round(sums, *others, lock=True):
        sums = [x for x in sums if len(x.came[0]) < plan.bits]
        if not sums:
            return []
        by_bit = {}
        for x in sums:
            for t in range(2):
                by_bit.setdefault(x.bit(t), []).append((x, t, x.segment(t)))
        bits = sorted(by_bit)
        if all(len(by_bit[b]) == 1 and not by_bit[b][0][0].came[0] for b in bits):
            outs = [by_bit[b][0][2][0][0][0] for b in bits]
        else:
            outs = run_round([[seg for _, _, seg in by_bit[b]] for b in bits])
        got = []
        for b, out in zip(bits, outs):
            here = swap_d(after(out, *others, *(one_round.last if lock else ())), b)
            row = 0
            for x, t, (_, rows_) in by_bit[b]:
                x.came[t].append((here, row))
                row += rows_
            got.append(here)
        one_round.last = got
        return got

    one_round.last = []

    def over_pairs(x):
        total = x
        for n in range(1, groups // 2):
            total = total + lax.ppermute(x, "group", [(i, (i + 2 * n) % groups) for i in range(groups)])
        return total

    part, e, z_keep, z_send, e_send, s2_1, sbf_1 = run_b2(plan, 1, idx, prm, gp1, r1, (cot,), mlp_w1)
    got = swap_x(part)
    mlp1 = Sum(run_g2(plan, idx, ucn1, swap_c(ucn1), e, swap_c(e_send), z_keep, swap_c(z_send)))
    got = after(got, *mlp1.first)
    one_round([mlp1])
    part, dr, keep, send, s1_1, dv1 = run_b1(plan, 1, idx, prm, (cot, part, got, r1, h1, q1, k1, v1, p1), att_w1)
    o1_far = swap_x(after(o1, got))
    got = swap_x(part)
    acts = [a1, sib1[0], o1, sib1[1], o1_far, swap_c(o1_far)]
    att1 = Sum(run_g1(plan, 1, idx, acts, keep, swap_c(send), ()))
    got = after(got, *att1.first)
    came = one_round([mlp1, att1])
    part, e, z_keep, z_send, e_send, s2_0, sbf_0 = run_b2(plan, 0, idx, prm, gp0, r0, (dr, part, got, h1), mlp_w0)
    got = swap_x(part)
    mlp0 = Sum(run_g2(plan, idx, ucn0, ucn0_sib, e, swap_c(e_send), z_keep, swap_c(z_send)))
    got = after(got, *mlp0.first, *came)
    came = one_round([mlp1, att1, mlp0])
    oo_far = swap_x(after(oo0, got))
    part, dr, keep, send, s1_0 = run_b1(plan, 0, idx, prm, (e, part, got, r0, h0, q0, k0, v0, p0, dv1), att_w0)
    acts = [a0, sib0[0], o0, sib0[1], oo_far, oo_far]
    att0 = Sum(run_g1(plan, 0, idx, acts, keep, swap_c(after(send, came[-1])), (s2_0, s1_0, sbf_0, s2_1, s1_1, sbf_1)))
    sums = [att0, att1, mlp0, mlp1]
    x_got = swap_x(after(part, oo_far))
    y_got = swap_x(after(y_part, oo_far))
    res = run_ends(plan, idx, (prm, r1, y_part, y_got, dr, part, x_got, h0)).reshape(1, seqs, seq, width)
    one_round(sums)
    for _ in range(plan.bits - 2):
        one_round(sums, x_got, y_got)

    def ending(sums, first, *others):
        own, send = (over_pairs(x) for x in run_pick(plan, after(idx, *first), [(x.terms(t, 0), x.rows[t]) for t in range(2) for x in sums]))
        far = after(swap_x(send), *others)
        return [own, swap_c(own), far, swap_c(far)], send

    arrived = one_round.last
    one_round(sums, lock=False)
    e_mlp, _ = ending((mlp0, mlp1), arrived)
    o_fc, o_proj = run_finish_mlp(plan, idx, e_mlp)
    e_att, sent = ending((att0, att1), (), o_fc, res)
    o_qk, o_val, o_out, o_gain, o_shift, o_bf, o_vs = run_finish_att(plan, idx, e_att + [sent, swap_c(sent)])

    return (res, o_qk[None], o_val, o_out[None], o_fc[None], o_proj[None], o_gain[None], o_shift[None], o_bf, o_vs[0])


def solution(mesh):
    placed = (
        P("section", ("group", "dp"), None, None),
        P("section", "dp", None),
        P("dp", None),
        P("section", "dp", None),
        P("section", "dp", None),
        P("section", "dp", None),
        P("section", None, "dp"),
        P("section", None, "dp"),
        P("section", "dp"),
        P("dp"),
    )
    return jax.shard_map(per_device, mesh=mesh, in_specs=placed, out_specs=placed, check_vma=False)
```

```python
import functools

import jax
import jax.numpy as jnp
import numpy as np
from jax import lax
from jax.experimental import pallas as pl
from jax.experimental.pallas import tpu as pltpu
from jax.sharding import PartitionSpec as P

HEADS = 12
BF = jnp.bfloat16
F32 = jnp.float32
norm_eps = 1e-05
masked_score = -1e30
TAIL = 32
SMALL = 16
STEP = 32
VMEM_BYTES = 16 * 1024 * 1024


def dot(a, b):
    return jnp.dot(a, b, preferred_element_type=F32)


def dot_tn(a, b):
    return lax.dot_general(a, b, (((0,), (0,)), ((), ())), preferred_element_type=F32)


def dot_nt(a, b):
    return lax.dot_general(a, b, (((1,), (1,)), ((), ())), preferred_element_type=F32)


def unit_rows(v):
    centered = v - jnp.mean(v, axis=-1, keepdims=True)
    inv = lax.rsqrt(jnp.mean(centered * centered, axis=-1, keepdims=True) + norm_eps)
    return centered * inv, inv


def norm_back(dn, x, inv, gain):
    scaled = dn * gain
    inner = jnp.mean(scaled * x, axis=-1, keepdims=True)
    return inv * (scaled - jnp.mean(scaled, axis=-1, keepdims=True) - x * inner)


def row_sum(v):
    return jnp.sum(v, axis=0, keepdims=True)


def ring_order(count):
    wide = 2 if count < 16 else 4
    tall = count // wide
    order = [i * wide for i in range(tall)]
    for n, row in enumerate(reversed(range(tall))):
        cols = range(1, wide)
        order += [row * wide + col for col in (cols if n % 2 == 0 else reversed(cols))]
    return order


class Plan:
    def __init__(self, count, rows, width, ff, values, tokens, seq, heads):
        self.count, self.rows, self.width, self.half = count, rows, width, width // 2
        self.ff, self.fh, self.unit, self.values = ff, ff // 2, ff // count // 2, values
        self.tokens, self.seq, self.seqs = tokens, seq, tokens // seq
        self.pairs = heads // 2
        self.bits = count.bit_length() - 1
        down = [1 << i for i in reversed(range(self.bits))]
        other = down[:-2] + [down[-1], down[-2]]
        self.orders = (down, other)
        self.masks = []
        for order in self.orders:
            mask = [0] * count
            for j in range(count):
                for k, bit in enumerate(order):
                    if j >> k & 1:
                        mask[j] ^= bit
            self.masks.append(mask)

    def core_at(self):
        return 7 * self.count

    def side_at(self):
        return 7 * self.count + 1

    def table(self, groups):
        n = self.count
        out = np.zeros((2, groups, n, 7 * n + 2), np.int32)
        order = ring_order(n)
        for p, d in enumerate(order):
            for t in range(2):
                out[:, :, d, t * n : (t + 1) * n] = [d ^ m for m in self.masks[t]]
                out[:, :, d, (3 + t) * n : (4 + t) * n] = [order[(p - (1 - 2 * t) * j) % n] for j in range(n)]
            for j, m in enumerate(self.masks[0]):
                out[:, :, d, 2 * n + (d ^ m)] = j
            for j in range(n):
                for t in range(2):
                    out[:, :, d, (5 + t) * n + order[(p - (1 - 2 * t) * j) % n]] = j
        out[:, :, :, 7 * n] = (np.arange(groups) % 2)[None, :, None]
        out[:, :, :, 7 * n + 1] = np.arange(2)[:, None, None]
        return out


def aligned(x, size):
    return x if isinstance(x, int) else pl.multiple_of(x, size)


def dma(src, dst, sem):
    return pltpu.make_async_copy(src, dst, sem)


def wait_all(ref, sem):
    dma(ref, ref, sem).wait()


def chunk_refs(plan, idx, chunks, row):
    for j in range(plan.count):
        for t in range(2):
            for other in range(2):
                ref = chunks[(t * 2 + other) * plan.count + j]
                yield t, other, idx[(3 + t) * plan.count + j], ref.at[pl.ds(row, plan.rows), :]


def place_att(plan, layer, idx, chunks, wqk, wv, wo):
    r_, h_ = plan.rows, plan.half
    c = idx[plan.core_at()]
    for t, other, sh, src in chunk_refs(plan, idx, chunks, 3 * r_ * layer):
        core = 1 - c if other else c
        row = pl.multiple_of(sh * r_, 16)

        @pl.when(core == 0)
        def _():
            wqk[pl.ds(row, r_), t * h_ : (t + 1) * h_] = src[...]

        @pl.when(core == 1)
        def _():
            if t == 0:
                wv[pl.ds(row, r_), :] = src[...]
            else:
                orow = pl.multiple_of((sh // 2) * r_, 16)
                ocol = pl.multiple_of((sh % 2) * h_, 128)
                wo[pl.ds(orow, r_), pl.ds(ocol, h_)] = src[...]


def place_mlp(plan, idx, chunks, wfc, wproj):
    r_, h_ = plan.rows, plan.half
    c = idx[plan.core_at()]
    for kind in range(2):
        for t, other, sh, src in chunk_refs(plan, idx, chunks, (1 + kind) * r_):
            core = 1 - c if other else c
            place_mlp_block(plan, kind, t, core, sh, src, wfc, wproj)


def place_mlp_block(plan, kind, t, core, sh, src, wfc, wproj):
    r_, h_ = plan.rows, plan.half
    if kind == 0:
        row = pl.multiple_of(sh * r_, 16)
        col = pl.multiple_of((2 * core + t) * h_, 128)
        wfc[pl.ds(row, r_), pl.ds(col, h_)] = src[...]
    else:
        row = pl.multiple_of(sh * 2 * r_ + t * r_, 16)
        col = pl.multiple_of(core * h_, 128)
        wproj[pl.ds(row, r_), pl.ds(col, h_)] = src[...]


def put_blocks(plan, idx, outs, pick, row0):
    n_, r_ = plan.count, plan.rows
    half = n_ // 2
    for j in reversed(range(n_)):
        for t in range(2):
            out = outs[2 * (0 if j >= half else 1) + t]
            at = j % half * (out.shape[0] // half) + row0
            out[at : at + r_, :] = pick(t, idx[t * n_ + j])


def pack_kernel(plan, *refs):
    from_hbm, (mine, send, o_a, o_b, small), here, sems = refs[:7], refs[7:12], refs[12:19], refs[19]
    for i, ref in enumerate(here):
        dma(from_hbm[i], ref, sems.at[i]).start()
    for i, ref in enumerate(here):
        wait_all(ref, sems.at[i])
    wqk, wfc, wproj, wout, gains, shifts, fc_shift = here
    r_, h_, d_, u_ = plan.rows, plan.half, plan.width, plan.unit
    per = h_ // u_
    s, c = lax.axis_index("section"), lax.rem(lax.axis_index("group"), 2)
    lo, hi = wout[:, :h_], wout[:, h_:]
    o_a[...] = jnp.where(s == 0, lo, hi)
    o_b[...] = jnp.where(s == 0, hi, lo)
    rows = [gains[...], shifts[...]] + [fc_shift[:, i * r_ : (i + 1) * r_] for i in range(4)]
    rows = jnp.concatenate([x.astype(F32) for x in rows] + [jnp.zeros((SMALL - 11, r_), F32)], axis=0)
    small[...] = jnp.concatenate([rows, jnp.zeros((SMALL, h_ - r_), F32)], axis=1).astype(BF)
    for side in range(2):
        for core in range(2):
            for keep in range(2):
                out = mine if keep else send

                @pl.when(jnp.logical_and(c == core, s == (side if keep else 1 - side)))
                def _():
                    for t in range(2):
                        lo = t * d_ + side * h_
                        out[t, :r_] = wqk[:, lo : lo + h_]
                        q = 2 * core + t
                        cols = [(q * per + i) * 2 * u_ + side * u_ for i in range(per)]
                        out[t, r_ : 2 * r_] = jnp.concatenate([wfc[:, x : x + u_] for x in cols], axis=1)
                        row = side * 2 * r_ + t * r_
                        out[t, 2 * r_ :] = wproj[row : row + r_, core * h_ : (core + 1) * h_]


def param_kernel(plan, idx, *refs):
    n_, r_, h_, d_ = plan.count, plan.rows, plan.half, plan.width
    s = idx[plan.side_at()]
    steps, (prm, bf, stack) = refs[: 2 * n_], refs[2 * n_ :]
    for j, ref in enumerate(steps):
        stack[j // n_, j % n_] = ref[4 * r_ :, :]
    pairs = [[stack[t, idx[(5 + t) * n_ + sh]][:, :r_].astype(F32) for t in range(2)] for sh in range(n_)]
    more = plan.values // n_ - r_
    vals = jnp.concatenate([x for b, _ in pairs for x in (b[11:12, :], b[12:13, :more])], axis=1)
    for l in range(2):
        blocks = [b[l] for b in pairs]
        m = jnp.concatenate([b[:7] for b in blocks], axis=1)
        prm[l, 0:7] = m
        bq = jnp.where(s == 0, m[4:5, :h_], m[4:5, h_:])
        prm[l, 4:5] = jnp.concatenate([bq, jnp.zeros((1, d_ - h_), F32)], axis=1)
        if l == 0:
            bv = jnp.where(s == 0, vals[:, :h_], vals[:, h_:d_])
        else:
            bv = vals[:, d_:]
        prm[l, 7:8] = jnp.concatenate([bv, jnp.zeros((1, d_ - h_), F32)], axis=1)
        sides = []
        for side in range(2):
            row = 7 + 2 * side
            sides.append(jnp.concatenate([b[row + i : row + i + 1] for b in blocks for i in range(2)], axis=1))
        bf[l] = jnp.where(s == 0, sides[0], sides[1])


def att_weights_kernel(plan, layer, *refs):
    place_att(plan, layer, refs[0], refs[1:-3], *refs[-3:])


def mlp_weights_kernel(plan, *refs):
    place_mlp(plan, refs[0], refs[1 : 1 + 4 * plan.count], *refs[1 + 4 * plan.count :])


def late_weights_kernel(plan, *refs):
    n_, r_ = plan.count, plan.rows
    idx, parts, (wfc, wproj) = refs[0], refs[1:9], refs[9:]
    c = idx[plan.core_at()]
    for t in range(2):
        for other in range(2):
            core = 1 - c if other else c
            for j in range(n_):
                part = parts[(2 * t + other) * 2 + j // (n_ // 2)]
                for kind in range(2):
                    src = part.at[pl.ds((j % (n_ // 2) * 2 + kind) * r_, r_), :]
                    place_mlp_block(plan, kind, t, core, idx[t * n_ + j], src, wfc, wproj)


def pair_mask(seq, lanes):
    return lax.broadcasted_iota(jnp.int32, (seq, lanes), 1) < lanes // 2


def stack_pair(x, low):
    zero = jnp.zeros_like(x)
    return jnp.concatenate([jnp.where(low, x, zero), jnp.where(low, zero, x)], axis=0)


def f1_kernel(plan, layer, *refs):
    h_, t_, sq = plan.half, plan.tokens, plan.seq
    idx, prm, refs = refs[0], refs[1], refs[2:]
    if layer == 1:
        r_up, pa, pb, v_old = refs[:4]
        refs = refs[4:]
    else:
        here, there = refs[:2]
        refs = refs[2:]
    weights, refs = refs[:3], refs[3:]
    part, q, k, v, p, o, a, h = refs[:8]
    if layer == 0:
        cot = refs[8]
    wqk, wv, wo = weights
    first = idx[plan.side_at()] == 0
    for i in range(0, t_, STEP):
        sl = slice(i, i + STEP)
        if layer == 1:
            hh = r_up[sl, :] + (pa[sl, :].astype(F32) + pb[sl, :].astype(F32)) + prm[0, 6:7, :]
            h[sl, :] = hh.astype(BF)
        else:
            mine, theirs = here[sl, :], there[sl, :]
            h[sl, :] = jnp.where(first, mine, theirs)
            cot[sl, :] = jnp.where(first, theirs, mine)
        x, _ = unit_rows(h[sl, :].astype(F32))
        a[sl, :] = (x * prm[layer, 0:1, :] + prm[layer, 2:3, :]).astype(BF)
    qk = dot(a[...], wqk[...])
    q[...] = (qk[:, :h_] + prm[layer, 4:5, :h_]).astype(BF)
    k[...] = qk[:, h_:].astype(BF)
    val = (dot(a[...], wv[...]) + prm[layer, 7:8, :h_]).astype(BF)
    if layer == 1:
        val = jnp.where(idx[plan.side_at()] == 1, v_old[...], val)
    v[...] = val
    lanes = h_ // plan.pairs
    low = pair_mask(sq, lanes)
    causal = lax.broadcasted_iota(jnp.int32, (2 * sq, sq), 0) % sq >= lax.broadcasted_iota(jnp.int32, (2 * sq, sq), 1)
    scale = (lanes // 2) ** -0.5
    for s_ in range(plan.seqs):
        for j in range(plan.pairs):
            rws, cls = slice(s_ * sq, (s_ + 1) * sq), slice(j * lanes, (j + 1) * lanes)
            q2 = stack_pair(q[rws, cls], low)
            sc = jnp.where(causal, dot_nt(q2, k[rws, cls]) * scale, masked_score)
            ex = jnp.exp(sc - jnp.max(sc, axis=-1, keepdims=True))
            pr = (ex / jnp.sum(ex, axis=-1, keepdims=True)).astype(BF)
            p[s_ * plan.pairs + j] = pr
            o2 = dot(pr, v[rws, cls])
            o[rws, cls] = jnp.where(low, o2[:sq], o2[sq:]).astype(BF)
    part[...] = dot(o[...], wo[...]).astype(BF)


def f2_kernel(plan, layer, *refs):
    t_ = plan.tokens
    idx, prm, bf, h, pa, pb = refs[:6]
    if layer == 1:
        o_up, refs = refs[8:10], refs[:8] + refs[10:]
    weights, refs = refs[6:8], refs[8:]
    part, r, ucn, gp, *oo, z = refs
    wfc, wproj = weights
    f_ = plan.fh
    for i in range(0, t_, STEP):
        sl = slice(i, i + STEP)
        rr = h[sl, :].astype(F32) + (pa[sl, :].astype(F32) + pb[sl, :].astype(F32)) + prm[layer, 5:6, :]
        r[sl, :] = rr
        x, _ = unit_rows(rr)
        ucn[sl, f_:] = (x * prm[layer, 1:2, :] + prm[layer, 3:4, :]).astype(BF)
    cols = plan.fh // 3
    for j in range(3):
        cs = slice(j * cols, (j + 1) * cols)
        z[...] = dot(ucn[:, f_:], wfc[:, cs])

        def body(i, carry):
            sl = pl.ds(pl.multiple_of(i * STEP, STEP), STEP)
            zz = z[sl, :] + bf[layer, :, cs]
            sq_ = zz * zz
            th = jnp.tanh(0.7978845608 * zz * (1.0 + 0.044715 * sq_))
            hp = 0.5 * (1.0 + th)
            ucn[sl, cs] = (zz * hp).astype(BF)
            slope = 0.7978845608 * (1.0 + 3 * 0.044715 * sq_)
            gp[sl, cs] = (hp + 0.5 * zz * (1.0 - th * th) * slope).astype(BF)
            return carry

        lax.fori_loop(0, t_ // STEP, body, 0)
    part[...] = dot(ucn[:, :f_], wproj[...]).astype(BF)
    if layer == 1:
        oo[0][:, : plan.half] = o_up[0][...]
        oo[0][:, plan.half :] = o_up[1][...]


def b2_kernel(plan, layer, *refs):
    d_, t_, f_ = plan.width, plan.tokens, plan.fh
    idx, prm, gp, r = refs[:4]
    refs = refs[4:]
    if layer == 1:
        e, refs = refs[0], refs[1:]
    else:
        dr, da_a, da_b, h_up = refs[:4]
        refs = refs[4:]
    weights, refs = refs[:2], refs[2:]
    part, e_out, z_keep, z_send, e_send, sums, sbf = refs[:7]
    h_, c = plan.half, idx[plan.core_at()]
    wfc, wproj = weights
    acc, dz = refs[-2:]
    zero = jnp.zeros((1, d_), F32)
    sb4 = zero
    for i in range(0, t_, STEP):
        sl = slice(i, i + STEP)
        if layer == 0:
            x, inv = unit_rows(h_up[sl, :].astype(F32))
            dn = da_a[sl, :].astype(F32) + da_b[sl, :].astype(F32)
            ee = (dr[sl, :] + norm_back(dn, x, inv, prm[1, 0:1, :])).astype(BF)
        else:
            ee = e[sl, :]
        e_out[sl, :] = ee
        sb4 = sb4 + row_sum(ee.astype(F32))
    cols = f_ // 3
    for j in range(3):
        cs = slice(j * cols, (j + 1) * cols)
        dzj = (dot_nt(e_out[...], wproj[cs, :]) * gp[:, cs].astype(F32)).astype(BF)
        dz[:, cs] = dzj
        sbf[:, cs] = row_sum(dzj.astype(F32))
    z_keep[...] = dz[:, pl.ds(pl.multiple_of(c * d_, 128), d_)]
    z_send[...] = dz[:, pl.ds(pl.multiple_of((1 - c) * d_, 128), d_)]
    e_send[...] = e_out[:, pl.ds(pl.multiple_of((1 - c) * h_, 128), h_)]
    acc[...] = dot_nt(dz[...], wfc[...])
    sg1, sb1 = zero, zero
    for i in range(0, t_, STEP):
        sl = slice(i, i + STEP)
        dn = acc[sl, :]
        part[sl, :] = dn.astype(BF)
        x, _ = unit_rows(r[sl, :])
        sg1 = sg1 + row_sum(dn * x)
        sb1 = sb1 + row_sum(dn)
    sums[0:1, :], sums[1:2, :], sums[2:3, :] = sg1, sb1, 0.5 * sb4


def g2_kernel(plan, *refs):
    r_, h_, f_ = plan.rows, plan.half, plan.fh
    idx, ucn, ucn_sib, e, e_sib, dz, dz_sib = refs[:7]
    outs, (gfc, gproj) = refs[7:-2], refs[-2:]
    c = idx[plan.core_at()]
    ecols = pl.ds(pl.multiple_of(c * h_, 128), h_)
    gproj[...] = (dot_tn(ucn[:, :f_], e[:, ecols]) + dot_tn(ucn_sib[:, :f_], e_sib[...])).astype(BF)
    put_blocks(plan, idx, outs, lambda t, sh: gproj[pl.ds(pl.multiple_of(sh * 2 * r_ + t * r_, 16), r_), :], r_)
    gfc[...] = (dot_tn(ucn[:, f_:], dz[...]) + dot_tn(ucn_sib[:, f_:], dz_sib[...])).astype(BF)
    put_blocks(plan, idx, outs, lambda t, sh: gfc[pl.ds(pl.multiple_of(sh * r_, 16), r_), t * h_ : (t + 1) * h_], 0)


def b1_kernel(plan, layer, *refs):
    h_, d_, t_, sq = plan.half, plan.width, plan.tokens, plan.seq
    idx, prm, e, dc_a, dc_b, r, h, q, k, v, p = refs[:11]
    refs = refs[11:]
    if layer == 0:
        extra, refs = refs[0], refs[1:]
    weights, refs = refs[:3], refs[3:]
    part, dr, keep, send, sums = refs[:5]
    refs = refs[5:]
    if layer == 1:
        dv_out, refs = refs[0], refs[1:]
    else:
        dv_out, refs = refs[-1], refs[:-1]
    wqk, wv, wo = weights
    dy, dqk, do, acc = refs
    s, c = idx[plan.side_at()], idx[plan.core_at()]
    zero = jnp.zeros((1, d_), F32)
    sb3 = zero
    for i in range(0, t_, STEP):
        sl = slice(i, i + STEP)
        x, inv = unit_rows(r[sl, :])
        dn = dc_a[sl, :].astype(F32) + dc_b[sl, :].astype(F32)
        dd = e[sl, :].astype(F32) + norm_back(dn, x, inv, prm[layer, 1:2, :])
        dr[sl, :] = dd
        dyb = dd.astype(BF)
        dy[sl, :] = dyb
        sb3 = sb3 + row_sum(dyb.astype(F32))
    do[...] = dot_nt(dy[...], wo[...]).astype(BF)
    lanes = h_ // plan.pairs
    low = pair_mask(sq, lanes)
    scale = (lanes // 2) ** -0.5
    for s_ in range(plan.seqs):
        for j in range(plan.pairs):
            rws, cls = slice(s_ * sq, (s_ + 1) * sq), slice(j * lanes, (j + 1) * lanes)
            kcls = slice(h_ + j * lanes, h_ + (j + 1) * lanes)
            q2 = stack_pair(q[rws, cls], low)
            do2 = stack_pair(do[rws, cls], low)
            pr = p[s_ * plan.pairs + j]
            dp = dot_nt(do2, v[rws, cls])
            dv = dot_tn(pr, do2)
            if layer == 0:
                dv = dv + extra[rws, cls].astype(F32) * (s == 1).astype(F32)
            dv_out[rws, cls] = dv.astype(BF)
            pf = pr.astype(F32)
            ds = (pf * (dp - jnp.sum(pf * dp, axis=-1, keepdims=True))).astype(BF)
            dq2 = dot(ds, k[rws, cls])
            dqk[rws, cls] = (jnp.where(low, dq2[:sq], dq2[sq:]) * scale).astype(BF)
            dqk[rws, kcls] = (dot_tn(ds, q2) * scale).astype(BF)
    da = dot_nt(dqk[...], wqk[...])
    dav = dot_nt(dv_out[...], wv[...])
    if layer == 1:
        dav = dav * (s == 0).astype(F32)
    acc[...] = da + dav
    dys = pl.ds(pl.multiple_of(s * h_, 128), h_)
    for core in range(2):

        @pl.when(c == core)
        def _():
            one, two = (keep, send) if core == 0 else (send, keep)
            one[...] = dqk[...]
            two[:, :h_] = dv_out[...]
            two[:, h_:] = dy[:, dys]

    sg0, sb0 = zero, zero
    for i in range(0, t_, STEP):
        sl = slice(i, i + STEP)
        dn = acc[sl, :]
        part[sl, :] = dn.astype(BF)
        x, _ = unit_rows(h[sl, :].astype(F32))
        sg0 = sg0 + row_sum(dn * x)
        sb0 = sb0 + row_sum(dn)
    sums[0:1, :], sums[1:2, :], sums[2:3, :] = sg0, sb0, 0.5 * sb3
    sq_ = row_sum(dqk[...].astype(F32))[:, :h_]
    none = jnp.zeros((1, h_), F32)
    sums[3:4, :] = jnp.where(s == 0, jnp.concatenate([sq_, none], axis=1), jnp.concatenate([none, sq_], axis=1))
    sums[4:5, :] = jnp.concatenate([row_sum(dv_out[...].astype(F32)), none], axis=1)


def g1_kernel(plan, layer, *refs):
    r_, h_, d_, n_ = plan.rows, plan.half, plan.width, plan.count
    idx, a, a_sib, o, o_sib, far, far_sib, keep, got = refs[:9]
    refs = refs[9:]
    if layer == 0:
        tiny, refs = refs[:6], refs[6:]
    outs, refs = refs[:4], refs[4:]
    gatt = refs[0]
    c = idx[plan.core_at()]

    @pl.when(c == 0)
    def _():
        gatt[...] = (dot_tn(a[...], keep[...]) + dot_tn(a_sib[...], got[...])).astype(BF)

    @pl.when(c == 1)
    def _():
        gatt[:, :h_] = (dot_tn(a[...], keep[:, :h_]) + dot_tn(a_sib[...], got[:, :h_])).astype(BF)
        s = idx[plan.side_at()]
        apart = far.shape[1] - h_
        for side, x, y, at in ((s, o, o_sib, 0), (1 - s, far, far_sib, apart)):
            rows = pl.ds(pl.multiple_of(side * h_, 16), h_)
            gatt[rows, h_:] = (dot_tn(x[:, :h_], keep[:, h_:]) + dot_tn(y[:, at:], got[:, h_:])).astype(BF)

    put_blocks(plan, idx, outs, lambda t, sh: gatt[pl.ds(pl.multiple_of(sh * r_, 16), r_), t * h_ : (t + 1) * h_], 0)
    if layer == 0:
        tail = refs[1]
        small_sums(plan, idx, tiny, tail)
        half = n_ // 2
        for j in range(n_):
            out, at = outs[0 if j >= half else 2], j % half * (r_ + TAIL) + r_
            out[at : at + TAIL, :] = tail[j]


def small_sums(plan, idx, tiny, tail):
    n_, r_, h_, d_, u_ = plan.count, plan.rows, plan.half, plan.width, plan.unit
    s = idx[plan.side_at()]
    rows = []
    for l in range(2):
        s2, s1, sbf = tiny[3 * l : 3 * l + 3]
        rows += [s1[0:1], s2[0:1], s1[1:2], s2[1:2], s1[3:4], s1[2:3], s2[2:3]]
        bf = sbf[...]
        cut = [jnp.concatenate([bf[:, sh * u_ + i * r_ : sh * u_ + (i + 1) * r_] for sh in range(n_)], axis=1) for i in range(2)]
        for side in range(2):
            on = (s == side).astype(F32)
            rows += [cut[0] * on, cut[1] * on]
    v1, v2 = tiny[1][4:5, :h_], tiny[4][4:5, :h_]
    first = (s == 0).astype(F32)
    vals = jnp.concatenate([v1 * first, v1 * (1.0 - first), v2 * first], axis=1)
    each = plan.values // n_
    pad = jnp.zeros((1, 2 * r_ - each), F32)
    rows.append(jnp.concatenate([vals[:, sh * each : sh * each + r_] for sh in range(n_)], axis=1))
    rows.append(jnp.concatenate([x for sh in range(n_) for x in (vals[:, sh * each + r_ : (sh + 1) * each], pad)], axis=1))
    rows.append(jnp.zeros((TAIL - 24, d_), F32))
    full = jnp.concatenate(rows, axis=0).astype(BF)
    for sh in range(n_):
        block = jnp.concatenate([full[:, sh * r_ : (sh + 1) * r_], jnp.zeros((TAIL, h_ - r_), BF)], axis=1)
        tail[idx[2 * n_ + sh]] = block


def total(refs, terms, rows):
    x = None
    for at, row in terms:
        y = refs[at][row : row + rows, :].astype(F32)
        x = y if x is None else x + y
    return x.astype(BF)


def round_kernel(plans, n, *refs):
    for out, segments in zip(refs[n:], plans):
        row = 0
        for terms, rows in segments:
            out[row : row + rows, :] = total(refs, terms, rows)
            row += rows


def listed(segments):
    arrays, plans = [], []
    for terms, rows in segments:
        named = []
        for x, row in terms:
            at = next((i for i, y in enumerate(arrays) if y is x), len(arrays))
            if at == len(arrays):
                arrays.append(x)
            named.append((at, row))
        plans.append((named, rows))
    return arrays, plans


def run_round(outs):
    arrays, plans = listed([seg for segments in outs for seg in segments])
    cut, at = [], 0
    for segments in outs:
        cut.append(plans[at : at + len(segments)])
        at += len(segments)
    width = arrays[0].shape[1]
    shapes = [((sum(rows for _, rows in segments), width), BF, VM) for segments in outs]
    return call(functools.partial(round_kernel, cut, len(arrays)), vm(*arrays), shapes, [], 1.2)


def pick_kernel(plans, n, side_at, idx, *refs):
    own, send = refs[n:]
    first = idx[side_at] == 0
    sums = [total(refs, terms, rows) for terms, rows in plans]
    size = sums[1].shape[0]
    for t in range(2):
        x, y = sums[2 * t][:size], sums[2 * t + 1]
        own[t * size : (t + 1) * size] = jnp.where(first, x, y)
        send[t * size : (t + 1) * size] = jnp.where(first, y, x)
    if sums[0].shape[0] > size:
        for ref in (own, send):
            ref[2 * size :] = sums[0]


def run_pick(plan, idx, segments):
    arrays, plans = listed(segments)
    one, two = segments[0][1], segments[1][1]
    shape = (2 * two + (one if one > two else 0), plan.half)
    kernel = functools.partial(pick_kernel, plans, len(arrays), plan.side_at())
    return call(kernel, [(idx, SM)] + vm(*arrays), [(shape, BF, VM)] * 2, [], 1.0)


def finish_mlp_kernel(plan, idx, *refs):
    r_, h_, u_ = plan.rows, plan.half, plan.unit
    mlp, (o_fc, o_proj) = refs[:4], refs[4:]
    s, c = idx[plan.side_at()], idx[plan.core_at()]
    per = h_ // u_
    for t in range(2):
        fc = [[None] * 2, [None] * 2]
        for i in range(2):
            a, b = mlp[2 * i], mlp[2 * i + 1]
            for core in range(2):
                x = jnp.where(c == core, a[2 * t * r_ : (2 * t + 2) * r_, :], b[2 * t * r_ : (2 * t + 2) * r_, :])
                fc[i][core] = x[:r_]
                for side in range(2):

                    @pl.when((s == side) if i == 0 else (s != side))
                    def _():
                        lo = side * 2 * r_ + t * r_
                        o_proj[lo : lo + r_, core * h_ : (core + 1) * h_] = x[r_:].astype(F32)

        for core in range(2):
            q = 2 * core + t
            b0 = jnp.where(s == 0, fc[0][core], fc[1][core]).astype(F32)
            b1 = jnp.where(s == 0, fc[1][core], fc[0][core]).astype(F32)
            pieces = [x[:, i * u_ : (i + 1) * u_] for i in range(per) for x in (b0, b1)]
            o_fc[:, 2 * q * h_ : 2 * (q + 1) * h_] = jnp.concatenate(pieces, axis=1)


def finish_att_kernel(plan, idx, *refs):
    r_, h_, d_ = plan.rows, plan.half, plan.width
    att, val = refs[:4], refs[4:6]
    o_qk, o_val, o_out, o_gain, o_shift, o_bf, o_vs = refs[6:]
    s, c = idx[plan.side_at()], idx[plan.core_at()]

    def block(side, core, lo, hi):
        pick = [jnp.where(c == core, att[2 * i][lo:hi, :], att[2 * i + 1][lo:hi, :]) for i in range(2)]
        return jnp.where(s == side, pick[0], pick[1]).astype(F32)

    sm = sum(x[3 * r_ :, :r_].astype(F32) for x in att)
    mine = jnp.where(s == 0, sm[:11], sm[11:22])
    o_gain[...] = mine[0:2]
    o_shift[...] = mine[2:7]
    o_bf[...] = jnp.concatenate([mine[7 + i : 8 + i] for i in range(4)], axis=1)
    o_vs[...] = jnp.concatenate([sm[22:23], sm[23:24, : plan.values // plan.count - r_]], axis=1)
    low, high = block(0, 1, 0, r_), block(1, 1, 0, r_)
    other, rest = jnp.where(c == 1, val[0][:r_, :], val[1][:r_, :]).astype(F32), block(0, 1, 2 * r_, 3 * r_)
    o_val[:, :h_] = jnp.where(s == 0, low, rest)
    o_val[:, h_:d_] = jnp.where(s == 0, high, other)
    o_val[:, d_:] = jnp.where(s == 0, other, low)
    for side in range(2):
        o_out[:, side * h_ : (side + 1) * h_] = block(side, 1, r_, 2 * r_)
        for t in range(2):
            o_qk[:, t * d_ + side * h_ : t * d_ + (side + 1) * h_] = block(side, 0, t * r_, (t + 1) * r_)


def ends_kernel(plan, idx, prm, r, y_a, y_b, dr, da_a, da_b, h, out):
    s = idx[plan.side_at()]

    @pl.when(s == 1)
    def _():
        for i in range(0, plan.tokens, STEP):
            sl = slice(i, i + STEP)
            out[sl, :] = (r[sl, :] + (y_a[sl, : plan.width].astype(F32) + y_b[sl, : plan.width].astype(F32)) + prm[1, 6:7, :]).astype(BF)

    @pl.when(s == 0)
    def _():
        for i in range(0, plan.tokens, STEP):
            sl = slice(i, i + STEP)
            x, inv = unit_rows(h[sl, :].astype(F32))
            dn = da_a[sl, :].astype(F32) + da_b[sl, :].astype(F32)
            out[sl, :] = (dr[sl, :] + norm_back(dn, x, inv, prm[0, 0:1, :])).astype(BF)


VM = pl.BlockSpec(memory_space=pltpu.VMEM)
SM = pl.BlockSpec(memory_space=pltpu.SMEM)
ANY = pl.BlockSpec(memory_space=pl.ANY)
HBM = pl.BlockSpec(memory_space=pltpu.HBM)


def call(kernel, ins, outs, scratch, us, vmem=VMEM_BYTES):
    return pl.pallas_call(
        kernel,
        out_shape=[jax.ShapeDtypeStruct(sh, dt) for sh, dt, _ in outs],
        in_specs=[sp for _, sp in ins],
        out_specs=[sp for _, _, sp in outs],
        scratch_shapes=scratch,
        compiler_params=pltpu.CompilerParams(vmem_limit_bytes=vmem),
        cost_estimate=pl.CostEstimate(flops=int(us * 4.2e8), bytes_accessed=1000, transcendentals=0),
    )(*[x for x, _ in ins])


def vm(*arrays):
    return [(x, VM) for x in arrays]


def hbm(arrays):
    return [(x, ANY) for x in arrays]


def run_weights(plan, layer, idx, chunks):
    w, h, f = plan.width, plan.half, plan.fh
    ins = [(idx, SM)] + vm(*chunks)
    att = call(functools.partial(att_weights_kernel, plan, layer), ins, [((w, w), BF, VM), ((w, h), BF, VM), ((h, w), BF, VM)], [], 1.2)
    mlp = None
    if layer == 0:
        mlp = call(functools.partial(mlp_weights_kernel, plan), ins, [((w, f), BF, VM), ((f, w), BF, VM)], [], 1.5)
    return att, mlp


def run_late(plan, idx, parts):
    outs = [((plan.width, plan.fh), BF, VM), ((plan.fh, plan.width), BF, VM)]
    return call(functools.partial(late_weights_kernel, plan), [(idx, SM)] + vm(*parts), outs, [], 1.5)


def dma_sems(n):
    return pltpu.SemaphoreType.DMA((n,))


def run_pack(plan, arrays):
    r_, h_ = plan.rows, plan.half
    both, one = ((2, 3 * r_, h_), BF, VM), ((r_, h_), BF, VM)
    outs = [both, both, one, one, ((SMALL, h_), BF, VM)]
    scratch = [pltpu.VMEM(x.shape, BF) for x in arrays] + [dma_sems(7)]
    ins = [(x, HBM) for x in arrays]
    return call(functools.partial(pack_kernel, plan), ins, outs, scratch, 1.5, 60 * 1024 * 1024)


def run_param(plan, idx, arrays):
    outs = [((2, 8, plan.width), F32, VM), ((2, 1, plan.fh), F32, VM)]
    scratch = [pltpu.VMEM((2, plan.count, SMALL, plan.half), BF)]
    return call(functools.partial(param_kernel, plan), [(idx, SM)] + vm(*arrays), outs, scratch, 1.0)


def run_f1(plan, layer, idx, prm, inputs, weights):
    t_, h_, d_ = plan.tokens, plan.half, plan.width
    narrow, wide = ((t_, h_), BF, VM), ((t_, d_), BF, VM)
    outs = [wide, narrow, narrow, narrow, ((plan.seqs * plan.pairs, 2 * plan.seq, plan.seq), BF, VM), narrow, wide]
    outs += [wide] if layer else [wide, wide]
    scratch = []
    ins = [(idx, SM)] + vm(prm, *inputs, *weights)
    return call(functools.partial(f1_kernel, plan, layer), ins, outs, scratch, 2.5)


def run_f2(plan, layer, idx, prm, bf, h, pa, pb, weights, *more):
    t_, d_, f_ = plan.tokens, plan.width, plan.fh
    wide = ((t_, d_), BF, VM)
    outs = [wide, ((t_, d_), F32, VM), ((t_, f_ + d_), BF, VM), ((t_, f_), BF, VM)] + ([wide] if layer else [])
    scratch = [pltpu.VMEM((t_, f_ // 3), F32)]
    ins = [(idx, SM)] + vm(prm, bf, h, pa, pb, *weights, *more)
    return call(functools.partial(f2_kernel, plan, layer), ins, outs, scratch, 4.4)


def run_b2(plan, layer, idx, prm, gp, r, more, weights):
    t_, d_, f_ = plan.tokens, plan.width, plan.fh
    outs = [((t_, d_), BF, VM)] * 4 + [((t_, plan.half), BF, VM), ((3, d_), F32, VM), ((1, f_), F32, VM)]
    scratch = [pltpu.VMEM((t_, d_), F32), pltpu.VMEM((t_, f_), BF)]
    ins = [(idx, SM)] + vm(prm, gp, r, *more, *weights)
    return call(functools.partial(b2_kernel, plan, layer), ins, outs, scratch, 2.6 if layer else 0.3)


def grad_outs(plan, rows, tail=0):
    return [((plan.count // 2 * r, plan.half), BF, VM) for r in (rows + tail, rows) * 2]


def run_g2(plan, idx, *arrays):
    d_, f_, h_ = plan.width, plan.fh, plan.half
    scratch = [pltpu.VMEM((d_, d_), BF), pltpu.VMEM((f_, h_), BF)]
    ins = [(idx, SM)] + vm(*arrays)
    return call(functools.partial(g2_kernel, plan), ins, grad_outs(plan, 2 * plan.rows), scratch, 4.6)


def run_b1(plan, layer, idx, prm, more, weights):
    t_, d_, h_ = plan.tokens, plan.width, plan.half
    wide, narrow = (t_, d_), (t_, h_)
    outs = [(wide, BF, VM), (wide, F32, VM), (wide, BF, VM), (wide, BF, VM), ((5, d_), F32, VM)]
    scratch = [pltpu.VMEM(wide, BF), pltpu.VMEM(wide, BF), pltpu.VMEM(narrow, BF), pltpu.VMEM(wide, F32)]
    if layer:
        outs.append((narrow, BF, VM))
    else:
        scratch.append(pltpu.VMEM(narrow, BF))
    ins = [(idx, SM)] + vm(prm, *more, *weights)
    return call(functools.partial(b1_kernel, plan, layer), ins, outs, scratch, 0.5 if layer else 4.5)


def run_g1(plan, layer, idx, acts, keep, got, tiny):
    d_, h_ = plan.width, plan.half
    scratch = [pltpu.VMEM((d_, d_), BF)]
    if layer == 0:
        scratch += [pltpu.VMEM((plan.count, TAIL, h_), BF)]
    ins = [(idx, SM)] + vm(*acts, keep, got, *tiny)
    return call(functools.partial(g1_kernel, plan, layer), ins, grad_outs(plan, plan.rows, 0 if layer else TAIL), scratch, 0.3 if layer else 1.8)


def run_finish_mlp(plan, idx, arrays):
    outs = [(sh, F32, VM) for sh in ((plan.rows, plan.ff), (4 * plan.rows, plan.width))]
    return call(functools.partial(finish_mlp_kernel, plan), [(idx, SM)] + vm(*arrays), outs, [], 3.0)


def run_finish_att(plan, idx, arrays):
    r_, d_ = plan.rows, plan.width
    outs = [(sh, F32, VM) for sh in ((r_, 2 * d_), (r_, plan.values), (r_, d_), (2, r_), (5, r_), (1, 4 * r_), (1, plan.values // plan.count))]
    return call(functools.partial(finish_att_kernel, plan), [(idx, SM)] + vm(*arrays), outs, [], 2.5)


def run_ends(plan, idx, arrays):
    return call(functools.partial(ends_kernel, plan), [(idx, SM)] + vm(*arrays), [((plan.tokens, plan.width), BF, VM)], [], 1.9)[0]


def after(x, *earlier):
    return lax.optimization_barrier((x,) + earlier)[0]


def per_device(ends, w_qk, w_value, w_out, w_fc, w_proj, gains, shifts, fc_shift, value_shift):
    s, grp, d = lax.axis_index("section"), lax.axis_index("group"), lax.axis_index("dp")
    c = grp % 2
    count, groups = lax.axis_size("dp"), lax.axis_size("group")
    rows, width = w_qk.shape[1], ends.shape[3]
    half = width // 2
    seqs, seq = ends.shape[1], ends.shape[2]
    tokens = seqs * seq
    plan = Plan(count, rows, width, w_fc.shape[2], w_value.shape[1], tokens, seq, HEADS // 2)
    table = plan.table(groups)
    idx = lax.dynamic_slice(jnp.asarray(table), (s, grp, d, 0), (1, 1, 1, table.shape[3])).reshape(-1)
    first, even = s == 0, d % 2 == 0

    def swap_x(x):
        return lax.ppermute(x, "section", [(0, 1), (1, 0)])

    def swap_c(x):
        return lax.ppermute(x, "group", [(i, i ^ 1) for i in range(groups)])

    def swap_d(x, bit):
        return lax.ppermute(x, "dp", [(i, i ^ bit) for i in range(count)])

    hc = count // 2
    spread = [
        [(l * count + i, (i // hc) * count + 2 * (i % hc) + (l if w == 0 else 1 - l)) for l in range(2) for i in range(count)]
        for w in range(2)
    ]
    mine, send, o_lo, o_hi, small = run_pack(
        plan, (w_qk[0], w_fc[0], w_proj[0], w_out[0], gains[0], shifts[0], fc_shift)
    )
    got = swap_x(send)
    small_got = swap_x(small)
    o_a = lax.ppermute(o_lo, ("section", "dp"), spread[0])
    o_b = lax.ppermute(o_hi, ("section", "dp"), spread[1])
    ends_own = ends[0].reshape(tokens, width)
    ends_got = swap_x(after(ends_own, got))
    v_side = (lax.dynamic_slice_in_dim(w_value, s * half, half, 1), w_value[:, width:])
    o_side = (jnp.where(even, o_a, o_b), jnp.where(even, o_b, o_a))

    def head(t, l, other):
        x = jnp.where(first if l == 0 else ~first, mine[t, :rows], got[t, :rows])
        return jnp.where(c == 0, x, other)

    vs_rows = [jnp.pad(x, (0, half - x.shape[0]))[None] for x in (value_shift[:rows], value_shift[rows:])]
    vs_rows = jnp.pad(jnp.concatenate(vs_rows, axis=0), ((11, SMALL - 13), (0, 0)))
    params = [jnp.where(first, x, y) + vs_rows for x, y in ((small, small_got), (small_got, small))]
    early, late = [], []
    for t, side in ((0, v_side), (1, o_side)):
        x, y = mine[t, rows:], got[t, rows:]
        second = jnp.where(first, y, x)
        early.append(jnp.concatenate([head(t, 0, side[0]), jnp.where(first, x, y), head(t, 1, side[1]), params[t]], axis=0))
        late.append(second)

    routes = [[(a, b) for a, b in zip(order, order[1:] + order[:1])] for order in (ring_order(count), ring_order(count)[::-1])]

    def ring(x):
        return [lax.ppermute(x[t], "dp", routes[t]) for t in range(2)]

    steps = [[after(x, idx) for x in early]]
    sibs = []
    for n in range(count - 1):
        sibs.append([swap_c(x) for x in steps[-1]])
        steps.append(ring(steps[-1]))
        if n == 2:
            steps[-1] = [after(x, ends_got) for x in steps[-1]]
        if n >= 2:
            steps[-1] = [after(x, y) for x, y in zip(steps[-1], sibs[n - 1])]
    sibs.append([swap_c(x) for x in steps[-1]])
    chunks = [y for t in range(2) for y in [x[t] for x in steps] + [x[t] for x in sibs]]
    prm, bf = run_param(plan, idx, [x[t] for t in range(2) for x in steps])
    (att_w0, mlp_w0), (att_w1, _) = (run_weights(plan, l, idx, chunks) for l in range(2))

    def doubled(x, *others):
        k = (x[0].shape[0] // late[0].shape[0]).bit_length() - 1
        bits = [plan.orders[t][k] for t in range(2)]
        if bits[0] == bits[1]:
            size = x[0].shape[0]
            both = swap_d(after(jnp.concatenate(x, axis=0), *others), bits[0])
            got = [both[:size], both[size:]]
        else:
            got = [swap_d(after(x[t], *others), bits[t]) for t in range(2)]
        return got

    have = late
    got = first_got = doubled(have, *steps[-2])
    part, q0, k0, v0, p0, o0, a0, h0, cot = run_f1(plan, 0, idx, prm, (ends_own, ends_got), att_w0)
    sib0 = [swap_c(a0), swap_c(o0)]
    for _ in range(plan.bits - 2):
        have = [jnp.concatenate(x, axis=0) for x in zip(have, got)]
        got = doubled(have, part)
    sib0 += list(att_w1)
    second = got
    have = [jnp.concatenate(x, axis=0) for x in zip(have, got)]
    got = after(swap_x(part), *sib0, *first_got)
    part, r0, ucn0, gp0 = run_f2(plan, 0, idx, prm, bf, h0, part, got, mlp_w0)
    have_sib = [swap_c(after(x, part)) for x in have]
    ucn0_sib = swap_c(ucn0)
    got = after(swap_x(part), ucn0_sib, *second)
    more = doubled(have, got)
    part, q1, k1, v1, p1, o1, a1, h1 = run_f1(plan, 1, idx, prm, (r0, part, got, v0), att_w1)
    sib1 = [swap_c(a1), swap_c(o1)]
    got = after(swap_x(part), *sib1)
    parts = [x for t in range(2) for x in (have[t], more[t], have_sib[t], swap_c(after(more[t], part)))]
    mlp_w1 = run_late(plan, idx, parts)
    y_part, r1, ucn1, gp1, oo0 = run_f2(plan, 1, idx, prm, bf, h1, part, got, mlp_w1, o0, sib0[1])

    class Sum:
        def __init__(self, g):
            self.first, self.keep = g[:2], g[2:]
            self.rows = [x.shape[0] // hc for x in self.keep]
            self.came = [[], []]

        def terms(self, t, low):
            return [(self.keep[t], low * self.rows[t])] + [(x, at + low * self.rows[t]) for x, at in self.came[t]]

        def bit(self, t):
            return plan.orders[t][plan.bits - 1 - len(self.came[t])]

        def segment(self, t):
            steps = len(self.came[t])
            if steps == 0:
                return [(self.first[t], 0)], self.first[t].shape[0]
            low = count >> (steps + 1)
            return self.terms(t, low), low * self.rows[t]

    def one_round(sums, *others, lock=True):
        sums = [x for x in sums if len(x.came[0]) < plan.bits]
        if not sums:
            return []
        by_bit = {}
        for x in sums:
            for t in range(2):
                by_bit.setdefault(x.bit(t), []).append((x, t, x.segment(t)))
        bits = sorted(by_bit)
        if all(len(by_bit[b]) == 1 and not by_bit[b][0][0].came[0] for b in bits):
            outs = [by_bit[b][0][2][0][0][0] for b in bits]
        else:
            outs = run_round([[seg for _, _, seg in by_bit[b]] for b in bits])
        got = []
        for b, out in zip(bits, outs):
            here = swap_d(after(out, *others, *(one_round.last if lock else ())), b)
            row = 0
            for x, t, (_, rows_) in by_bit[b]:
                x.came[t].append((here, row))
                row += rows_
            got.append(here)
        one_round.last = got
        return got

    one_round.last = []

    def over_pairs(x):
        total = x
        for n in range(1, groups // 2):
            total = total + lax.ppermute(x, "group", [(i, (i + 2 * n) % groups) for i in range(groups)])
        return total

    part, e, z_keep, z_send, e_send, s2_1, sbf_1 = run_b2(plan, 1, idx, prm, gp1, r1, (cot,), mlp_w1)
    got = swap_x(part)
    mlp1 = Sum(run_g2(plan, idx, ucn1, swap_c(ucn1), e, swap_c(e_send), z_keep, swap_c(z_send)))
    got = after(got, *mlp1.first)
    one_round([mlp1])
    part, dr, keep, send, s1_1, dv1 = run_b1(plan, 1, idx, prm, (cot, part, got, r1, h1, q1, k1, v1, p1), att_w1)
    o1_far = swap_x(after(o1, got))
    got = swap_x(part)
    acts = [a1, sib1[0], o1, sib1[1], o1_far, swap_c(o1_far)]
    att1 = Sum(run_g1(plan, 1, idx, acts, keep, swap_c(send), ()))
    got = after(got, *att1.first)
    came = one_round([mlp1, att1])
    part, e, z_keep, z_send, e_send, s2_0, sbf_0 = run_b2(plan, 0, idx, prm, gp0, r0, (dr, part, got, h1), mlp_w0)
    got = swap_x(part)
    mlp0 = Sum(run_g2(plan, idx, ucn0, ucn0_sib, e, swap_c(e_send), z_keep, swap_c(z_send)))
    got = after(got, *mlp0.first, *came)
    came = one_round([mlp1, att1, mlp0])
    oo_far = swap_x(after(oo0, got))
    part, dr, keep, send, s1_0 = run_b1(plan, 0, idx, prm, (e, part, got, r0, h0, q0, k0, v0, p0, dv1), att_w0)
    acts = [a0, sib0[0], o0, sib0[1], oo_far, oo_far]
    att0 = Sum(run_g1(plan, 0, idx, acts, keep, swap_c(after(send, came[-1])), (s2_0, s1_0, sbf_0, s2_1, s1_1, sbf_1)))
    sums = [att0, att1, mlp0, mlp1]
    x_got = swap_x(after(part, oo_far))
    y_got = swap_x(after(y_part, oo_far))
    res = run_ends(plan, idx, (prm, r1, y_part, y_got, dr, part, x_got, h0)).reshape(1, seqs, seq, width)
    one_round(sums)
    for _ in range(plan.bits - 2):
        one_round(sums, x_got, y_got)

    def ending(sums, first, *others):
        own, send = (over_pairs(x) for x in run_pick(plan, after(idx, *first), [(x.terms(t, 0), x.rows[t]) for t in range(2) for x in sums]))
        far = after(swap_x(send), *others)
        return [own, swap_c(own), far, swap_c(far)], send

    arrived = one_round.last
    one_round(sums, lock=False)
    e_mlp, _ = ending((mlp0, mlp1), arrived)
    o_fc, o_proj = run_finish_mlp(plan, idx, e_mlp)
    e_att, sent = ending((att0, att1), (), o_fc, res)
    o_qk, o_val, o_out, o_gain, o_shift, o_bf, o_vs = run_finish_att(plan, idx, e_att + [sent, swap_c(sent)])

    return (res, o_qk[None], o_val, o_out[None], o_fc[None], o_proj[None], o_gain[None], o_shift[None], o_bf, o_vs[0])


def solution(mesh):
    placed = (
        P("section", ("group", "dp"), None, None),
        P("section", "dp", None),
        P("dp", None),
        P("section", "dp", None),
        P("section", "dp", None),
        P("section", "dp", None),
        P("section", None, "dp"),
        P("section", None, "dp"),
        P("section", "dp"),
        P("dp"),
    )
    return jax.shard_map(per_device, mesh=mesh, in_specs=placed, out_specs=placed, check_vma=False)
```

```python
import functools

import jax
import jax.numpy as jnp
import numpy as np
from jax import lax
from jax.experimental import pallas as pl
from jax.experimental.pallas import tpu as pltpu
from jax.sharding import PartitionSpec as P

HEADS = 12
BF = jnp.bfloat16
F32 = jnp.float32
norm_eps = 1e-05
masked_score = -1e30
TAIL = 32
SMALL = 16
STEP = 32
VMEM_BYTES = 16 * 1024 * 1024


def dot(a, b):
    return jnp.dot(a, b, preferred_element_type=F32)


def dot_tn(a, b):
    return lax.dot_general(a, b, (((0,), (0,)), ((), ())), preferred_element_type=F32)


def dot_nt(a, b):
    return lax.dot_general(a, b, (((1,), (1,)), ((), ())), preferred_element_type=F32)


def unit_rows(v):
    centered = v - jnp.mean(v, axis=-1, keepdims=True)
    inv = lax.rsqrt(jnp.mean(centered * centered, axis=-1, keepdims=True) + norm_eps)
    return centered * inv, inv


def norm_back(dn, x, inv, gain):
    scaled = dn * gain
    inner = jnp.mean(scaled * x, axis=-1, keepdims=True)
    return inv * (scaled - jnp.mean(scaled, axis=-1, keepdims=True) - x * inner)


def row_sum(v):
    return jnp.sum(v, axis=0, keepdims=True)


def ring_order(count):
    wide = 2 if count < 16 else 4
    tall = count // wide
    order = [i * wide for i in range(tall)]
    for n, row in enumerate(reversed(range(tall))):
        cols = range(1, wide)
        order += [row * wide + col for col in (cols if n % 2 == 0 else reversed(cols))]
    return order


class Plan:
    def __init__(self, count, rows, width, ff, values, tokens, seq, heads):
        self.count, self.rows, self.width, self.half = count, rows, width, width // 2
        self.ff, self.fh, self.unit, self.values = ff, ff // 2, ff // count // 2, values
        self.tokens, self.seq, self.seqs = tokens, seq, tokens // seq
        self.pairs = heads // 2
        self.bits = count.bit_length() - 1
        down = [1 << i for i in reversed(range(self.bits))]
        other = down[:-2] + [down[-1], down[-2]]
        self.orders = (down, other)
        self.masks = []
        for order in self.orders:
            mask = [0] * count
            for j in range(count):
                for k, bit in enumerate(order):
                    if j >> k & 1:
                        mask[j] ^= bit
            self.masks.append(mask)

    def core_at(self):
        return 7 * self.count

    def side_at(self):
        return 7 * self.count + 1

    def table(self, groups):
        n = self.count
        out = np.zeros((2, groups, n, 7 * n + 2), np.int32)
        order = ring_order(n)
        for p, d in enumerate(order):
            for t in range(2):
                out[:, :, d, t * n : (t + 1) * n] = [d ^ m for m in self.masks[t]]
                out[:, :, d, (3 + t) * n : (4 + t) * n] = [order[(p - (1 - 2 * t) * j) % n] for j in range(n)]
            for j, m in enumerate(self.masks[0]):
                out[:, :, d, 2 * n + (d ^ m)] = j
            for j in range(n):
                for t in range(2):
                    out[:, :, d, (5 + t) * n + order[(p - (1 - 2 * t) * j) % n]] = j
        out[:, :, :, 7 * n] = (np.arange(groups) % 2)[None, :, None]
        out[:, :, :, 7 * n + 1] = np.arange(2)[:, None, None]
        return out


def aligned(x, size):
    return x if isinstance(x, int) else pl.multiple_of(x, size)


def dma(src, dst, sem):
    return pltpu.make_async_copy(src, dst, sem)


def wait_all(ref, sem):
    dma(ref, ref, sem).wait()


def chunk_refs(plan, idx, chunks, row):
    for j in range(plan.count):
        for t in range(2):
            for other in range(2):
                ref = chunks[(t * 2 + other) * plan.count + j]
                yield t, other, idx[(3 + t) * plan.count + j], ref.at[pl.ds(row, plan.rows), :]


def place_att(plan, layer, idx, chunks, wqk, wv, wo):
    r_, h_ = plan.rows, plan.half
    c = idx[plan.core_at()]
    for t, other, sh, src in chunk_refs(plan, idx, chunks, 3 * r_ * layer):
        core = 1 - c if other else c
        row = pl.multiple_of(sh * r_, 16)

        @pl.when(core == 0)
        def _():
            wqk[pl.ds(row, r_), t * h_ : (t + 1) * h_] = src[...]

        @pl.when(core == 1)
        def _():
            if t == 0:
                wv[pl.ds(row, r_), :] = src[...]
            else:
                orow = pl.multiple_of((sh // 2) * r_, 16)
                ocol = pl.multiple_of((sh % 2) * h_, 128)
                wo[pl.ds(orow, r_), pl.ds(ocol, h_)] = src[...]


def place_mlp(plan, idx, chunks, wfc, wproj):
    r_, h_ = plan.rows, plan.half
    c = idx[plan.core_at()]
    for kind in range(2):
        for t, other, sh, src in chunk_refs(plan, idx, chunks, (1 + kind) * r_):
            core = 1 - c if other else c
            place_mlp_block(plan, kind, t, core, sh, src, wfc, wproj)


def place_mlp_block(plan, kind, t, core, sh, src, wfc, wproj):
    r_, h_ = plan.rows, plan.half
    if kind == 0:
        row = pl.multiple_of(sh * r_, 16)
        col = pl.multiple_of((2 * core + t) * h_, 128)
        wfc[pl.ds(row, r_), pl.ds(col, h_)] = src[...]
    else:
        row = pl.multiple_of(sh * 2 * r_ + t * r_, 16)
        col = pl.multiple_of(core * h_, 128)
        wproj[pl.ds(row, r_), pl.ds(col, h_)] = src[...]


def put_blocks(plan, idx, outs, pick, row0):
    n_, r_ = plan.count, plan.rows
    half = n_ // 2
    for j in reversed(range(n_)):
        for t in range(2):
            out = outs[2 * (0 if j >= half else 1) + t]
            at = j % half * (out.shape[0] // half) + row0
            out[at : at + r_, :] = pick(t, idx[t * n_ + j])


def pack_kernel(plan, *refs):
    from_hbm, (mine, send, o_a, o_b, small), here, sems = refs[:7], refs[7:12], refs[12:19], refs[19]
    for i, ref in enumerate(here):
        dma(from_hbm[i], ref, sems.at[i]).start()
    for i, ref in enumerate(here):
        wait_all(ref, sems.at[i])
    wqk, wfc, wproj, wout, gains, shifts, fc_shift = here
    r_, h_, d_, u_ = plan.rows, plan.half, plan.width, plan.unit
    per = h_ // u_
    s, c = lax.axis_index("section"), lax.rem(lax.axis_index("group"), 2)
    lo, hi = wout[:, :h_], wout[:, h_:]
    o_a[...] = jnp.where(s == 0, lo, hi)
    o_b[...] = jnp.where(s == 0, hi, lo)
    rows = [gains[...], shifts[...]] + [fc_shift[:, i * r_ : (i + 1) * r_] for i in range(4)]
    rows = jnp.concatenate([x.astype(F32) for x in rows] + [jnp.zeros((SMALL - 11, r_), F32)], axis=0)
    small[...] = jnp.concatenate([rows, jnp.zeros((SMALL, h_ - r_), F32)], axis=1).astype(BF)
    for side in range(2):
        for core in range(2):
            for keep in range(2):
                out = mine if keep else send

                @pl.when(jnp.logical_and(c == core, s == (side if keep else 1 - side)))
                def _():
                    for t in range(2):
                        lo = t * d_ + side * h_
                        out[t, :r_] = wqk[:, lo : lo + h_]
                        q = 2 * core + t
                        cols = [(q * per + i) * 2 * u_ + side * u_ for i in range(per)]
                        out[t, r_ : 2 * r_] = jnp.concatenate([wfc[:, x : x + u_] for x in cols], axis=1)
                        row = side * 2 * r_ + t * r_
                        out[t, 2 * r_ :] = wproj[row : row + r_, core * h_ : (core + 1) * h_]


def param_kernel(plan, idx, *refs):
    n_, r_, h_, d_ = plan.count, plan.rows, plan.half, plan.width
    s = idx[plan.side_at()]
    steps, (prm, bf, stack) = refs[: 2 * n_], refs[2 * n_ :]
    for j, ref in enumerate(steps):
        stack[j // n_, j % n_] = ref[4 * r_ :, :]
    pairs = [[stack[t, idx[(5 + t) * n_ + sh]][:, :r_].astype(F32) for t in range(2)] for sh in range(n_)]
    more = plan.values // n_ - r_
    vals = jnp.concatenate([x for b, _ in pairs for x in (b[11:12, :], b[12:13, :more])], axis=1)
    for l in range(2):
        blocks = [b[l] for b in pairs]
        m = jnp.concatenate([b[:7] for b in blocks], axis=1)
        prm[l, 0:7] = m
        bq = jnp.where(s == 0, m[4:5, :h_], m[4:5, h_:])
        prm[l, 4:5] = jnp.concatenate([bq, jnp.zeros((1, d_ - h_), F32)], axis=1)
        if l == 0:
            bv = jnp.where(s == 0, vals[:, :h_], vals[:, h_:d_])
        else:
            bv = vals[:, d_:]
        prm[l, 7:8] = jnp.concatenate([bv, jnp.zeros((1, d_ - h_), F32)], axis=1)
        sides = []
        for side in range(2):
            row = 7 + 2 * side
            sides.append(jnp.concatenate([b[row + i : row + i + 1] for b in blocks for i in range(2)], axis=1))
        bf[l] = jnp.where(s == 0, sides[0], sides[1])


def att_weights_kernel(plan, layer, *refs):
    place_att(plan, layer, refs[0], refs[1:-3], *refs[-3:])


def mlp_weights_kernel(plan, *refs):
    place_mlp(plan, refs[0], refs[1 : 1 + 4 * plan.count], *refs[1 + 4 * plan.count :])


def late_weights_kernel(plan, *refs):
    n_, r_ = plan.count, plan.rows
    idx, parts, (wfc, wproj) = refs[0], refs[1:9], refs[9:]
    c = idx[plan.core_at()]
    for t in range(2):
        for other in range(2):
            core = 1 - c if other else c
            for j in range(n_):
                part = parts[(2 * t + other) * 2 + j // (n_ // 2)]
                for kind in range(2):
                    src = part.at[pl.ds((j % (n_ // 2) * 2 + kind) * r_, r_), :]
                    place_mlp_block(plan, kind, t, core, idx[t * n_ + j], src, wfc, wproj)


def pair_mask(seq, lanes):
    return lax.broadcasted_iota(jnp.int32, (seq, lanes), 1) < lanes // 2


def stack_pair(x, low):
    zero = jnp.zeros_like(x)
    return jnp.concatenate([jnp.where(low, x, zero), jnp.where(low, zero, x)], axis=0)


def f1_kernel(plan, layer, *refs):
    h_, t_, sq = plan.half, plan.tokens, plan.seq
    idx, prm, refs = refs[0], refs[1], refs[2:]
    if layer == 1:
        r_up, pa, pb, v_old = refs[:4]
        refs = refs[4:]
    else:
        here, there = refs[:2]
        refs = refs[2:]
    weights, refs = refs[:3], refs[3:]
    part, q, k, v, p, o, a, h = refs[:8]
    if layer == 0:
        cot = refs[8]
    wqk, wv, wo = weights
    first = idx[plan.side_at()] == 0
    for i in range(0, t_, STEP):
        sl = slice(i, i + STEP)
        if layer == 1:
            hh = r_up[sl, :] + (pa[sl, :].astype(F32) + pb[sl, :].astype(F32)) + prm[0, 6:7, :]
            h[sl, :] = hh.astype(BF)
        else:
            mine, theirs = here[sl, :], there[sl, :]
            h[sl, :] = jnp.where(first, mine, theirs)
            cot[sl, :] = jnp.where(first, theirs, mine)
        x, _ = unit_rows(h[sl, :].astype(F32))
        a[sl, :] = (x * prm[layer, 0:1, :] + prm[layer, 2:3, :]).astype(BF)
    qk = dot(a[...], wqk[...])
    q[...] = (qk[:, :h_] + prm[layer, 4:5, :h_]).astype(BF)
    k[...] = qk[:, h_:].astype(BF)
    val = (dot(a[...], wv[...]) + prm[layer, 7:8, :h_]).astype(BF)
    if layer == 1:
        val = jnp.where(idx[plan.side_at()] == 1, v_old[...], val)
    v[...] = val
    lanes = h_ // plan.pairs
    low = pair_mask(sq, lanes)
    causal = lax.broadcasted_iota(jnp.int32, (2 * sq, sq), 0) % sq >= lax.broadcasted_iota(jnp.int32, (2 * sq, sq), 1)
    scale = (lanes // 2) ** -0.5
    for s_ in range(plan.seqs):
        for j in range(plan.pairs):
            rws, cls = slice(s_ * sq, (s_ + 1) * sq), slice(j * lanes, (j + 1) * lanes)
            q2 = stack_pair(q[rws, cls], low)
            sc = jnp.where(causal, dot_nt(q2, k[rws, cls]) * scale, masked_score)
            ex = jnp.exp(sc - jnp.max(sc, axis=-1, keepdims=True))
            pr = (ex / jnp.sum(ex, axis=-1, keepdims=True)).astype(BF)
            p[s_ * plan.pairs + j] = pr
            o2 = dot(pr, v[rws, cls])
            o[rws, cls] = jnp.where(low, o2[:sq], o2[sq:]).astype(BF)
    part[...] = dot(o[...], wo[...]).astype(BF)


def f2_kernel(plan, layer, *refs):
    t_ = plan.tokens
    idx, prm, bf, h, pa, pb = refs[:6]
    if layer == 1:
        o_up, refs = refs[8:10], refs[:8] + refs[10:]
    weights, refs = refs[6:8], refs[8:]
    part, r, ucn, gp, *oo, z = refs
    wfc, wproj = weights
    f_ = plan.fh
    for i in range(0, t_, STEP):
        sl = slice(i, i + STEP)
        rr = h[sl, :].astype(F32) + (pa[sl, :].astype(F32) + pb[sl, :].astype(F32)) + prm[layer, 5:6, :]
        r[sl, :] = rr
        x, _ = unit_rows(rr)
        ucn[sl, f_:] = (x * prm[layer, 1:2, :] + prm[layer, 3:4, :]).astype(BF)
    cols = plan.fh // 3
    for j in range(3):
        cs = slice(j * cols, (j + 1) * cols)
        z[...] = dot(ucn[:, f_:], wfc[:, cs])

        def body(i, carry):
            sl = pl.ds(pl.multiple_of(i * STEP, STEP), STEP)
            zz = z[sl, :] + bf[layer, :, cs]
            sq_ = zz * zz
            th = jnp.tanh(0.7978845608 * zz * (1.0 + 0.044715 * sq_))
            hp = 0.5 * (1.0 + th)
            ucn[sl, cs] = (zz * hp).astype(BF)
            slope = 0.7978845608 * (1.0 + 3 * 0.044715 * sq_)
            gp[sl, cs] = (hp + 0.5 * zz * (1.0 - th * th) * slope).astype(BF)
            return carry

        lax.fori_loop(0, t_ // STEP, body, 0)
    part[...] = dot(ucn[:, :f_], wproj[...]).astype(BF)
    if layer == 1:
        oo[0][:, : plan.half] = o_up[0][...]
        oo[0][:, plan.half :] = o_up[1][...]


def b2_kernel(plan, layer, *refs):
    d_, t_, f_ = plan.width, plan.tokens, plan.fh
    idx, prm, gp, r = refs[:4]
    refs = refs[4:]
    if layer == 1:
        e, refs = refs[0], refs[1:]
    else:
        dr, da_a, da_b, h_up = refs[:4]
        refs = refs[4:]
    weights, refs = refs[:2], refs[2:]
    part, e_out, z_keep, z_send, e_send, sums, sbf = refs[:7]
    h_, c = plan.half, idx[plan.core_at()]
    wfc, wproj = weights
    acc, dz = refs[-2:]
    zero = jnp.zeros((1, d_), F32)
    sb4 = zero
    for i in range(0, t_, STEP):
        sl = slice(i, i + STEP)
        if layer == 0:
            x, inv = unit_rows(h_up[sl, :].astype(F32))
            dn = da_a[sl, :].astype(F32) + da_b[sl, :].astype(F32)
            ee = (dr[sl, :] + norm_back(dn, x, inv, prm[1, 0:1, :])).astype(BF)
        else:
            ee = e[sl, :]
        e_out[sl, :] = ee
        sb4 = sb4 + row_sum(ee.astype(F32))
    cols = f_ // 3
    for j in range(3):
        cs = slice(j * cols, (j + 1) * cols)
        dzj = (dot_nt(e_out[...], wproj[cs, :]) * gp[:, cs].astype(F32)).astype(BF)
        dz[:, cs] = dzj
        sbf[:, cs] = row_sum(dzj.astype(F32))
    z_keep[...] = dz[:, pl.ds(pl.multiple_of(c * d_, 128), d_)]
    z_send[...] = dz[:, pl.ds(pl.multiple_of((1 - c) * d_, 128), d_)]
    e_send[...] = e_out[:, pl.ds(pl.multiple_of((1 - c) * h_, 128), h_)]
    acc[...] = dot_nt(dz[...], wfc[...])
    sg1, sb1 = zero, zero
    for i in range(0, t_, STEP):
        sl = slice(i, i + STEP)
        dn = acc[sl, :]
        part[sl, :] = dn.astype(BF)
        x, _ = unit_rows(r[sl, :])
        sg1 = sg1 + row_sum(dn * x)
        sb1 = sb1 + row_sum(dn)
    sums[0:1, :], sums[1:2, :], sums[2:3, :] = sg1, sb1, 0.5 * sb4


def g2_kernel(plan, *refs):
    r_, h_, f_ = plan.rows, plan.half, plan.fh
    idx, ucn, ucn_sib, e, e_sib, dz, dz_sib = refs[:7]
    outs, (gfc, gproj) = refs[7:-2], refs[-2:]
    c = idx[plan.core_at()]
    ecols = pl.ds(pl.multiple_of(c * h_, 128), h_)
    gproj[...] = (dot_tn(ucn[:, :f_], e[:, ecols]) + dot_tn(ucn_sib[:, :f_], e_sib[...])).astype(BF)
    put_blocks(plan, idx, outs, lambda t, sh: gproj[pl.ds(pl.multiple_of(sh * 2 * r_ + t * r_, 16), r_), :], r_)
    gfc[...] = (dot_tn(ucn[:, f_:], dz[...]) + dot_tn(ucn_sib[:, f_:], dz_sib[...])).astype(BF)
    put_blocks(plan, idx, outs, lambda t, sh: gfc[pl.ds(pl.multiple_of(sh * r_, 16), r_), t * h_ : (t + 1) * h_], 0)


def b1_kernel(plan, layer, *refs):
    h_, d_, t_, sq = plan.half, plan.width, plan.tokens, plan.seq
    idx, prm, e, dc_a, dc_b, r, h, q, k, v, p = refs[:11]
    refs = refs[11:]
    if layer == 0:
        extra, refs = refs[0], refs[1:]
    weights, refs = refs[:3], refs[3:]
    part, dr, keep, send, sums = refs[:5]
    refs = refs[5:]
    if layer == 1:
        dv_out, refs = refs[0], refs[1:]
    else:
        dv_out, refs = refs[-1], refs[:-1]
    wqk, wv, wo = weights
    dy, dqk, do, acc = refs
    s, c = idx[plan.side_at()], idx[plan.core_at()]
    zero = jnp.zeros((1, d_), F32)
    sb3 = zero
    for i in range(0, t_, STEP):
        sl = slice(i, i + STEP)
        x, inv = unit_rows(r[sl, :])
        dn = dc_a[sl, :].astype(F32) + dc_b[sl, :].astype(F32)
        dd = e[sl, :].astype(F32) + norm_back(dn, x, inv, prm[layer, 1:2, :])
        dr[sl, :] = dd
        dyb = dd.astype(BF)
        dy[sl, :] = dyb
        sb3 = sb3 + row_sum(dyb.astype(F32))
    do[...] = dot_nt(dy[...], wo[...]).astype(BF)
    lanes = h_ // plan.pairs
    low = pair_mask(sq, lanes)
    scale = (lanes // 2) ** -0.5
    for s_ in range(plan.seqs):
        for j in range(plan.pairs):
            rws, cls = slice(s_ * sq, (s_ + 1) * sq), slice(j * lanes, (j + 1) * lanes)
            kcls = slice(h_ + j * lanes, h_ + (j + 1) * lanes)
            q2 = stack_pair(q[rws, cls], low)
            do2 = stack_pair(do[rws, cls], low)
            pr = p[s_ * plan.pairs + j]
            dp = dot_nt(do2, v[rws, cls])
            dv = dot_tn(pr, do2)
            if layer == 0:
                dv = dv + extra[rws, cls].astype(F32) * (s == 1).astype(F32)
            dv_out[rws, cls] = dv.astype(BF)
            pf = pr.astype(F32)
            ds = (pf * (dp - jnp.sum(pf * dp, axis=-1, keepdims=True))).astype(BF)
            dq2 = dot(ds, k[rws, cls])
            dqk[rws, cls] = (jnp.where(low, dq2[:sq], dq2[sq:]) * scale).astype(BF)
            dqk[rws, kcls] = (dot_tn(ds, q2) * scale).astype(BF)
    da = dot_nt(dqk[...], wqk[...])
    dav = dot_nt(dv_out[...], wv[...])
    if layer == 1:
        dav = dav * (s == 0).astype(F32)
    acc[...] = da + dav
    dys = pl.ds(pl.multiple_of(s * h_, 128), h_)
    for core in range(2):

        @pl.when(c == core)
        def _():
            one, two = (keep, send) if core == 0 else (send, keep)
            one[...] = dqk[...]
            two[:, :h_] = dv_out[...]
            two[:, h_:] = dy[:, dys]

    sg0, sb0 = zero, zero
    for i in range(0, t_, STEP):
        sl = slice(i, i + STEP)
        dn = acc[sl, :]
        part[sl, :] = dn.astype(BF)
        x, _ = unit_rows(h[sl, :].astype(F32))
        sg0 = sg0 + row_sum(dn * x)
        sb0 = sb0 + row_sum(dn)
    sums[0:1, :], sums[1:2, :], sums[2:3, :] = sg0, sb0, 0.5 * sb3
    sq_ = row_sum(dqk[...].astype(F32))[:, :h_]
    none = jnp.zeros((1, h_), F32)
    sums[3:4, :] = jnp.where(s == 0, jnp.concatenate([sq_, none], axis=1), jnp.concatenate([none, sq_], axis=1))
    sums[4:5, :] = jnp.concatenate([row_sum(dv_out[...].astype(F32)), none], axis=1)


def g1_kernel(plan, layer, *refs):
    r_, h_, d_, n_ = plan.rows, plan.half, plan.width, plan.count
    idx, a, a_sib, o, o_sib, far, far_sib, keep, got = refs[:9]
    refs = refs[9:]
    if layer == 0:
        tiny, refs = refs[:6], refs[6:]
    outs, refs = refs[:4], refs[4:]
    gatt = refs[0]
    c = idx[plan.core_at()]

    @pl.when(c == 0)
    def _():
        gatt[...] = (dot_tn(a[...], keep[...]) + dot_tn(a_sib[...], got[...])).astype(BF)

    @pl.when(c == 1)
    def _():
        gatt[:, :h_] = (dot_tn(a[...], keep[:, :h_]) + dot_tn(a_sib[...], got[:, :h_])).astype(BF)
        s = idx[plan.side_at()]
        apart = far.shape[1] - h_
        for side, x, y, at in ((s, o, o_sib, 0), (1 - s, far, far_sib, apart)):
            rows = pl.ds(pl.multiple_of(side * h_, 16), h_)
            gatt[rows, h_:] = (dot_tn(x[:, :h_], keep[:, h_:]) + dot_tn(y[:, at:], got[:, h_:])).astype(BF)

    put_blocks(plan, idx, outs, lambda t, sh: gatt[pl.ds(pl.multiple_of(sh * r_, 16), r_), t * h_ : (t + 1) * h_], 0)
    if layer == 0:
        tail = refs[1]
        small_sums(plan, idx, tiny, tail)
        half = n_ // 2
        for j in range(n_):
            out, at = outs[0 if j >= half else 2], j % half * (r_ + TAIL) + r_
            out[at : at + TAIL, :] = tail[j]


def small_sums(plan, idx, tiny, tail):
    n_, r_, h_, d_, u_ = plan.count, plan.rows, plan.half, plan.width, plan.unit
    s = idx[plan.side_at()]
    rows = []
    for l in range(2):
        s2, s1, sbf = tiny[3 * l : 3 * l + 3]
        rows += [s1[0:1], s2[0:1], s1[1:2], s2[1:2], s1[3:4], s1[2:3], s2[2:3]]
        bf = sbf[...]
        cut = [jnp.concatenate([bf[:, sh * u_ + i * r_ : sh * u_ + (i + 1) * r_] for sh in range(n_)], axis=1) for i in range(2)]
        for side in range(2):
            on = (s == side).astype(F32)
            rows += [cut[0] * on, cut[1] * on]
    v1, v2 = tiny[1][4:5, :h_], tiny[4][4:5, :h_]
    first = (s == 0).astype(F32)
    vals = jnp.concatenate([v1 * first, v1 * (1.0 - first), v2 * first], axis=1)
    each = plan.values // n_
    pad = jnp.zeros((1, 2 * r_ - each), F32)
    rows.append(jnp.concatenate([vals[:, sh * each : sh * each + r_] for sh in range(n_)], axis=1))
    rows.append(jnp.concatenate([x for sh in range(n_) for x in (vals[:, sh * each + r_ : (sh + 1) * each], pad)], axis=1))
    rows.append(jnp.zeros((TAIL - 24, d_), F32))
    full = jnp.concatenate(rows, axis=0).astype(BF)
    for sh in range(n_):
        block = jnp.concatenate([full[:, sh * r_ : (sh + 1) * r_], jnp.zeros((TAIL, h_ - r_), BF)], axis=1)
        tail[idx[2 * n_ + sh]] = block


def total(refs, terms, rows):
    x = None
    for at, row in terms:
        y = refs[at][row : row + rows, :].astype(F32)
        x = y if x is None else x + y
    return x.astype(BF)


def round_kernel(plans, n, *refs):
    for out, segments in zip(refs[n:], plans):
        row = 0
        for terms, rows in segments:
            out[row : row + rows, :] = total(refs, terms, rows)
            row += rows


def listed(segments):
    arrays, plans = [], []
    for terms, rows in segments:
        named = []
        for x, row in terms:
            at = next((i for i, y in enumerate(arrays) if y is x), len(arrays))
            if at == len(arrays):
                arrays.append(x)
            named.append((at, row))
        plans.append((named, rows))
    return arrays, plans


def run_round(outs):
    arrays, plans = listed([seg for segments in outs for seg in segments])
    cut, at = [], 0
    for segments in outs:
        cut.append(plans[at : at + len(segments)])
        at += len(segments)
    width = arrays[0].shape[1]
    shapes = [((sum(rows for _, rows in segments), width), BF, VM) for segments in outs]
    return call(functools.partial(round_kernel, cut, len(arrays)), vm(*arrays), shapes, [], 1.2)


def pick_kernel(plans, n, side_at, idx, *refs):
    own, send = refs[n:]
    first = idx[side_at] == 0
    sums = [total(refs, terms, rows) for terms, rows in plans]
    size = sums[1].shape[0]
    for t in range(2):
        x, y = sums[2 * t][:size], sums[2 * t + 1]
        own[t * size : (t + 1) * size] = jnp.where(first, x, y)
        send[t * size : (t + 1) * size] = jnp.where(first, y, x)
    if sums[0].shape[0] > size:
        for ref in (own, send):
            ref[2 * size :] = sums[0]


def run_pick(plan, idx, segments):
    arrays, plans = listed(segments)
    one, two = segments[0][1], segments[1][1]
    shape = (2 * two + (one if one > two else 0), plan.half)
    kernel = functools.partial(pick_kernel, plans, len(arrays), plan.side_at())
    return call(kernel, [(idx, SM)] + vm(*arrays), [(shape, BF, VM)] * 2, [], 1.0)


def finish_mlp_kernel(plan, idx, *refs):
    r_, h_, u_ = plan.rows, plan.half, plan.unit
    mlp, (o_fc, o_proj) = refs[:4], refs[4:]
    s, c = idx[plan.side_at()], idx[plan.core_at()]
    per = h_ // u_
    for t in range(2):
        fc = [[None] * 2, [None] * 2]
        for i in range(2):
            a, b = mlp[2 * i], mlp[2 * i + 1]
            for core in range(2):
                x = jnp.where(c == core, a[2 * t * r_ : (2 * t + 2) * r_, :], b[2 * t * r_ : (2 * t + 2) * r_, :])
                fc[i][core] = x[:r_]
                for side in range(2):

                    @pl.when((s == side) if i == 0 else (s != side))
                    def _():
                        lo = side * 2 * r_ + t * r_
                        o_proj[lo : lo + r_, core * h_ : (core + 1) * h_] = x[r_:].astype(F32)

        for core in range(2):
            q = 2 * core + t
            b0 = jnp.where(s == 0, fc[0][core], fc[1][core]).astype(F32)
            b1 = jnp.where(s == 0, fc[1][core], fc[0][core]).astype(F32)
            pieces = [x[:, i * u_ : (i + 1) * u_] for i in range(per) for x in (b0, b1)]
            o_fc[:, 2 * q * h_ : 2 * (q + 1) * h_] = jnp.concatenate(pieces, axis=1)


def finish_att_kernel(plan, idx, *refs):
    r_, h_, d_ = plan.rows, plan.half, plan.width
    att, val = refs[:4], refs[4:6]
    o_qk, o_val, o_out, o_gain, o_shift, o_bf, o_vs = refs[6:]
    s, c = idx[plan.side_at()], idx[plan.core_at()]

    def block(side, core, lo, hi):
        pick = [jnp.where(c == core, att[2 * i][lo:hi, :], att[2 * i + 1][lo:hi, :]) for i in range(2)]
        return jnp.where(s == side, pick[0], pick[1]).astype(F32)

    sm = sum(x[3 * r_ :, :r_].astype(F32) for x in att)
    mine = jnp.where(s == 0, sm[:11], sm[11:22])
    o_gain[...] = mine[0:2]
    o_shift[...] = mine[2:7]
    o_bf[...] = jnp.concatenate([mine[7 + i : 8 + i] for i in range(4)], axis=1)
    o_vs[...] = jnp.concatenate([sm[22:23], sm[23:24, : plan.values // plan.count - r_]], axis=1)
    low, high = block(0, 1, 0, r_), block(1, 1, 0, r_)
    other, rest = jnp.where(c == 1, val[0][:r_, :], val[1][:r_, :]).astype(F32), block(0, 1, 2 * r_, 3 * r_)
    o_val[:, :h_] = jnp.where(s == 0, low, rest)
    o_val[:, h_:d_] = jnp.where(s == 0, high, other)
    o_val[:, d_:] = jnp.where(s == 0, other, low)
    for side in range(2):
        o_out[:, side * h_ : (side + 1) * h_] = block(side, 1, r_, 2 * r_)
        for t in range(2):
            o_qk[:, t * d_ + side * h_ : t * d_ + (side + 1) * h_] = block(side, 0, t * r_, (t + 1) * r_)


def ends_kernel(plan, idx, prm, r, y_a, y_b, dr, da_a, da_b, h, out):
    s = idx[plan.side_at()]

    @pl.when(s == 1)
    def _():
        for i in range(0, plan.tokens, STEP):
            sl = slice(i, i + STEP)
            out[sl, :] = (r[sl, :] + (y_a[sl, : plan.width].astype(F32) + y_b[sl, : plan.width].astype(F32)) + prm[1, 6:7, :]).astype(BF)

    @pl.when(s == 0)
    def _():
        for i in range(0, plan.tokens, STEP):
            sl = slice(i, i + STEP)
            x, inv = unit_rows(h[sl, :].astype(F32))
            dn = da_a[sl, :].astype(F32) + da_b[sl, :].astype(F32)
            out[sl, :] = (dr[sl, :] + norm_back(dn, x, inv, prm[0, 0:1, :])).astype(BF)


VM = pl.BlockSpec(memory_space=pltpu.VMEM)
SM = pl.BlockSpec(memory_space=pltpu.SMEM)
ANY = pl.BlockSpec(memory_space=pl.ANY)
HBM = pl.BlockSpec(memory_space=pltpu.HBM)


def call(kernel, ins, outs, scratch, us, vmem=VMEM_BYTES):
    return pl.pallas_call(
        kernel,
        out_shape=[jax.ShapeDtypeStruct(sh, dt) for sh, dt, _ in outs],
        in_specs=[sp for _, sp in ins],
        out_specs=[sp for _, _, sp in outs],
        scratch_shapes=scratch,
        compiler_params=pltpu.CompilerParams(vmem_limit_bytes=vmem),
        cost_estimate=pl.CostEstimate(flops=int(us * 4.2e8), bytes_accessed=1000, transcendentals=0),
    )(*[x for x, _ in ins])


def vm(*arrays):
    return [(x, VM) for x in arrays]


def hbm(arrays):
    return [(x, ANY) for x in arrays]


def run_weights(plan, layer, idx, chunks):
    w, h, f = plan.width, plan.half, plan.fh
    ins = [(idx, SM)] + vm(*chunks)
    att = call(functools.partial(att_weights_kernel, plan, layer), ins, [((w, w), BF, VM), ((w, h), BF, VM), ((h, w), BF, VM)], [], 1.2)
    mlp = None
    if layer == 0:
        mlp = call(functools.partial(mlp_weights_kernel, plan), ins, [((w, f), BF, VM), ((f, w), BF, VM)], [], 1.5)
    return att, mlp


def run_late(plan, idx, parts):
    outs = [((plan.width, plan.fh), BF, VM), ((plan.fh, plan.width), BF, VM)]
    return call(functools.partial(late_weights_kernel, plan), [(idx, SM)] + vm(*parts), outs, [], 1.5)


def dma_sems(n):
    return pltpu.SemaphoreType.DMA((n,))


def run_pack(plan, arrays):
    r_, h_ = plan.rows, plan.half
    both, one = ((2, 3 * r_, h_), BF, VM), ((r_, h_), BF, VM)
    outs = [both, both, one, one, ((SMALL, h_), BF, VM)]
    scratch = [pltpu.VMEM(x.shape, BF) for x in arrays] + [dma_sems(7)]
    ins = [(x, HBM) for x in arrays]
    return call(functools.partial(pack_kernel, plan), ins, outs, scratch, 1.5, 60 * 1024 * 1024)


def run_param(plan, idx, arrays):
    outs = [((2, 8, plan.width), F32, VM), ((2, 1, plan.fh), F32, VM)]
    scratch = [pltpu.VMEM((2, plan.count, SMALL, plan.half), BF)]
    return call(functools.partial(param_kernel, plan), [(idx, SM)] + vm(*arrays), outs, scratch, 1.0)


def run_f1(plan, layer, idx, prm, inputs, weights):
    t_, h_, d_ = plan.tokens, plan.half, plan.width
    narrow, wide = ((t_, h_), BF, VM), ((t_, d_), BF, VM)
    outs = [wide, narrow, narrow, narrow, ((plan.seqs * plan.pairs, 2 * plan.seq, plan.seq), BF, VM), narrow, wide]
    outs += [wide] if layer else [wide, wide]
    scratch = []
    ins = [(idx, SM)] + vm(prm, *inputs, *weights)
    return call(functools.partial(f1_kernel, plan, layer), ins, outs, scratch, 2.5)


def run_f2(plan, layer, idx, prm, bf, h, pa, pb, weights, *more):
    t_, d_, f_ = plan.tokens, plan.width, plan.fh
    wide = ((t_, d_), BF, VM)
    outs = [wide, ((t_, d_), F32, VM), ((t_, f_ + d_), BF, VM), ((t_, f_), BF, VM)] + ([wide] if layer else [])
    scratch = [pltpu.VMEM((t_, f_ // 3), F32)]
    ins = [(idx, SM)] + vm(prm, bf, h, pa, pb, *weights, *more)
    return call(functools.partial(f2_kernel, plan, layer), ins, outs, scratch, 4.4)


def run_b2(plan, layer, idx, prm, gp, r, more, weights):
    t_, d_, f_ = plan.tokens, plan.width, plan.fh
    outs = [((t_, d_), BF, VM)] * 4 + [((t_, plan.half), BF, VM), ((3, d_), F32, VM), ((1, f_), F32, VM)]
    scratch = [pltpu.VMEM((t_, d_), F32), pltpu.VMEM((t_, f_), BF)]
    ins = [(idx, SM)] + vm(prm, gp, r, *more, *weights)
    return call(functools.partial(b2_kernel, plan, layer), ins, outs, scratch, 2.6 if layer else 0.3)


def grad_outs(plan, rows, tail=0):
    return [((plan.count // 2 * r, plan.half), BF, VM) for r in (rows + tail, rows) * 2]


def run_g2(plan, idx, *arrays):
    d_, f_, h_ = plan.width, plan.fh, plan.half
    scratch = [pltpu.VMEM((d_, d_), BF), pltpu.VMEM((f_, h_), BF)]
    ins = [(idx, SM)] + vm(*arrays)
    return call(functools.partial(g2_kernel, plan), ins, grad_outs(plan, 2 * plan.rows), scratch, 4.6)


def run_b1(plan, layer, idx, prm, more, weights):
    t_, d_, h_ = plan.tokens, plan.width, plan.half
    wide, narrow = (t_, d_), (t_, h_)
    outs = [(wide, BF, VM), (wide, F32, VM), (wide, BF, VM), (wide, BF, VM), ((5, d_), F32, VM)]
    scratch = [pltpu.VMEM(wide, BF), pltpu.VMEM(wide, BF), pltpu.VMEM(narrow, BF), pltpu.VMEM(wide, F32)]
    if layer:
        outs.append((narrow, BF, VM))
    else:
        scratch.append(pltpu.VMEM(narrow, BF))
    ins = [(idx, SM)] + vm(prm, *more, *weights)
    return call(functools.partial(b1_kernel, plan, layer), ins, outs, scratch, 0.5 if layer else 4.5)


def run_g1(plan, layer, idx, acts, keep, got, tiny):
    d_, h_ = plan.width, plan.half
    scratch = [pltpu.VMEM((d_, d_), BF)]
    if layer == 0:
        scratch += [pltpu.VMEM((plan.count, TAIL, h_), BF)]
    ins = [(idx, SM)] + vm(*acts, keep, got, *tiny)
    return call(functools.partial(g1_kernel, plan, layer), ins, grad_outs(plan, plan.rows, 0 if layer else TAIL), scratch, 0.3 if layer else 1.8)


def run_finish_mlp(plan, idx, arrays):
    outs = [(sh, F32, VM) for sh in ((plan.rows, plan.ff), (4 * plan.rows, plan.width))]
    return call(functools.partial(finish_mlp_kernel, plan), [(idx, SM)] + vm(*arrays), outs, [], 3.0)


def run_finish_att(plan, idx, arrays):
    r_, d_ = plan.rows, plan.width
    outs = [(sh, F32, VM) for sh in ((r_, 2 * d_), (r_, plan.values), (r_, d_), (2, r_), (5, r_), (1, 4 * r_), (1, plan.values // plan.count))]
    return call(functools.partial(finish_att_kernel, plan), [(idx, SM)] + vm(*arrays), outs, [], 2.5)


def run_ends(plan, idx, arrays):
    return call(functools.partial(ends_kernel, plan), [(idx, SM)] + vm(*arrays), [((plan.tokens, plan.width), BF, VM)], [], 1.9)[0]


def after(x, *earlier):
    return lax.optimization_barrier((x,) + earlier)[0]


def per_device(ends, w_qk, w_value, w_out, w_fc, w_proj, gains, shifts, fc_shift, value_shift):
    s, grp, d = lax.axis_index("section"), lax.axis_index("group"), lax.axis_index("dp")
    c = grp % 2
    count, groups = lax.axis_size("dp"), lax.axis_size("group")
    rows, width = w_qk.shape[1], ends.shape[3]
    half = width // 2
    seqs, seq = ends.shape[1], ends.shape[2]
    tokens = seqs * seq
    plan = Plan(count, rows, width, w_fc.shape[2], w_value.shape[1], tokens, seq, HEADS // 2)
    table = plan.table(groups)
    idx = lax.dynamic_slice(jnp.asarray(table), (s, grp, d, 0), (1, 1, 1, table.shape[3])).reshape(-1)
    first, even = s == 0, d % 2 == 0

    def swap_x(x):
        return lax.ppermute(x, "section", [(0, 1), (1, 0)])

    def swap_c(x):
        return lax.ppermute(x, "group", [(i, i ^ 1) for i in range(groups)])

    def swap_d(x, bit):
        return lax.ppermute(x, "dp", [(i, i ^ bit) for i in range(count)])

    hc = count // 2
    spread = [
        [(l * count + i, (i // hc) * count + 2 * (i % hc) + (l if w == 0 else 1 - l)) for l in range(2) for i in range(count)]
        for w in range(2)
    ]
    mine, send, o_lo, o_hi, small = run_pack(
        plan, (w_qk[0], w_fc[0], w_proj[0], w_out[0], gains[0], shifts[0], fc_shift)
    )
    got = swap_x(send)
    small_got = swap_x(small)
    o_a = lax.ppermute(o_lo, ("section", "dp"), spread[0])
    o_b = lax.ppermute(o_hi, ("section", "dp"), spread[1])
    ends_own = ends[0].reshape(tokens, width)
    ends_got = swap_x(after(ends_own, got))
    v_side = (lax.dynamic_slice_in_dim(w_value, s * half, half, 1), w_value[:, width:])
    o_side = (jnp.where(even, o_a, o_b), jnp.where(even, o_b, o_a))

    def head(t, l, other):
        x = jnp.where(first if l == 0 else ~first, mine[t, :rows], got[t, :rows])
        return jnp.where(c == 0, x, other)

    vs_rows = [jnp.pad(x, (0, half - x.shape[0]))[None] for x in (value_shift[:rows], value_shift[rows:])]
    vs_rows = jnp.pad(jnp.concatenate(vs_rows, axis=0), ((11, SMALL - 13), (0, 0)))
    params = [jnp.where(first, x, y) + vs_rows for x, y in ((small, small_got), (small_got, small))]
    early, late = [], []
    for t, side in ((0, v_side), (1, o_side)):
        x, y = mine[t, rows:], got[t, rows:]
        second = jnp.where(first, y, x)
        early.append(jnp.concatenate([head(t, 0, side[0]), jnp.where(first, x, y), head(t, 1, side[1]), params[t]], axis=0))
        late.append(second)

    routes = [[(a, b) for a, b in zip(order, order[1:] + order[:1])] for order in (ring_order(count), ring_order(count)[::-1])]

    def ring(x):
        return [lax.ppermute(x[t], "dp", routes[t]) for t in range(2)]

    steps = [[after(x, idx) for x in early]]
    sibs = []
    for n in range(count - 1):
        sibs.append([swap_c(x) for x in steps[-1]])
        steps.append(ring(steps[-1]))
        if n == 2:
            steps[-1] = [after(x, ends_got) for x in steps[-1]]
        if n >= 2:
            steps[-1] = [after(x, y) for x, y in zip(steps[-1], sibs[n - 2])]
    sibs.append([swap_c(x) for x in steps[-1]])
    chunks = [y for t in range(2) for y in [x[t] for x in steps] + [x[t] for x in sibs]]
    prm, bf = run_param(plan, idx, [x[t] for t in range(2) for x in steps])
    (att_w0, mlp_w0), (att_w1, _) = (run_weights(plan, l, idx, chunks) for l in range(2))

    def doubled(x, *others):
        k = (x[0].shape[0] // late[0].shape[0]).bit_length() - 1
        bits = [plan.orders[t][k] for t in range(2)]
        if bits[0] == bits[1]:
            size = x[0].shape[0]
            both = swap_d(after(jnp.concatenate(x, axis=0), *others), bits[0])
            got = [both[:size], both[size:]]
        else:
            got = [swap_d(after(x[t], *others), bits[t]) for t in range(2)]
        return got

    have = late
    got = first_got = doubled(have, *steps[-2])
    part, q0, k0, v0, p0, o0, a0, h0, cot = run_f1(plan, 0, idx, prm, (ends_own, ends_got), att_w0)
    sib0 = [swap_c(a0), swap_c(o0)]
    for _ in range(plan.bits - 2):
        have = [jnp.concatenate(x, axis=0) for x in zip(have, got)]
        got = doubled(have, part)
    sib0 += list(att_w1)
    second = got
    have = [jnp.concatenate(x, axis=0) for x in zip(have, got)]
    got = after(swap_x(part), *sib0, *first_got)
    part, r0, ucn0, gp0 = run_f2(plan, 0, idx, prm, bf, h0, part, got, mlp_w0)
    have_sib = [swap_c(after(x, part)) for x in have]
    ucn0_sib = swap_c(ucn0)
    got = after(swap_x(part), ucn0_sib, *second)
    more = doubled(have, got)
    part, q1, k1, v1, p1, o1, a1, h1 = run_f1(plan, 1, idx, prm, (r0, part, got, v0), att_w1)
    sib1 = [swap_c(a1), swap_c(o1)]
    got = after(swap_x(part), *sib1)
    parts = [x for t in range(2) for x in (have[t], more[t], have_sib[t], swap_c(after(more[t], part)))]
    mlp_w1 = run_late(plan, idx, parts)
    y_part, r1, ucn1, gp1, oo0 = run_f2(plan, 1, idx, prm, bf, h1, part, got, mlp_w1, o0, sib0[1])

    class Sum:
        def __init__(self, g):
            self.first, self.keep = g[:2], g[2:]
            self.rows = [x.shape[0] // hc for x in self.keep]
            self.came = [[], []]

        def terms(self, t, low):
            return [(self.keep[t], low * self.rows[t])] + [(x, at + low * self.rows[t]) for x, at in self.came[t]]

        def bit(self, t):
            return plan.orders[t][plan.bits - 1 - len(self.came[t])]

        def segment(self, t):
            steps = len(self.came[t])
            if steps == 0:
                return [(self.first[t], 0)], self.first[t].shape[0]
            low = count >> (steps + 1)
            return self.terms(t, low), low * self.rows[t]

    def one_round(sums, *others, lock=True):
        sums = [x for x in sums if len(x.came[0]) < plan.bits]
        if not sums:
            return []
        by_bit = {}
        for x in sums:
            for t in range(2):
                by_bit.setdefault(x.bit(t), []).append((x, t, x.segment(t)))
        bits = sorted(by_bit)
        if all(len(by_bit[b]) == 1 and not by_bit[b][0][0].came[0] for b in bits):
            outs = [by_bit[b][0][2][0][0][0] for b in bits]
        else:
            outs = run_round([[seg for _, _, seg in by_bit[b]] for b in bits])
        got = []
        for b, out in zip(bits, outs):
            here = swap_d(after(out, *others, *(one_round.last if lock else ())), b)
            row = 0
            for x, t, (_, rows_) in by_bit[b]:
                x.came[t].append((here, row))
                row += rows_
            got.append(here)
        one_round.last = got
        return got

    one_round.last = []

    def over_pairs(x):
        total = x
        for n in range(1, groups // 2):
            total = total + lax.ppermute(x, "group", [(i, (i + 2 * n) % groups) for i in range(groups)])
        return total

    part, e, z_keep, z_send, e_send, s2_1, sbf_1 = run_b2(plan, 1, idx, prm, gp1, r1, (cot,), mlp_w1)
    got = swap_x(part)
    mlp1 = Sum(run_g2(plan, idx, ucn1, swap_c(ucn1), e, swap_c(e_send), z_keep, swap_c(z_send)))
    got = after(got, *mlp1.first)
    one_round([mlp1])
    part, dr, keep, send, s1_1, dv1 = run_b1(plan, 1, idx, prm, (cot, part, got, r1, h1, q1, k1, v1, p1), att_w1)
    o1_far = swap_x(after(o1, got))
    got = swap_x(part)
    acts = [a1, sib1[0], o1, sib1[1], o1_far, swap_c(o1_far)]
    att1 = Sum(run_g1(plan, 1, idx, acts, keep, swap_c(send), ()))
    got = after(got, *att1.first)
    came = one_round([mlp1, att1])
    part, e, z_keep, z_send, e_send, s2_0, sbf_0 = run_b2(plan, 0, idx, prm, gp0, r0, (dr, part, got, h1), mlp_w0)
    got = swap_x(part)
    mlp0 = Sum(run_g2(plan, idx, ucn0, ucn0_sib, e, swap_c(e_send), z_keep, swap_c(z_send)))
    got = after(got, *mlp0.first, *came)
    came = one_round([mlp1, att1, mlp0])
    oo_far = swap_x(after(oo0, got))
    part, dr, keep, send, s1_0 = run_b1(plan, 0, idx, prm, (e, part, got, r0, h0, q0, k0, v0, p0, dv1), att_w0)
    acts = [a0, sib0[0], o0, sib0[1], oo_far, oo_far]
    att0 = Sum(run_g1(plan, 0, idx, acts, keep, swap_c(after(send, came[-1])), (s2_0, s1_0, sbf_0, s2_1, s1_1, sbf_1)))
    sums = [att0, att1, mlp0, mlp1]
    x_got = swap_x(after(part, oo_far))
    y_got = swap_x(after(y_part, oo_far))
    res = run_ends(plan, idx, (prm, r1, y_part, y_got, dr, part, x_got, h0)).reshape(1, seqs, seq, width)
    one_round(sums)
    for _ in range(plan.bits - 2):
        one_round(sums, x_got, y_got)

    def ending(sums, first, *others):
        own, send = (over_pairs(x) for x in run_pick(plan, after(idx, *first), [(x.terms(t, 0), x.rows[t]) for t in range(2) for x in sums]))
        far = after(swap_x(send), *others)
        return [own, swap_c(own), far, swap_c(far)], send

    arrived = one_round.last
    one_round(sums, lock=False)
    e_mlp, _ = ending((mlp0, mlp1), arrived)
    o_fc, o_proj = run_finish_mlp(plan, idx, e_mlp)
    e_att, sent = ending((att0, att1), (), o_fc, res)
    o_qk, o_val, o_out, o_gain, o_shift, o_bf, o_vs = run_finish_att(plan, idx, e_att + [sent, swap_c(sent)])

    return (res, o_qk[None], o_val, o_out[None], o_fc[None], o_proj[None], o_gain[None], o_shift[None], o_bf, o_vs[0])


def solution(mesh):
    placed = (
        P("section", ("group", "dp"), None, None),
        P("section", "dp", None),
        P("dp", None),
        P("section", "dp", None),
        P("section", "dp", None),
        P("section", "dp", None),
        P("section", None, "dp"),
        P("section", None, "dp"),
        P("section", "dp"),
        P("dp"),
    )
    return jax.shard_map(per_device, mesh=mesh, in_specs=placed, out_specs=placed, check_vma=False)
```
